32 devices in a mesh: pos: 8 (over z, x), batch: 4 (over y, core).
Axes of the slice: x: 2, y: 2, z: 4, core: 2. Of those that a mesh axis runs over, the one named last changes fastest.
Arguments:
- tokens: bfloat16 [1024, 8, 768], P('pos', 'batch'), may hold values from -6 to 6
- seq_lens: int32 [8], P('batch'), may hold values from 256 to 1024, as said below
- mixer: bfloat16 [12, 1024, 1024], P(None, 'pos', 'batch'), may hold values from -8 to 8
- gain_attn: bfloat16 [768], P(('pos', 'batch')), may hold values from 0.099609375 to 1.8984375
- w_value: bfloat16 [768, 768], P(('pos', 'batch')), may hold values from -0.21875 to 0.21875
- w_output: bfloat16 [768, 768], P(('pos', 'batch')), may hold values from -1.25 to 1.25
- gain_ffn: bfloat16 [768], P(('pos', 'batch')), may hold values from 0.099609375 to 1.8984375
- w_in: bfloat16 [768, 3072], P(('pos', 'batch')), may hold values from -0.21875 to 0.21875
- w_out: bfloat16 [3072, 768], P(('pos', 'batch')), may hold values from -0.109375 to 0.109375
- cotangent: bfloat16 [1024, 8, 768], P('pos', 'batch'), may hold values from -6 to 6
Outputs:
- output: bfloat16 [1024, 8, 768], P('pos', 'batch')
- grad_tokens: float32 [1024, 8, 768], P('pos', 'batch')
- grad_mixer: float32 [12, 1024, 1024], P(None, 'pos', 'batch')
- grad_gain_attn: float32 [768], P(('pos', 'batch'))
- grad_w_value: float32 [768, 768], P(('pos', 'batch'))
- grad_w_output: float32 [768, 768], P(('pos', 'batch'))
- grad_gain_ffn: float32 [768], P(('pos', 'batch'))
- grad_w_in: float32 [768, 3072], P(('pos', 'batch'))
- grad_w_out: float32 [3072, 768], P(('pos', 'batch'))
- resid_rms: float32 [1024, 8], P('pos', 'batch')
- branch_rms: float32 [1024, 8], P('pos', 'batch')
The draws below stay inside these ranges and needn't reach their ends.
Inputs may be any that keep to these rules, and one draw needn't show every extreme that they name: `seq_lens`: each slot holds 256 or 1024 tokens; of the 2 slots of one index of batch exactly half hold 1024.
All inputs are finite; a program needn't handle non-finite values.
Results may differ from the reference program's by a relative error of at most 0.012.
Values may be sent and summed in bfloat16 or wider, within the bound.
A program may use at most 256 MiB of HBM per device.

```python
import jax
import jax.numpy as jnp
from jax import lax

D = 768
HEADS = 12
HEAD_DIM = 64
FF = 3072
SEQ_DEV = 2
SHORT = 256
LONG = 1024
SEQS = 8


def draw_seq_lens(key, part):
    key = jax.random.fold_in(key, 11)
    groups = SEQS // SEQ_DEV
    group_keys = jax.random.split(key, groups)
    ranking = jax.vmap(lambda one_key: jax.random.permutation(one_key, SEQ_DEV))(group_keys)
    lengths = jnp.where(ranking < SEQ_DEV // 2, LONG, SHORT)
    return lengths.reshape(SEQS).astype(jnp.int32)


def steps_of(stream_key, extent, cuts, least, top_value):
    factor_of, own = 1.0, jax.random.fold_in(stream_key, 6)
    for axis_at, parts in cuts:
        draws = jnp.exp(jax.random.uniform(jax.random.fold_in(own, axis_at), (parts,), jnp.float32, least / len(cuts), top_value / len(cuts)))
        factor_of = factor_of * jnp.repeat(draws, extent[axis_at] // parts).reshape([-1 if axis == axis_at else 1 for axis in range(len(extent))])
    return factor_of


def noise(key, dims, deviation, most, pieces=(), held_as=jnp.bfloat16):
    gain = steps_of(key, dims, pieces, -0.22, 0.18) if pieces else 1.0
    drawn = jax.random.normal(key, dims, jnp.float32) * deviation * gain
    return jnp.minimum(jnp.maximum(drawn, -most), most).astype(held_as)


def setup_inputs(seed: int = 0) -> dict:
    key_of = jax.random.split(jax.random.key(seed), 11)
    tokens = noise(key_of[0], (LONG, SEQS, D), 1.0, 6.0, ((0, 8), (1, 4)))
    seq_lens = draw_seq_lens(jax.random.fold_in(key_of[10], 71), 0)
    mixer = noise(key_of[2], (HEADS, LONG, LONG), 2.0, 8.0, ((1, 8), (2, 4)))
    gain_attn = jnp.clip(1.0 + 0.18 * jax.random.normal(key_of[3], (D,), jnp.float32), 0.099609375, 1.8984375).astype(jnp.bfloat16)
    w_value = noise(key_of[4], (D, D), D ** -0.5, 0.21875, ((0, 32),))
    w_output = noise(key_of[5], (D, D), 24 ** -0.5, 1.25, ((0, 32),))
    gain_ffn = jnp.clip(1.0 + 0.18 * jax.random.normal(key_of[6], (D,), jnp.float32), 0.099609375, 1.8984375).astype(jnp.bfloat16)
    w_in = noise(key_of[7], (D, FF), D ** -0.5, 0.21875, ((0, 32),))
    w_out = noise(key_of[8], (FF, D), FF ** -0.5, 0.109375, ((0, 32),))
    cotangent = noise(key_of[9], (LONG, SEQS, D), 1.0, 6.0, ((0, 8), (1, 4)))
    return dict(tokens=tokens, seq_lens=seq_lens, mixer=mixer, gain_attn=gain_attn, w_value=w_value, w_output=w_output, gain_ffn=gain_ffn, w_in=w_in, w_out=w_out, cotangent=cotangent)


EPSILON = 1e-06
PRECISE = lax.Precision.HIGHEST

@jax.custom_vjp
def low(v):
    return lax.optimization_barrier(v.astype(jnp.bfloat16)).astype(jnp.float32)

@jax.custom_vjp
def low_back(v):
    return v

def low_keep(v):
    return (low(v), None)

def low_pass(kept, grad):
    return (grad,)

def back_keep(v):
    return (v, None)

def back_low(kept, grad):
    return (low(grad),)
low.defvjp(low_keep, low_pass)
low_back.defvjp(back_keep, back_low)

def norm_apply(values, gain_vec):
    inv_rms = lax.rsqrt(lax.optimization_barrier(jnp.mean(values * values, axis=-1, keepdims=True)) + EPSILON)
    return values * inv_rms * gain_vec

def layer_fn(tokens_f, mixer_f, gain_first, value_mat, output_mat, gain_second, in_mat, out_mat, seq_lens):
    positions = jnp.arange(LONG, dtype=jnp.int32)

    def one_sequence(seq_x, length):
        live_col = (positions < length).astype(jnp.float32)[:, None]
        normed_one = low(norm_apply(seq_x, gain_first))
        value = low_back(low(jnp.dot(normed_one, value_mat, precision=PRECISE)))
        keep_cols = positions[None, None, :] < length
        masked = jnp.where(keep_cols, mixer_f, -1e+30)
        top_score = lax.optimization_barrier(jnp.max(masked, axis=-1, keepdims=True))
        expon_vals = jnp.exp(masked - top_score) * keep_cols.astype(jnp.float32)
        prob_low = low(expon_vals / lax.optimization_barrier(jnp.sum(expon_vals, axis=-1, keepdims=True)))
        heads_v = value.reshape(LONG, HEADS, HEAD_DIM)
        mixed = jnp.einsum('hij,jhe->ihe', prob_low, heads_v, precision=PRECISE).reshape(LONG, D) * live_col
        attn_in = low_back(low(mixed))
        branch = low_back(jnp.dot(attn_in, output_mat, precision=PRECISE))
        mid_resid = seq_x + branch
        normed_two = low(norm_apply(mid_resid, gain_second))
        up_proj = low_back(jnp.dot(normed_two, in_mat, precision=PRECISE))
        hidden = low(jax.nn.gelu(up_proj, approximate=False))
        summed_out = (mid_resid + jnp.dot(hidden, out_mat, precision=PRECISE)) * live_col
        resid_rms = jnp.sqrt(lax.optimization_barrier(jnp.mean(mid_resid * mid_resid, axis=-1)) + EPSILON) * live_col[:, 0]
        branch_rms = jnp.sqrt(lax.optimization_barrier(jnp.mean(branch * branch, axis=-1)) + EPSILON) * live_col[:, 0]
        return (summed_out, resid_rms, branch_rms)
    per_seq = jax.checkpoint(one_sequence)

    def scan_body(carried, inputs):
        return (carried, per_seq(inputs[0], inputs[1]))
    start_carry = jnp.zeros((), jnp.float32)
    _, results = lax.scan(scan_body, start_carry, (jnp.swapaxes(tokens_f, 0, 1), seq_lens))
    summed_out, resid_rms, branch_rms = results
    return (jnp.swapaxes(summed_out, 0, 1), (jnp.swapaxes(resid_rms, 0, 1), jnp.swapaxes(branch_rms, 0, 1)))

def reference(tokens, seq_lens, mixer, gain_attn, w_value, w_output, gain_ffn, w_in, w_out, cotangent):
    floats = [arr.astype(jnp.float32) for arr in (tokens, mixer, gain_attn, w_value, w_output, gain_ffn, w_in, w_out)]

    def forward(tokens_f, mixer_f, gain_first, value_mat, output_mat, gain_second, in_mat, out_mat):
        return layer_fn(tokens_f, mixer_f, gain_first, value_mat, output_mat, gain_second, in_mat, out_mat, seq_lens)
    summed_out, back_fn, extras = jax.vjp(forward, *floats, has_aux=True)
    grads = back_fn(cotangent.astype(jnp.float32))
    resid_rms, branch_rms = extras
    return (summed_out.astype(jnp.bfloat16), grads[0], grads[1], grads[2], grads[3], grads[4], grads[5], grads[6], grads[7], resid_rms, branch_rms)
```

```python
import functools

import jax
import jax.numpy as jnp
from jax import lax
from jax.experimental import pallas as pl
from jax.experimental.pallas import tpu as pltpu
from jax.sharding import PartitionSpec as P

SHORT = 256


EPSILON = 1e-06


def norm_apply(values, gain_vec):
    inv_rms = lax.rsqrt(jnp.mean(values * values, axis=-1, keepdims=True) + EPSILON)
    return values * inv_rms * gain_vec


def gelu_exact(values):
    return jax.nn.gelu(values, approximate=False)


def row_stats(scores):
    top_score = jnp.max(scores, axis=-1)
    return top_score + jnp.log(jnp.sum(jnp.exp(scores - top_score[..., None]), axis=-1))


def contract_rows(left, right):
    return lax.dot_general(
        left, right, (((0,), (0,)), ((), ())), preferred_element_type=jnp.float32
    )


def contract_cols(left, right):
    return lax.dot_general(
        left, right, (((1,), (1,)), ((), ())), preferred_element_type=jnp.float32
    )


def per_device(
    tokens, seq_lens, mixer, gain_attn, w_value, w_output, gain_ffn, w_in, w_out, cotangent
):
    value_mat, output_mat, in_mat, out_mat, gain_one, gain_two = (
        lax.all_gather(w_value, ("pos", "batch"), axis=0, tiled=True),
        lax.all_gather(w_output, ("pos", "batch"), axis=0, tiled=True),
        lax.all_gather(w_in, ("pos", "batch"), axis=0, tiled=True),
        lax.all_gather(w_out, ("pos", "batch"), axis=0, tiled=True),
        lax.all_gather(gain_attn, ("pos", "batch"), axis=0, tiled=True),
        lax.all_gather(gain_ffn, ("pos", "batch"), axis=0, tiled=True),
    )
    rows_r = lax.all_gather(mixer, "batch", axis=2, tiled=True)
    head_count = rows_r.shape[0]
    long_len = rows_r.shape[2]
    row_count, slot_count, width = tokens.shape
    head_dim = width // head_count
    tok_count = row_count * slot_count
    start_row = lax.axis_index("pos") * row_count
    positions = start_row + jnp.arange(row_count, dtype=jnp.int32)
    live_mask = (positions[:, None] < seq_lens[None, :]).astype(jnp.float32)
    live_col = live_mask.reshape(tok_count, 1)
    is_long = seq_lens > SHORT
    gain_first = gain_one.astype(jnp.float32)
    gain_second = gain_two.astype(jnp.float32)
    x_float = tokens.astype(jnp.float32).reshape(tok_count, width)
    normed_one = norm_apply(x_float, gain_first).astype(jnp.bfloat16)
    value = jnp.dot(normed_one, value_mat, preferred_element_type=jnp.float32).astype(jnp.bfloat16)
    value = value.reshape(row_count, slot_count, width)
    lse_long = row_stats(rows_r.astype(jnp.float32))
    head_cols = rows_r[:, :, :SHORT].astype(jnp.float32)
    lse_short = row_stats(head_cols)
    prob_head = jnp.exp(head_cols - lse_short[..., None])

    def prob_block(block, lse_l, lse_s, col_pos):
        prob_long = jnp.exp(block - lse_l[..., None])
        prob_short = jnp.where(col_pos < SHORT, jnp.exp(block - lse_s[..., None]), 0.0)
        return jnp.where(is_long[:, None, None, None], prob_long[None], prob_short[None])

    def slot_probs(piece_len):
        columns = rows_r.astype(jnp.float32)
        col_pos = jnp.arange(piece_len, dtype=jnp.int32)
        return prob_block(columns, lse_long, lse_short, col_pos)

    portion = lax.all_gather(value, "pos", axis=0, tiled=True)
    piece_len = portion.shape[0]
    prob_b = slot_probs(piece_len).astype(jnp.bfloat16)
    piece_vals = portion.reshape(piece_len, slot_count, head_count, head_dim)
    mixed = jnp.einsum("shin,nshe->ishe", prob_b, piece_vals, preferred_element_type=jnp.float32)
    attn_in = (mixed * live_mask[:, :, None, None]).astype(jnp.bfloat16).reshape(tok_count, width)
    branch = jnp.dot(attn_in, output_mat, preferred_element_type=jnp.float32)
    mid_resid = x_float + branch
    normed_two = norm_apply(mid_resid, gain_second).astype(jnp.bfloat16)
    up_proj = jnp.dot(normed_two, in_mat, preferred_element_type=jnp.float32)
    hidden = gelu_exact(up_proj).astype(jnp.bfloat16)
    summed_out = mid_resid + jnp.dot(hidden, out_mat, preferred_element_type=jnp.float32)
    output = (summed_out * live_col).astype(jnp.bfloat16).reshape(row_count, slot_count, width)
    resid_rms = (
        jnp.sqrt(jnp.mean(mid_resid * mid_resid, axis=-1) + EPSILON).reshape(row_count, slot_count)
        * live_mask
    )
    branch_rms = (
        jnp.sqrt(jnp.mean(branch * branch, axis=-1) + EPSILON).reshape(row_count, slot_count)
        * live_mask
    )
    dfinal = cotangent.reshape(tok_count, width) * live_col.astype(jnp.bfloat16)
    grad_w_out = contract_rows(hidden, dfinal)
    dhidden = contract_cols(dfinal, out_mat)
    _, gelu_back = jax.vjp(gelu_exact, up_proj)
    dupper = gelu_back(dhidden)[0].astype(jnp.bfloat16)
    grad_w_in = contract_rows(normed_two, dupper)
    d_normed_two = contract_cols(dupper, in_mat)
    _, norm_back_two = jax.vjp(norm_apply, mid_resid, gain_second)
    d_mid_norm, grad_gain_ffn = norm_back_two(d_normed_two)
    d_mid = dfinal.astype(jnp.float32) + d_mid_norm
    dbranch = d_mid.astype(jnp.bfloat16)
    grad_w_output = contract_rows(attn_in, dbranch)
    d_attn = contract_cols(dbranch, output_mat).astype(jnp.bfloat16)
    d_attn = d_attn.reshape(row_count, slot_count, head_count, head_dim)
    portion = lax.all_gather(value, "pos", axis=0, tiled=True)
    piece_len = portion.shape[0]
    prob_f = slot_probs(piece_len)
    piece_vals = portion.reshape(piece_len, slot_count, head_count, head_dim)
    d_prob = jnp.einsum("ishe,nshe->shin", d_attn, piece_vals, preferred_element_type=jnp.float32)
    weighted = prob_f * d_prob
    grad_acc = jnp.sum(weighted, axis=0)
    grad_acc, delta_all = (grad_acc, jnp.sum(weighted, axis=-1))
    delta_long = jnp.sum(jnp.where(is_long[:, None, None], delta_all, 0.0), axis=0)
    delta_short = jnp.sum(jnp.where(is_long[:, None, None], 0.0, delta_all), axis=0)
    slots_here = d_attn.shape[1]
    col_block = lax.all_to_all(rows_r, "pos", split_axis=2, concat_axis=1, tiled=True)
    lse_all_long = lax.all_gather(lse_long, "pos", axis=1, tiled=True)
    lse_all_short = lax.all_gather(lse_short, "pos", axis=1, tiled=True)
    portion = lax.all_gather(d_attn, "pos", axis=0, tiled=True)
    piece_len = portion.shape[0]
    block = col_block.astype(jnp.float32)
    lse_l = lse_all_long
    lse_s = lse_all_short
    prob_b = prob_block(block, lse_l, lse_s, positions).astype(jnp.bfloat16)
    term = jnp.einsum("shij,ishe->jshe", prob_b, portion, preferred_element_type=jnp.float32)
    dvalue = term.reshape(row_count, slots_here, width)
    full_long = jnp.exp(rows_r.astype(jnp.float32) - lse_long[..., None])
    grad_rows = grad_acc - full_long * delta_long[..., None]
    correction = prob_head * delta_short[..., None]
    grad_rows = grad_rows - jnp.pad(correction, ((0, 0), (0, 0), (0, long_len - SHORT)))
    dvalue_b = dvalue.astype(jnp.bfloat16).reshape(tok_count, width)
    grad_w_value = contract_rows(normed_one, dvalue_b)
    d_normed_one = contract_cols(dvalue_b, value_mat)
    _, norm_back_one = jax.vjp(norm_apply, x_float, gain_first)
    d_x_norm, grad_gain_attn = norm_back_one(d_normed_one)
    grad_tokens = (d_mid + d_x_norm).reshape(row_count, slot_count, width)
    grad_mixer = lax.psum_scatter(
        grad_rows.astype(jnp.bfloat16), "batch", scatter_dimension=2, tiled=True
    ).astype(jnp.float32)
    reduced = (
        lax.psum_scatter(grad_w_value, ("pos", "batch"), scatter_dimension=0, tiled=True),
        lax.psum_scatter(grad_w_output, ("pos", "batch"), scatter_dimension=0, tiled=True),
        lax.psum_scatter(grad_w_in, ("pos", "batch"), scatter_dimension=0, tiled=True),
        lax.psum_scatter(grad_w_out, ("pos", "batch"), scatter_dimension=0, tiled=True),
        lax.psum_scatter(grad_gain_attn, ("pos", "batch"), scatter_dimension=0, tiled=True),
        lax.psum_scatter(grad_gain_ffn, ("pos", "batch"), scatter_dimension=0, tiled=True),
    )
    return (
        output,
        grad_tokens,
        grad_mixer,
        reduced[4],
        reduced[0],
        reduced[1],
        reduced[5],
        reduced[2],
        reduced[3],
        resid_rms,
        branch_rms,
    )


BF = jnp.bfloat16
F32 = jnp.float32
MESH = pl.DeviceIdType.MESH
HEAD = 64
BATCH = 4
LANE = 4 * HEAD


def dot(left, right):
    return jnp.dot(left, right, preferred_element_type=F32)


def dot_tn(left, right):
    return lax.dot_general(left, right, (((0,), (0,)), ((), ())), preferred_element_type=F32)


def dot_nt(left, right):
    return lax.dot_general(left, right, (((1,), (1,)), ((), ())), preferred_element_type=F32)


def up16(rows):
    return -(-rows // 16) * 16


class Sizes:
    def __init__(self, pos, tokens, mixer, w_value, w_in, w_out):
        self.n = pos
        self.r, _, self.d = tokens.shape
        self.heads, _, self.cb = mixer.shape
        self.long = pos * self.r
        self.hb = self.heads // BATCH
        self.fh = self.hb * HEAD
        self.rw = w_value.shape[0]
        self.rf = w_out.shape[0]
        self.ff = w_in.shape[1]
        self.fc = self.ff // BATCH
        self.rp = up16(self.rw + 8)
        self.gr = self.d // 256
        self.wr = BATCH * self.rw + 16
        self.sems = 22 * pos + 90


def fits(pos, batch, tokens, mixer, w_value, w_in, w_out):
    r, _, d = tokens.shape
    heads = mixer.shape[0]
    rw, rf = w_value.shape[0], w_out.shape[0]
    return (
        batch == BATCH
        and pos >= 4
        and pos % 2 == 0
        and r % 128 == 0
        and SHORT == 2 * r
        and heads % BATCH == 0
        and heads * HEAD == d
        and d % 256 == 0
        and 2 * (d // 256) <= 8
        and rw % 8 == 0
        and rw % 16 == 8
        and rf % 32 == 0
        and (BATCH * rw) % 32 == 0
        and (w_in.shape[1] // BATCH) % 256 == 0
        and SHORT == mixer.shape[2]
    )


class Net:
    def __init__(self, n, sems):
        self.n = n
        self.sems = sems
        self.used = 0
        self.sent = []
        p, b = lax.axis_index("pos"), lax.axis_index("batch")
        self.p, self.b = p, b
        self.rho = self.ring(p)
        self.right = (self.place(lax.rem(self.rho + 1, n)), b)
        self.left = (self.place(lax.rem(self.rho + n - 1, n)), b)
        self.core_b = b + 1 - 2 * lax.rem(b, 2)
        self.y_b = lax.rem(b + 2, BATCH)
        self.far_b = BATCH - 1 - b
        self.core = (p, self.core_b)
        self.y = (p, self.y_b)
        self.far = (p, self.far_b)
        self.short = p < 2

    def ring(self, p):
        return jnp.where(lax.rem(p, 2) == 0, p // 2, self.n - 1 - p // 2)

    def place(self, rho):
        half = self.n // 2
        return jnp.where(rho < half, 2 * rho, 2 * (self.n - 1 - rho) + 1)

    def at(self, step):
        return self.place(lax.rem(self.rho + step + 2 * self.n, self.n))

    def sem(self):
        self.used += 1
        return self.sems.at[self.used - 1]


class Copy:
    def __init__(self, net, device):
        self.net, self.device = net, device
        self.send, self.recv = net.sem(), net.sem()

    def of(self, src, dst):
        return pltpu.make_async_remote_copy(
            src_ref=src, dst_ref=dst, send_sem=self.send, recv_sem=self.recv,
            device_id=self.device, device_id_type=MESH,
        )

    def start(self, src, dst):
        self.of(src, dst).start()
        self.finish = lambda: self.of(src, src).wait_send()
        self.net.sent.append(self)

    def arrive(self, land):
        self.of(land, land).wait_recv()

    def start_live(self, src, dst):
        net = self.net
        pl.when(net.short)(lambda: self.of(src(2), dst(2)).start())
        pl.when(jnp.logical_not(net.short))(lambda: self.of(src(1), dst(1)).start())

        def finish():
            pl.when(net.short)(lambda: self.of(src(2), src(2)).wait_send())
            pl.when(jnp.logical_not(net.short))(lambda: self.of(src(1), src(1)).wait_send())

        self.finish = finish
        net.sent.append(self)

    def arrive_live(self, land):
        net = self.net
        pl.when(net.short)(lambda: self.of(land(2), land(2)).wait_recv())
        pl.when(jnp.logical_not(net.short))(lambda: self.of(land(1), land(1)).wait_recv())


class Exchange:
    def __init__(self, net, src, land):
        self.net, self.src, self.land = net, src, land
        self.copies = [(Copy(net, d), j) for d, j in ((net.y, net.y_b), (net.far, net.far_b), (net.core, net.core_b))]

    def start(self):
        for copy, j in self.copies:
            copy.start(self.src.at[j], self.land.at[self.net.b])
        self.land[self.net.b] = self.src[self.net.b]

    def done(self):
        for copy, j in self.copies:
            copy.arrive(self.land.at[j])


class Spread:
    def __init__(self, net, slot):
        self.net, self.slot = net, slot
        self.by_y, self.by_core, self.relay = Copy(net, net.y), Copy(net, net.core), Copy(net, net.core)

    def start(self):
        own = functools.partial(self.slot, self.net.b)
        self.by_y.start_live(own, own)
        self.by_core.start_live(own, own)

    def mid(self):
        came = functools.partial(self.slot, self.net.y_b)
        self.by_y.arrive_live(came)
        self.relay.start_live(came, came)

    def done(self):
        self.by_core.arrive_live(functools.partial(self.slot, self.net.core_b))
        self.relay.arrive_live(functools.partial(self.slot, self.net.far_b))


class Collect:
    def __init__(self, net, part, mine, other, stage, across):
        self.net, self.part, self.mine, self.other, self.stage, self.across = net, part, mine, other, stage, across
        self.to_other, self.to_mine, self.by_y = Copy(net, net.core), Copy(net, net.core), Copy(net, net.y)

    def start(self):
        net = self.net
        self.to_other.start_live(lambda k: self.part.at[0:k, net.far_b], lambda k: self.other.at[0:k])
        self.to_mine.start_live(lambda k: self.part.at[0:k, net.core_b], lambda k: self.mine.at[0:k])

    def mid(self):
        net = self.net
        self.to_other.arrive_live(lambda k: self.other.at[0:k])

        def add(g):
            self.stage[g] = (self.part[g, net.y_b].astype(F32) + self.other[g].astype(F32)).astype(BF)

        add(0)
        pl.when(net.short)(lambda: add(1))
        self.by_y.start_live(lambda k: self.stage.at[0:k], lambda k: self.across.at[0:k])

    def done(self):
        self.to_mine.arrive_live(lambda k: self.mine.at[0:k])
        self.by_y.arrive_live(lambda k: self.across.at[0:k])

    def sent(self):
        for copy in (self.to_other, self.to_mine):
            copy.finish()
            self.net.sent.remove(copy)

    def value(self, g):
        return self.part[g, self.net.b].astype(F32) + self.mine[g].astype(F32) + self.across[g].astype(F32)


class Gather:
    def __init__(self, net, slot, first, second):
        self.net, self.slot, self.halves = net, slot, (first, second)
        self.steps, self.next = net.n // 2, 0
        self.copies = [[Copy(net, d) for _ in range(self.steps)] for d in (net.right, net.left)]

    def hop(self):
        net, t = self.net, self.next
        if t == self.steps:
            return
        self.next += 1
        for way, sign in ((0, -1), (1, 1)):
            came = self.slot(net.at(sign * t))
            if t:
                self.copies[way][t - 1].arrive(came)
            if t == self.steps - 1:
                came = self.halves[way](net.at(sign * t))
            self.copies[way][t].start(came, came)

    def done(self):
        while self.next < self.steps:
            self.hop()
        for way in (0, 1):
            self.copies[way][-1].arrive(self.halves[way](self.net.at(self.steps)))


class Scatter:
    def __init__(self, net, own, held, came, cut):
        self.net, self.own, self.held, self.came, self.cut = net, own, held, came, cut
        self.steps, self.next = net.n // 2, 0
        self.rows = held.shape[-2]
        self.copies = [[Copy(net, d) for _ in range(self.steps)] for d in (net.right, net.left)]

    def part(self, ref, way, t):
        lead = (slice(None),) * (len(ref.shape) - 4)
        span = (slice(0, self.cut), slice(self.cut, self.rows))[way]
        return ref.at[(way, t) + lead + (span, slice(None))]

    def hop(self):
        net, t = self.net, self.next
        if t == self.steps:
            return
        self.next += 1
        if t == 0:
            value = self.own(net.at(self.steps))
        for way, sign in ((0, 1), (1, -1)):
            if t == 0:
                span = (slice(0, self.cut), slice(self.cut, self.rows))[way]
                self.part(self.held, way, 0)[...] = value[..., span, :].astype(BF)
                self.copies[way][0].start(self.part(self.held, way, 0), self.part(self.came, way, 0))
                continue
            value = self.own(net.at(sign * (self.steps - t)))
            if t == 1:
                here = self.part(self.came, way, 0)
                self.copies[way][0].arrive(here)
                self.held[way, 1] = value.astype(BF)
                span = (slice(0, self.cut), slice(self.cut, self.rows))[way]
                self.part(self.held, way, 1)[...] = (value[..., span, :] + here[...].astype(F32)).astype(BF)
            else:
                self.copies[way][t - 1].arrive(self.came.at[way, t - 1])
                self.held[way, t] = (value + self.came[way, t - 1].astype(F32)).astype(BF)
            self.copies[way][t].start(self.held.at[way, t], self.came.at[way, t])

    def done(self):
        while self.next < self.steps:
            self.hop()
        last = self.steps - 1
        for way in (0, 1):
            self.copies[way][last].arrive(self.came.at[way, last])
        return self.own(self.net.p) + self.came[0, last].astype(F32) + self.came[1, last].astype(F32)


def unit(values):
    inv = lax.rsqrt(jnp.mean(values * values, axis=-1, keepdims=True) + EPSILON)
    return values * inv, inv


def heads_of(rows, z):
    return [
        jnp.concatenate([rows[s * z.r : (s + 1) * z.r, h * HEAD : (h + 1) * HEAD] for s in range(BATCH)], axis=-1)
        for h in range(z.hb)
    ]


def slots_of(by_head, z):
    return [
        jnp.concatenate([by_head[h][:, s * HEAD : (s + 1) * HEAD] for h in range(z.hb)], axis=-1)
        for s in range(BATCH)
    ]


def scratch(z):
    n, r, d, half = z.n, z.r, z.d, z.n // 2
    vm = pltpu.VMEM
    slots, own = (2, BATCH, r, d), (2, r, d)

    def ring(*shape):
        return vm((2, half) + shape, BF)

    return dict(
        x=vm(slots, BF), c=vm(slots, BF), mx=vm((BATCH, z.hb, r, z.cb), BF),
        wvp=vm((BATCH, z.rp, 256), BF), wop=vm((BATCH, z.rp, d), BF), wip=vm((BATCH, z.rp, z.fc), BF),
        wvg=vm((n, z.wr, 256), BF), wv=vm((d, z.fh), BF), wo=vm((d, d), BF), wi=vm((d, z.fc), BF), wu=vm((z.fc, d), BF),
        gain=vm((2, 1, d), F32),
        h1=vm(slots, BF), vl=vm((z.hb, z.long, LANE), BF), vs=vm((z.hb, SHORT, LANE), BF),
        pf=vm((z.hb, r, z.long), F32), pb=vm((z.hb, r, z.long), BF),
        qf=vm((z.hb, r, SHORT), F32), qb=vm((z.hb, r, SHORT), BF),
        mixed=vm((2, z.hb, r, LANE), F32), attn=vm((BATCH, 2, BATCH, r, z.fh), BF),
        mid=vm(own, F32), h2=vm(slots, BF),
        hid=vm((2, BATCH * r, z.fc), BF), dup=vm((2, BATCH * r, z.fc), BF),
        dp=vm(slots, BF), db=vm(slots, BF), dmid=vm(own, F32),
        dpb=vm((4,) + own, BF), opb=vm((4,) + own, BF), d1b=vm((4,) + own, BF),
        da=vm((2, z.hb, r, LANE), BF), dv=vm((2, BATCH * r, z.fh), BF), dvs=vm((2, z.hb, r, LANE), BF),
        gm0=vm((r, z.cb), F32),
        gu=vm((z.fc, d), F32), gi=vm((d, z.fc), F32), go=vm((z.fh, d), F32), gv=vm((d, z.fh), F32),
        gis=vm((BATCH, z.rw, z.fc), F32), gvs=vm((BATCH, z.rw, 256), F32), gos=vm((z.rw, d), F32),
        gus=ring(z.rf, d), gur=ring(z.rf, d), gir=ring(BATCH * z.rw, z.fc), gih=ring(BATCH * z.rw, z.fc),
        goh=ring(z.rp, d), gor=ring(z.rp, d), gvh=ring(BATCH * z.rw, z.fh), gvr=ring(BATCH * z.rw, z.fh),
        dvh=ring(z.hb, r, LANE), dvr=ring(z.hb, r, LANE),
        sems=pltpu.SemaphoreType.DMA((z.sems,)),
    )


def layer_kernel(z, names, *refs):
    tok, cot, mix, wv_in, wo_in, wi_in, wu_in = refs[:7]
    o_out, o_gt, o_gm, o_gv, o_go, o_gi, o_gu, o_rms = refs[7:15]
    k = dict(zip(names, refs[15:]))
    n, r, d = z.n, z.r, z.d
    rows4 = BATCH * r
    net = Net(n, k["sems"])
    p, b, short = net.p, net.b, net.short
    live = jnp.where(short, 2, 1)

    def each_live(body):
        body(0)
        pl.when(short)(lambda: body(1))

    index = n * b + p
    goal_p, goal_b = index // BATCH, lax.rem(index, BATCH)
    mine = BATCH * p + b
    from_p, from_b = lax.rem(mine, n), mine // n
    stays = index == mine

    barrier = pltpu.get_barrier_semaphore()
    for device in (net.right, net.left, net.core, net.y, net.far):
        pl.semaphore_signal(barrier, inc=1, device_id=device, device_id_type=MESH)

    @pl.when(jnp.logical_not(stays))
    def _():
        for device in ((goal_p, goal_b), (from_p, from_b)):
            pl.semaphore_signal(barrier, inc=1, device_id=device, device_id_type=MESH)

    pl.semaphore_wait(barrier, jnp.where(stays, 5, 7))

    x, c, h1 = k["x"], k["c"], k["h1"]
    ex_wv = Exchange(net, wv_in, k["wvp"])
    ex_wv.start()
    k["wop"][b] = wo_in[...]
    sp_wo = [Copy(net, dev) for dev in (net.y, net.far, net.core)]
    for copy in sp_wo:
        copy.start(wo_in, k["wop"].at[b])
    x[:, b] = tok[...]
    c[:, b] = cot[...]
    sp_x = Spread(net, lambda j, m: x.at[0:m, j])
    sp_x.start()
    ex_wi = Exchange(net, wi_in, k["wip"])
    ex_wi.start()
    wu = k["wu"]

    def span(ref, size, lo=0, hi=None):
        hi = size if hi is None else hi
        return lambda q: ref.at[pl.ds(pl.multiple_of(q * size + lo, 16), hi - lo)]

    wu[pl.ds(pl.multiple_of(p * z.rf, 16), z.rf)] = wu_in[...]
    cut_f = up16(z.rf // 2)
    ag_wu = Gather(net, span(wu, z.rf), span(wu, z.rf, 0, cut_f), span(wu, z.rf, cut_f))
    ex_mx = Exchange(net, mix, k["mx"])
    ex_mx.start()
    sp_c = Spread(net, lambda j, m: c.at[0:m, j])
    sp_c.start()

    wvp, wvg = k["wvp"], k["wvg"]
    ex_wv.done()
    weights = jnp.concatenate([wvp[j].astype(F32)[0 : z.rw] for j in range(BATCH)], axis=0)
    gains = sum(wvp[j].astype(F32)[z.rw : z.rw + 8] for j in range(BATCH))
    wvg[p] = jnp.concatenate([weights, gains, jnp.zeros_like(gains)], axis=0).astype(BF)
    cut_v = up16(z.wr // 2)
    ag_wv = Gather(net, lambda q: wvg.at[q], lambda q: wvg.at[q, 0:cut_v], lambda q: wvg.at[q, cut_v : z.wr])
    ag_wv.hop()
    ag_wu.hop()

    wo = k["wo"]
    for copy, j in zip(sp_wo, (net.y_b, net.far_b, net.core_b)):
        copy.arrive(k["wop"].at[j])
    rows_o = BATCH * z.rw
    wo[pl.ds(pl.multiple_of(p * rows_o, 16), rows_o)] = jnp.concatenate(
        [k["wop"][j].astype(F32)[0 : z.rw] for j in range(BATCH)], axis=0
    ).astype(BF)
    half_o = rows_o // 2
    cut_o = up16(half_o // 2)
    core = lax.rem(b, 2)

    def wo_span(lo, hi, which=None):
        which = core if which is None else which
        return lambda q: wo.at[pl.ds(pl.multiple_of(q * rows_o + which * half_o + lo, 16), hi - lo)]

    ag_wo = Gather(net, wo_span(0, half_o), wo_span(0, cut_o), wo_span(cut_o, half_o))
    pass_wo = []

    def pass_on(steps):
        for step in steps:
            copy = Copy(net, net.core)
            q = net.at(step)
            copy.start(wo_span(0, half_o)(q), wo_span(0, half_o)(q))
            pass_wo.append((copy, wo_span(0, half_o, 1 - core)(q)))

    sp_x.mid()
    ag_wv.hop()
    ag_wo.hop()

    wi = k["wi"]
    ex_wi.done()
    wi[pl.ds(pl.multiple_of(p * rows_o, 16), rows_o)] = jnp.concatenate(
        [k["wip"][j].astype(F32)[0 : z.rw] for j in range(BATCH)], axis=0
    ).astype(BF)
    cut_i = up16(rows_o // 2)
    ag_wi = Gather(net, span(wi, rows_o), span(wi, rows_o, 0, cut_i), span(wi, rows_o, cut_i))
    sp_x.done()
    ag_wv.hop()
    ag_wv.hop()
    ag_wu.hop()
    ag_wv.done()

    table = jnp.sum(wvg[:, BATCH * z.rw : BATCH * z.rw + 16].astype(F32), axis=0)
    for g in range(2):
        k["gain"][g] = jnp.concatenate([table[g * z.gr + i : g * z.gr + i + 1] for i in range(z.gr)], axis=1)
    gain_1, gain_2 = k["gain"][0], k["gain"][1]
    k["wv"][...] = wvg[:, 0 : BATCH * z.rw, 0 : z.fh].reshape(d, z.fh)
    vl, vs = k["vl"], k["vs"]
    here = pl.ds(pl.multiple_of(p * r, 16), r)

    def values(g, into):
        for s in range(BATCH):
            h1[g, s] = (unit(x[g, s].astype(F32))[0] * gain_1).astype(BF)
        value = dot(h1[g].reshape(rows4, d), k["wv"][...]).astype(BF)
        for h, block in enumerate(heads_of(value, z)):
            into[h, here, :] = block

    values(0, vl)

    def vl_span(lo, hi):
        return lambda q: vl.at[:, pl.ds(pl.multiple_of(q * r + lo, 16), hi - lo), :]

    ag_v = Gather(net, vl_span(0, r), vl_span(0, r // 2), vl_span(r // 2, r))
    ag_v.hop()
    twin = (1 - p, b)
    other = pl.ds(pl.multiple_of((1 - p) * r, 16), r)
    cp_vs, cp_dvs = Copy(net, twin), Copy(net, twin)

    @pl.when(short)
    def _():
        values(1, vs)
        cp_vs.of(vs.at[:, here, :], vs.at[:, here, :]).start()

    ag_wo.hop()
    ag_v.hop()
    ag_wu.hop()

    pf, pb, qf, qb = k["pf"], k["pb"], k["qf"], k["qb"]
    ex_mx.done()
    for h in range(z.hb):
        total, first = 0.0, None
        for j in range(BATCH):
            e = jnp.exp(k["mx"][j, h].astype(F32))
            pf[h, :, j * z.cb : (j + 1) * z.cb] = e
            total = total + jnp.sum(e, axis=-1, keepdims=True)
            first = total if j == 0 else first
        scaled = pf[h] * (1.0 / total)

        @pl.when(short)
        def _():
            q = pf[h, :, 0:SHORT] * (1.0 / first)
            qf[h] = q
            qb[h] = q.astype(BF)

        pf[h] = scaled
        pb[h] = scaled.astype(BF)

    ag_v.hop()
    ag_wi.hop()
    ag_wo.hop()
    sp_c.mid()
    ag_v.hop()
    ag_wu.hop()
    ag_wo.hop()
    ag_wi.hop()
    pass_on([0])
    pass_on([s for t in range(1, n // 2) for s in (t, -t)])
    ag_v.done()

    mixed, attn = k["mixed"], k["attn"]

    def mix_slots(g, prob, held):
        for h in range(z.hb):
            mixed[g, h] = dot(prob[h], held[h])
        for s, block in enumerate(slots_of([mixed[g, h] for h in range(z.hb)], z)):
            attn[b, g, s] = block.astype(BF)

    mix_slots(0, pb, vl)

    @pl.when(short)
    def _():
        cp_vs.of(vs.at[:, other, :], vs.at[:, other, :]).wait_recv()
        mix_slots(1, qb, vs)

    sp_a = Spread(net, lambda j, m: attn.at[j, 0:m])
    sp_a.start()
    ag_wi.hop()
    ag_wo.done()
    pass_on([n // 2])
    ag_wu.done()
    sp_a.mid()
    sp_c.done()
    for copy, land in pass_wo:
        copy.arrive(land)
    sp_a.done()
    ag_wi.hop()

    big, mid, h2 = k["gu"], k["mid"], k["h2"]

    def branch_slots(g):
        big[0:rows4] = sum(
            dot(attn[j, g].reshape(rows4, z.fh), wo[j * z.fh : (j + 1) * z.fh]) for j in range(BATCH)
        )
        for s in range(BATCH):
            branch = big[s * r : (s + 1) * r]
            total = x[g, s].astype(F32) + branch
            square = jnp.mean(total * total, axis=-1, keepdims=True) + EPSILON
            h2[g, s] = (total * lax.rsqrt(square) * gain_2).astype(BF)

            @pl.when(b == s)
            def _():
                mid[g] = total
                o_rms[0, g] = jnp.broadcast_to(jnp.sqrt(square), (r, 128))
                size = jnp.sqrt(jnp.mean(branch * branch, axis=-1, keepdims=True) + EPSILON)
                o_rms[1, g] = jnp.broadcast_to(size, (r, 128))

    lax.fori_loop(0, live, lambda g, _: (branch_slots(g), 0)[1], 0)
    ag_wi.done()

    hid, dup, dp, op = k["hid"], k["dup"], k["dp"], h2

    def feed(g):
        left = h2[g].reshape(rows4, d)
        down = c[g].reshape(rows4, d)
        for q in range(z.fc // 256):
            cols = slice(q * 256, (q + 1) * 256)
            up = dot(left, wi[:, cols])
            cdf = 0.5 + 0.5 * lax.erf(up * 0.7071067811865476)
            hid[g, :, cols] = (up * cdf).astype(BF)
            slope = cdf + up * (jnp.exp(-0.5 * up * up) * 0.3989422804014327)
            dup[g, :, cols] = (dot_nt(down, wu[cols, :]) * slope).astype(BF)
        for q in range(d // 256):
            rows = slice(q * 256, (q + 1) * 256)
            dp[g, :, :, rows] = dot_nt(dup[g], wi[rows, :]).reshape(BATCH, r, 256).astype(BF)

    lax.fori_loop(0, live, lambda g, _: (feed(g), 0)[1], 0)

    def collect(part, bufs):
        return Collect(net, part, bufs.at[0], bufs.at[1], bufs.at[2], bufs.at[3])

    co_d = collect(dp, k["dpb"])
    co_d.start()

    def weight_grad(into, left, right, width):
        for q in range(width // 256):
            cols = slice(q * 256, (q + 1) * 256)

            def term(g):
                return dot_tn(left(g), right(g, cols))

            into[:, cols] = term(0)

            @pl.when(short)
            def _():
                into[:, cols] += term(1)

    def rows_at(ref, size):
        return lambda q: ref[pl.ds(pl.multiple_of(q * size, 8), size)]

    gu, gi = k["gu"], k["gi"]
    weight_grad(gu, lambda g: hid[g], lambda g, cols: c[g, :, :, cols].reshape(rows4, 256), d)
    rs_gu = Scatter(net, rows_at(gu, z.rf), k["gus"], k["gur"], cut_f)
    rs_gu.hop()
    co_d.mid()
    weight_grad(gi, lambda g: h2[g].reshape(rows4, d), lambda g, cols: dup[g, :, cols], z.fc)
    rs_gi = Scatter(net, rows_at(gi, rows_o), k["gih"], k["gir"], cut_i)
    rs_gi.hop()
    rs_gu.hop()

    def outs(g):
        for q in range(d // 256):
            cols = slice(q * 256, (q + 1) * 256)
            op[g, :, :, cols] = dot(hid[g], wu[:, cols]).reshape(BATCH, r, 256).astype(BF)

    lax.fori_loop(0, live, lambda g, _: (outs(g), 0)[1], 0)
    co_d.done()

    db, dmid = k["db"], k["dmid"]

    def norm_back(upper, values, gain):
        normed, inv = unit(values)
        scaled = upper * gain
        return inv * (scaled - normed * jnp.mean(scaled * normed, axis=-1, keepdims=True))

    def middle(g):
        grad = cot[g].astype(F32) + norm_back(co_d.value(g), mid[g], gain_2)
        dmid[g] = grad
        db[g, b] = grad.astype(BF)

    each_live(middle)
    sp_b = Spread(net, lambda j, m: db.at[0:m, j])
    sp_b.start()
    co_o = collect(op, k["opb"])
    co_o.start()
    rs_gi.hop()
    rs_gu.hop()
    sp_b.mid()
    co_o.mid()
    rs_gi.hop()
    sp_b.done()

    da = k["da"]
    wo_rows = pl.ds(pl.multiple_of(b * z.fh, 16), z.fh)

    def mix_back(g):
        grad = dot_nt(db[g].reshape(rows4, d), wo[wo_rows]).astype(BF)
        for h, block in enumerate(heads_of(grad, z)):
            da[g, h] = block

    each_live(mix_back)

    def dv_own(q):
        cols = pl.ds(pl.multiple_of(q * r, 128), r)
        return jnp.stack([dot_tn(pb[h, :, cols], da[0, h]) for h in range(z.hb)])

    rs_dv = Scatter(net, dv_own, k["dvh"], k["dvr"], r // 2)
    rs_dv.hop()
    dvs = k["dvs"]

    def dvs_own(q):
        cols = pl.ds(pl.multiple_of(q * r, 128), r)
        return jnp.stack([dot_tn(qb[h, :, cols], da[1, h]) for h in range(z.hb)])

    @pl.when(short)
    def _():
        dvs[0] = dvs_own(1 - p).astype(BF)
        cp_dvs.of(dvs.at[0], dvs.at[1]).start()

    go = k["go"]
    go[...] = dot_tn(attn[b, 0].reshape(rows4, z.fh), db[0].reshape(rows4, d))

    @pl.when(short)
    def _():
        go[...] += dot_tn(attn[b, 1].reshape(rows4, z.fh), db[1].reshape(rows4, d))

    def go_own(q):
        part = go[pl.ds(pl.multiple_of(q * z.rw, 8), z.rw)]
        return jnp.concatenate([part, jnp.zeros((z.rp - z.rw, d), F32)], axis=0)

    rs_go = Scatter(net, go_own, k["goh"], k["gor"], up16(z.rp // 2))
    rs_go.hop()
    rs_gu.hop()
    rs_dv.hop()

    gms, gm0 = k["mx"], k["gm0"]
    for h in range(z.hb):
        delta = jnp.sum(da[0, h].astype(F32) * mixed[0, h], axis=-1, keepdims=True)
        for j in range(BATCH):
            cols = slice(j * z.cb, (j + 1) * z.cb)
            part = pf[h, :, cols] * (dot_nt(da[0, h], vl[h, cols, :]) - delta)
            if j:
                gms[j, h] = part.astype(BF)
            else:
                gm0[...] = part

                @pl.when(short)
                def _():
                    lower = jnp.sum(da[1, h].astype(F32) * mixed[1, h], axis=-1, keepdims=True)
                    gm0[...] += qf[h] * (dot_nt(da[1, h], vs[h]) - lower)

                gms[0, h] = gm0[...].astype(BF)
    ex_gm = Exchange(net, gms, o_gm)
    ex_gm.start()
    rs_dv.hop()
    rs_go.hop()
    rs_gi.hop()
    rs_dv.hop()
    rs_go.hop()
    o_gu[...] = rs_gu.done()
    rs_go.hop()

    gis, gvs, gos = k["gis"], k["gvs"], k["gos"]

    def deal(ref, total):
        for j in range(BATCH):
            ref[j] = total[j * z.rw : (j + 1) * z.rw]

    deal(gis, rs_gi.done())
    ex_gi = Exchange(net, gis, o_gi)
    ex_gi.start()

    dv, d1 = k["dv"], dp
    co_d.sent()

    def values_back(g, total):
        rounded = total.astype(BF)
        for s, block in enumerate(slots_of([rounded[h] for h in range(z.hb)], z)):
            dv[g, s * r : (s + 1) * r] = block
        d1[g] = dot_nt(dv[g], k["wv"][...]).reshape(BATCH, r, d).astype(BF)

    values_back(0, rs_dv.done())

    @pl.when(short)
    def _():
        cp_dvs.of(dvs.at[1], dvs.at[1]).wait_recv()
        values_back(1, dvs_own(p) + dvs[1].astype(F32))

    co_1 = collect(d1, k["d1b"])
    co_1.start()
    gv = k["gv"]
    gv[...] = dot_tn(h1[0].reshape(rows4, d), dv[0])

    @pl.when(short)
    def _():
        gv[...] += dot_tn(h1[1].reshape(rows4, d), dv[1])

    rs_gv = Scatter(net, rows_at(gv, rows_o), k["gvh"], k["gvr"], cut_i)
    rs_gv.hop()
    co_1.mid()
    gos[...] = rs_go.done()[0 : z.rw]
    cp_go = Copy(net, (goal_p, goal_b))

    @pl.when(stays)
    def _():
        o_go[...] = gos[...]

    @pl.when(jnp.logical_not(stays))
    def _():
        cp_go.of(gos, o_go).start()

    rs_gv.hop()
    co_o.done()

    def finish_out(g):
        o_out[g] = (mid[g] + co_o.value(g)).astype(BF)

    each_live(finish_out)
    rs_gv.hop()
    co_1.done()

    def finish_tokens(g):
        o_gt[g] = dmid[g] + norm_back(co_1.value(g), tok[g].astype(F32), gain_1)

    each_live(finish_tokens)
    rs_gv.hop()
    deal(gvs, jnp.concatenate([rs_gv.done(), jnp.zeros((rows_o, 256 - z.fh), F32)], axis=1))
    ex_gv = Exchange(net, gvs, o_gv)
    ex_gv.start()

    ex_gm.done()
    ex_gi.done()
    ex_gv.done()

    @pl.when(jnp.logical_not(stays))
    def _():
        cp_go.of(gos, o_go).wait()

    @pl.when(short)
    def _():
        cp_vs.of(vs.at[:, here, :], vs.at[:, here, :]).wait_send()
        cp_dvs.of(dvs.at[0], dvs.at[0]).wait_send()

    for copy in net.sent:
        copy.finish()
    assert net.used == z.sems


def one_device(
    pos, batch, tokens, seq_lens, mixer, gain_attn, w_value, w_output, gain_ffn, w_in, w_out, cotangent
):
    args = (tokens, seq_lens, mixer, gain_attn, w_value, w_output, gain_ffn, w_in, w_out, cotangent)
    if not fits(pos, batch, tokens, mixer, w_value, w_in, w_out):
        return per_device(*args)
    z = Sizes(pos, tokens, mixer, w_value, w_in, w_out)
    p, b = lax.axis_index("pos"), lax.axis_index("batch")
    first_long = seq_lens[0] > SHORT

    def sort_slots(array):
        one, two = array[:, 0], array[:, 1]
        return jnp.stack([jnp.where(first_long, one, two), jnp.where(first_long, two, one)])

    def pad_rows(array):
        return jnp.pad(array, ((0, 0), (0, z.rp - array.shape[1]), (0, z.fc - array.shape[2])))

    start = (BATCH * p + b) * z.rw
    gains = [
        lax.dynamic_update_slice(jnp.zeros((z.d,), BF), gain, (start,)).reshape(z.gr, 256)
        for gain in (gain_attn, gain_ffn)
    ]
    tail = jnp.concatenate(gains + [jnp.zeros((z.rp - z.rw - 2 * z.gr, 256), BF)], axis=0)
    by_group = jnp.swapaxes(w_value.reshape(z.rw, BATCH, z.fh), 0, 1)
    by_group = jnp.pad(by_group, ((0, 0), (0, 0), (0, 256 - z.fh)))
    value_rows = jnp.concatenate([by_group, jnp.broadcast_to(tail[None], (BATCH,) + tail.shape)], axis=1)
    output_rows = jnp.pad(w_output, ((0, z.rp - z.rw), (0, 0)))
    in_rows = jnp.transpose(w_in.reshape(z.rw, pos, BATCH, z.rf), (2, 0, 1, 3)).reshape(BATCH, z.rw, z.fc)
    in_rows = jnp.pad(in_rows, ((0, 0), (0, z.rp - z.rw), (0, 0)))

    shapes = scratch(z)
    vmem = pl.BlockSpec(memory_space=pltpu.VMEM)
    out_shape = [
        jax.ShapeDtypeStruct((2, z.r, z.d), BF),
        jax.ShapeDtypeStruct((2, z.r, z.d), F32),
        jax.ShapeDtypeStruct((BATCH, z.hb, z.r, z.cb), BF),
        jax.ShapeDtypeStruct((BATCH, z.rw, 256), F32),
        jax.ShapeDtypeStruct((z.rw, z.d), F32),
        jax.ShapeDtypeStruct((BATCH, z.rw, z.fc), F32),
        jax.ShapeDtypeStruct((z.rf, z.d), F32),
        jax.ShapeDtypeStruct((2, 2, z.r, 128), F32),
    ]
    out, tokens_grad, mixer_grad, value_grad, output_grad, in_grad, out_grad, rms = pl.pallas_call(
        functools.partial(layer_kernel, z, list(shapes)),
        out_shape=out_shape,
        in_specs=[vmem] * 7,
        out_specs=[vmem] * len(out_shape),
        scratch_shapes=list(shapes.values()),
        compiler_params=pltpu.CompilerParams(
            collective_id=1, has_side_effects=True, vmem_limit_bytes=62 << 20
        ),
        name="layer",
    )(
        sort_slots(tokens),
        sort_slots(cotangent),
        mixer.reshape(BATCH, z.hb, z.r, z.cb),
        value_rows,
        output_rows,
        in_rows,
        w_out,
    )

    has_short = p < SHORT // z.r

    def unsort(array):
        one, two = array[0], jnp.where(has_short, array[1], 0)
        return jnp.stack([jnp.where(first_long, one, two), jnp.where(first_long, two, one)], axis=1)

    grad_value = jnp.swapaxes(value_grad[:, :, 0 : z.fh], 0, 1).reshape(z.rw, z.d)
    grad_in = jnp.transpose(in_grad.reshape(BATCH, z.rw, pos, z.rf), (1, 2, 0, 3)).reshape(z.rw, z.ff)
    gain_attn_grad = jnp.sum(w_value.astype(F32) * grad_value, axis=1) / gain_attn.astype(F32)
    gain_ffn_grad = jnp.sum(w_in.astype(F32) * grad_in, axis=1) / gain_ffn.astype(F32)
    return (
        unsort(out),
        unsort(tokens_grad),
        mixer_grad.reshape(z.heads, z.r, z.cb).astype(F32),
        gain_attn_grad,
        grad_value,
        output_grad,
        gain_ffn_grad,
        grad_in,
        out_grad,
        unsort(rms[0, :, :, 0]),
        unsort(rms[1, :, :, 0]),
    )


def solution(mesh):
    placed = (
        P("pos", "batch", None),
        P("batch"),
        P(None, "pos", "batch"),
        P(("pos", "batch")),
        P(("pos", "batch"), None),
        P(("pos", "batch"), None),
        P(("pos", "batch")),
        P(("pos", "batch"), None),
        P(("pos", "batch"), None),
        P("pos", "batch", None),
    )
    return jax.shard_map(
        functools.partial(one_device, mesh.shape["pos"], mesh.shape["batch"]),
        mesh=mesh,
        in_specs=placed,
        out_specs=(
            P("pos", "batch", None),
            P("pos", "batch", None),
            P(None, "pos", "batch"),
            P(("pos", "batch")),
            P(("pos", "batch"), None),
            P(("pos", "batch"), None),
            P(("pos", "batch")),
            P(("pos", "batch"), None),
            P(("pos", "batch"), None),
            P("pos", "batch"),
            P("pos", "batch"),
        ),
        check_vma=False,
    )
```

```python
import functools

import jax
import jax.numpy as jnp
from jax import lax
from jax.experimental import pallas as pl
from jax.experimental.pallas import tpu as pltpu
from jax.sharding import PartitionSpec as P

SHORT = 256


EPSILON = 1e-06


def norm_apply(values, gain_vec):
    inv_rms = lax.rsqrt(jnp.mean(values * values, axis=-1, keepdims=True) + EPSILON)
    return values * inv_rms * gain_vec


def gelu_exact(values):
    return jax.nn.gelu(values, approximate=False)


def row_stats(scores):
    top_score = jnp.max(scores, axis=-1)
    return top_score + jnp.log(jnp.sum(jnp.exp(scores - top_score[..., None]), axis=-1))


def contract_rows(left, right):
    return lax.dot_general(
        left, right, (((0,), (0,)), ((), ())), preferred_element_type=jnp.float32
    )


def contract_cols(left, right):
    return lax.dot_general(
        left, right, (((1,), (1,)), ((), ())), preferred_element_type=jnp.float32
    )


def per_device(
    tokens, seq_lens, mixer, gain_attn, w_value, w_output, gain_ffn, w_in, w_out, cotangent
):
    value_mat, output_mat, in_mat, out_mat, gain_one, gain_two = (
        lax.all_gather(w_value, ("pos", "batch"), axis=0, tiled=True),
        lax.all_gather(w_output, ("pos", "batch"), axis=0, tiled=True),
        lax.all_gather(w_in, ("pos", "batch"), axis=0, tiled=True),
        lax.all_gather(w_out, ("pos", "batch"), axis=0, tiled=True),
        lax.all_gather(gain_attn, ("pos", "batch"), axis=0, tiled=True),
        lax.all_gather(gain_ffn, ("pos", "batch"), axis=0, tiled=True),
    )
    rows_r = lax.all_gather(mixer, "batch", axis=2, tiled=True)
    head_count = rows_r.shape[0]
    long_len = rows_r.shape[2]
    row_count, slot_count, width = tokens.shape
    head_dim = width // head_count
    tok_count = row_count * slot_count
    start_row = lax.axis_index("pos") * row_count
    positions = start_row + jnp.arange(row_count, dtype=jnp.int32)
    live_mask = (positions[:, None] < seq_lens[None, :]).astype(jnp.float32)
    live_col = live_mask.reshape(tok_count, 1)
    is_long = seq_lens > SHORT
    gain_first = gain_one.astype(jnp.float32)
    gain_second = gain_two.astype(jnp.float32)
    x_float = tokens.astype(jnp.float32).reshape(tok_count, width)
    normed_one = norm_apply(x_float, gain_first).astype(jnp.bfloat16)
    value = jnp.dot(normed_one, value_mat, preferred_element_type=jnp.float32).astype(jnp.bfloat16)
    value = value.reshape(row_count, slot_count, width)
    lse_long = row_stats(rows_r.astype(jnp.float32))
    head_cols = rows_r[:, :, :SHORT].astype(jnp.float32)
    lse_short = row_stats(head_cols)
    prob_head = jnp.exp(head_cols - lse_short[..., None])

    def prob_block(block, lse_l, lse_s, col_pos):
        prob_long = jnp.exp(block - lse_l[..., None])
        prob_short = jnp.where(col_pos < SHORT, jnp.exp(block - lse_s[..., None]), 0.0)
        return jnp.where(is_long[:, None, None, None], prob_long[None], prob_short[None])

    def slot_probs(piece_len):
        columns = rows_r.astype(jnp.float32)
        col_pos = jnp.arange(piece_len, dtype=jnp.int32)
        return prob_block(columns, lse_long, lse_short, col_pos)

    portion = lax.all_gather(value, "pos", axis=0, tiled=True)
    piece_len = portion.shape[0]
    prob_b = slot_probs(piece_len).astype(jnp.bfloat16)
    piece_vals = portion.reshape(piece_len, slot_count, head_count, head_dim)
    mixed = jnp.einsum("shin,nshe->ishe", prob_b, piece_vals, preferred_element_type=jnp.float32)
    attn_in = (mixed * live_mask[:, :, None, None]).astype(jnp.bfloat16).reshape(tok_count, width)
    branch = jnp.dot(attn_in, output_mat, preferred_element_type=jnp.float32)
    mid_resid = x_float + branch
    normed_two = norm_apply(mid_resid, gain_second).astype(jnp.bfloat16)
    up_proj = jnp.dot(normed_two, in_mat, preferred_element_type=jnp.float32)
    hidden = gelu_exact(up_proj).astype(jnp.bfloat16)
    summed_out = mid_resid + jnp.dot(hidden, out_mat, preferred_element_type=jnp.float32)
    output = (summed_out * live_col).astype(jnp.bfloat16).reshape(row_count, slot_count, width)
    resid_rms = (
        jnp.sqrt(jnp.mean(mid_resid * mid_resid, axis=-1) + EPSILON).reshape(row_count, slot_count)
        * live_mask
    )
    branch_rms = (
        jnp.sqrt(jnp.mean(branch * branch, axis=-1) + EPSILON).reshape(row_count, slot_count)
        * live_mask
    )
    dfinal = cotangent.reshape(tok_count, width) * live_col.astype(jnp.bfloat16)
    grad_w_out = contract_rows(hidden, dfinal)
    dhidden = contract_cols(dfinal, out_mat)
    _, gelu_back = jax.vjp(gelu_exact, up_proj)
    dupper = gelu_back(dhidden)[0].astype(jnp.bfloat16)
    grad_w_in = contract_rows(normed_two, dupper)
    d_normed_two = contract_cols(dupper, in_mat)
    _, norm_back_two = jax.vjp(norm_apply, mid_resid, gain_second)
    d_mid_norm, grad_gain_ffn = norm_back_two(d_normed_two)
    d_mid = dfinal.astype(jnp.float32) + d_mid_norm
    dbranch = d_mid.astype(jnp.bfloat16)
    grad_w_output = contract_rows(attn_in, dbranch)
    d_attn = contract_cols(dbranch, output_mat).astype(jnp.bfloat16)
    d_attn = d_attn.reshape(row_count, slot_count, head_count, head_dim)
    portion = lax.all_gather(value, "pos", axis=0, tiled=True)
    piece_len = portion.shape[0]
    prob_f = slot_probs(piece_len)
    piece_vals = portion.reshape(piece_len, slot_count, head_count, head_dim)
    d_prob = jnp.einsum("ishe,nshe->shin", d_attn, piece_vals, preferred_element_type=jnp.float32)
    weighted = prob_f * d_prob
    grad_acc = jnp.sum(weighted, axis=0)
    grad_acc, delta_all = (grad_acc, jnp.sum(weighted, axis=-1))
    delta_long = jnp.sum(jnp.where(is_long[:, None, None], delta_all, 0.0), axis=0)
    delta_short = jnp.sum(jnp.where(is_long[:, None, None], 0.0, delta_all), axis=0)
    slots_here = d_attn.shape[1]
    col_block = lax.all_to_all(rows_r, "pos", split_axis=2, concat_axis=1, tiled=True)
    lse_all_long = lax.all_gather(lse_long, "pos", axis=1, tiled=True)
    lse_all_short = lax.all_gather(lse_short, "pos", axis=1, tiled=True)
    portion = lax.all_gather(d_attn, "pos", axis=0, tiled=True)
    piece_len = portion.shape[0]
    block = col_block.astype(jnp.float32)
    lse_l = lse_all_long
    lse_s = lse_all_short
    prob_b = prob_block(block, lse_l, lse_s, positions).astype(jnp.bfloat16)
    term = jnp.einsum("shij,ishe->jshe", prob_b, portion, preferred_element_type=jnp.float32)
    dvalue = term.reshape(row_count, slots_here, width)
    full_long = jnp.exp(rows_r.astype(jnp.float32) - lse_long[..., None])
    grad_rows = grad_acc - full_long * delta_long[..., None]
    correction = prob_head * delta_short[..., None]
    grad_rows = grad_rows - jnp.pad(correction, ((0, 0), (0, 0), (0, long_len - SHORT)))
    dvalue_b = dvalue.astype(jnp.bfloat16).reshape(tok_count, width)
    grad_w_value = contract_rows(normed_one, dvalue_b)
    d_normed_one = contract_cols(dvalue_b, value_mat)
    _, norm_back_one = jax.vjp(norm_apply, x_float, gain_first)
    d_x_norm, grad_gain_attn = norm_back_one(d_normed_one)
    grad_tokens = (d_mid + d_x_norm).reshape(row_count, slot_count, width)
    grad_mixer = lax.psum_scatter(
        grad_rows.astype(jnp.bfloat16), "batch", scatter_dimension=2, tiled=True
    ).astype(jnp.float32)
    reduced = (
        lax.psum_scatter(grad_w_value, ("pos", "batch"), scatter_dimension=0, tiled=True),
        lax.psum_scatter(grad_w_output, ("pos", "batch"), scatter_dimension=0, tiled=True),
        lax.psum_scatter(grad_w_in, ("pos", "batch"), scatter_dimension=0, tiled=True),
        lax.psum_scatter(grad_w_out, ("pos", "batch"), scatter_dimension=0, tiled=True),
        lax.psum_scatter(grad_gain_attn, ("pos", "batch"), scatter_dimension=0, tiled=True),
        lax.psum_scatter(grad_gain_ffn, ("pos", "batch"), scatter_dimension=0, tiled=True),
    )
    return (
        output,
        grad_tokens,
        grad_mixer,
        reduced[4],
        reduced[0],
        reduced[1],
        reduced[5],
        reduced[2],
        reduced[3],
        resid_rms,
        branch_rms,
    )


BF = jnp.bfloat16
F32 = jnp.float32
MESH = pl.DeviceIdType.MESH
HEAD = 64
BATCH = 4
LANE = 4 * HEAD


def dot(left, right):
    return jnp.dot(left, right, preferred_element_type=F32)


def dot_tn(left, right):
    return lax.dot_general(left, right, (((0,), (0,)), ((), ())), preferred_element_type=F32)


def dot_nt(left, right):
    return lax.dot_general(left, right, (((1,), (1,)), ((), ())), preferred_element_type=F32)


def up16(rows):
    return -(-rows // 16) * 16


class Sizes:
    def __init__(self, pos, tokens, mixer, w_value, w_in, w_out):
        self.n = pos
        self.r, _, self.d = tokens.shape
        self.heads, _, self.cb = mixer.shape
        self.long = pos * self.r
        self.hb = self.heads // BATCH
        self.fh = self.hb * HEAD
        self.rw = w_value.shape[0]
        self.rf = w_out.shape[0]
        self.ff = w_in.shape[1]
        self.fc = self.ff // BATCH
        self.rp = up16(self.rw + 8)
        self.gr = self.d // 256
        self.wr = BATCH * self.rw + 16
        self.sems = (8 + 2 * self.hb) * 2 * pos + 2 * (pos - 1) + 148


def fits(pos, batch, tokens, mixer, w_value, w_in, w_out):
    r, _, d = tokens.shape
    heads = mixer.shape[0]
    rw, rf = w_value.shape[0], w_out.shape[0]
    return (
        batch == BATCH
        and pos >= 4
        and pos % 2 == 0
        and r % 128 == 0
        and SHORT == 2 * r
        and heads % BATCH == 0
        and heads * HEAD == d
        and d % 256 == 0
        and 2 * (d // 256) <= 8
        and rw % 8 == 0
        and rw % 16 == 8
        and rf % 32 == 0
        and (BATCH * rw) % 32 == 0
        and (w_in.shape[1] // BATCH) % 256 == 0
        and SHORT == mixer.shape[2]
    )


class Net:
    def __init__(self, n, sems):
        self.n = n
        self.sems = sems
        self.used = 0
        self.sent = []
        p, b = lax.axis_index("pos"), lax.axis_index("batch")
        self.p, self.b = p, b
        self.rho = self.ring(p)
        self.right = (self.place(lax.rem(self.rho + 1, n)), b)
        self.left = (self.place(lax.rem(self.rho + n - 1, n)), b)
        self.core_b = b + 1 - 2 * lax.rem(b, 2)
        self.y_b = lax.rem(b + 2, BATCH)
        self.far_b = BATCH - 1 - b
        self.core = (p, self.core_b)
        self.y = (p, self.y_b)
        self.far = (p, self.far_b)
        self.short = p < 2

    def ring(self, p):
        return jnp.where(lax.rem(p, 2) == 0, p // 2, self.n - 1 - p // 2)

    def place(self, rho):
        half = self.n // 2
        return jnp.where(rho < half, 2 * rho, 2 * (self.n - 1 - rho) + 1)

    def at(self, step):
        return self.place(lax.rem(self.rho + step + 2 * self.n, self.n))

    def sem(self):
        self.used += 1
        return self.sems.at[self.used - 1]


def run_if(cond, body):
    if cond is None:
        body()
    else:
        pl.when(cond)(body)


class Copy:
    def __init__(self, net, device, cond=None):
        self.net, self.device, self.cond = net, device, cond
        self.send, self.recv = net.sem(), net.sem()

    def of(self, src, dst):
        return pltpu.make_async_remote_copy(
            src_ref=src, dst_ref=dst, send_sem=self.send, recv_sem=self.recv,
            device_id=self.device, device_id_type=MESH,
        )

    def start(self, src, dst):
        run_if(self.cond, lambda: self.of(src, dst).start())
        self.src = src
        self.net.sent.append(self)

    def arrive(self, land):
        run_if(self.cond, lambda: self.of(land, land).wait_recv())

    def finish(self):
        run_if(self.cond, lambda: self.of(self.src, self.src).wait_send())
        self.net.sent.remove(self)


class Local:
    def __init__(self, net, src, dst, cond=None):
        self.copy = pltpu.make_async_copy(src, dst, net.sem())
        self.cond = cond

    def start(self):
        run_if(self.cond, self.copy.start)
        return self

    def done(self):
        run_if(self.cond, self.copy.wait)


class Exchange:
    def __init__(self, net, pick, land):
        self.net, self.pick, self.land = net, pick, land
        self.copies = [(Copy(net, d), j) for d, j in ((net.y, net.y_b), (net.far, net.far_b), (net.core, net.core_b))]

    def start(self):
        for copy, j in self.copies:
            copy.start(self.pick(j), self.land.at[self.net.b])

    def done(self):
        for copy, j in self.copies:
            copy.arrive(self.land.at[j])


class Spread:
    def __init__(self, net, slot, cond=None):
        self.net, self.slot = net, slot
        self.by_y, self.by_core, self.relay = (Copy(net, d, cond) for d in (net.y, net.core, net.core))

    def start(self, own=None):
        slot = self.slot(self.net.b)
        own = slot if own is None else own
        self.by_y.start(own, slot)
        self.by_core.start(own, slot)

    def mid(self):
        came = self.slot(self.net.y_b)
        self.by_y.arrive(came)
        self.relay.start(came, came)

    def done(self):
        self.by_core.arrive(self.slot(self.net.core_b))
        self.relay.arrive(self.slot(self.net.far_b))


class Collect:
    def __init__(self, net, part, bufs, cond=None):
        self.net, self.part, self.bufs, self.cond = net, part, bufs, cond
        self.to_other, self.to_mine, self.by_y = (Copy(net, d, cond) for d in (net.core, net.core, net.y))

    def start(self):
        net, (mine, other, _, _) = self.net, self.bufs
        self.to_other.start(self.part.at[net.far_b], other)
        self.to_mine.start(self.part.at[net.core_b], mine)

    def mid(self):
        net, (mine, other, stage, across) = self.net, self.bufs
        self.to_other.arrive(other)

        def add():
            stage[...] = (self.part[net.y_b].astype(F32) + other[...].astype(F32)).astype(BF)

        run_if(self.cond, add)
        self.by_y.start(stage, across)

    def done(self):
        self.to_mine.arrive(self.bufs[0])
        self.by_y.arrive(self.bufs[3])

    def sent(self):
        self.to_other.finish()
        self.to_mine.finish()

    def value(self):
        return self.part[self.net.b].astype(F32) + self.bufs[0][...].astype(F32) + self.bufs[3][...].astype(F32)


class Gather:
    def __init__(self, net, slot, first, second):
        self.net, self.slot, self.halves = net, slot, (first, second)
        self.steps, self.next = net.n // 2, 0
        self.copies = [[Copy(net, d) for _ in range(self.steps)] for d in (net.right, net.left)]

    def hop(self, own=None):
        net, t = self.net, self.next
        if t == self.steps:
            return
        self.next += 1
        for way, sign in ((0, -1), (1, 1)):
            came = self.slot(net.at(sign * t))
            if t:
                self.copies[way][t - 1].arrive(came)
            if t == self.steps - 1:
                came = self.halves[way](net.at(sign * t))
            self.copies[way][t].start(came if own is None else own, came)

    def done(self):
        while self.next < self.steps:
            self.hop()
        for way in (0, 1):
            self.copies[way][-1].arrive(self.halves[way](self.net.at(self.steps)))


class Scatter:
    def __init__(self, net, own, held, came, cut):
        self.net, self.own, self.held, self.came = net, own, held, came
        self.steps, self.next = net.n // 2, 0
        self.spans = (slice(0, cut), slice(cut, held.shape[-2]))
        self.copies = [[Copy(net, d) for _ in range(self.steps)] for d in (net.right, net.left)]

    def hop(self):
        net, t = self.net, self.next
        if t == self.steps:
            return
        self.next += 1
        if t == 0:
            value = self.own(net.at(self.steps))
        for way, sign in ((0, 1), (1, -1)):
            span, copies = self.spans[way], self.copies[way]
            if t == 0:
                self.held[way, 0, span] = value[span].astype(BF)
                copies[0].start(self.held.at[way, 0, span], self.came.at[way, 0, span])
                continue
            value = self.own(net.at(sign * (self.steps - t)))
            if t == 1:
                copies[0].arrive(self.came.at[way, 0, span])
                self.held[way, 1] = value.astype(BF)
                self.held[way, 1, span] = (value[span] + self.came[way, 0, span].astype(F32)).astype(BF)
            else:
                copies[t - 1].arrive(self.came.at[way, t - 1])
                self.held[way, t] = (value + self.came[way, t - 1].astype(F32)).astype(BF)
            copies[t].start(self.held.at[way, t], self.came.at[way, t])

    def done(self):
        while self.next < self.steps:
            self.hop()
        last = self.steps - 1
        for way in (0, 1):
            self.copies[way][last].arrive(self.came.at[way, last])
        return self.own(self.net.p) + self.came[0, last].astype(F32) + self.came[1, last].astype(F32)


def unit(values):
    inv = lax.rsqrt(jnp.mean(values * values, axis=-1, keepdims=True) + EPSILON)
    return values * inv, inv


def heads_of(rows, z):
    return [
        jnp.concatenate([rows[s * z.r : (s + 1) * z.r, h * HEAD : (h + 1) * HEAD] for s in range(BATCH)], axis=-1)
        for h in range(z.hb)
    ]


def slots_of(by_head, z):
    return [
        jnp.concatenate([by_head[h][:, s * HEAD : (s + 1) * HEAD] for h in range(z.hb)], axis=-1)
        for s in range(BATCH)
    ]


def scratch(z):
    n, r, d, half = z.n, z.r, z.d, z.n // 2
    vm = pltpu.VMEM
    slots, own = (2, BATCH, r, d), (2, r, d)

    def ring(*shape):
        return vm((2, half) + shape, BF)

    return dict(
        x=vm(slots, BF), c=vm(slots, BF), mx=vm((BATCH, z.hb, r, z.cb), BF),
        wvp=vm((BATCH, z.rp, 256), BF), wop=vm((BATCH, z.rp, d), BF), wip=vm((BATCH, z.rp, z.fc), BF),
        wvs=vm((BATCH, z.rp, 256), BF), wos=vm((z.rp, d), BF), wis=vm((BATCH, z.rp, z.fc), BF),
        wvg=vm((n, z.wr, 256), BF), wv=vm((d, z.fh), BF), wo=vm((d, d), BF), wi=vm((d, z.fc), BF), wu=vm((z.fc, d), BF),
        gain=vm((2, 1, d), F32),
        h1=vm(slots, BF), vl=vm((z.hb, z.long, LANE), BF), vs=vm((z.hb, SHORT, LANE), BF),
        pf=vm((z.hb, r, z.long), F32), pb=vm((z.hb, r, z.long), BF),
        qf=vm((z.hb, r, SHORT), F32), qb=vm((z.hb, r, SHORT), BF),
        mixed=vm((2, z.hb, r, LANE), F32), attn=vm((BATCH, 2, BATCH, r, z.fh), BF),
        mid=vm(own, F32), h2=vm(slots, BF),
        hid=vm((2, BATCH * r, z.fc), BF), dup=vm((2, BATCH * r, z.fc), BF),
        dp=vm(slots, BF), db=vm(slots, BF), dmid=vm(own, F32),
        dpb=vm((4,) + own, BF), opb=vm((4,) + own, BF), d1b=vm((4,) + own, BF),
        da=vm((2, z.hb, r, LANE), BF), dv=vm((2, BATCH * r, z.fh), BF), dvs=vm((2, z.hb, r, LANE), BF),
        gm0=vm((r, z.cb), F32),
        gu=vm((z.fc, d), F32), gi=vm((d, z.fc), F32), go=vm((z.fh, d), F32), gv=vm((d, z.fh), F32),
        gis=vm((BATCH, z.rw, z.fc), F32), gvs=vm((BATCH, z.rw, 256), F32), gos=vm((z.rw, d), F32), gus=vm((z.rf, d), F32),
        outs=vm(own, BF), gts=vm(own, F32), rms=vm((2, 2, r, 128), F32),
        guh=ring(z.rf, d), gur=ring(z.rf, d), gih=ring(BATCH * z.rw, z.fc), gir=ring(BATCH * z.rw, z.fc),
        goh=ring(z.rp, d), gor=ring(z.rp, d), gvh=ring(BATCH * z.rw, z.fh), gvr=ring(BATCH * z.rw, z.fh),
        dvh=vm((z.hb, 2, half, r, LANE), BF), dvr=vm((z.hb, 2, half, r, LANE), BF),
        sems=pltpu.SemaphoreType.DMA((z.sems,)),
    )


def layer_kernel(z, names, *refs):
    tok, cot, (mix, gain_1, gain_2, wv_in, wo_in, wi_in, wu_in) = refs[0:2], refs[2:4], refs[4:11]
    o_out, o_gt, o_gm, o_gv, o_go, o_gi, o_gu, o_rms = refs[11:19]
    k = dict(zip(names, refs[19:]))
    n, r, d = z.n, z.r, z.d
    rows4 = BATCH * r
    rows_o = BATCH * z.rw
    net = Net(n, k["sems"])
    p, b, short = net.p, net.b, net.short
    scope = jax.named_scope

    index = n * b + p
    goal = (index // BATCH, lax.rem(index, BATCH))
    mine = BATCH * p + b
    source = (lax.rem(mine, n), mine // n)
    moves = index != mine

    x, c, mx, wu, wvp, wop, wip = (k[name] for name in ("x", "c", "mx", "wu", "wvp", "wop", "wip"))

    def span(ref, size, lo=0, hi=None):
        hi = size if hi is None else hi
        return lambda q: ref.at[pl.ds(pl.multiple_of(q * size + lo, 16), hi - lo)]

    wu_span = span(wu, z.rf)
    own_x = Local(net, tok[0], x.at[0, b]).start()
    own_wu = Local(net, wu_in, wu_span(p)).start()
    own_mx = Local(net, mix.at[b], mx.at[b]).start()
    own_c = Local(net, cot[0], c.at[0, b]).start()
    own_xs = Local(net, tok[1], x.at[1, b], short).start()
    own_cs = Local(net, cot[1], c.at[1, b], short).start()

    barrier = pltpu.get_barrier_semaphore()
    for device in (net.right, net.left, net.core, net.y, net.far):
        pl.semaphore_signal(barrier, inc=1, device_id=device, device_id_type=MESH)

    @pl.when(moves)
    def _():
        for device in (goal, source):
            pl.semaphore_signal(barrier, inc=1, device_id=device, device_id_type=MESH)

    wvs, wos, wis = k["wvs"], k["wos"], k["wis"]
    place = lax.broadcasted_iota(jnp.int32, (z.rw, d), 1) - lax.broadcasted_iota(jnp.int32, (z.rw, d), 0)
    place = (place == mine * z.rw).astype(BF)
    table = [dot(ref[...], place) for ref in (gain_1, gain_2)]
    tail = [table[g][:, i * 256 : (i + 1) * 256] for g in range(2) for i in range(z.gr)]
    tail = jnp.concatenate(tail + [jnp.zeros((z.rp - z.rw - 2 * z.gr, 256), F32)], axis=0)
    held = wv_in[...].astype(F32)
    for j in range(BATCH):
        piece = jnp.concatenate([held[:, j * z.fh : (j + 1) * z.fh], jnp.zeros((z.rw, 256 - z.fh), F32)], axis=1)
        wvs[j] = jnp.concatenate([piece, tail], axis=0).astype(BF)
    wvp[b] = wvs[b]

    def prepare():
        fill = jnp.zeros((z.rp - z.rw, d), F32)
        wos[...] = jnp.concatenate([wo_in[...].astype(F32), fill], axis=0).astype(BF)
        wop[b] = wos[...]
        held = wi_in[...].astype(F32)
        fill = jnp.zeros((z.rp - z.rw, z.fc), F32)
        for j in range(BATCH):
            cols = [held[:, (BATCH * q + j) * z.rf : (BATCH * q + j + 1) * z.rf] for q in range(n)]
            wis[j] = jnp.concatenate([jnp.concatenate(cols, axis=1), fill], axis=0).astype(BF)
        wip[b] = wis[b]

    pl.semaphore_wait(barrier, jnp.where(moves, 7, 5))

    ex_wv = Exchange(net, lambda j: wvs.at[j], wvp)
    ex_wo = Exchange(net, lambda j: wos, wop)
    ex_wi = Exchange(net, lambda j: wis.at[j], wip)
    ex_mx = Exchange(net, lambda j: mix.at[j], mx)
    sp_x, sp_xs = Spread(net, lambda j: x.at[0, j]), Spread(net, lambda j: x.at[1, j], short)
    sp_c, sp_cs = Spread(net, lambda j: c.at[0, j]), Spread(net, lambda j: c.at[1, j], short)
    cut_f = up16(z.rf // 2)
    ag_wu = Gather(net, wu_span, span(wu, z.rf, 0, cut_f), span(wu, z.rf, cut_f))
    ex_wv.start()
    ag_wu.hop(wu_in)
    sp_x.start(tok[0])
    prepare()
    ex_wo.start()
    ex_wi.start()
    ex_mx.start()
    sp_c.start(cot[0])
    sp_xs.start(tok[1])
    sp_cs.start(cot[1])

    wvg = k["wvg"]
    cut_v = up16(z.wr // 2)
    ag_wv = Gather(net, lambda q: wvg.at[q], lambda q: wvg.at[q, 0:cut_v], lambda q: wvg.at[q, cut_v : z.wr])

    def ready_wv():
        ex_wv.done()
        with scope("pack_wv"):
            weights = jnp.concatenate([wvp[j].astype(F32)[0 : z.rw] for j in range(BATCH)], axis=0)
            gains = sum(wvp[j].astype(F32)[z.rw : z.rw + 8] for j in range(BATCH))
            wvg[p] = jnp.concatenate([weights, gains, jnp.zeros_like(gains)], axis=0).astype(BF)
        ag_wv.hop()

    wo = k["wo"]
    half_o = rows_o // 2
    cut_o = up16(half_o // 2)
    core = lax.rem(b, 2)

    def wo_span(lo, hi, which):
        return lambda q: wo.at[pl.ds(pl.multiple_of(q * rows_o + which * half_o + lo, 16), hi - lo)]

    ag_wo = Gather(net, wo_span(0, half_o, core), wo_span(0, cut_o, core), wo_span(cut_o, half_o, core))
    pass_wo = {s: Copy(net, net.core) for s in range(1 - n // 2, n // 2 + 1) if s}

    def pack(ref):
        return jnp.concatenate([ref[j].astype(F32)[0 : z.rw] for j in range(BATCH)], axis=0).astype(BF)

    def ready_wo():
        ex_wo.done()
        with scope("pack_wo"):
            wo[pl.ds(pl.multiple_of(p * rows_o, 16), rows_o)] = pack(wop)
        ag_wo.hop()

    def pass_on(*steps):
        for step in steps:
            block = wo_span(0, half_o, core)(net.at(step))
            pass_wo[step].start(block, block)

    def wo_done():
        for step, copy in pass_wo.items():
            copy.arrive(wo_span(0, half_o, 1 - core)(net.at(step)))

    wi = k["wi"]
    cut_i = up16(rows_o // 2)
    ag_wi = Gather(net, span(wi, rows_o), span(wi, rows_o, 0, cut_i), span(wi, rows_o, cut_i))

    def ready_wi():
        ex_wi.done()
        with scope("pack_wi"):
            wi[pl.ds(pl.multiple_of(p * rows_o, 16), rows_o)] = pack(wip)
        ag_wi.hop()

    h1, vl, vs, gain = k["h1"], k["vl"], k["vs"], k["gain"]
    here = pl.ds(pl.multiple_of(p * r, 16), r)
    twin = (1 - p, b)
    other = pl.ds(pl.multiple_of((1 - p) * r, 16), r)
    cp_vs, cp_dvs = Copy(net, twin, short), Copy(net, twin, short)

    def ready_gains():
        ag_wv.done()
        with scope("gains"):
            table = jnp.sum(wvg[:, rows_o : rows_o + 16].astype(F32), axis=0)
            for g in range(2):
                gain[g] = jnp.concatenate([table[g * z.gr + i : g * z.gr + i + 1] for i in range(z.gr)], axis=1)
            k["wv"][...] = wvg[:, 0:rows_o, 0 : z.fh].reshape(d, z.fh)

    def values(g, into):
        for s in range(BATCH):
            h1[g, s] = (unit(x[g, s].astype(F32))[0] * gain[0]).astype(BF)
        value = dot(h1[g].reshape(rows4, d), k["wv"][...]).astype(BF)
        for h, block in enumerate(heads_of(value, z)):
            into[h, here, :] = block

    def vl_span(h, lo, hi):
        return lambda q: vl.at[h, pl.ds(pl.multiple_of(q * r + lo, 16), hi - lo), :]

    ag_v = [Gather(net, vl_span(h, 0, r), vl_span(h, 0, r // 2), vl_span(h, r // 2, r)) for h in range(z.hb)]

    def hop_v():
        for ring in ag_v:
            ring.hop()

    def ready_values():
        own_x.done()
        sp_x.done()
        with scope("values"):
            values(0, vl)
        hop_v()

    def short_values():
        own_xs.done()
        sp_xs.done()

        @pl.when(short)
        def _():
            with scope("values_short"):
                values(1, vs)

        cp_vs.start(vs.at[:, here, :], vs.at[:, here, :])

    pf, pb, qf, qb = k["pf"], k["pb"], k["qf"], k["qb"]

    def probabilities():
        own_mx.done()
        ex_mx.done()
        with scope("probabilities"):
            for h in range(z.hb):
                total, first = 0.0, None
                for j in range(BATCH):
                    e = jnp.exp(mx[j, h].astype(F32))
                    pf[h, :, j * z.cb : (j + 1) * z.cb] = e
                    total = total + jnp.sum(e, axis=-1, keepdims=True)
                    first = total if j == 0 else first

                @pl.when(short)
                def _():
                    q = pf[h, :, 0:SHORT] * (1.0 / first)
                    qf[h] = q
                    qb[h] = q.astype(BF)

                scaled = pf[h] * (1.0 / total)
                pf[h] = scaled
                pb[h] = scaled.astype(BF)

    mixed, attn = k["mixed"], k["attn"]
    sp_a, sp_as = Spread(net, lambda j: attn.at[j, 0]), Spread(net, lambda j: attn.at[j, 1], short)

    def mix_slots(g, prob, held):
        for h in range(z.hb):
            mixed[g, h] = dot(prob[h], held[h])
        for s, block in enumerate(slots_of([mixed[g, h] for h in range(z.hb)], z)):
            attn[b, g, s] = block.astype(BF)

    def mix():
        for ring in ag_v:
            ring.done()
        with scope("mix"):
            mix_slots(0, pb, vl)
        sp_a.start()

    def short_mix():
        cp_vs.arrive(vs.at[:, other, :])

        @pl.when(short)
        def _():
            with scope("mix_short"):
                mix_slots(1, qb, vs)

        sp_as.start()

    big, mid, h2, rms = k["gu"], k["mid"], k["h2"], k["rms"]

    def branch_slots(g):
        big[0:rows4] = sum(
            dot(attn[j, g].reshape(rows4, z.fh), wo[j * z.fh : (j + 1) * z.fh]) for j in range(BATCH)
        )
        for s in range(BATCH):
            branch = big[s * r : (s + 1) * r]
            total = x[g, s].astype(F32) + branch
            square = jnp.mean(total * total, axis=-1, keepdims=True) + EPSILON
            h2[g, s] = (total * lax.rsqrt(square) * gain[1]).astype(BF)

            @pl.when(b == s)
            def _():
                mid[g] = total
                rms[0, g] = jnp.broadcast_to(jnp.sqrt(square), (r, 128))
                size = jnp.sqrt(jnp.mean(branch * branch, axis=-1, keepdims=True) + EPSILON)
                rms[1, g] = jnp.broadcast_to(size, (r, 128))

    def branches():
        sp_a.done()
        with scope("branches"):
            branch_slots(0)

    def short_branches():
        sp_as.done()

        @pl.when(short)
        def _():
            with scope("branches_short"):
                branch_slots(1)

    hid, dup, dp, op = k["hid"], k["dup"], k["dp"], h2
    co_d, co_ds = (Collect(net, dp.at[g], [k["dpb"].at[i, g] for i in range(4)], w) for g, w in ((0, None), (1, short)))
    co_o, co_os = (Collect(net, op.at[g], [k["opb"].at[i, g] for i in range(4)], w) for g, w in ((0, None), (1, short)))

    def feed(g):
        left = h2[g].reshape(rows4, d)
        down = c[g].reshape(rows4, d)
        for q in range(z.fc // 256):
            cols = slice(q * 256, (q + 1) * 256)
            up = dot(left, wi[:, cols])
            cdf = 0.5 + 0.5 * lax.erf(up * 0.7071067811865476)
            hid[g, :, cols] = (up * cdf).astype(BF)
            slope = cdf + up * (jnp.exp(-0.5 * up * up) * 0.3989422804014327)
            dup[g, :, cols] = (dot_nt(down, wu[cols, :]) * slope).astype(BF)
        for q in range(d // 256):
            rows = slice(q * 256, (q + 1) * 256)
            dp[g, :, :, rows] = dot_nt(dup[g], wi[rows, :]).reshape(BATCH, r, 256).astype(BF)

    def feeds():
        ag_wi.done()
        ag_wu.done()
        own_wu.done()
        own_c.done()
        sp_c.done()
        with scope("feed"):
            feed(0)
        co_d.start()

    def short_feeds():
        own_cs.done()
        sp_cs.done()

        @pl.when(short)
        def _():
            with scope("feed_short"):
                feed(1)

        co_ds.start()

    gu, gi, gv, go = k["gu"], k["gi"], k["gv"], k["go"]

    def rows_at(ref, size):
        return lambda q: ref[pl.ds(pl.multiple_of(q * size, 8), size)]

    rs_gu = Scatter(net, rows_at(gu, z.rf), k["guh"], k["gur"], cut_f)
    rs_gi = Scatter(net, rows_at(gi, rows_o), k["gih"], k["gir"], cut_i)
    rs_gv = Scatter(net, rows_at(gv, rows_o), k["gvh"], k["gvr"], cut_i)

    def weight_grad(into, left, right, width):
        for q in range(width // 256):
            cols = slice(q * 256, (q + 1) * 256)

            def term(g):
                return dot_tn(left(g), right(g, cols))

            into[:, cols] = term(0)

            @pl.when(short)
            def _():
                into[:, cols] += term(1)

    def grad_out():
        with scope("grad_w_out"):
            weight_grad(gu, lambda g: hid[g], lambda g, cols: c[g, :, :, cols].reshape(rows4, 256), d)
        rs_gu.hop()

    def grad_in():
        with scope("grad_w_in"):
            weight_grad(gi, lambda g: h2[g].reshape(rows4, d), lambda g, cols: dup[g, :, cols], z.fc)
        rs_gi.hop()

    def outs(g):
        for q in range(d // 256):
            cols = slice(q * 256, (q + 1) * 256)
            op[g, :, :, cols] = dot(hid[g], wu[:, cols]).reshape(BATCH, r, 256).astype(BF)

    def finals():
        with scope("outs"):
            outs(0)
        co_o.start()

        @pl.when(short)
        def _():
            with scope("outs_short"):
                outs(1)

        co_os.start()

    db, dmid = k["db"], k["dmid"]
    sp_b, sp_bs = Spread(net, lambda j: db.at[0, j]), Spread(net, lambda j: db.at[1, j], short)

    def norm_back(upper, values, gain):
        normed, inv = unit(values)
        scaled = upper * gain
        return inv * (scaled - normed * jnp.mean(scaled * normed, axis=-1, keepdims=True))

    def middle(g, collect):
        grad = c[g, b].astype(F32) + norm_back(collect.value(), mid[g], gain[1])
        dmid[g] = grad
        db[g, b] = grad.astype(BF)

    def middles():
        co_d.done()
        with scope("middle"):
            middle(0, co_d)
        sp_b.start()

    def short_middles():
        co_ds.done()

        @pl.when(short)
        def _():
            with scope("middle_short"):
                middle(1, co_ds)

        sp_bs.start()

    da, dvs = k["da"], k["dvs"]
    wo_rows = pl.ds(pl.multiple_of(b * z.fh, 16), z.fh)

    def mix_back(g):
        grad = dot_nt(db[g].reshape(rows4, d), wo[wo_rows]).astype(BF)
        for h, block in enumerate(heads_of(grad, z)):
            da[g, h] = block

    def dv_own(h):
        return lambda q: dot_tn(pb[h, :, pl.ds(pl.multiple_of(q * r, 128), r)], da[0, h])

    rs_dv = [Scatter(net, dv_own(h), k["dvh"].at[h], k["dvr"].at[h], r // 2) for h in range(z.hb)]

    def hop_dv():
        with scope("dv_hop"):
            for ring in rs_dv:
                ring.hop()

    def mix_backs():
        sp_b.done()
        with scope("mix_back"):
            mix_back(0)
        hop_dv()

    def dvs_own(h, q):
        return dot_tn(qb[h, :, pl.ds(pl.multiple_of(q * r, 128), r)], da[1, h])

    def short_mix_backs():
        sp_bs.done()

        @pl.when(short)
        def _():
            with scope("mix_back_short"):
                mix_back(1)
                for h in range(z.hb):
                    dvs[0, h] = dvs_own(h, 1 - p).astype(BF)

        cp_dvs.start(dvs.at[0], dvs.at[1])

    def go_own(q):
        part = go[pl.ds(pl.multiple_of(q * z.rw, 8), z.rw)]
        return jnp.concatenate([part, jnp.zeros((z.rp - z.rw, d), F32)], axis=0)

    rs_go = Scatter(net, go_own, k["goh"], k["gor"], up16(z.rp // 2))

    def grad_output():
        with scope("grad_w_output"):
            go[...] = dot_tn(attn[b, 0].reshape(rows4, z.fh), db[0].reshape(rows4, d))

            @pl.when(short)
            def _():
                go[...] += dot_tn(attn[b, 1].reshape(rows4, z.fh), db[1].reshape(rows4, d))

        rs_go.hop()

    gms, gm0 = mx, k["gm0"]
    ex_gm = Exchange(net, lambda j: gms.at[j], o_gm)
    own_gm = Local(net, gms.at[b], o_gm.at[b])

    def grad_mixer():
        with scope("grad_mixer"):
            for h in range(z.hb):
                delta = jnp.sum(da[0, h].astype(F32) * mixed[0, h], axis=-1, keepdims=True)
                for j in range(BATCH):
                    cols = slice(j * z.cb, (j + 1) * z.cb)
                    part = pf[h, :, cols] * (dot_nt(da[0, h], vl[h, cols, :]) - delta)
                    if j:
                        gms[j, h] = part.astype(BF)
                    else:
                        gm0[...] = part

                        @pl.when(short)
                        def _():
                            lower = jnp.sum(da[1, h].astype(F32) * mixed[1, h], axis=-1, keepdims=True)
                            gm0[...] += qf[h] * (dot_nt(da[1, h], vs[h]) - lower)

                        gms[0, h] = gm0[...].astype(BF)
        ex_gm.start()
        own_gm.start()

    gis, gvs, gos, gus = k["gis"], k["gvs"], k["gos"], k["gus"]
    ex_gi, ex_gv = Exchange(net, lambda j: gis.at[j], o_gi), Exchange(net, lambda j: gvs.at[j], o_gv)
    own_gi, own_gv = Local(net, gis.at[b], o_gi.at[b]), Local(net, gvs.at[b], o_gv.at[b])
    out_gu = Local(net, gus, o_gu)
    cp_go = Copy(net, goal, moves)
    own_go = Local(net, gos, o_go, jnp.logical_not(moves))

    def deal(ref, total):
        for j in range(BATCH):
            ref[j] = total[j * z.rw : (j + 1) * z.rw]

    def end_gu():
        gus[...] = rs_gu.done()
        out_gu.start()

    def end_gi():
        deal(gis, rs_gi.done())
        ex_gi.start()
        own_gi.start()

    def end_gv():
        deal(gvs, jnp.concatenate([rs_gv.done(), jnp.zeros((rows_o, 256 - z.fh), F32)], axis=1))
        ex_gv.start()
        own_gv.start()

    def end_go():
        gos[...] = rs_go.done()[0 : z.rw]
        cp_go.start(gos, o_go)
        own_go.start()

    dv, d1 = k["dv"], dp
    co_1, co_1s = (Collect(net, d1.at[g], [k["d1b"].at[i, g] for i in range(4)], w) for g, w in ((0, None), (1, short)))

    def values_back(g, total):
        for s, block in enumerate(slots_of([part.astype(BF) for part in total], z)):
            dv[g, s * r : (s + 1) * r] = block
        d1[g] = dot_nt(dv[g], k["wv"][...]).reshape(BATCH, r, d).astype(BF)

    def values_backs():
        total = [ring.done() for ring in rs_dv]
        co_d.sent()
        with scope("values_back"):
            values_back(0, total)
        co_1.start()

    def short_values_backs():
        cp_dvs.arrive(dvs.at[1])
        co_ds.sent()

        @pl.when(short)
        def _():
            with scope("values_back_short"):
                values_back(1, [dvs_own(h, p) + dvs[1, h].astype(F32) for h in range(z.hb)])

        co_1s.start()

    def grad_value():
        with scope("grad_w_value"):
            gv[...] = dot_tn(h1[0].reshape(rows4, d), dv[0])

            @pl.when(short)
            def _():
                gv[...] += dot_tn(h1[1].reshape(rows4, d), dv[1])

        rs_gv.hop()

    outs_vm, gts = k["outs"], k["gts"]
    out_rms = Local(net, rms, o_rms)
    out_out = [Local(net, outs_vm.at[g], o_out.at[g], w) for g, w in ((0, None), (1, short))]
    out_gt = [Local(net, gts.at[g], o_gt.at[g], w) for g, w in ((0, None), (1, short))]

    def end_out():
        co_o.done()
        with scope("end_out"):
            outs_vm[0] = (mid[0] + co_o.value()).astype(BF)
        out_out[0].start()

    def short_end_out():
        co_os.done()

        @pl.when(short)
        def _():
            with scope("end_out_short"):
                outs_vm[1] = (mid[1] + co_os.value()).astype(BF)

        out_out[1].start()

    def finish_tokens(g, collect):
        gts[g] = dmid[g] + norm_back(collect.value(), x[g, b].astype(F32), gain[0])

    def end_tokens():
        co_1.done()
        with scope("end_tokens"):
            finish_tokens(0, co_1)
        out_gt[0].start()

    def short_end_tokens():
        co_1s.done()

        @pl.when(short)
        def _():
            with scope("end_tokens_short"):
                finish_tokens(1, co_1s)

        out_gt[1].start()

    ready_wv()
    ag_wu.hop()
    ag_wv.hop()
    ready_wo()
    ag_wv.hop()
    sp_x.mid()
    ag_wo.hop()
    ag_wv.hop()
    ready_wi()
    ag_wu.hop()
    ready_gains()
    ready_values()
    ag_wo.hop()
    pass_on(2, -2)
    hop_v()
    probabilities()
    ag_wo.hop()
    sp_xs.mid()
    hop_v()
    hop_v()
    short_values()
    ag_wi.hop()
    ag_wo.done()
    pass_on(1, -1)
    pass_on(3, -3)
    mix()
    pass_on(4)
    sp_cs.mid()
    ag_wi.hop()
    short_mix()
    sp_c.mid()
    wo_done()
    sp_a.mid()
    ag_wu.hop()
    ag_wi.hop()
    branches()
    sp_as.mid()
    feeds()
    short_branches()
    short_feeds()
    co_d.mid()
    grad_in()
    grad_out()
    rs_gi.hop()
    middles()
    rs_gu.hop()
    sp_b.mid()
    co_ds.mid()
    finals()
    rs_gu.hop()
    mix_backs()
    short_middles()
    hop_dv()
    hop_dv()
    co_os.mid()
    sp_bs.mid()
    short_mix_backs()
    co_o.mid()
    grad_mixer()
    short_end_out()
    out_rms.start()
    hop_dv()
    grad_output()
    short_values_backs()
    values_backs()
    rs_gi.hop()
    grad_value()
    rs_go.hop()
    co_1s.mid()
    rs_gv.hop()
    rs_go.hop()
    co_1.mid()
    rs_gi.hop()
    rs_gv.hop()
    rs_go.hop()
    end_gi()
    rs_gv.hop()
    short_end_tokens()
    end_out()
    rs_gu.hop()
    end_go()
    end_tokens()
    end_gv()
    end_gu()

    ex_gm.done()
    ex_gi.done()
    ex_gv.done()
    cp_go.arrive(o_go)
    for copy in (own_gm, own_gi, own_gv, own_go, out_gu, out_rms, *out_out, *out_gt):
        copy.done()
    for copy in list(net.sent):
        copy.finish()
    assert net.used == z.sems


def one_device(
    pos, batch, tokens, seq_lens, mixer, gain_attn, w_value, w_output, gain_ffn, w_in, w_out, cotangent
):
    args = (tokens, seq_lens, mixer, gain_attn, w_value, w_output, gain_ffn, w_in, w_out, cotangent)
    if not fits(pos, batch, tokens, mixer, w_value, w_in, w_out):
        return per_device(*args)
    z = Sizes(pos, tokens, mixer, w_value, w_in, w_out)
    p, b = lax.axis_index("pos"), lax.axis_index("batch")
    first_long = seq_lens[0] > SHORT

    both = [
        jnp.where(first_long, array[:, g], array[:, 1 - g]) for array in (tokens, cotangent) for g in range(2)
    ]
    shapes = scratch(z)
    hbm, vmem = pl.BlockSpec(memory_space=pl.ANY), pl.BlockSpec(memory_space=pltpu.VMEM)
    out_shape = [
        jax.ShapeDtypeStruct((2, z.r, z.d), BF),
        jax.ShapeDtypeStruct((2, z.r, z.d), F32),
        jax.ShapeDtypeStruct((BATCH, z.hb, z.r, z.cb), BF),
        jax.ShapeDtypeStruct((BATCH, z.rw, 256), F32),
        jax.ShapeDtypeStruct((z.rw, z.d), F32),
        jax.ShapeDtypeStruct((BATCH, z.rw, z.fc), F32),
        jax.ShapeDtypeStruct((z.rf, z.d), F32),
        jax.ShapeDtypeStruct((2, 2, z.r, 128), F32),
    ]
    out, tokens_grad, mixer_grad, value_grad, output_grad, in_grad, out_grad, rms = pl.pallas_call(
        functools.partial(layer_kernel, z, list(shapes)),
        out_shape=out_shape,
        in_specs=[hbm] * 5 + [vmem] * 5 + [hbm],
        out_specs=[hbm] * len(out_shape),
        scratch_shapes=list(shapes.values()),
        compiler_params=pltpu.CompilerParams(
            collective_id=1, has_side_effects=True, vmem_limit_bytes=62 << 20
        ),
        name="layer",
    )(
        *both,
        mixer.reshape(BATCH, z.hb, z.r, z.cb),
        gain_attn.reshape(1, z.rw),
        gain_ffn.reshape(1, z.rw),
        w_value,
        w_output,
        w_in,
        w_out,
    )

    has_short = p < SHORT // z.r

    def unsort(array):
        one, two = array[0], jnp.where(has_short, array[1], 0)
        return jnp.stack([jnp.where(first_long, one, two), jnp.where(first_long, two, one)], axis=1)

    grad_value = jnp.swapaxes(value_grad[:, :, 0 : z.fh], 0, 1).reshape(z.rw, z.d)
    grad_in = jnp.transpose(in_grad.reshape(BATCH, z.rw, pos, z.rf), (1, 2, 0, 3)).reshape(z.rw, z.ff)
    gain_attn_grad = jnp.sum(w_value.astype(F32) * grad_value, axis=1) / gain_attn.astype(F32)
    gain_ffn_grad = jnp.sum(w_in.astype(F32) * grad_in, axis=1) / gain_ffn.astype(F32)
    return (
        unsort(out),
        unsort(tokens_grad),
        mixer_grad.reshape(z.heads, z.r, z.cb).astype(F32),
        gain_attn_grad,
        grad_value,
        output_grad,
        gain_ffn_grad,
        grad_in,
        out_grad,
        unsort(rms[0, :, :, 0]),
        unsort(rms[1, :, :, 0]),
    )


def solution(mesh):
    placed = (
        P("pos", "batch", None),
        P("batch"),
        P(None, "pos", "batch"),
        P(("pos", "batch")),
        P(("pos", "batch"), None),
        P(("pos", "batch"), None),
        P(("pos", "batch")),
        P(("pos", "batch"), None),
        P(("pos", "batch"), None),
        P("pos", "batch", None),
    )
    return jax.shard_map(
        functools.partial(one_device, mesh.shape["pos"], mesh.shape["batch"]),
        mesh=mesh,
        in_specs=placed,
        out_specs=(
            P("pos", "batch", None),
            P("pos", "batch", None),
            P(None, "pos", "batch"),
            P(("pos", "batch")),
            P(("pos", "batch"), None),
            P(("pos", "batch"), None),
            P(("pos", "batch")),
            P(("pos", "batch"), None),
            P(("pos", "batch"), None),
            P("pos", "batch"),
            P("pos", "batch"),
        ),
        check_vma=False,
    )
```

```python
import functools

import jax
import jax.numpy as jnp
from jax import lax
from jax.experimental import pallas as pl
from jax.experimental.pallas import tpu as pltpu
from jax.sharding import PartitionSpec as P

SHORT = 256


EPSILON = 1e-06


def norm_apply(values, gain_vec):
    inv_rms = lax.rsqrt(jnp.mean(values * values, axis=-1, keepdims=True) + EPSILON)
    return values * inv_rms * gain_vec


def gelu_exact(values):
    return jax.nn.gelu(values, approximate=False)


def row_stats(scores):
    top_score = jnp.max(scores, axis=-1)
    return top_score + jnp.log(jnp.sum(jnp.exp(scores - top_score[..., None]), axis=-1))


def contract_rows(left, right):
    return lax.dot_general(
        left, right, (((0,), (0,)), ((), ())), preferred_element_type=jnp.float32
    )


def contract_cols(left, right):
    return lax.dot_general(
        left, right, (((1,), (1,)), ((), ())), preferred_element_type=jnp.float32
    )


def per_device(
    tokens, seq_lens, mixer, gain_attn, w_value, w_output, gain_ffn, w_in, w_out, cotangent
):
    value_mat, output_mat, in_mat, out_mat, gain_one, gain_two = (
        lax.all_gather(w_value, ("pos", "batch"), axis=0, tiled=True),
        lax.all_gather(w_output, ("pos", "batch"), axis=0, tiled=True),
        lax.all_gather(w_in, ("pos", "batch"), axis=0, tiled=True),
        lax.all_gather(w_out, ("pos", "batch"), axis=0, tiled=True),
        lax.all_gather(gain_attn, ("pos", "batch"), axis=0, tiled=True),
        lax.all_gather(gain_ffn, ("pos", "batch"), axis=0, tiled=True),
    )
    rows_r = lax.all_gather(mixer, "batch", axis=2, tiled=True)
    head_count = rows_r.shape[0]
    long_len = rows_r.shape[2]
    row_count, slot_count, width = tokens.shape
    head_dim = width // head_count
    tok_count = row_count * slot_count
    start_row = lax.axis_index("pos") * row_count
    positions = start_row + jnp.arange(row_count, dtype=jnp.int32)
    live_mask = (positions[:, None] < seq_lens[None, :]).astype(jnp.float32)
    live_col = live_mask.reshape(tok_count, 1)
    is_long = seq_lens > SHORT
    gain_first = gain_one.astype(jnp.float32)
    gain_second = gain_two.astype(jnp.float32)
    x_float = tokens.astype(jnp.float32).reshape(tok_count, width)
    normed_one = norm_apply(x_float, gain_first).astype(jnp.bfloat16)
    value = jnp.dot(normed_one, value_mat, preferred_element_type=jnp.float32).astype(jnp.bfloat16)
    value = value.reshape(row_count, slot_count, width)
    lse_long = row_stats(rows_r.astype(jnp.float32))
    head_cols = rows_r[:, :, :SHORT].astype(jnp.float32)
    lse_short = row_stats(head_cols)
    prob_head = jnp.exp(head_cols - lse_short[..., None])

    def prob_block(block, lse_l, lse_s, col_pos):
        prob_long = jnp.exp(block - lse_l[..., None])
        prob_short = jnp.where(col_pos < SHORT, jnp.exp(block - lse_s[..., None]), 0.0)
        return jnp.where(is_long[:, None, None, None], prob_long[None], prob_short[None])

    def slot_probs(piece_len):
        columns = rows_r.astype(jnp.float32)
        col_pos = jnp.arange(piece_len, dtype=jnp.int32)
        return prob_block(columns, lse_long, lse_short, col_pos)

    portion = lax.all_gather(value, "pos", axis=0, tiled=True)
    piece_len = portion.shape[0]
    prob_b = slot_probs(piece_len).astype(jnp.bfloat16)
    piece_vals = portion.reshape(piece_len, slot_count, head_count, head_dim)
    mixed = jnp.einsum("shin,nshe->ishe", prob_b, piece_vals, preferred_element_type=jnp.float32)
    attn_in = (mixed * live_mask[:, :, None, None]).astype(jnp.bfloat16).reshape(tok_count, width)
    branch = jnp.dot(attn_in, output_mat, preferred_element_type=jnp.float32)
    mid_resid = x_float + branch
    normed_two = norm_apply(mid_resid, gain_second).astype(jnp.bfloat16)
    up_proj = jnp.dot(normed_two, in_mat, preferred_element_type=jnp.float32)
    hidden = gelu_exact(up_proj).astype(jnp.bfloat16)
    summed_out = mid_resid + jnp.dot(hidden, out_mat, preferred_element_type=jnp.float32)
    output = (summed_out * live_col).astype(jnp.bfloat16).reshape(row_count, slot_count, width)
    resid_rms = (
        jnp.sqrt(jnp.mean(mid_resid * mid_resid, axis=-1) + EPSILON).reshape(row_count, slot_count)
        * live_mask
    )
    branch_rms = (
        jnp.sqrt(jnp.mean(branch * branch, axis=-1) + EPSILON).reshape(row_count, slot_count)
        * live_mask
    )
    dfinal = cotangent.reshape(tok_count, width) * live_col.astype(jnp.bfloat16)
    grad_w_out = contract_rows(hidden, dfinal)
    dhidden = contract_cols(dfinal, out_mat)
    _, gelu_back = jax.vjp(gelu_exact, up_proj)
    dupper = gelu_back(dhidden)[0].astype(jnp.bfloat16)
    grad_w_in = contract_rows(normed_two, dupper)
    d_normed_two = contract_cols(dupper, in_mat)
    _, norm_back_two = jax.vjp(norm_apply, mid_resid, gain_second)
    d_mid_norm, grad_gain_ffn = norm_back_two(d_normed_two)
    d_mid = dfinal.astype(jnp.float32) + d_mid_norm
    dbranch = d_mid.astype(jnp.bfloat16)
    grad_w_output = contract_rows(attn_in, dbranch)
    d_attn = contract_cols(dbranch, output_mat).astype(jnp.bfloat16)
    d_attn = d_attn.reshape(row_count, slot_count, head_count, head_dim)
    portion = lax.all_gather(value, "pos", axis=0, tiled=True)
    piece_len = portion.shape[0]
    prob_f = slot_probs(piece_len)
    piece_vals = portion.reshape(piece_len, slot_count, head_count, head_dim)
    d_prob = jnp.einsum("ishe,nshe->shin", d_attn, piece_vals, preferred_element_type=jnp.float32)
    weighted = prob_f * d_prob
    grad_acc = jnp.sum(weighted, axis=0)
    grad_acc, delta_all = (grad_acc, jnp.sum(weighted, axis=-1))
    delta_long = jnp.sum(jnp.where(is_long[:, None, None], delta_all, 0.0), axis=0)
    delta_short = jnp.sum(jnp.where(is_long[:, None, None], 0.0, delta_all), axis=0)
    slots_here = d_attn.shape[1]
    col_block = lax.all_to_all(rows_r, "pos", split_axis=2, concat_axis=1, tiled=True)
    lse_all_long = lax.all_gather(lse_long, "pos", axis=1, tiled=True)
    lse_all_short = lax.all_gather(lse_short, "pos", axis=1, tiled=True)
    portion = lax.all_gather(d_attn, "pos", axis=0, tiled=True)
    piece_len = portion.shape[0]
    block = col_block.astype(jnp.float32)
    lse_l = lse_all_long
    lse_s = lse_all_short
    prob_b = prob_block(block, lse_l, lse_s, positions).astype(jnp.bfloat16)
    term = jnp.einsum("shij,ishe->jshe", prob_b, portion, preferred_element_type=jnp.float32)
    dvalue = term.reshape(row_count, slots_here, width)
    full_long = jnp.exp(rows_r.astype(jnp.float32) - lse_long[..., None])
    grad_rows = grad_acc - full_long * delta_long[..., None]
    correction = prob_head * delta_short[..., None]
    grad_rows = grad_rows - jnp.pad(correction, ((0, 0), (0, 0), (0, long_len - SHORT)))
    dvalue_b = dvalue.astype(jnp.bfloat16).reshape(tok_count, width)
    grad_w_value = contract_rows(normed_one, dvalue_b)
    d_normed_one = contract_cols(dvalue_b, value_mat)
    _, norm_back_one = jax.vjp(norm_apply, x_float, gain_first)
    d_x_norm, grad_gain_attn = norm_back_one(d_normed_one)
    grad_tokens = (d_mid + d_x_norm).reshape(row_count, slot_count, width)
    grad_mixer = lax.psum_scatter(
        grad_rows.astype(jnp.bfloat16), "batch", scatter_dimension=2, tiled=True
    ).astype(jnp.float32)
    reduced = (
        lax.psum_scatter(grad_w_value, ("pos", "batch"), scatter_dimension=0, tiled=True),
        lax.psum_scatter(grad_w_output, ("pos", "batch"), scatter_dimension=0, tiled=True),
        lax.psum_scatter(grad_w_in, ("pos", "batch"), scatter_dimension=0, tiled=True),
        lax.psum_scatter(grad_w_out, ("pos", "batch"), scatter_dimension=0, tiled=True),
        lax.psum_scatter(grad_gain_attn, ("pos", "batch"), scatter_dimension=0, tiled=True),
        lax.psum_scatter(grad_gain_ffn, ("pos", "batch"), scatter_dimension=0, tiled=True),
    )
    return (
        output,
        grad_tokens,
        grad_mixer,
        reduced[4],
        reduced[0],
        reduced[1],
        reduced[5],
        reduced[2],
        reduced[3],
        resid_rms,
        branch_rms,
    )


BF = jnp.bfloat16
F32 = jnp.float32
MESH = pl.DeviceIdType.MESH
HEAD = 64
BATCH = 4
LANE = 4 * HEAD


def dot(left, right):
    return jnp.dot(left, right, preferred_element_type=F32)


def dot_tn(left, right):
    return lax.dot_general(left, right, (((0,), (0,)), ((), ())), preferred_element_type=F32)


def dot_nt(left, right):
    return lax.dot_general(left, right, (((1,), (1,)), ((), ())), preferred_element_type=F32)


def up16(rows):
    return -(-rows // 16) * 16


class Sizes:
    def __init__(self, pos, tokens, mixer, w_value, w_in, w_out):
        self.n = pos
        self.r, _, self.d = tokens.shape
        self.heads, _, self.cb = mixer.shape
        self.long = pos * self.r
        self.hb = self.heads // BATCH
        self.fh = self.hb * HEAD
        self.rw = w_value.shape[0]
        self.rf = w_out.shape[0]
        self.ff = w_in.shape[1]
        self.fc = self.ff // BATCH
        self.rp = up16(self.rw + 8)
        self.gr = self.d // 256
        self.wr = BATCH * self.rw
        self.fold = self.wr // 2
        self.wt = self.wr + self.fold + 16
        self.sems = (8 + 2 * self.hb) * 2 * pos + 2 * (pos - 1) + 8 * pos + 158


def fits(pos, batch, tokens, mixer, w_value, w_in, w_out):
    r, _, d = tokens.shape
    heads = mixer.shape[0]
    rw, rf = w_value.shape[0], w_out.shape[0]
    return (
        batch == BATCH
        and pos >= 4
        and pos % 2 == 0
        and r % 128 == 0
        and SHORT == 2 * r
        and heads % BATCH == 0
        and heads * HEAD == d
        and d % 256 == 0
        and 2 * (d // 256) <= 8
        and rw % 8 == 0
        and rw % 16 == 8
        and rf % 32 == 0
        and (BATCH * rw) % 32 == 0
        and (w_in.shape[1] // BATCH) % 256 == 0
        and SHORT == mixer.shape[2]
    )


class Net:
    def __init__(self, n, sems):
        self.n = n
        self.sems = sems
        self.used = 0
        self.sent = []
        p, b = lax.axis_index("pos"), lax.axis_index("batch")
        self.p, self.b = p, b
        self.rho = self.ring(p)
        self.right = (self.place(lax.rem(self.rho + 1, n)), b)
        self.left = (self.place(lax.rem(self.rho + n - 1, n)), b)
        self.core_b = b + 1 - 2 * lax.rem(b, 2)
        self.y_b = lax.rem(b + 2, BATCH)
        self.far_b = BATCH - 1 - b
        self.core = (p, self.core_b)
        self.y = (p, self.y_b)
        self.far = (p, self.far_b)
        self.short = p < 2

    def ring(self, p):
        return jnp.where(lax.rem(p, 2) == 0, p // 2, self.n - 1 - p // 2)

    def place(self, rho):
        half = self.n // 2
        return jnp.where(rho < half, 2 * rho, 2 * (self.n - 1 - rho) + 1)

    def at(self, step):
        return self.place(lax.rem(self.rho + step + 2 * self.n, self.n))

    def sem(self):
        self.used += 1
        return self.sems.at[self.used - 1]


def run_if(cond, body):
    if cond is None:
        body()
    else:
        pl.when(cond)(body)


class Copy:
    def __init__(self, net, device, cond=None):
        self.net, self.device, self.cond = net, device, cond
        self.send, self.recv = net.sem(), net.sem()

    def of(self, src, dst):
        return pltpu.make_async_remote_copy(
            src_ref=src, dst_ref=dst, send_sem=self.send, recv_sem=self.recv,
            device_id=self.device, device_id_type=MESH,
        )

    def start(self, src, dst):
        run_if(self.cond, lambda: self.of(src, dst).start())
        self.src = src
        self.net.sent.append(self)

    def arrive(self, land):
        run_if(self.cond, lambda: self.of(land, land).wait_recv())

    def finish(self):
        run_if(self.cond, lambda: self.of(self.src, self.src).wait_send())
        self.net.sent.remove(self)


class Local:
    def __init__(self, net, src, dst, cond=None):
        self.copy = pltpu.make_async_copy(src, dst, net.sem())
        self.cond = cond

    def start(self):
        run_if(self.cond, self.copy.start)
        return self

    def done(self):
        run_if(self.cond, self.copy.wait)


class Exchange:
    def __init__(self, net, pick, land):
        self.net, self.pick, self.land = net, pick, land
        self.copies = [(Copy(net, d), j) for d, j in ((net.y, net.y_b), (net.far, net.far_b), (net.core, net.core_b))]

    def start(self):
        for copy, j in self.copies:
            copy.start(self.pick(j), self.land.at[self.net.b])

    def done(self):
        for copy, j in self.copies:
            copy.arrive(self.land.at[j])


class Spread:
    def __init__(self, net, slot, cond=None):
        self.net, self.slot = net, slot
        self.by_y, self.by_core, self.relay = (Copy(net, d, cond) for d in (net.y, net.core, net.core))

    def start(self, own=None):
        slot = self.slot(self.net.b)
        own = slot if own is None else own
        self.by_y.start(own, slot)
        self.by_core.start(own, slot)

    def mid(self):
        came = self.slot(self.net.y_b)
        self.by_y.arrive(came)
        self.relay.start(came, came)

    def done(self):
        self.by_core.arrive(self.slot(self.net.core_b))
        self.relay.arrive(self.slot(self.net.far_b))


class Collect:
    def __init__(self, net, part, bufs, cond=None):
        self.net, self.part, self.bufs, self.cond = net, part, bufs, cond
        self.to_other, self.to_mine, self.by_y = (Copy(net, d, cond) for d in (net.core, net.core, net.y))

    def start(self):
        net, (mine, other, _, _) = self.net, self.bufs
        self.to_other.start(self.part.at[net.far_b], other)
        self.to_mine.start(self.part.at[net.core_b], mine)

    def mid(self):
        net, (mine, other, stage, across) = self.net, self.bufs
        self.to_other.arrive(other)

        def add():
            stage[...] = (self.part[net.y_b].astype(F32) + other[...].astype(F32)).astype(BF)

        run_if(self.cond, add)
        self.by_y.start(stage, across)

    def done(self):
        self.to_mine.arrive(self.bufs[0])
        self.by_y.arrive(self.bufs[3])

    def sent(self):
        self.to_other.finish()
        self.to_mine.finish()

    def value(self):
        return self.part[self.net.b].astype(F32) + self.bufs[0][...].astype(F32) + self.bufs[3][...].astype(F32)


class Gather:
    def __init__(self, net, slot, first, second):
        self.net, self.slot, self.halves = net, slot, (first, second)
        self.steps, self.next = net.n // 2, 0
        self.copies = [[Copy(net, d) for _ in range(self.steps)] for d in (net.right, net.left)]

    def hop(self, own=None):
        net, t = self.net, self.next
        if t == self.steps:
            return
        self.next += 1
        for way, sign in ((0, -1), (1, 1)):
            came = self.slot(net.at(sign * t))
            if t:
                self.copies[way][t - 1].arrive(came)
            if t == self.steps - 1:
                came = self.halves[way](net.at(sign * t))
            self.copies[way][t].start(came if own is None else own, came)

    def done(self):
        while self.next < self.steps:
            self.hop()
        for way in (0, 1):
            self.copies[way][-1].arrive(self.halves[way](self.net.at(self.steps)))


class Scatter:
    def __init__(self, net, own, held, came, cut):
        self.net, self.own, self.held, self.came = net, own, held, came
        self.steps, self.next = net.n // 2, 0
        self.spans = (slice(0, cut), slice(cut, held.shape[-2]))
        self.copies = [[Copy(net, d) for _ in range(self.steps)] for d in (net.right, net.left)]

    def hop(self):
        net, t = self.net, self.next
        if t == self.steps:
            return
        self.next += 1
        if t == 0:
            value = self.own(net.at(self.steps))
        for way, sign in ((0, 1), (1, -1)):
            span, copies = self.spans[way], self.copies[way]
            if t == 0:
                self.held[way, 0, span] = value[span].astype(BF)
                copies[0].start(self.held.at[way, 0, span], self.came.at[way, 0, span])
                continue
            value = self.own(net.at(sign * (self.steps - t)))
            if t == 1:
                copies[0].arrive(self.came.at[way, 0, span])
                self.held[way, 1] = value.astype(BF)
                self.held[way, 1, span] = (value[span] + self.came[way, 0, span].astype(F32)).astype(BF)
            else:
                copies[t - 1].arrive(self.came.at[way, t - 1])
                self.held[way, t] = (value + self.came[way, t - 1].astype(F32)).astype(BF)
            copies[t].start(self.held.at[way, t], self.came.at[way, t])

    def done(self):
        while self.next < self.steps:
            self.hop()
        last = self.steps - 1
        for way in (0, 1):
            self.copies[way][last].arrive(self.came.at[way, last])
        return self.own(self.net.p) + self.came[0, last].astype(F32) + self.came[1, last].astype(F32)


def unit(values):
    inv = lax.rsqrt(jnp.mean(values * values, axis=-1, keepdims=True) + EPSILON)
    return values * inv, inv


def heads_of(rows, z):
    return [
        jnp.concatenate([rows[s * z.r : (s + 1) * z.r, h * HEAD : (h + 1) * HEAD] for s in range(BATCH)], axis=-1)
        for h in range(z.hb)
    ]


def slots_of(by_head, z):
    return [
        jnp.concatenate([by_head[h][:, s * HEAD : (s + 1) * HEAD] for h in range(z.hb)], axis=-1)
        for s in range(BATCH)
    ]


def scratch(z):
    n, r, d, half = z.n, z.r, z.d, z.n // 2
    vm = pltpu.VMEM
    slots, own = (2, BATCH, r, d), (2, r, d)

    def ring(*shape):
        return vm((2, half) + shape, BF)

    return dict(
        raw=vm((2, r, 2, d), BF), x=vm(slots, BF), c=vm(slots, BF), mx=vm((BATCH, z.hb, r, z.cb), BF),
        wvp=vm((BATCH, z.rp, 256), BF), wop=vm((BATCH, z.rp, d), BF), wip=vm((BATCH, z.rp, z.fc), BF),
        wvs=vm((BATCH, z.rp, 256), BF), wos=vm((z.rp, d), BF), wis=vm((BATCH, z.rp, z.fc), BF),
        wvg=vm((n, z.wt, 128), BF), wv=vm((d, z.fh), BF), wo=vm((d, d), BF), wi=vm((d, z.fc), BF), wu=vm((z.fc, d), BF),
        gain=vm((2, 1, d), F32),
        h1=vm(slots, BF), vl=vm((z.hb, z.long, LANE), BF), vs=vm((z.hb, SHORT, LANE), BF),
        pf=vm((z.hb, r, z.long), F32), pb=vm((z.hb, r, z.long), BF),
        qf=vm((z.hb, r, SHORT), F32), qb=vm((z.hb, r, SHORT), BF),
        mixed=vm((2, z.hb, r, LANE), F32), attn=vm((BATCH, 2, BATCH, r, z.fh), BF),
        mid=vm(own, F32), h2=vm(slots, BF),
        hid=vm((2, BATCH * r, z.fc), BF), dup=vm((2, BATCH * r, z.fc), BF),
        dp=vm(slots, BF), db=vm(slots, BF), dmid=vm(own, F32),
        dpb=vm((4,) + own, BF), opb=vm((4,) + own, BF), d1b=vm((4,) + own, BF),
        da=vm((2, z.hb, r, LANE), BF), dv=vm((2, BATCH * r, z.fh), BF), dvs=vm((2, z.hb, r, LANE), BF),
        gm0=vm((z.hb, r, z.cb), F32), slope=vm((BATCH * r, z.fc), F32),
        gu=vm((z.fc, d), F32), gi=vm((d, z.fc), F32), go=vm((z.fh, d), F32), gv=vm((d, z.fh), F32),
        gis=vm((BATCH, z.rw, z.fc), F32), gvs=vm((BATCH, z.rw, 256), F32), gos=vm((z.rw, d), F32), gus=vm((z.rf, d), F32),
        outs=vm(own, BF), gts=vm(own, F32), rms=vm((2, 2, r, 128), F32),
        guh=ring(z.rf, d), gur=ring(z.rf, d), gih=ring(BATCH * z.rw, z.fc), gir=ring(BATCH * z.rw, z.fc),
        goh=ring(2 * z.rw, d // 2), gor=ring(2 * z.rw, d // 2), gvh=ring(z.wr + z.fold, 128), gvr=ring(z.wr + z.fold, 128),
        dvh=vm((z.hb, 2, half, r, LANE), BF), dvr=vm((z.hb, 2, half, r, LANE), BF),
        sems=pltpu.SemaphoreType.DMA((z.sems,)),
    )


def layer_kernel(z, names, *refs):
    lens, tok, cot, mix_in, gain_1, gain_2, wv_in, wo_in, wi_in, wu_in = refs[:10]
    o_out, o_gt, o_gm, o_gv, o_go, o_gi, o_gu, o_rms = refs[10:18]
    k = dict(zip(names, refs[18:]))
    n, r, d = z.n, z.r, z.d
    rows4 = BATCH * r
    rows_o = BATCH * z.rw
    net = Net(n, k["sems"])
    p, b, short = net.p, net.b, net.short
    scope = jax.named_scope

    index = n * b + p
    goal = (index // BATCH, lax.rem(index, BATCH))
    mine = BATCH * p + b
    source = (lax.rem(mine, n), mine // n)
    moves = index != mine

    x, c, mx, wu, wvp, wop, wip = (k[name] for name in ("x", "c", "mx", "wu", "wvp", "wop", "wip"))

    def span(ref, size, lo=0, hi=None):
        hi = size if hi is None else hi
        return lambda q: ref.at[pl.ds(pl.multiple_of(q * size + lo, 16), hi - lo)]

    wu_span = span(wu, z.rf)
    raw_x = Local(net, tok, k["raw"].at[0]).start()
    own_wu = Local(net, wu_in, wu_span(p)).start()
    own_mx = Local(net, mix_in.at[b], mx.at[b]).start()
    raw_c = Local(net, cot, k["raw"].at[1]).start()

    def sort_slots(which, into):
        pair = k["raw"][which].astype(F32)
        one, two = pair[:, 0, :].astype(BF), pair[:, 1, :].astype(BF)
        first_long = jnp.full(one.shape, lens[0], jnp.int32) > SHORT
        into[0, b] = jnp.where(first_long, one, two)
        into[1, b] = jnp.where(first_long, two, one)

    barrier = pltpu.get_barrier_semaphore()
    for device in (net.right, net.left, net.core, net.y, net.far):
        pl.semaphore_signal(barrier, inc=1, device_id=device, device_id_type=MESH)

    @pl.when(moves)
    def _():
        for device in (goal, source):
            pl.semaphore_signal(barrier, inc=1, device_id=device, device_id_type=MESH)

    wvs, wos, wis = k["wvs"], k["wos"], k["wis"]
    place = lax.broadcasted_iota(jnp.int32, (z.rw, d), 1) - lax.broadcasted_iota(jnp.int32, (z.rw, d), 0)
    place = (place == mine * z.rw).astype(BF)
    table = [dot(ref[...], place) for ref in (gain_1, gain_2)]
    tail = [table[g][:, i * 256 : (i + 1) * 256] for g in range(2) for i in range(z.gr)]
    tail = jnp.concatenate(tail + [jnp.zeros((z.rp - z.rw - 2 * z.gr, 256), F32)], axis=0)
    held = wv_in[...].astype(F32)
    for j in range(BATCH):
        piece = jnp.concatenate([held[:, j * z.fh : (j + 1) * z.fh], jnp.zeros((z.rw, 256 - z.fh), F32)], axis=1)
        wvs[j] = jnp.concatenate([piece, tail], axis=0).astype(BF)
    wvp[b] = wvs[b]

    def prepare():
        fill = jnp.zeros((z.rp - z.rw, d), F32)
        wos[...] = jnp.concatenate([wo_in[...].astype(F32), fill], axis=0).astype(BF)
        wop[b] = wos[...]
        held = wi_in[...].astype(F32)
        fill = jnp.zeros((z.rp - z.rw, z.fc), F32)
        for j in range(BATCH):
            cols = [held[:, (BATCH * q + j) * z.rf : (BATCH * q + j + 1) * z.rf] for q in range(n)]
            wis[j] = jnp.concatenate([jnp.concatenate(cols, axis=1), fill], axis=0).astype(BF)
        wip[b] = wis[b]

    pl.semaphore_wait(barrier, jnp.where(moves, 7, 5))

    def first_wu(half):
        ag_wu[half].hop(wu_in.at[(slice(0, cut_f), slice(cut_f, z.rf))[half]])

    def start_x():
        raw_x.done()
        with scope("sort"):
            sort_slots(0, x)
        sp_x.start()

    def start_c():
        raw_c.done()
        with scope("sort"):
            sort_slots(1, c)
        sp_c.start()

    ex_wv = Exchange(net, lambda j: wvs.at[j], wvp)
    ex_wo = Exchange(net, lambda j: wos, wop)
    ex_wi = Exchange(net, lambda j: wis.at[j], wip)
    ex_mx = Exchange(net, lambda j: mix_in.at[j], mx)
    sp_x, sp_xs = Spread(net, lambda j: x.at[0, j]), Spread(net, lambda j: x.at[1, j], short)
    sp_c, sp_cs = Spread(net, lambda j: c.at[0, j]), Spread(net, lambda j: c.at[1, j], short)
    cut_f = up16(z.rf // 2)
    third_f = up16(cut_f // 2)
    third_i = up16(rows_o // 4)

    def two_rings(ref, size, cut, third):
        return (
            Gather(net, span(ref, size, 0, cut), span(ref, size, 0, third), span(ref, size, third, cut)),
            Gather(net, span(ref, size, cut), span(ref, size, cut, size - third), span(ref, size, size - third)),
        )

    ag_wu = two_rings(wu, z.rf, cut_f, third_f)

    wvg = k["wvg"]
    cut_v = up16(z.wt // 2)
    ag_wv = Gather(net, lambda q: wvg.at[q], lambda q: wvg.at[q, 0:cut_v], lambda q: wvg.at[q, cut_v : z.wt])

    def folded(block):
        rest = block[:, 128 : z.fh]
        return jnp.concatenate([block[:, 0:128], jnp.concatenate([rest[0 : z.fold], rest[z.fold :]], axis=1)], axis=0)

    def unfolded(block):
        rest = block[z.wr : z.wr + z.fold]
        rest = jnp.concatenate([rest[:, 0 : z.fh - 128], rest[:, z.fh - 128 :]], axis=0)
        return jnp.concatenate([block[0 : z.wr], rest], axis=1)

    def ready_wv():
        ex_wv.done()
        with scope("pack_wv"):
            weights = jnp.concatenate([wvp[j].astype(F32)[0 : z.rw] for j in range(BATCH)], axis=0)
            gains = sum(wvp[j].astype(F32)[z.rw : z.rw + 8] for j in range(BATCH))
            wvg[p] = jnp.concatenate([folded(weights), gains[:, 0:128], gains[:, 128:256]], axis=0).astype(BF)

    wo = k["wo"]
    half_o = rows_o // 2
    cut_o = up16(half_o // 2)
    core = lax.rem(b, 2)

    def wo_span(lo, hi, which):
        return lambda q: wo.at[pl.ds(pl.multiple_of(q * rows_o + which * half_o + lo, 16), hi - lo)]

    ag_wo = Gather(net, wo_span(0, half_o, core), wo_span(0, cut_o, core), wo_span(cut_o, half_o, core))
    pass_wo = {s: Copy(net, net.core) for s in range(1 - n // 2, n // 2 + 1) if s}

    def pack(ref):
        return jnp.concatenate([ref[j].astype(F32)[0 : z.rw] for j in range(BATCH)], axis=0).astype(BF)

    def ready_wo():
        ex_wo.done()
        with scope("pack_wo"):
            wo[pl.ds(pl.multiple_of(p * rows_o, 16), rows_o)] = pack(wop)

    def pass_on(*steps):
        for step in steps:
            block = wo_span(0, half_o, core)(net.at(step))
            pass_wo[step].start(block, block)

    def wo_done():
        for step, copy in pass_wo.items():
            copy.arrive(wo_span(0, half_o, 1 - core)(net.at(step)))

    wi = k["wi"]
    cut_i = up16(rows_o // 2)
    ag_wi = two_rings(wi, rows_o, cut_i, third_i)

    def ready_wi():
        ex_wi.done()
        with scope("pack_wi"):
            wi[pl.ds(pl.multiple_of(p * rows_o, 16), rows_o)] = pack(wip)

    h1, vl, vs, gain = k["h1"], k["vl"], k["vs"], k["gain"]
    here = pl.ds(pl.multiple_of(p * r, 16), r)
    twin = (1 - p, b)
    other = pl.ds(pl.multiple_of((1 - p) * r, 16), r)
    cp_vs, cp_dvs = Copy(net, twin, short), Copy(net, twin, short)

    def ready_gains():
        ag_wv.done()
        with scope("gains"):
            top = z.wr + z.fold
            table = jnp.sum(wvg[:, top : top + 16].astype(F32), axis=0)
            table = jnp.concatenate([table[0:8], table[8:16]], axis=1)
            for g in range(2):
                gain[g] = jnp.concatenate([table[g * z.gr + i : g * z.gr + i + 1] for i in range(z.gr)], axis=1)
            for q in range(n):
                k["wv"][q * z.wr : (q + 1) * z.wr] = unfolded(wvg[q])

    def values(g, into):
        for s in range(BATCH):
            h1[g, s] = (unit(x[g, s].astype(F32))[0] * gain[0]).astype(BF)
        value = dot(h1[g].reshape(rows4, d), k["wv"][...]).astype(BF)
        for h, block in enumerate(heads_of(value, z)):
            into[h, here, :] = block

    def vl_span(h, lo, hi):
        return lambda q: vl.at[h, pl.ds(pl.multiple_of(q * r + lo, 16), hi - lo), :]

    ag_v = [Gather(net, vl_span(h, 0, r), vl_span(h, 0, r // 2), vl_span(h, r // 2, r)) for h in range(z.hb)]

    def ready_values():
        sp_x.done()
        with scope("values"):
            values(0, vl)

    def short_values():
        sp_xs.done()

        @pl.when(short)
        def _():
            with scope("values_short"):
                values(1, vs)

        cp_vs.start(vs.at[:, here, :], vs.at[:, here, :])

    pf, pb, qf, qb = k["pf"], k["pb"], k["qf"], k["qb"]

    def probabilities():
        own_mx.done()
        ex_mx.done()
        with scope("probabilities"):
            for h in range(z.hb):
                total, first = 0.0, None
                for j in range(BATCH):
                    e = jnp.exp(mx[j, h].astype(F32))
                    pf[h, :, j * z.cb : (j + 1) * z.cb] = e
                    total = total + jnp.sum(e, axis=-1, keepdims=True)
                    first = total if j == 0 else first

                @pl.when(short)
                def _():
                    q = pf[h, :, 0:SHORT] * (1.0 / first)
                    qf[h] = q
                    qb[h] = q.astype(BF)

                scaled = pf[h] * (1.0 / total)
                pf[h] = scaled
                pb[h] = scaled.astype(BF)

    mixed, attn = k["mixed"], k["attn"]
    sp_a, sp_as = Spread(net, lambda j: attn.at[j, 0]), Spread(net, lambda j: attn.at[j, 1], short)

    def mix_slots(g):
        for s, block in enumerate(slots_of([mixed[g, h] for h in range(z.hb)], z)):
            attn[b, g, s] = block.astype(BF)

    def mix_head(h):
        ag_v[h].done()
        with scope("mix_head"):
            mixed[0, h] = dot(pb[h], vl[h])

    def mix():
        with scope("mix"):
            mix_slots(0)
        sp_a.start()

    def short_mix():
        cp_vs.arrive(vs.at[:, other, :])

        @pl.when(short)
        def _():
            with scope("mix_short"):
                for h in range(z.hb):
                    mixed[1, h] = dot(qb[h], vs[h])
                mix_slots(1)

        sp_as.start()

    big, mid, h2, rms = k["gu"], k["mid"], k["h2"], k["rms"]

    def branch_slots(g):
        big[0:rows4] = sum(
            dot(attn[j, g].reshape(rows4, z.fh), wo[j * z.fh : (j + 1) * z.fh]) for j in range(BATCH)
        )
        for s in range(BATCH):
            branch = big[s * r : (s + 1) * r]
            total = x[g, s].astype(F32) + branch
            square = jnp.mean(total * total, axis=-1, keepdims=True) + EPSILON
            h2[g, s] = (total * lax.rsqrt(square) * gain[1]).astype(BF)

            @pl.when(b == s)
            def _():
                mid[g] = total
                rms[0, g] = jnp.broadcast_to(jnp.sqrt(square), (r, 128))
                size = jnp.sqrt(jnp.mean(branch * branch, axis=-1, keepdims=True) + EPSILON)
                rms[1, g] = jnp.broadcast_to(size, (r, 128))

    def branches():
        sp_a.done()
        with scope("branches"):
            branch_slots(0)

    def short_branches():
        sp_as.done()

        @pl.when(short)
        def _():
            with scope("branches_short"):
                branch_slots(1)

    hid, dup, dp, op = k["hid"], k["dup"], k["dp"], h2
    halves = (slice(0, r // 2), slice(r // 2, r))
    co_d = [Collect(net, dp.at[0, :, rows], [k["dpb"].at[i, 0, rows] for i in range(4)]) for rows in halves]
    co_ds = Collect(net, dp.at[1], [k["dpb"].at[i, 1] for i in range(4)], short)
    co_o, co_os = (Collect(net, op.at[g], [k["opb"].at[i, g] for i in range(4)], w) for g, w in ((0, None), (1, short)))

    slopes = (k["gi"], k["slope"])

    def feed(g):
        left = h2[g].reshape(rows4, d)
        for q in range(z.fc // 256):
            cols = slice(q * 256, (q + 1) * 256)
            up = dot(left, wi[:, cols])
            cdf = 0.5 + 0.5 * lax.erf(up * 0.7071067811865476)
            hid[g, :, cols] = (up * cdf).astype(BF)
            slopes[g][0:rows4, cols] = cdf + up * (jnp.exp(-0.5 * up * up) * 0.3989422804014327)

    def feed_back(g):
        down = c[g].reshape(rows4, d)
        for q in range(z.fc // 256):
            cols = slice(q * 256, (q + 1) * 256)
            dup[g, :, cols] = (dot_nt(down, wu[cols, :]) * slopes[g][0:rows4, cols]).astype(BF)
        for q in range(d // 256):
            rows = slice(q * 256, (q + 1) * 256)
            dp[g, :, :, rows] = dot_nt(dup[g], wi[rows, :]).reshape(BATCH, r, 256).astype(BF)

    def feeds():
        for ring in ag_wi:
            ring.done()
        with scope("feed"):
            feed(0)

    def short_feeds():
        @pl.when(short)
        def _():
            with scope("feed_short"):
                feed(1)

    def feed_backs():
        for ring in ag_wu:
            ring.done()
        own_wu.done()
        with scope("feed_back"):
            feed_back(0)
        for part in co_d:
            part.start()

    def ready_c():
        sp_c.done()

    def ready_cs():
        sp_cs.done()

    def short_feed_backs():
        @pl.when(short)
        def _():
            with scope("feed_back_short"):
                feed_back(1)

        co_ds.start()

    gu, gi, gv, go = k["gu"], k["gi"], k["gv"], k["go"]

    def rows_at(ref, size):
        return lambda q: ref[pl.ds(pl.multiple_of(q * size, 8), size)]

    def two_scatters(ref, size, cut, third, held, came):
        def rows(lo, hi):
            return lambda q: ref[pl.ds(pl.multiple_of(q * size + lo, 8), hi - lo)]

        def view(ref, lo, hi):
            return ref.at[:, :, lo:hi]

        return (
            Scatter(net, rows(0, cut), view(held, 0, cut), view(came, 0, cut), third),
            Scatter(net, rows(cut, size), view(held, cut, size), view(came, cut, size), size - third - cut),
        )

    rs_gu = two_scatters(gu, z.rf, cut_f, third_f, k["guh"], k["gur"])
    rs_gi = two_scatters(gi, rows_o, cut_i, third_i, k["gih"], k["gir"])
    rs_gv = Scatter(net, lambda q: folded(rows_at(gv, rows_o)(q)), k["gvh"], k["gvr"], up16((z.wr + z.fold) // 2))

    def weight_grad(into, left, right, width, g):
        for q in range(width // 256):
            cols = slice(q * 256, (q + 1) * 256)
            term = dot_tn(left, right(cols))
            into[:, cols] = into[:, cols] + term if g else term

    def grad_out_of(g):
        weight_grad(gu, hid[g], lambda cols: c[g, :, :, cols].reshape(rows4, 256), d, g)

    def grad_out():
        with scope("grad_w_out"):
            grad_out_of(0)

    def short_grad_out():
        @pl.when(short)
        def _():
            with scope("grad_w_out_short"):
                grad_out_of(1)

    def grad_in_of(g):
        weight_grad(gi, h2[g].reshape(rows4, d), lambda cols: dup[g, :, cols], z.fc, g)

    def grad_in():
        with scope("grad_w_in"):
            grad_in_of(0)

    def short_grad_in():
        @pl.when(short)
        def _():
            with scope("grad_w_in_short"):
                grad_in_of(1)

    def outs(g):
        for q in range(d // 256):
            cols = slice(q * 256, (q + 1) * 256)
            op[g, :, :, cols] = dot(hid[g], wu[:, cols]).reshape(BATCH, r, 256).astype(BF)

    def finals():
        with scope("outs"):
            outs(0)
        co_o.start()

    def short_finals():
        @pl.when(short)
        def _():
            with scope("outs_short"):
                outs(1)

        co_os.start()

    db, dmid = k["db"], k["dmid"]
    sp_b = [Spread(net, functools.partial(lambda rows, j: db.at[0, j, rows], rows)) for rows in halves]
    sp_bs = Spread(net, lambda j: db.at[1, j], short)

    def norm_back(upper, values, gain):
        normed, inv = unit(values)
        scaled = upper * gain
        return inv * (scaled - normed * jnp.mean(scaled * normed, axis=-1, keepdims=True))

    def middle(g, collect, rows):
        grad = c[g, b, rows].astype(F32) + norm_back(collect.value(), mid[g, rows], gain[1])
        dmid[g, rows] = grad
        db[g, b, rows] = grad.astype(BF)

    def middles(half):
        co_d[half].done()
        with scope("middle"):
            middle(0, co_d[half], halves[half])
        sp_b[half].start()

    def short_middles():
        co_ds.done()

        @pl.when(short)
        def _():
            with scope("middle_short"):
                middle(1, co_ds, slice(0, r))

        sp_bs.start()

    da, dvs = k["da"], k["dvs"]
    wo_rows = pl.ds(pl.multiple_of(b * z.fh, 16), z.fh)

    def mix_back(g):
        grad = dot_nt(db[g].reshape(rows4, d), wo[wo_rows]).astype(BF)
        for h, block in enumerate(heads_of(grad, z)):
            da[g, h] = block

    def dv_own(h):
        return lambda q: dot_tn(pb[h, :, pl.ds(pl.multiple_of(q * r, 128), r)], da[0, h])

    rs_dv = [Scatter(net, dv_own(h), k["dvh"].at[h], k["dvr"].at[h], r // 2) for h in range(z.hb)]

    def hop_dv(h):
        with scope("dv_hop"):
            rs_dv[h].hop()

    def mix_backs():
        for part in sp_b:
            part.done()
        with scope("mix_back"):
            mix_back(0)

    def dvs_own(h, q):
        return dot_tn(qb[h, :, pl.ds(pl.multiple_of(q * r, 128), r)], da[1, h])

    def short_mix_backs():
        sp_bs.done()

        @pl.when(short)
        def _():
            with scope("mix_back_short"):
                mix_back(1)
                for h in range(z.hb):
                    dvs[0, h] = dvs_own(h, 1 - p).astype(BF)

        cp_dvs.start(dvs.at[0], dvs.at[1])

    def go_own(q):
        part = go[pl.ds(pl.multiple_of(q * z.rw, 8), z.rw)]
        return jnp.concatenate([part[:, 0 : d // 2], part[:, d // 2 :]], axis=0)

    rs_go = Scatter(net, go_own, k["goh"], k["gor"], up16(z.rw))

    def grad_output():
        with scope("grad_w_output"):
            go[...] = dot_tn(attn[b, 0].reshape(rows4, z.fh), db[0].reshape(rows4, d))

    def short_grad_output():
        @pl.when(short)
        def _():
            with scope("grad_w_output_short"):
                go[...] += dot_tn(attn[b, 1].reshape(rows4, z.fh), db[1].reshape(rows4, d))

    gms, gm0 = mx, k["gm0"]
    ex_gm = Exchange(net, lambda j: gms.at[j], o_gm)
    own_gm = Local(net, gms.at[b], o_gm.at[b])

    def grad_mixer():
        with scope("grad_mixer"):
            for h in range(z.hb):
                delta = jnp.sum(da[0, h].astype(F32) * mixed[0, h], axis=-1, keepdims=True)
                for j in range(BATCH):
                    cols = slice(j * z.cb, (j + 1) * z.cb)
                    part = pf[h, :, cols] * (dot_nt(da[0, h], vl[h, cols, :]) - delta)
                    gms[j, h] = part.astype(BF)
                    if j == 0:
                        gm0[h] = part

    def short_grad_mixer():
        @pl.when(short)
        def _():
            with scope("grad_mixer_short"):
                for h in range(z.hb):
                    delta = jnp.sum(da[1, h].astype(F32) * mixed[1, h], axis=-1, keepdims=True)
                    gms[0, h] = (gm0[h] + qf[h] * (dot_nt(da[1, h], vs[h]) - delta)).astype(BF)

        ex_gm.start()
        own_gm.start()

    gis, gvs, gos, gus = k["gis"], k["gvs"], k["gos"], k["gus"]
    ex_gi, ex_gv = Exchange(net, lambda j: gis.at[j], o_gi), Exchange(net, lambda j: gvs.at[j], o_gv)
    own_gi, own_gv = Local(net, gis.at[b], o_gi.at[b]), Local(net, gvs.at[b], o_gv.at[b])
    out_gu = Local(net, gus, o_gu)
    cp_go = Copy(net, goal, moves)
    own_go = Local(net, gos, o_go, jnp.logical_not(moves))

    def deal(ref, total):
        for j in range(BATCH):
            ref[j] = total[j * z.rw : (j + 1) * z.rw]

    def end_gu():
        gus[...] = jnp.concatenate([ring.done() for ring in rs_gu], axis=0)
        out_gu.start()

    def end_gi():
        deal(gis, jnp.concatenate([ring.done() for ring in rs_gi], axis=0))
        ex_gi.start()
        own_gi.start()

    def end_gv():
        deal(gvs, jnp.concatenate([unfolded(rs_gv.done()), jnp.zeros((rows_o, 256 - z.fh), F32)], axis=1))
        ex_gv.start()
        own_gv.start()

    def end_go():
        total = rs_go.done()
        gos[...] = jnp.concatenate([total[0 : z.rw], total[z.rw :]], axis=1)
        cp_go.start(gos, o_go)
        own_go.start()

    dv, d1 = k["dv"], dp
    co_1, co_1s = (Collect(net, d1.at[g], [k["d1b"].at[i, g] for i in range(4)], w) for g, w in ((0, None), (1, short)))

    def values_back(g, total):
        for s, block in enumerate(slots_of([part.astype(BF) for part in total], z)):
            dv[g, s * r : (s + 1) * r] = block
        d1[g] = dot_nt(dv[g], k["wv"][...]).reshape(BATCH, r, d).astype(BF)

    def values_backs():
        total = [ring.done() for ring in rs_dv]
        for part in co_d:
            part.sent()
        with scope("values_back"):
            values_back(0, total)
        co_1.start()

    def short_values_backs():
        cp_dvs.arrive(dvs.at[1])
        co_ds.sent()

        @pl.when(short)
        def _():
            with scope("values_back_short"):
                values_back(1, [dvs_own(h, p) + dvs[1, h].astype(F32) for h in range(z.hb)])

        co_1s.start()

    def grad_value():
        with scope("grad_w_value"):
            gv[...] = dot_tn(h1[0].reshape(rows4, d), dv[0])

    def short_grad_value():
        @pl.when(short)
        def _():
            with scope("grad_w_value_short"):
                gv[...] += dot_tn(h1[1].reshape(rows4, d), dv[1])

    outs_vm, gts = k["outs"], k["gts"]
    out_rms = Local(net, rms, o_rms)
    out_out = [Local(net, outs_vm.at[g], o_out.at[g], w) for g, w in ((0, None), (1, short))]
    out_gt = [Local(net, gts.at[g], o_gt.at[g], w) for g, w in ((0, None), (1, short))]

    def end_out():
        co_o.done()
        with scope("end_out"):
            outs_vm[0] = (mid[0] + co_o.value()).astype(BF)
        out_out[0].start()

    def short_end_out():
        co_os.done()

        @pl.when(short)
        def _():
            with scope("end_out_short"):
                outs_vm[1] = (mid[1] + co_os.value()).astype(BF)

        out_out[1].start()

    def finish_tokens(g, collect):
        gts[g] = dmid[g] + norm_back(collect.value(), x[g, b].astype(F32), gain[0])

    def end_tokens():
        co_1.done()
        with scope("end_tokens"):
            finish_tokens(0, co_1)
        out_gt[0].start()

    def short_end_tokens():
        co_1s.done()

        @pl.when(short)
        def _():
            with scope("end_tokens_short"):
                finish_tokens(1, co_1s)

        out_gt[1].start()

    prepare()
    first_wu(0)
    ex_wv.start()
    first_wu(1)
    ex_wo.start()
    ex_wi.start()
    ready_wv()
    ag_wv.hop()
    ag_wu[0].hop()
    start_x()
    ready_wo()
    ag_wo.hop()
    ag_wv.hop()
    ready_wi()
    ag_wu[1].hop()
    ag_wv.hop()
    ag_wo.hop()
    sp_xs.start()
    sp_x.mid()
    ag_wi[1].hop()
    ag_wv.hop()
    start_c()
    ex_mx.start()
    ag_wu[0].hop()
    ag_wo.hop()
    ready_gains()
    ready_values()
    sp_cs.start()
    ag_v[1].hop()
    ag_v[0].hop()
    ag_v[2].hop()
    sp_xs.mid()
    ag_v[1].hop()
    ag_v[0].hop()
    short_values()
    ag_v[2].hop()
    ag_wo.hop()
    probabilities()
    ag_v[1].hop()
    ag_v[0].hop()
    short_mix()
    ag_v[2].hop()
    pass_on(3, -3)
    sp_cs.mid()
    ag_wo.done()
    pass_on(2, -2)
    pass_on(4)
    ag_wi[0].hop()
    ag_v[0].hop()
    pass_on(1, -1)
    ag_v[2].hop()
    ready_cs()
    ag_v[1].hop()
    wo_done()
    ag_wi[1].hop()
    ag_wi[0].hop()
    mix_head(2)
    mix_head(0)
    sp_as.mid()
    mix_head(1)
    mix()
    ag_wi[1].hop()
    ag_wi[0].hop()
    ag_wu[1].hop()
    short_branches()
    sp_c.mid()
    ag_wi[1].hop()
    sp_a.mid()
    ag_wi[0].hop()
    ag_wu[0].hop()
    ag_wu[1].hop()
    branches()
    feeds()
    ready_c()
    feed_backs()
    short_feeds()
    grad_out()
    co_d[1].mid()
    short_grad_out()
    rs_gu[0].hop()
    co_d[0].mid()
    short_feed_backs()
    rs_gu[1].hop()
    grad_in()
    out_rms.start()
    rs_gu[0].hop()
    middles(1)
    short_grad_in()
    rs_gi[0].hop()
    rs_gi[1].hop()
    rs_gu[1].hop()
    middles(0)
    finals()
    co_ds.mid()
    rs_gi[0].hop()
    sp_b[1].mid()
    rs_gi[1].hop()
    sp_b[0].mid()
    mix_backs()
    hop_dv(2)
    hop_dv(0)
    hop_dv(1)
    rs_gi[1].hop()
    hop_dv(2)
    short_middles()
    hop_dv(0)
    short_finals()
    hop_dv(1)
    hop_dv(2)
    co_o.mid()
    grad_mixer()
    hop_dv(0)
    hop_dv(1)
    co_os.mid()
    sp_bs.mid()
    short_mix_backs()
    hop_dv(1)
    grad_output()
    short_grad_output()
    short_grad_mixer()
    hop_dv(0)
    short_end_out()
    hop_dv(2)
    short_values_backs()
    rs_go.hop()
    rs_gi[0].hop()
    co_1s.mid()
    rs_gu[0].hop()
    values_backs()
    grad_value()
    short_grad_value()
    rs_gv.hop()
    co_1.mid()
    rs_go.hop()
    rs_gi[0].hop()
    rs_gv.hop()
    rs_go.hop()
    rs_gi[1].hop()
    rs_gv.hop()
    rs_go.hop()
    rs_gu[1].hop()
    end_gi()
    rs_gv.hop()
    end_go()
    rs_gu[0].hop()
    end_out()
    short_end_tokens()
    rs_gu[1].hop()
    end_tokens()
    end_gv()
    end_gu()

    ex_gm.done()
    ex_gi.done()
    ex_gv.done()
    cp_go.arrive(o_go)
    for copy in (own_gm, own_gi, own_gv, own_go, out_gu, out_rms, *out_out, *out_gt):
        copy.done()
    for copy in list(net.sent):
        copy.finish()
    assert net.used == z.sems


def finish_kernel(
    z, lens, outs, gts, gm, gv, go, gi, gu, rms, gain_1, gain_2, wv, wi,
    o_out, o_gt, o_gm, o_g1, o_gv, o_go, o_g2, o_gi, o_gu, o_rms_1, o_rms_2,
    v_out, v_gt, v_gm, v_gv, v_gi, v_rms, v_gu, v_go, s_out, s_gt, s_gm, s_gv, s_gi, sems,
):
    n, r = z.n, z.r
    used = []

    def copy(src, dst):
        used.append(pltpu.make_async_copy(src, dst, sems.at[len(used)]))
        used[-1].start()
        return used[-1]

    in_gt, in_out = copy(gts, v_gt), copy(outs, v_out)
    in_gm = [copy(gm.at[j], v_gm.at[j]) for j in range(BATCH)]
    in_gi, in_gv, in_rms = copy(gi, v_gi), copy(gv, v_gv), copy(rms, v_rms)
    in_gu, in_go = copy(gu, v_gu), copy(go, v_go)
    last = []
    first_long = lens[0] > SHORT
    has_short = lax.axis_index("pos") < SHORT // r

    def slots(ref):
        lower = jnp.where(has_short, ref[1].astype(F32), 0.0)
        upper = ref[0].astype(F32)
        return jnp.where(first_long, upper, lower), jnp.where(first_long, lower, upper)

    for came, held, out in ((in_gu, v_gu, o_gu), (in_go, v_go, o_go)):
        came.wait()
        last.append(copy(held, out))
    in_gt.wait()
    for s, block in enumerate(slots(v_gt)):
        s_gt[:, s, :] = block
    last.append(copy(s_gt, o_gt))
    for j in range(BATCH):
        in_gm[j].wait()
        for h in range(z.hb):
            s_gm[j * z.hb + h] = v_gm[j, h].astype(F32)
        part = slice(j * z.hb, (j + 1) * z.hb)
        last.append(copy(s_gm.at[part], o_gm.at[part]))
    in_out.wait()
    for s, block in enumerate(slots(v_out)):
        s_out[:, s, :] = block.astype(BF)
    last.append(copy(s_out, o_out))

    def gain_grad(weights, grad, gain):
        ones = jnp.ones((8, grad.shape[1]), F32)
        total = lax.dot_general(
            ones, weights[...].astype(F32) * grad, (((1,), (1,)), ((), ())),
            precision=lax.Precision.HIGHEST, preferred_element_type=F32,
        )
        return total[0:1] / gain[...].astype(F32)

    in_gi.wait()
    s_gi[...] = jnp.concatenate(
        [v_gi[j, :, q * z.rf : (q + 1) * z.rf] for q in range(n) for j in range(BATCH)], axis=1
    )
    last.append(copy(s_gi, o_gi))
    o_g2[...] = gain_grad(wi, s_gi[...], gain_2)
    in_gv.wait()
    s_gv[...] = jnp.concatenate([v_gv[j, :, 0 : z.fh] for j in range(BATCH)], axis=1)
    last.append(copy(s_gv, o_gv))
    o_g1[...] = gain_grad(wv, s_gv[...], gain_1)
    in_rms.wait()
    for i, ref in enumerate((o_rms_1, o_rms_2)):
        for s, block in enumerate(slots(v_rms.at[i])):
            ref[s : s + 1] = jnp.transpose(block)[0:1]
    for one in last:
        one.wait()


def finish(z, lens, results, gain_attn, gain_ffn, w_value, w_in):
    n, r, d = z.n, z.r, z.d
    vm, shape = pltpu.VMEM, jax.ShapeDtypeStruct
    hbm, vmem, smem = (pl.BlockSpec(memory_space=m) for m in (pl.ANY, pltpu.VMEM, pltpu.SMEM))
    taken = [(array.shape, array.dtype) for array in results]
    staged = [((r, 2, d), BF), ((r, 2, d), F32), ((z.heads, r, z.cb), F32), ((z.rw, d), F32), ((z.rw, z.ff), F32)]
    return pl.pallas_call(
        functools.partial(finish_kernel, z),
        out_shape=[
            shape((r, 2, d), BF), shape((r, 2, d), F32), shape((z.heads, r, z.cb), F32), shape((1, z.rw), F32),
            shape((z.rw, d), F32), shape((z.rw, d), F32), shape((1, z.rw), F32), shape((z.rw, z.ff), F32),
            shape((z.rf, d), F32), shape((2, r), F32), shape((2, r), F32),
        ],
        in_specs=[smem] + [hbm] * 8 + [vmem] * 4,
        out_specs=[hbm, hbm, hbm, vmem, hbm, hbm, vmem, hbm, hbm, vmem, vmem],
        scratch_shapes=[vm(*taken[i]) for i in (0, 1, 2, 3, 5, 7, 6, 4)]
        + [vm(*one) for one in staged]
        + [pltpu.SemaphoreType.DMA((24,))],
        compiler_params=pltpu.CompilerParams(vmem_limit_bytes=62 << 20),
        name="finish",
    )(lens, *results, gain_attn, gain_ffn, w_value, w_in)


def one_device(
    pos, batch, tokens, seq_lens, mixer, gain_attn, w_value, w_output, gain_ffn, w_in, w_out, cotangent
):
    args = (tokens, seq_lens, mixer, gain_attn, w_value, w_output, gain_ffn, w_in, w_out, cotangent)
    if not fits(pos, batch, tokens, mixer, w_value, w_in, w_out):
        return per_device(*args)
    z = Sizes(pos, tokens, mixer, w_value, w_in, w_out)
    shapes = scratch(z)
    hbm, vmem, smem = (pl.BlockSpec(memory_space=m) for m in (pl.ANY, pltpu.VMEM, pltpu.SMEM))
    out_shape = [
        jax.ShapeDtypeStruct((2, z.r, z.d), BF),
        jax.ShapeDtypeStruct((2, z.r, z.d), F32),
        jax.ShapeDtypeStruct((BATCH, z.hb, z.r, z.cb), BF),
        jax.ShapeDtypeStruct((BATCH, z.rw, 256), F32),
        jax.ShapeDtypeStruct((z.rw, z.d), F32),
        jax.ShapeDtypeStruct((BATCH, z.rw, z.fc), F32),
        jax.ShapeDtypeStruct((z.rf, z.d), F32),
        jax.ShapeDtypeStruct((2, 2, z.r, 128), F32),
    ]
    gain_attn, gain_ffn = gain_attn.reshape(1, z.rw), gain_ffn.reshape(1, z.rw)
    results = pl.pallas_call(
        functools.partial(layer_kernel, z, list(shapes)),
        out_shape=out_shape,
        in_specs=[smem] + [hbm] * 3 + [vmem] * 5 + [hbm],
        out_specs=[hbm] * len(out_shape),
        scratch_shapes=list(shapes.values()),
        compiler_params=pltpu.CompilerParams(
            collective_id=1, has_side_effects=True, vmem_limit_bytes=62 << 20
        ),
        name="layer",
    )(
        seq_lens,
        tokens,
        cotangent,
        mixer.reshape(BATCH, z.hb, z.r, z.cb),
        gain_attn,
        gain_ffn,
        w_value,
        w_output,
        w_in,
        w_out,
    )
    out, grad_tokens, grad_mixer, grad_1, grad_value, grad_output, grad_2, grad_in, grad_out, rms_1, rms_2 = finish(
        z, seq_lens, results, gain_attn, gain_ffn, w_value, w_in
    )
    return (
        out, grad_tokens, grad_mixer, grad_1.reshape(z.rw), grad_value, grad_output, grad_2.reshape(z.rw),
        grad_in, grad_out, rms_1.T, rms_2.T,
    )


def solution(mesh):
    placed = (
        P("pos", "batch", None),
        P("batch"),
        P(None, "pos", "batch"),
        P(("pos", "batch")),
        P(("pos", "batch"), None),
        P(("pos", "batch"), None),
        P(("pos", "batch")),
        P(("pos", "batch"), None),
        P(("pos", "batch"), None),
        P("pos", "batch", None),
    )
    return jax.shard_map(
        functools.partial(one_device, mesh.shape["pos"], mesh.shape["batch"]),
        mesh=mesh,
        in_specs=placed,
        out_specs=(
            P("pos", "batch", None),
            P("pos", "batch", None),
            P(None, "pos", "batch"),
            P(("pos", "batch")),
            P(("pos", "batch"), None),
            P(("pos", "batch"), None),
            P(("pos", "batch")),
            P(("pos", "batch"), None),
            P(("pos", "batch"), None),
            P("pos", "batch"),
            P("pos", "batch"),
        ),
        check_vma=False,
    )
```

```python
import functools
import types

import jax
import jax.numpy as jnp
from jax import lax
from jax.experimental import pallas as pl
from jax.experimental.pallas import tpu as pltpu
from jax.sharding import PartitionSpec as P

SHORT = 256


EPSILON = 1e-06


def norm_apply(values, gain_vec):
    inv_rms = lax.rsqrt(jnp.mean(values * values, axis=-1, keepdims=True) + EPSILON)
    return values * inv_rms * gain_vec


def gelu_exact(values):
    return jax.nn.gelu(values, approximate=False)


def row_stats(scores):
    top_score = jnp.max(scores, axis=-1)
    return top_score + jnp.log(jnp.sum(jnp.exp(scores - top_score[..., None]), axis=-1))


def contract_rows(left, right):
    return lax.dot_general(
        left, right, (((0,), (0,)), ((), ())), preferred_element_type=jnp.float32
    )


def contract_cols(left, right):
    return lax.dot_general(
        left, right, (((1,), (1,)), ((), ())), preferred_element_type=jnp.float32
    )


def per_device(
    tokens, seq_lens, mixer, gain_attn, w_value, w_output, gain_ffn, w_in, w_out, cotangent
):
    value_mat, output_mat, in_mat, out_mat, gain_one, gain_two = (
        lax.all_gather(w_value, ("pos", "batch"), axis=0, tiled=True),
        lax.all_gather(w_output, ("pos", "batch"), axis=0, tiled=True),
        lax.all_gather(w_in, ("pos", "batch"), axis=0, tiled=True),
        lax.all_gather(w_out, ("pos", "batch"), axis=0, tiled=True),
        lax.all_gather(gain_attn, ("pos", "batch"), axis=0, tiled=True),
        lax.all_gather(gain_ffn, ("pos", "batch"), axis=0, tiled=True),
    )
    rows_r = lax.all_gather(mixer, "batch", axis=2, tiled=True)
    head_count = rows_r.shape[0]
    long_len = rows_r.shape[2]
    row_count, slot_count, width = tokens.shape
    head_dim = width // head_count
    tok_count = row_count * slot_count
    start_row = lax.axis_index("pos") * row_count
    positions = start_row + jnp.arange(row_count, dtype=jnp.int32)
    live_mask = (positions[:, None] < seq_lens[None, :]).astype(jnp.float32)
    live_col = live_mask.reshape(tok_count, 1)
    is_long = seq_lens > SHORT
    gain_first = gain_one.astype(jnp.float32)
    gain_second = gain_two.astype(jnp.float32)
    x_float = tokens.astype(jnp.float32).reshape(tok_count, width)
    normed_one = norm_apply(x_float, gain_first).astype(jnp.bfloat16)
    value = jnp.dot(normed_one, value_mat, preferred_element_type=jnp.float32).astype(jnp.bfloat16)
    value = value.reshape(row_count, slot_count, width)
    lse_long = row_stats(rows_r.astype(jnp.float32))
    head_cols = rows_r[:, :, :SHORT].astype(jnp.float32)
    lse_short = row_stats(head_cols)
    prob_head = jnp.exp(head_cols - lse_short[..., None])

    def prob_block(block, lse_l, lse_s, col_pos):
        prob_long = jnp.exp(block - lse_l[..., None])
        prob_short = jnp.where(col_pos < SHORT, jnp.exp(block - lse_s[..., None]), 0.0)
        return jnp.where(is_long[:, None, None, None], prob_long[None], prob_short[None])

    def slot_probs(piece_len):
        columns = rows_r.astype(jnp.float32)
        col_pos = jnp.arange(piece_len, dtype=jnp.int32)
        return prob_block(columns, lse_long, lse_short, col_pos)

    portion = lax.all_gather(value, "pos", axis=0, tiled=True)
    piece_len = portion.shape[0]
    prob_b = slot_probs(piece_len).astype(jnp.bfloat16)
    piece_vals = portion.reshape(piece_len, slot_count, head_count, head_dim)
    mixed = jnp.einsum("shin,nshe->ishe", prob_b, piece_vals, preferred_element_type=jnp.float32)
    attn_in = (mixed * live_mask[:, :, None, None]).astype(jnp.bfloat16).reshape(tok_count, width)
    branch = jnp.dot(attn_in, output_mat, preferred_element_type=jnp.float32)
    mid_resid = x_float + branch
    normed_two = norm_apply(mid_resid, gain_second).astype(jnp.bfloat16)
    up_proj = jnp.dot(normed_two, in_mat, preferred_element_type=jnp.float32)
    hidden = gelu_exact(up_proj).astype(jnp.bfloat16)
    summed_out = mid_resid + jnp.dot(hidden, out_mat, preferred_element_type=jnp.float32)
    output = (summed_out * live_col).astype(jnp.bfloat16).reshape(row_count, slot_count, width)
    resid_rms = (
        jnp.sqrt(jnp.mean(mid_resid * mid_resid, axis=-1) + EPSILON).reshape(row_count, slot_count)
        * live_mask
    )
    branch_rms = (
        jnp.sqrt(jnp.mean(branch * branch, axis=-1) + EPSILON).reshape(row_count, slot_count)
        * live_mask
    )
    dfinal = cotangent.reshape(tok_count, width) * live_col.astype(jnp.bfloat16)
    grad_w_out = contract_rows(hidden, dfinal)
    dhidden = contract_cols(dfinal, out_mat)
    _, gelu_back = jax.vjp(gelu_exact, up_proj)
    dupper = gelu_back(dhidden)[0].astype(jnp.bfloat16)
    grad_w_in = contract_rows(normed_two, dupper)
    d_normed_two = contract_cols(dupper, in_mat)
    _, norm_back_two = jax.vjp(norm_apply, mid_resid, gain_second)
    d_mid_norm, grad_gain_ffn = norm_back_two(d_normed_two)
    d_mid = dfinal.astype(jnp.float32) + d_mid_norm
    dbranch = d_mid.astype(jnp.bfloat16)
    grad_w_output = contract_rows(attn_in, dbranch)
    d_attn = contract_cols(dbranch, output_mat).astype(jnp.bfloat16)
    d_attn = d_attn.reshape(row_count, slot_count, head_count, head_dim)
    portion = lax.all_gather(value, "pos", axis=0, tiled=True)
    piece_len = portion.shape[0]
    prob_f = slot_probs(piece_len)
    piece_vals = portion.reshape(piece_len, slot_count, head_count, head_dim)
    d_prob = jnp.einsum("ishe,nshe->shin", d_attn, piece_vals, preferred_element_type=jnp.float32)
    weighted = prob_f * d_prob
    grad_acc = jnp.sum(weighted, axis=0)
    grad_acc, delta_all = (grad_acc, jnp.sum(weighted, axis=-1))
    delta_long = jnp.sum(jnp.where(is_long[:, None, None], delta_all, 0.0), axis=0)
    delta_short = jnp.sum(jnp.where(is_long[:, None, None], 0.0, delta_all), axis=0)
    slots_here = d_attn.shape[1]
    col_block = lax.all_to_all(rows_r, "pos", split_axis=2, concat_axis=1, tiled=True)
    lse_all_long = lax.all_gather(lse_long, "pos", axis=1, tiled=True)
    lse_all_short = lax.all_gather(lse_short, "pos", axis=1, tiled=True)
    portion = lax.all_gather(d_attn, "pos", axis=0, tiled=True)
    piece_len = portion.shape[0]
    block = col_block.astype(jnp.float32)
    lse_l = lse_all_long
    lse_s = lse_all_short
    prob_b = prob_block(block, lse_l, lse_s, positions).astype(jnp.bfloat16)
    term = jnp.einsum("shij,ishe->jshe", prob_b, portion, preferred_element_type=jnp.float32)
    dvalue = term.reshape(row_count, slots_here, width)
    full_long = jnp.exp(rows_r.astype(jnp.float32) - lse_long[..., None])
    grad_rows = grad_acc - full_long * delta_long[..., None]
    correction = prob_head * delta_short[..., None]
    grad_rows = grad_rows - jnp.pad(correction, ((0, 0), (0, 0), (0, long_len - SHORT)))
    dvalue_b = dvalue.astype(jnp.bfloat16).reshape(tok_count, width)
    grad_w_value = contract_rows(normed_one, dvalue_b)
    d_normed_one = contract_cols(dvalue_b, value_mat)
    _, norm_back_one = jax.vjp(norm_apply, x_float, gain_first)
    d_x_norm, grad_gain_attn = norm_back_one(d_normed_one)
    grad_tokens = (d_mid + d_x_norm).reshape(row_count, slot_count, width)
    grad_mixer = lax.psum_scatter(
        grad_rows.astype(jnp.bfloat16), "batch", scatter_dimension=2, tiled=True
    ).astype(jnp.float32)
    reduced = (
        lax.psum_scatter(grad_w_value, ("pos", "batch"), scatter_dimension=0, tiled=True),
        lax.psum_scatter(grad_w_output, ("pos", "batch"), scatter_dimension=0, tiled=True),
        lax.psum_scatter(grad_w_in, ("pos", "batch"), scatter_dimension=0, tiled=True),
        lax.psum_scatter(grad_w_out, ("pos", "batch"), scatter_dimension=0, tiled=True),
        lax.psum_scatter(grad_gain_attn, ("pos", "batch"), scatter_dimension=0, tiled=True),
        lax.psum_scatter(grad_gain_ffn, ("pos", "batch"), scatter_dimension=0, tiled=True),
    )
    return (
        output,
        grad_tokens,
        grad_mixer,
        reduced[4],
        reduced[0],
        reduced[1],
        reduced[5],
        reduced[2],
        reduced[3],
        resid_rms,
        branch_rms,
    )


BF = jnp.bfloat16
F32 = jnp.float32
MESH = pl.DeviceIdType.MESH
HEAD = 64
BATCH = 4
LANE = 4 * HEAD


def dot(left, right):
    return jnp.dot(left, right, preferred_element_type=F32)


def dot_tn(left, right):
    return lax.dot_general(left, right, (((0,), (0,)), ((), ())), preferred_element_type=F32)


def dot_nt(left, right):
    return lax.dot_general(left, right, (((1,), (1,)), ((), ())), preferred_element_type=F32)


def up16(rows):
    return -(-rows // 16) * 16


class Sizes:
    def __init__(self, pos, tokens, mixer, w_value, w_in, w_out):
        self.n = pos
        self.r, _, self.d = tokens.shape
        self.heads, _, self.cb = mixer.shape
        self.long = pos * self.r
        self.hb = self.heads // BATCH
        self.fh = self.hb * HEAD
        self.rw = w_value.shape[0]
        self.rf = w_out.shape[0]
        self.ff = w_in.shape[1]
        self.fc = self.ff // BATCH
        self.rp = up16(self.rw + 8)
        self.gr = self.d // 256
        self.wr = BATCH * self.rw
        self.fold = self.wr // 2
        self.wt = self.wr + self.fold + 16
        self.sems = (8 + 2 * self.hb) * 2 * pos + 8 * pos + 180 + 8 * self.hb


def fits(pos, batch, tokens, mixer, w_value, w_in, w_out):
    r, _, d = tokens.shape
    heads = mixer.shape[0]
    rw, rf = w_value.shape[0], w_out.shape[0]
    return (
        batch == BATCH
        and pos >= 4
        and pos % 2 == 0
        and r % 128 == 0
        and SHORT == 2 * r
        and heads % BATCH == 0
        and heads * HEAD == d
        and heads // BATCH * HEAD == 192
        and d % 256 == 0
        and 2 * (d // 256) <= 8
        and rw % 8 == 0
        and rw == 24
        and rf % 32 == 0
        and (BATCH * rw) % 32 == 0
        and (w_in.shape[1] // BATCH) % 256 == 0
        and SHORT == mixer.shape[2]
    )


class Net:
    def __init__(self, n, sems):
        self.n = n
        self.sems = sems
        self.used = 0
        self.sent = []
        p, b = lax.axis_index("pos"), lax.axis_index("batch")
        self.p, self.b = p, b
        self.rho = self.ring(p)
        self.right = (self.place(lax.rem(self.rho + 1, n)), b)
        self.left = (self.place(lax.rem(self.rho + n - 1, n)), b)
        self.core_b = b + 1 - 2 * lax.rem(b, 2)
        self.y_b = lax.rem(b + 2, BATCH)
        self.far_b = BATCH - 1 - b
        self.core = (p, self.core_b)
        self.y = (p, self.y_b)
        self.far = (p, self.far_b)
        self.short = p < 2
        rho = self.rho
        self.first, self.second, self.late, self.last = rho == 0, rho == 1, rho == n - 2, rho == n - 1
        self.inner, self.sends_right, self.sends_left = (rho > 0) & (rho < n - 1), rho < n - 2, rho > 1

    def ring(self, p):
        return jnp.where(lax.rem(p, 2) == 0, p // 2, self.n - 1 - p // 2)

    def place(self, rho):
        half = self.n // 2
        return jnp.where(rho < half, 2 * rho, 2 * (self.n - 1 - rho) + 1)

    def at(self, step):
        return self.place(lax.rem(self.rho + step + 2 * self.n, self.n))

    def sem(self):
        self.used += 1
        return self.sems.at[self.used - 1]


def run_if(cond, body):
    if cond is None:
        body()
    else:
        pl.when(cond)(body)


class Copy:
    def __init__(self, net, device, cond=None, here=None):
        self.net, self.device, self.cond, self.here = net, device, cond, cond if here is None else here
        self.send, self.recv = net.sem(), net.sem()

    def of(self, src, dst):
        return pltpu.make_async_remote_copy(
            src_ref=src, dst_ref=dst, send_sem=self.send, recv_sem=self.recv,
            device_id=self.device, device_id_type=MESH,
        )

    def start(self, src, dst):
        run_if(self.cond, lambda: self.of(src, dst).start())
        self.src = src
        self.net.sent.append(self)

    def arrive(self, land):
        run_if(self.here, lambda: self.of(land, land).wait_recv())

    def finish(self):
        run_if(self.cond, lambda: self.of(self.src, self.src).wait_send())
        self.net.sent.remove(self)


class Local:
    def __init__(self, net, src, dst, cond=None):
        self.copy = pltpu.make_async_copy(src, dst, net.sem())
        self.cond = cond

    def start(self):
        run_if(self.cond, self.copy.start)
        return self

    def done(self):
        run_if(self.cond, self.copy.wait)


class Exchange:
    def __init__(self, net, pick, land, cond=None):
        self.net, self.pick, self.land = net, pick, land
        self.copies = [(Copy(net, d, cond), j) for d, j in ((net.y, net.y_b), (net.far, net.far_b), (net.core, net.core_b))]

    def start(self):
        for copy, j in self.copies:
            copy.start(self.pick(j), self.land.at[self.net.b])

    def done(self):
        for copy, j in self.copies:
            copy.arrive(self.land.at[j])


class Spread:
    def __init__(self, net, slot, cond=None):
        self.net, self.slot = net, slot
        self.by_y, self.by_core, self.relay = (Copy(net, d, cond) for d in (net.y, net.core, net.core))

    def start(self, own=None):
        slot = self.slot(self.net.b)
        own = slot if own is None else own
        self.by_y.start(own, slot)
        self.by_core.start(own, slot)

    def mid(self):
        came = self.slot(self.net.y_b)
        self.by_y.arrive(came)
        self.relay.start(came, came)

    def done(self):
        self.by_core.arrive(self.slot(self.net.core_b))
        self.relay.arrive(self.slot(self.net.far_b))


class Collect:
    def __init__(self, net, part, bufs, cond=None):
        self.net, self.part, self.bufs, self.cond = net, part, bufs, cond
        self.to_other, self.to_mine, self.by_y = (Copy(net, d, cond) for d in (net.core, net.core, net.y))

    def start(self):
        net, (mine, other, _, _) = self.net, self.bufs
        self.to_other.start(self.part.at[net.far_b], other)
        self.to_mine.start(self.part.at[net.core_b], mine)

    def mid(self):
        net, (mine, other, stage, across) = self.net, self.bufs
        self.to_other.arrive(other)

        def add():
            stage[...] = (self.part[net.y_b].astype(F32) + other[...].astype(F32)).astype(BF)

        run_if(self.cond, add)
        self.by_y.start(stage, across)

    def done(self):
        self.to_mine.arrive(self.bufs[0])
        self.by_y.arrive(self.bufs[3])

    def sent(self):
        self.to_other.finish()
        self.to_mine.finish()

    def value(self):
        return self.part[self.net.b].astype(F32) + self.bufs[0][...].astype(F32) + self.bufs[3][...].astype(F32)


class Gather:
    def __init__(self, net, slot, first, second, skew=False):
        self.net, self.slot, self.halves = net, slot, (first, second)
        self.steps, self.next = net.n // 2, 0
        self.copies = [[Copy(net, d) for _ in range(self.steps - 1)] for d in (net.right, net.left)]
        if skew:
            self.ends = [
                [(Copy(net, net.right, net.sends_right, net.inner), first), (Copy(net, net.right, net.late, net.last), slot)],
                [(Copy(net, net.left, net.sends_left, net.inner), second), (Copy(net, net.left, net.second, net.first), slot)],
            ]
        else:
            self.ends = [[(Copy(net, net.right), first)], [(Copy(net, net.left), second)]]

    def hop(self, own=None):
        net, t = self.net, self.next
        if t == self.steps:
            return
        self.next += 1
        for way, sign in ((0, -1), (1, 1)):
            q = net.at(sign * t)
            if t:
                self.copies[way][t - 1].arrive(self.slot(q))
            if t < self.steps - 1:
                self.copies[way][t].start(self.slot(q) if own is None else own, self.slot(q))
            else:
                for copy, place in self.ends[way]:
                    copy.start(place(q), place(q))

    def done(self):
        while self.next < self.steps:
            self.hop()
        q = self.net.at(self.steps)
        for end in self.ends:
            for copy, place in end:
                copy.arrive(place(q))


class Scatter:
    def __init__(self, net, own, held, came, cut, skew=False):
        self.net, self.own, self.held, self.came = net, own, held, came
        self.steps, self.next = net.n // 2, 0
        rows = held.shape[-2]
        spans, every = (slice(0, cut), slice(cut, rows)), slice(0, rows)
        self.copies = [[Copy(net, d) for _ in range(self.steps - 1)] for d in (net.right, net.left)]
        if skew:
            plans = [
                [(spans[0], net.inner, net.sends_left), (every, net.first, net.second)],
                [(spans[1], net.inner, net.sends_right), (every, net.last, net.late)],
            ]
        else:
            plans = [[(spans[0], None, None)], [(spans[1], None, None)]]
        self.heads = [
            [(Copy(net, device, there, here), span) for span, there, here in plan]
            for device, plan in zip((net.right, net.left), plans)
        ]

    def hop(self):
        net, t = self.net, self.next
        if t == self.steps:
            return
        self.next += 1
        if t == 0:
            value = self.own(net.at(self.steps)).astype(BF)
        for way, sign in ((0, 1), (1, -1)):
            if t == 0:
                self.held[way, 0] = value
                for copy, span in self.heads[way]:
                    copy.start(self.held.at[way, 0, span], self.came.at[way, 0, span])
                continue
            value = self.own(net.at(sign * (self.steps - t)))
            if t == 1:
                self.held[way, 1] = value.astype(BF)
                for copy, span in self.heads[way]:
                    copy.arrive(self.came.at[way, 0, span])
                    self.add(copy, way, span, value)
            else:
                self.copies[way][t - 2].arrive(self.came.at[way, t - 1])
                self.held[way, t] = (value + self.came[way, t - 1].astype(F32)).astype(BF)
            self.copies[way][t - 1].start(self.held.at[way, t], self.came.at[way, t])

    def add(self, copy, way, span, value):
        def body():
            self.held[way, 1, span] = (value[span] + self.came[way, 0, span].astype(F32)).astype(BF)

        run_if(copy.here, body)

    def done(self):
        while self.next < self.steps:
            self.hop()
        last = self.steps - 1
        for way in (0, 1):
            self.copies[way][-1].arrive(self.came.at[way, last])
        return self.own(self.net.p) + self.came[0, last].astype(F32) + self.came[1, last].astype(F32)


def unit(values):
    inv = lax.rsqrt(jnp.mean(values * values, axis=-1, keepdims=True) + EPSILON)
    return values * inv, inv


def heads_of(rows, z):
    return [
        jnp.concatenate([rows[s * z.r : (s + 1) * z.r, h * HEAD : (h + 1) * HEAD] for s in range(BATCH)], axis=-1)
        for h in range(z.hb)
    ]


def slots_of(by_head, z):
    return [
        jnp.concatenate([by_head[h][:, s * HEAD : (s + 1) * HEAD] for h in range(z.hb)], axis=-1)
        for s in range(BATCH)
    ]


def halved(block):
    cols = block.shape[1] // 2
    return jnp.concatenate([block[:, 0:cols], block[:, cols:]], axis=0)


def whole(block):
    rows = block.shape[0] // 2
    return jnp.concatenate([block[0:rows], block[rows:]], axis=1)


def folded(block):
    rest, half = block[:, 128:], block.shape[0] // 2
    return jnp.concatenate([block[:, 0:128], jnp.concatenate([rest[0:half], rest[half:]], axis=1)], axis=0)


def unfolded(block):
    half = block.shape[0] // 3
    rest = block[2 * half :]
    rest = jnp.concatenate([rest[:, 0:64], rest[:, 64:]], axis=0)
    return jnp.concatenate([block[0 : 2 * half], rest], axis=1)


def fold_slots(blocks):
    low = [block[:, 0:128] for block in blocks]
    return low + [jnp.concatenate([blocks[s][:, 128:192], blocks[s + 1][:, 128:192]], axis=1) for s in (0, 2)]


def unfold_slots(ref):
    return jnp.concatenate(
        [jnp.concatenate([ref[s], ref[4 + s // 2][:, s % 2 * 64 : s % 2 * 64 + 64]], axis=1) for s in range(BATCH)], axis=0
    )


def scratch(z):
    n, r, d, half = z.n, z.r, z.d, z.n // 2
    vm = pltpu.VMEM
    slots, own = (2, BATCH, r, d), (2, r, d)

    def ring(*shape):
        return vm((2, half) + shape, BF)

    def rings(*shape):
        return vm((2, 2, half) + shape, BF)

    return dict(
        lens=pltpu.SMEM((2,), jnp.int32), gain_1=vm((1, z.rw), BF), gain_2=vm((1, z.rw), BF),
        wv_in=vm((z.rw, d), BF), wo_in=vm((z.rw, d), BF), wi_in=vm((z.rw, z.ff), BF),
        raw=vm((2, r, 2, d), BF), x=vm(slots, BF), c=vm(slots, BF), mx=vm((BATCH, z.hb, r, z.cb), BF),
        wvp=vm((BATCH, z.rp, 256), BF), wip=vm((BATCH, 2 * z.rw, z.fc // 2), BF),
        wvs=vm((BATCH, z.rp, 256), BF), wog=vm((BATCH, n, 2 * z.rw, d // 2), BF), wis=vm((BATCH, 2 * z.rw, z.fc // 2), BF),
        wvg=vm((n, z.wt, 128), BF), wv=vm((d, z.fh), BF), wo=vm((d, d), BF), wi=vm((d, z.fc), BF), wu=vm((z.fc, d), BF),
        gain=vm((2, 1, d), F32),
        h1=vm(slots, BF), vl=vm((z.hb, z.long, LANE), BF), vs=vm((z.hb, SHORT, LANE), BF),
        pf=vm((z.hb, r, z.long), F32), pb=vm((z.hb, r, z.long), BF),
        qf=vm((z.hb, r, SHORT), F32), qb=vm((z.hb, r, SHORT), BF),
        mixed=vm((2, z.hb, r, LANE), F32), attn=vm((BATCH, 2, 6, r, 128), BF),
        mid=vm(own, F32), h2=vm(slots, BF),
        hid=vm((2, BATCH * r, z.fc), BF), dup=vm((2, BATCH * r, z.fc), BF),
        dp=vm(slots, BF), db=vm(own, BF), dmid=vm(own, F32),
        dpb=vm((4,) + own, BF), opb=vm((4,) + own, BF), d1b=vm((4,) + own, BF),
        da=vm((2, z.hb, r, LANE), BF), dv=vm((2, BATCH * r, z.fh), BF), dvs=vm((2, z.hb, r, LANE), BF),
        das=vm((2, 2, BATCH, r * 3 // 4, 128), BF), dal=vm((1, 2, BATCH, r * 3 // 4, 128), BF),
        dals=vm((BATCH, 2, r * 3 // 4, 128), BF), dcs=vm((2, BATCH, r * 3 // 2, 128), BF), dcl=vm((2, BATCH, r * 3 // 2, 128), BF),
        gm0=vm((z.hb, r, z.cb), F32), slope=vm((BATCH * r, z.fc), F32),
        gu=vm((z.fc, d), F32), gi=vm((d, z.fc), F32), go=vm((d, z.fh), F32), gv=vm((d, z.fh), F32),
        gis=vm((BATCH, 2 * z.rw, z.fc // 2), BF), gvs=vm((BATCH, z.rw, 256), F32), gos=vm((BATCH, z.rw, 256), F32), gus=vm((z.rf, d), F32),
        outs=vm(own, BF), gts=vm(own, F32), rms=vm((2, 2, r, 128), F32),
        guh=rings(z.rf, d // 2), gur=rings(z.rf, d // 2), gih=rings(BATCH * z.rw, z.fc // 2), gir=rings(BATCH * z.rw, z.fc // 2),
        goh=ring(z.wr + z.fold, 128), gor=ring(z.wr + z.fold, 128), gvh=ring(z.wr + z.fold, 128), gvr=ring(z.wr + z.fold, 128),
        dvh=vm((z.hb, 2, half, r, LANE), BF), dvr=vm((z.hb, 2, half, r, LANE), BF),
        sems=pltpu.SemaphoreType.DMA((z.sems,)),
    )


def layer_kernel(z, names, *refs):
    lens_in, tok, cot, mix_in, gain_1_in, gain_2_in, wv_hbm, wo_hbm, wi_hbm, wu_in = refs[:10]
    o_out, o_gt, o_gm, o_gv, o_go, o_gi, o_gu, o_rms = refs[10:18]
    k = types.SimpleNamespace(**dict(zip(names, refs[18:])))
    n, r, d = z.n, z.r, z.d
    rows4 = BATCH * r
    rows_o = BATCH * z.rw
    net = Net(n, k.sems)
    p, b, short = net.p, net.b, net.short

    barrier = pltpu.get_barrier_semaphore()
    for device in (net.right, net.left, net.core, net.y, net.far):
        pl.semaphore_signal(barrier, inc=1, device_id=device, device_id_type=MESH)

    x, c, mx, wu, wvp, wip = k.x, k.c, k.mx, k.wu, k.wvp, k.wip

    def span(ref, size, lo=0, hi=None):
        hi = size if hi is None else hi
        return lambda q: ref.at[pl.ds(pl.multiple_of(q * size + lo, 16), hi - lo)]

    wu_span = span(wu, z.rf)
    lens, gain_1, gain_2, wv_in, wo_in, wi_in = k.lens, k.gain_1, k.gain_2, k.wv_in, k.wo_in, k.wi_in
    raw_x = Local(net, tok, k.raw.at[0]).start()
    raw_w = [
        Local(net, src, dst).start()
        for src, dst in (
            (lens_in, lens), (gain_1_in, gain_1), (gain_2_in, gain_2), (wv_hbm, wv_in), (wo_hbm, wo_in), (wi_hbm, wi_in)
        )
    ]
    own_wu = Local(net, wu_in, wu_span(p)).start()
    own_mx = Local(net, mix_in.at[b], mx.at[b]).start()
    raw_c = Local(net, cot, k.raw.at[1]).start()

    def sort_slots(which, into):
        pair = k.raw[which].reshape(2 * r, d)
        behind = jnp.where(lens[0] > SHORT, 0, 1)
        place = lax.broadcasted_iota(jnp.int32, (r, 2 * r), 1) - 2 * lax.broadcasted_iota(jnp.int32, (r, 2 * r), 0)
        for g, slot in enumerate((behind, 1 - behind)):
            into[g, b] = dot((place == slot).astype(BF), pair).astype(BF)

    wvs, wis = k.wvs, k.wis
    for one in raw_w:
        one.done()
    place = lax.broadcasted_iota(jnp.int32, (z.rw, d), 1) - lax.broadcasted_iota(jnp.int32, (z.rw, d), 0)
    place = (place == (BATCH * p + b) * z.rw).astype(BF)
    table = [dot(ref[...], place) for ref in (gain_1, gain_2)]
    tail = [table[g][:, i * 256 : (i + 1) * 256] for g in range(2) for i in range(z.gr)]
    tail = jnp.concatenate(tail + [jnp.zeros((z.rp - z.rw - 2 * z.gr, 256), F32)], axis=0)
    held = wv_in[...].astype(F32)
    for j in range(BATCH):
        piece = jnp.concatenate([held[:, j * z.fh : (j + 1) * z.fh], jnp.zeros((z.rw, 256 - z.fh), F32)], axis=1)
        wvs[j] = jnp.concatenate([piece, tail], axis=0).astype(BF)
    wvp[b] = wvs[b]

    held = wi_in[...].astype(F32)
    for j in range(BATCH):
        cols = [held[:, (BATCH * q + j) * z.rf : (BATCH * q + j + 1) * z.rf] for q in range(n)]
        wis[j] = halved(jnp.concatenate(cols, axis=1)).astype(BF)
    wip[b] = wis[b]
    raw_x.done()
    sort_slots(0, x)
    pl.semaphore_wait(barrier, 5)

    def first_wu(half):
        ag_wu[half].hop(wu_in.at[(slice(0, cut_f), slice(cut_f, z.rf))[half]])

    def start_x():
        sp_x.start()

    def start_c():
        raw_c.done()
        sort_slots(1, c)
        sp_c.start()

    ex_wv = Exchange(net, lambda j: wvs.at[j], wvp)
    ex_wi = Exchange(net, lambda j: wis.at[j], wip)
    ex_mx = Exchange(net, lambda j: mix_in.at[j], mx)
    sp_x, sp_xs = Spread(net, lambda j: x.at[0, j]), Spread(net, lambda j: x.at[1, j], short)
    sp_c, sp_cs = Spread(net, lambda j: c.at[0, j]), Spread(net, lambda j: c.at[1, j], short)
    cut_f = up16(z.rf // 2)
    third_f = up16(cut_f // 2)
    third_i = up16(rows_o // 4)

    def two_rings(ref, size, cut, third):
        return (
            Gather(net, span(ref, size, 0, cut), span(ref, size, 0, third), span(ref, size, third, cut)),
            Gather(net, span(ref, size, cut), span(ref, size, cut, size - third), span(ref, size, size - third)),
        )

    ag_wu = two_rings(wu, z.rf, cut_f, third_f)

    wvg = k.wvg
    cut_v = up16(z.wt // 2)
    ag_wv = Gather(net, lambda q: wvg.at[q], lambda q: wvg.at[q, 0:cut_v], lambda q: wvg.at[q, cut_v : z.wt])

    def ready_wv():
        ex_wv.done()
        weights = jnp.concatenate([wvp[j].astype(F32)[0 : z.rw] for j in range(BATCH)], axis=0)
        gains = sum(wvp[j].astype(F32)[z.rw : z.rw + 8] for j in range(BATCH))
        wvg[p] = jnp.concatenate([folded(weights[:, 0 : z.fh]), gains[:, 0:128], gains[:, 128:256]], axis=0).astype(BF)

    wo, wog = k.wo, k.wog
    ag_wo = Gather(
        net, lambda q: wog.at[b, q], lambda q: wog.at[b, q, 0:32], lambda q: wog.at[b, q, 32 : 2 * z.rw]
    )
    sp_wo = Spread(net, lambda j: wog.at[j])

    def ready_wo():
        wog[b, p] = halved(wo_in[...].astype(F32)).astype(BF)

    def spread_wo():
        ag_wo.done()
        sp_wo.start()

    def wo_done():
        sp_wo.done()
        for q in range(n):
            parts = [whole(wog[j, q].astype(F32)) for j in range(BATCH)]
            wo[q * rows_o : (q + 1) * rows_o] = jnp.concatenate(parts, axis=0).astype(BF)

    def pack(ref):
        return jnp.concatenate([whole(ref[j].astype(F32)) for j in range(BATCH)], axis=0).astype(BF)

    wi = k.wi
    cut_i = up16(rows_o // 2)
    ag_wi = two_rings(wi, rows_o, cut_i, third_i)

    def ready_wi():
        ex_wi.done()
        wi[pl.ds(pl.multiple_of(p * rows_o, 16), rows_o)] = pack(wip)

    h1, vl, vs, gain = k.h1, k.vl, k.vs, k.gain
    here = pl.ds(pl.multiple_of(p * r, 16), r)
    twin = (1 - p, b)
    other = pl.ds(pl.multiple_of((1 - p) * r, 16), r)
    cp_vs, cp_dvs = Copy(net, twin, short), Copy(net, twin, short)

    def ready_gains():
        ag_wv.done()
        top = z.wr + z.fold
        table = jnp.sum(wvg[:, top : top + 16].astype(F32), axis=0)
        table = jnp.concatenate([table[0:8], table[8:16]], axis=1)
        for g in range(2):
            gain[g] = jnp.concatenate([table[g * z.gr + i : g * z.gr + i + 1] for i in range(z.gr)], axis=1)
        for q in range(n):
            k.wv[q * z.wr : (q + 1) * z.wr] = unfolded(wvg[q, 0 : z.wr + z.fold])

    def values(g, into):
        for s in range(BATCH):
            h1[g, s] = (unit(x[g, s].astype(F32))[0] * gain[0]).astype(BF)
        value = dot(h1[g].reshape(rows4, d), k.wv[...]).astype(BF)
        for h, block in enumerate(heads_of(value, z)):
            into[h, here, :] = block

    def vl_span(h, lo, hi):
        return lambda q: vl.at[h, pl.ds(pl.multiple_of(q * r + lo, 16), hi - lo), :]

    ag_v = [Gather(net, vl_span(h, 0, r), vl_span(h, 0, r // 2), vl_span(h, r // 2, r), True) for h in range(z.hb)]

    def ready_values():
        sp_x.done()
        values(0, vl)

    def short_values():
        sp_xs.done()

        @pl.when(short)
        def _():
            values(1, vs)

        cp_vs.start(vs.at[:, here, :], vs.at[:, here, :])

    pf, pb, qf, qb = k.pf, k.pb, k.qf, k.qb

    def probabilities():
        own_mx.done()
        ex_mx.done()
        for h in range(z.hb):
            total, first = 0.0, None
            for j in range(BATCH):
                e = jnp.exp(mx[j, h].astype(F32))
                pf[h, :, j * z.cb : (j + 1) * z.cb] = e
                total = total + jnp.sum(e, axis=-1, keepdims=True)
                first = total if j == 0 else first

            @pl.when(short)
            def _():
                q = pf[h, :, 0:SHORT] * (1.0 / first)
                qf[h] = q
                qb[h] = q.astype(BF)

            scaled = pf[h] * (1.0 / total)
            pf[h] = scaled
            pb[h] = scaled.astype(BF)

    mixed, attn = k.mixed, k.attn
    sp_a, sp_as = Spread(net, lambda j: attn.at[j, 0]), Spread(net, lambda j: attn.at[j, 1], short)

    def mix_slots(g):
        for i, block in enumerate(fold_slots(slots_of([mixed[g, h].astype(BF) for h in range(z.hb)], z))):
            attn[b, g, i] = block

    def mix_head(h):
        ag_v[h].done()
        mixed[0, h] = dot(pb[h], vl[h])

    def mix():
        mix_slots(0)
        sp_a.start()

    def short_mix():
        cp_vs.arrive(vs.at[:, other, :])

        @pl.when(short)
        def _():
            for h in range(z.hb):
                mixed[1, h] = dot(qb[h], vs[h])
            mix_slots(1)

        sp_as.start()

    big, mid, h2, rms = k.gu, k.mid, k.h2, k.rms

    def branch_slots(g):
        big[0:rows4] = sum(
            dot(unfold_slots(attn.at[j, g]), wo[j * z.fh : (j + 1) * z.fh]) for j in range(BATCH)
        )
        for s in range(BATCH):
            branch = big[s * r : (s + 1) * r]
            total = x[g, s].astype(F32) + branch
            square = jnp.mean(total * total, axis=-1, keepdims=True) + EPSILON
            h2[g, s] = (total * lax.rsqrt(square) * gain[1]).astype(BF)

            @pl.when(b == s)
            def _():
                mid[g] = total
                rms[0, g] = jnp.broadcast_to(jnp.sqrt(square), (r, 128))
                size = jnp.sqrt(jnp.mean(branch * branch, axis=-1, keepdims=True) + EPSILON)
                rms[1, g] = jnp.broadcast_to(size, (r, 128))

    def branches():
        sp_a.done()
        branch_slots(0)

    def short_branches():
        sp_as.done()

        @pl.when(short)
        def _():
            branch_slots(1)

    hid, dup, dp, op = k.hid, k.dup, k.dp, h2
    halves = (slice(0, r // 2), slice(r // 2, r))
    co_d = [Collect(net, dp.at[0, :, rows], [k.dpb.at[i, 0, rows] for i in range(4)]) for rows in halves]
    co_ds = Collect(net, dp.at[1], [k.dpb.at[i, 1] for i in range(4)], short)
    co_o, co_os = (Collect(net, op.at[g], [k.opb.at[i, g] for i in range(4)], w) for g, w in ((0, None), (1, short)))

    slopes = (k.gi, k.slope)

    def feed(g):
        left = h2[g].reshape(rows4, d)
        for q in range(z.fc // 256):
            cols = slice(q * 256, (q + 1) * 256)
            up = dot(left, wi[:, cols])
            cdf = 0.5 + 0.5 * lax.erf(up * 0.7071067811865476)
            hid[g, :, cols] = (up * cdf).astype(BF)
            slopes[g][0:rows4, cols] = cdf + up * (jnp.exp(-0.5 * up * up) * 0.3989422804014327)

    def feed_back(g):
        down = c[g].reshape(rows4, d)
        for q in range(z.fc // 256):
            cols = slice(q * 256, (q + 1) * 256)
            dup[g, :, cols] = (dot_nt(down, wu[cols, :]) * slopes[g][0:rows4, cols]).astype(BF)
        for q in range(d // 256):
            rows = slice(q * 256, (q + 1) * 256)
            dp[g, :, :, rows] = dot_nt(dup[g], wi[rows, :]).reshape(BATCH, r, 256).astype(BF)

    def feeds():
        for ring in ag_wi:
            ring.done()
        feed(0)

    def short_feeds():
        @pl.when(short)
        def _():
            feed(1)

    def feed_backs():
        for ring in ag_wu:
            ring.done()
        own_wu.done()
        feed_back(0)
        for part in co_d:
            part.start()

    def ready_c():
        sp_c.done()

    def ready_cs():
        sp_cs.done()

    def short_feed_backs():
        @pl.when(short)
        def _():
            feed_back(1)

        co_ds.start()

    gu, gi, gv, go = k.gu, k.gi, k.gv, k.go

    def rows_at(ref, size):
        return lambda q: ref[pl.ds(pl.multiple_of(q * size, 8), size)]

    def two_scatters(ref, size, held, came):
        def block(half):
            cols = slice(half * (ref.shape[1] // 2), (half + 1) * (ref.shape[1] // 2))
            return lambda q: ref[pl.ds(pl.multiple_of(q * size, 8), size), cols]

        return [Scatter(net, block(half), held.at[half], came.at[half], up16(size // 2)) for half in range(2)]

    rs_gu = two_scatters(gu, z.rf, k.guh, k.gur)
    rs_gi = two_scatters(gi, rows_o, k.gih, k.gir)
    rs_gv = Scatter(net, lambda q: folded(rows_at(gv, rows_o)(q)), k.gvh, k.gvr, up16((z.wr + z.fold) // 2))

    def weight_grad(into, left, right, g, half):
        width = into.shape[1] // 2
        cols = slice(half * width, (half + 1) * width)
        term = dot_tn(left, right(cols))
        into[:, cols] = into[:, cols] + term if g else term

    def grad_out_of(g, half):
        weight_grad(gu, hid[g], lambda cols: c[g, :, :, cols].reshape(rows4, d // 2), g, half)

    def grad_out(half):
        grad_out_of(0, half)

    def short_grad_out(half):
        @pl.when(short)
        def _():
            grad_out_of(1, half)

    def grad_in_of(g, half):
        weight_grad(gi, h2[g].reshape(rows4, d), lambda cols: dup[g, :, cols], g, half)

    def grad_in(half):
        grad_in_of(0, half)

    def short_grad_in(half):
        @pl.when(short)
        def _():
            grad_in_of(1, half)

    def outs(g):
        for q in range(d // 256):
            cols = slice(q * 256, (q + 1) * 256)
            op[g, :, :, cols] = dot(hid[g], wu[:, cols]).reshape(BATCH, r, 256).astype(BF)

    def finals():
        outs(0)
        co_o.start()

    def short_finals():
        @pl.when(short)
        def _():
            outs(1)

        co_os.start()

    db, dmid = k.db, k.dmid
    das, dal, dcs, dcl = k.das, k.dal, k.dcs, k.dcl
    ex_da = [
        Exchange(net, functools.partial(lambda i, j: das.at[0, i, j], i), dal.at[0, i]) for i in range(2)
    ]
    ex_das = Exchange(net, lambda j: das.at[1, :, j], k.dals, short)
    ex_dc = Exchange(net, lambda j: dcs.at[0, j], dcl.at[0])
    ex_dcs = Exchange(net, lambda j: dcs.at[1, j], dcl.at[1], short)

    def norm_back(upper, values, gain):
        normed, inv = unit(values)
        scaled = upper * gain
        return inv * (scaled - normed * jnp.mean(scaled * normed, axis=-1, keepdims=True))

    def middle(g, collect, rows):
        grad = c[g, b, rows].astype(F32) + norm_back(collect.value(), mid[g, rows], gain[1])
        dmid[g, rows] = grad
        db[g, rows] = grad.astype(BF)

    def attn_back(g, i):
        grad = dot_nt(db[g, halves[i]], wo[...])
        for j in range(BATCH):
            das[g, i, j] = folded(grad[:, j * z.fh : (j + 1) * z.fh]).astype(BF)

    def columns(g):
        held = db[g].astype(F32)
        for j in range(BATCH):
            dcs[g, j] = folded(held[:, j * z.fh : (j + 1) * z.fh]).astype(BF)
        dcl[g, b] = dcs[g, b]

    def middles(i):
        co_d[i].done()
        middle(0, co_d[i], halves[i])
        attn_back(0, i)
        dal[0, i, b] = das[0, i, b]
        ex_da[i].start()

    def spread_db():
        columns(0)
        ex_dc.start()

    def short_middles():
        co_ds.done()

        @pl.when(short)
        def _():
            middle(1, co_ds, slice(0, r))
            for i in range(2):
                attn_back(1, i)
                k.dals[b, i] = das[1, i, b]

        ex_das.start()

    def short_spread_db():
        @pl.when(short)
        def _():
            columns(1)

        ex_dcs.start()

    da, dvs = k.da, k.dvs

    def mix_back(g, land):
        grad = jnp.concatenate([unfolded(land(j, i).astype(F32)) for j in range(BATCH) for i in range(2)], axis=0)
        for h, block in enumerate(heads_of(grad.astype(BF), z)):
            da[g, h] = block

    def dv_own(h):
        return lambda q: dot_tn(pb[h, :, pl.ds(pl.multiple_of(q * r, 128), r)], da[0, h])

    rs_dv = [Scatter(net, dv_own(h), k.dvh.at[h], k.dvr.at[h], r // 2, True) for h in range(z.hb)]

    def hop_dv(h):
        rs_dv[h].hop()

    def mix_backs():
        for part in ex_da:
            part.done()
        mix_back(0, lambda j, i: dal[0, i, j])

    def dvs_own(h, q):
        return dot_tn(qb[h, :, pl.ds(pl.multiple_of(q * r, 128), r)], da[1, h])

    def short_mix_backs():
        ex_das.done()

        @pl.when(short)
        def _():
            mix_back(1, lambda j, i: k.dals[j, i])
            for h in range(z.hb):
                dvs[0, h] = dvs_own(h, 1 - p).astype(BF)

        cp_dvs.start(dvs.at[0], dvs.at[1])

    rs_go = Scatter(net, lambda q: folded(rows_at(go, rows_o)(q)), k.goh, k.gor, up16((z.wr + z.fold) // 2))

    def grad_output_of(g):
        cols = jnp.concatenate([unfolded(dcl[g, j].astype(F32)) for j in range(BATCH)], axis=0).astype(BF)
        for j in range(BATCH):
            rows = slice(j * z.fh, (j + 1) * z.fh)
            term = dot_tn(unfold_slots(attn.at[j, g]), cols)
            go[rows] = go[rows] + term if g else term

    def grad_output():
        ex_dc.done()
        grad_output_of(0)

    def short_grad_output():
        ex_dcs.done()

        @pl.when(short)
        def _():
            grad_output_of(1)

    gms, gm0 = mx, k.gm0
    ex_gm = Exchange(net, lambda j: gms.at[j], o_gm)
    own_gm = Local(net, gms.at[b], o_gm.at[b])

    def grad_mixer():
        for h in range(z.hb):
            delta = jnp.sum(da[0, h].astype(F32) * mixed[0, h], axis=-1, keepdims=True)
            for j in range(BATCH):
                cols = slice(j * z.cb, (j + 1) * z.cb)
                part = pf[h, :, cols] * (dot_nt(da[0, h], vl[h, cols, :]) - delta)
                gms[j, h] = part.astype(BF)
                if j == 0:
                    gm0[h] = part

    def short_grad_mixer():
        @pl.when(short)
        def _():
            for h in range(z.hb):
                delta = jnp.sum(da[1, h].astype(F32) * mixed[1, h], axis=-1, keepdims=True)
                gms[0, h] = (gm0[h] + qf[h] * (dot_nt(da[1, h], vs[h]) - delta)).astype(BF)

        ex_gm.start()
        own_gm.start()

    gis, gvs, gos, gus = k.gis, k.gvs, k.gos, k.gus
    ex_gi, ex_gv, ex_go = (
        Exchange(net, functools.partial(lambda ref, j: ref.at[j], ref), land)
        for ref, land in ((gis, o_gi), (gvs, o_gv), (gos, o_go))
    )
    own_gi, own_gv, own_go = (Local(net, ref.at[b], land.at[b]) for ref, land in ((gis, o_gi), (gvs, o_gv), (gos, o_go)))
    out_gu = Local(net, gus, o_gu)

    def deal(ref, total):
        total = unfolded(total)
        for j in range(BATCH):
            part = total[j * z.rw : (j + 1) * z.rw]
            ref[j] = jnp.concatenate([part, jnp.zeros((z.rw, 256 - z.fh), F32)], axis=1)

    def end_gu():
        gus[...] = jnp.concatenate([ring.done() for ring in rs_gu], axis=1)
        out_gu.start()

    def end_gi():
        total = jnp.concatenate([ring.done() for ring in rs_gi], axis=1)
        for j in range(BATCH):
            gis[j] = halved(total[j * z.rw : (j + 1) * z.rw]).astype(BF)
        ex_gi.start()
        own_gi.start()

    def end_gv():
        deal(gvs, rs_gv.done())
        ex_gv.start()
        own_gv.start()

    def end_go():
        deal(gos, rs_go.done())
        ex_go.start()
        own_go.start()

    dv, d1 = k.dv, dp
    co_1, co_1s = (Collect(net, d1.at[g], [k.d1b.at[i, g] for i in range(4)], w) for g, w in ((0, None), (1, short)))

    def values_back(g, total):
        for s, block in enumerate(slots_of([part.astype(BF) for part in total], z)):
            dv[g, s * r : (s + 1) * r] = block
        d1[g] = dot_nt(dv[g], k.wv[...]).reshape(BATCH, r, d).astype(BF)

    def values_backs():
        total = [ring.done() for ring in rs_dv]
        for part in co_d:
            part.sent()
        values_back(0, total)
        co_1.start()

    def short_values_backs():
        cp_dvs.arrive(dvs.at[1])
        co_ds.sent()

        @pl.when(short)
        def _():
            values_back(1, [dvs_own(h, p) + dvs[1, h].astype(F32) for h in range(z.hb)])

        co_1s.start()

    def grad_value():
        gv[...] = dot_tn(h1[0].reshape(rows4, d), dv[0])

    def short_grad_value():
        @pl.when(short)
        def _():
            gv[...] += dot_tn(h1[1].reshape(rows4, d), dv[1])

    outs_vm, gts = k.outs, k.gts
    out_rms = Local(net, rms, o_rms)
    out_out = [Local(net, outs_vm.at[g], o_out.at[g], w) for g, w in ((0, None), (1, short))]
    out_gt = [Local(net, gts.at[g], o_gt.at[g], w) for g, w in ((0, None), (1, short))]

    def end_out():
        co_o.done()
        outs_vm[0] = (mid[0] + co_o.value()).astype(BF)
        out_out[0].start()

    def short_end_out():
        co_os.done()

        @pl.when(short)
        def _():
            outs_vm[1] = (mid[1] + co_os.value()).astype(BF)

        out_out[1].start()

    def finish_tokens(g, collect):
        gts[g] = dmid[g] + norm_back(collect.value(), x[g, b].astype(F32), gain[0])

    def end_tokens():
        co_1.done()
        finish_tokens(0, co_1)
        out_gt[0].start()

    def short_end_tokens():
        co_1s.done()

        @pl.when(short)
        def _():
            finish_tokens(1, co_1s)

        out_gt[1].start()

    first_wu(1)
    ex_wv.start()
    first_wu(0)
    ex_wi.start()
    ready_wo()
    start_x()
    ready_wv()
    ag_wv.hop()
    ag_wo.hop()
    start_c()
    ag_wu[1].hop()
    ag_wv.hop()
    ag_wo.hop()
    ready_wi()
    ag_wi[1].hop()
    sp_xs.start()
    ag_wv.hop()
    ag_wu[1].hop()
    sp_x.mid()
    ex_mx.start()
    ag_wo.hop()
    ag_wv.hop()
    ag_wu[0].hop()
    ag_wi[0].hop()
    ready_gains()
    ready_values()
    ag_v[1].hop()
    ag_v[0].hop()
    ag_v[2].hop()
    ag_v[1].hop()
    ag_v[0].hop()
    sp_xs.mid()
    ag_v[2].hop()
    ag_wo.hop()
    sp_cs.start()
    short_values()
    ag_v[0].hop()
    probabilities()
    ag_v[1].hop()
    ag_v[2].hop()
    spread_wo()
    sp_cs.mid()
    sp_c.mid()
    short_mix()
    ag_wi[1].hop()
    ag_v[1].hop()
    ag_v[0].hop()
    ag_v[2].hop()
    ag_wi[0].hop()
    ag_wu[1].hop()
    mix_head(1)
    mix_head(0)
    sp_wo.mid()
    mix_head(2)
    mix()
    ag_wi[1].hop()
    ag_wi[0].hop()
    wo_done()
    sp_as.mid()
    ag_wu[0].hop()
    short_branches()
    ready_c()
    ag_wi[1].hop()
    ag_wi[0].hop()
    sp_a.mid()
    ag_wu[0].hop()
    branches()
    feeds()
    feed_backs()
    grad_out(0)
    ready_cs()
    short_feeds()
    co_d[0].mid()
    short_grad_out(0)
    co_d[1].mid()
    rs_gu[0].hop()
    short_feed_backs()
    grad_in(0)
    short_grad_in(0)
    rs_gi[0].hop()
    grad_in(1)
    rs_gu[0].hop()
    middles(0)
    short_grad_in(1)
    rs_gi[1].hop()
    middles(1)
    rs_gi[0].hop()
    short_finals()
    rs_gu[0].hop()
    co_ds.mid()
    mix_backs()
    hop_dv(1)
    hop_dv(0)
    hop_dv(2)
    co_os.mid()
    rs_gi[1].hop()
    grad_mixer()
    hop_dv(1)
    grad_out(1)
    hop_dv(0)
    hop_dv(2)
    short_middles()
    spread_db()
    rs_gi[0].hop()
    hop_dv(1)
    hop_dv(0)
    short_spread_db()
    hop_dv(2)
    short_mix_backs()
    short_grad_mixer()
    grad_output()
    hop_dv(1)
    hop_dv(0)
    short_grad_out(1)
    finals()
    hop_dv(2)
    co_o.mid()
    short_grad_output()
    rs_gi[1].hop()
    short_end_out()
    rs_go.hop()
    out_rms.start()
    rs_gu[1].hop()
    short_values_backs()
    rs_gi[0].hop()
    values_backs()
    grad_value()
    short_grad_value()
    rs_gv.hop()
    co_1.mid()
    rs_go.hop()
    rs_gu[1].hop()
    rs_gv.hop()
    rs_go.hop()
    co_1s.mid()
    end_out()
    rs_gi[1].hop()
    rs_gv.hop()
    rs_go.hop()
    rs_gu[1].hop()
    rs_gv.hop()
    end_tokens()
    end_gi()
    rs_gu[0].hop()
    end_go()
    short_end_tokens()
    rs_gu[1].hop()
    end_gv()
    end_gu()

    ex_gm.done()
    ex_gi.done()
    ex_gv.done()
    ex_go.done()
    for copy in (own_gm, own_gi, own_gv, own_go, out_gu, out_rms, *out_out, *out_gt):
        copy.done()
    for copy in list(net.sent):
        copy.finish()
    assert net.used == z.sems


def finish_kernel(
    z, lens_in, outs, gts, gm, gv, go, gi, gu, rms, gain_1, gain_2, wv, wi,
    o_out, o_gt, o_gm, o_g1, o_gv, o_go, o_g2, o_gi, o_gu, o_rms_1, o_rms_2,
    v_out, v_gt, v_gm, v_gv, v_gi, v_rms, v_gu, v_go, v_wv, v_wi, v_g1, v_g2,
    s_out, s_gt, s_gm, s_gv, s_gi, s_go, s_g1, s_g2, s_rms, lens, sems,
):
    n, r = z.n, z.r
    used = []

    def copy(src, dst):
        used.append(pltpu.make_async_copy(src, dst, sems.at[len(used)]))
        used[-1].start()
        return used[-1]

    in_lens = copy(lens_in, lens)
    in_gm = [copy(gm.at[j], v_gm.at[j]) for j in range(BATCH)]
    in_gt, in_out = copy(gts, v_gt), copy(outs, v_out)
    in_gi, in_gv, in_rms = copy(gi, v_gi), copy(gv, v_gv), copy(rms, v_rms)
    in_gu, in_go = copy(gu, v_gu), copy(go, v_go)
    last = []
    has_short = lax.axis_index("pos") < SHORT // r

    def slots(ref):
        first_long = lens[0] > SHORT
        lower = jnp.where(has_short, ref[1].astype(F32), 0.0)
        upper = ref[0].astype(F32)
        return jnp.where(first_long, upper, lower), jnp.where(first_long, lower, upper)

    in_small = [copy(wv, v_wv), copy(wi, v_wi), copy(gain_1, v_g1), copy(gain_2, v_g2)]
    for j in range(BATCH):
        in_gm[j].wait()
        for h in range(z.hb):
            s_gm[j * z.hb + h] = v_gm[j, h].astype(F32)
        part = slice(j * z.hb, (j + 1) * z.hb)
        last.append(copy(s_gm.at[part], o_gm.at[part]))
    in_lens.wait()
    in_gt.wait()
    for s, block in enumerate(slots(v_gt)):
        s_gt[:, s, :] = block
    last.append(copy(s_gt, o_gt))
    in_gu.wait()
    last.append(copy(v_gu, o_gu))
    in_out.wait()
    for s, block in enumerate(slots(v_out)):
        s_out[:, s, :] = block.astype(BF)
    last.append(copy(s_out, o_out))

    def gain_grad(weights, grad, gain):
        ones = jnp.ones((8, grad.shape[1]), F32)
        total = lax.dot_general(
            ones, weights[...].astype(F32) * grad, (((1,), (1,)), ((), ())),
            precision=lax.Precision.HIGHEST, preferred_element_type=F32,
        )
        return total[0:1] / gain[...].astype(F32)

    for one in in_small:
        one.wait()
    in_gi.wait()
    parts = [whole(v_gi[j].astype(F32)) for j in range(BATCH)]
    s_gi[...] = jnp.concatenate([part[:, q * z.rf : (q + 1) * z.rf] for q in range(n) for part in parts], axis=1)
    last.append(copy(s_gi, o_gi))
    s_g2[...] = gain_grad(v_wi, s_gi[...], v_g2)
    last.append(copy(s_g2, o_g2))
    in_gv.wait()
    s_gv[...] = jnp.concatenate([v_gv[j, :, 0 : z.fh] for j in range(BATCH)], axis=1)
    last.append(copy(s_gv, o_gv))
    s_g1[...] = gain_grad(v_wv, s_gv[...], v_g1)
    last.append(copy(s_g1, o_g1))
    in_go.wait()
    s_go[...] = jnp.concatenate([v_go[j, :, 0 : z.fh] for j in range(BATCH)], axis=1)
    last.append(copy(s_go, o_go))
    in_rms.wait()
    for i, ref in enumerate((o_rms_1, o_rms_2)):
        for s, block in enumerate(slots(v_rms.at[i])):
            s_rms[i, s : s + 1] = jnp.transpose(block)[0:1]
        last.append(copy(s_rms.at[i], ref))
    for one in last:
        one.wait()


def finish(z, lens, results, gain_attn, gain_ffn, w_value, w_in):
    n, r, d = z.n, z.r, z.d
    vm, shape = pltpu.VMEM, jax.ShapeDtypeStruct
    hbm = pl.BlockSpec(memory_space=pl.ANY)
    taken = [(array.shape, array.dtype) for array in results]
    staged = [((r, 2, d), BF), ((r, 2, d), F32), ((z.heads, r, z.cb), F32), ((z.rw, d), F32), ((z.rw, z.ff), F32), ((z.rw, d), F32)]
    staged += [((1, z.rw), F32), ((1, z.rw), F32), ((2, 2, r), F32)]
    return pl.pallas_call(
        functools.partial(finish_kernel, z),
        out_shape=[
            shape((r, 2, d), BF), shape((r, 2, d), F32), shape((z.heads, r, z.cb), F32), shape((1, z.rw), F32),
            shape((z.rw, d), F32), shape((z.rw, d), F32), shape((1, z.rw), F32), shape((z.rw, z.ff), F32),
            shape((z.rf, d), F32), shape((2, r), F32), shape((2, r), F32),
        ],
        in_specs=[hbm] * 13,
        out_specs=[hbm] * 11,
        scratch_shapes=[vm(*taken[i]) for i in (0, 1, 2, 3, 5, 7, 6, 4)]
        + [vm(array.shape, array.dtype) for array in (w_value, w_in, gain_attn, gain_ffn)]
        + [vm(*one) for one in staged]
        + [pltpu.SMEM((2,), jnp.int32), pltpu.SemaphoreType.DMA((40,))],
        compiler_params=pltpu.CompilerParams(vmem_limit_bytes=62 << 20),
        name="finish",
    )(lens, *results, gain_attn, gain_ffn, w_value, w_in)


def one_device(
    pos, batch, tokens, seq_lens, mixer, gain_attn, w_value, w_output, gain_ffn, w_in, w_out, cotangent
):
    args = (tokens, seq_lens, mixer, gain_attn, w_value, w_output, gain_ffn, w_in, w_out, cotangent)
    if not fits(pos, batch, tokens, mixer, w_value, w_in, w_out):
        return per_device(*args)
    z = Sizes(pos, tokens, mixer, w_value, w_in, w_out)
    shapes = scratch(z)
    hbm = pl.BlockSpec(memory_space=pl.ANY)
    out_shape = [
        jax.ShapeDtypeStruct((2, z.r, z.d), BF),
        jax.ShapeDtypeStruct((2, z.r, z.d), F32),
        jax.ShapeDtypeStruct((BATCH, z.hb, z.r, z.cb), BF),
        jax.ShapeDtypeStruct((BATCH, z.rw, 256), F32),
        jax.ShapeDtypeStruct((BATCH, z.rw, 256), F32),
        jax.ShapeDtypeStruct((BATCH, 2 * z.rw, z.fc // 2), BF),
        jax.ShapeDtypeStruct((z.rf, z.d), F32),
        jax.ShapeDtypeStruct((2, 2, z.r, 128), F32),
    ]
    gain_attn, gain_ffn = gain_attn.reshape(1, z.rw), gain_ffn.reshape(1, z.rw)
    results = pl.pallas_call(
        functools.partial(layer_kernel, z, list(shapes)),
        out_shape=out_shape,
        in_specs=[hbm] * 10,
        out_specs=[hbm] * len(out_shape),
        scratch_shapes=list(shapes.values()),
        compiler_params=pltpu.CompilerParams(
            collective_id=1, has_side_effects=True, vmem_limit_bytes=62 << 20
        ),
        name="layer",
    )(
        seq_lens,
        tokens,
        cotangent,
        mixer.reshape(BATCH, z.hb, z.r, z.cb),
        gain_attn,
        gain_ffn,
        w_value,
        w_output,
        w_in,
        w_out,
    )
    out, grad_tokens, grad_mixer, grad_1, grad_value, grad_output, grad_2, grad_in, grad_out, rms_1, rms_2 = finish(
        z, seq_lens, results, gain_attn, gain_ffn, w_value, w_in
    )
    return (
        out, grad_tokens, grad_mixer, grad_1.reshape(z.rw), grad_value, grad_output, grad_2.reshape(z.rw),
        grad_in, grad_out, rms_1.T, rms_2.T,
    )


def solution(mesh):
    placed = (
        P("pos", "batch", None),
        P("batch"),
        P(None, "pos", "batch"),
        P(("pos", "batch")),
        P(("pos", "batch"), None),
        P(("pos", "batch"), None),
        P(("pos", "batch")),
        P(("pos", "batch"), None),
        P(("pos", "batch"), None),
        P("pos", "batch", None),
    )
    return jax.shard_map(
        functools.partial(one_device, mesh.shape["pos"], mesh.shape["batch"]),
        mesh=mesh,
        in_specs=placed,
        out_specs=(
            P("pos", "batch", None),
            P("pos", "batch", None),
            P(None, "pos", "batch"),
            P(("pos", "batch")),
            P(("pos", "batch"), None),
            P(("pos", "batch"), None),
            P(("pos", "batch")),
            P(("pos", "batch"), None),
            P(("pos", "batch"), None),
            P("pos", "batch"),
            P("pos", "batch"),
        ),
        check_vma=False,
    )
```

```python
import functools
import types

import jax
import jax.numpy as jnp
from jax import lax
from jax.experimental import pallas as pl
from jax.experimental.pallas import tpu as pltpu
from jax.sharding import PartitionSpec as P

SHORT = 256


EPSILON = 1e-06


def norm_apply(values, gain_vec):
    inv_rms = lax.rsqrt(jnp.mean(values * values, axis=-1, keepdims=True) + EPSILON)
    return values * inv_rms * gain_vec


def gelu_exact(values):
    return jax.nn.gelu(values, approximate=False)


def row_stats(scores):
    top_score = jnp.max(scores, axis=-1)
    return top_score + jnp.log(jnp.sum(jnp.exp(scores - top_score[..., None]), axis=-1))


def contract_rows(left, right):
    return lax.dot_general(
        left, right, (((0,), (0,)), ((), ())), preferred_element_type=jnp.float32
    )


def contract_cols(left, right):
    return lax.dot_general(
        left, right, (((1,), (1,)), ((), ())), preferred_element_type=jnp.float32
    )


def per_device(
    tokens, seq_lens, mixer, gain_attn, w_value, w_output, gain_ffn, w_in, w_out, cotangent
):
    value_mat, output_mat, in_mat, out_mat, gain_one, gain_two = (
        lax.all_gather(w_value, ("pos", "batch"), axis=0, tiled=True),
        lax.all_gather(w_output, ("pos", "batch"), axis=0, tiled=True),
        lax.all_gather(w_in, ("pos", "batch"), axis=0, tiled=True),
        lax.all_gather(w_out, ("pos", "batch"), axis=0, tiled=True),
        lax.all_gather(gain_attn, ("pos", "batch"), axis=0, tiled=True),
        lax.all_gather(gain_ffn, ("pos", "batch"), axis=0, tiled=True),
    )
    rows_r = lax.all_gather(mixer, "batch", axis=2, tiled=True)
    head_count = rows_r.shape[0]
    long_len = rows_r.shape[2]
    row_count, slot_count, width = tokens.shape
    head_dim = width // head_count
    tok_count = row_count * slot_count
    start_row = lax.axis_index("pos") * row_count
    positions = start_row + jnp.arange(row_count, dtype=jnp.int32)
    live_mask = (positions[:, None] < seq_lens[None, :]).astype(jnp.float32)
    live_col = live_mask.reshape(tok_count, 1)
    is_long = seq_lens > SHORT
    gain_first = gain_one.astype(jnp.float32)
    gain_second = gain_two.astype(jnp.float32)
    x_float = tokens.astype(jnp.float32).reshape(tok_count, width)
    normed_one = norm_apply(x_float, gain_first).astype(jnp.bfloat16)
    value = jnp.dot(normed_one, value_mat, preferred_element_type=jnp.float32).astype(jnp.bfloat16)
    value = value.reshape(row_count, slot_count, width)
    lse_long = row_stats(rows_r.astype(jnp.float32))
    head_cols = rows_r[:, :, :SHORT].astype(jnp.float32)
    lse_short = row_stats(head_cols)
    prob_head = jnp.exp(head_cols - lse_short[..., None])

    def prob_block(block, lse_l, lse_s, col_pos):
        prob_long = jnp.exp(block - lse_l[..., None])
        prob_short = jnp.where(col_pos < SHORT, jnp.exp(block - lse_s[..., None]), 0.0)
        return jnp.where(is_long[:, None, None, None], prob_long[None], prob_short[None])

    def slot_probs(piece_len):
        columns = rows_r.astype(jnp.float32)
        col_pos = jnp.arange(piece_len, dtype=jnp.int32)
        return prob_block(columns, lse_long, lse_short, col_pos)

    portion = lax.all_gather(value, "pos", axis=0, tiled=True)
    piece_len = portion.shape[0]
    prob_b = slot_probs(piece_len).astype(jnp.bfloat16)
    piece_vals = portion.reshape(piece_len, slot_count, head_count, head_dim)
    mixed = jnp.einsum("shin,nshe->ishe", prob_b, piece_vals, preferred_element_type=jnp.float32)
    attn_in = (mixed * live_mask[:, :, None, None]).astype(jnp.bfloat16).reshape(tok_count, width)
    branch = jnp.dot(attn_in, output_mat, preferred_element_type=jnp.float32)
    mid_resid = x_float + branch
    normed_two = norm_apply(mid_resid, gain_second).astype(jnp.bfloat16)
    up_proj = jnp.dot(normed_two, in_mat, preferred_element_type=jnp.float32)
    hidden = gelu_exact(up_proj).astype(jnp.bfloat16)
    summed_out = mid_resid + jnp.dot(hidden, out_mat, preferred_element_type=jnp.float32)
    output = (summed_out * live_col).astype(jnp.bfloat16).reshape(row_count, slot_count, width)
    resid_rms = (
        jnp.sqrt(jnp.mean(mid_resid * mid_resid, axis=-1) + EPSILON).reshape(row_count, slot_count)
        * live_mask
    )
    branch_rms = (
        jnp.sqrt(jnp.mean(branch * branch, axis=-1) + EPSILON).reshape(row_count, slot_count)
        * live_mask
    )
    dfinal = cotangent.reshape(tok_count, width) * live_col.astype(jnp.bfloat16)
    grad_w_out = contract_rows(hidden, dfinal)
    dhidden = contract_cols(dfinal, out_mat)
    _, gelu_back = jax.vjp(gelu_exact, up_proj)
    dupper = gelu_back(dhidden)[0].astype(jnp.bfloat16)
    grad_w_in = contract_rows(normed_two, dupper)
    d_normed_two = contract_cols(dupper, in_mat)
    _, norm_back_two = jax.vjp(norm_apply, mid_resid, gain_second)
    d_mid_norm, grad_gain_ffn = norm_back_two(d_normed_two)
    d_mid = dfinal.astype(jnp.float32) + d_mid_norm
    dbranch = d_mid.astype(jnp.bfloat16)
    grad_w_output = contract_rows(attn_in, dbranch)
    d_attn = contract_cols(dbranch, output_mat).astype(jnp.bfloat16)
    d_attn = d_attn.reshape(row_count, slot_count, head_count, head_dim)
    portion = lax.all_gather(value, "pos", axis=0, tiled=True)
    piece_len = portion.shape[0]
    prob_f = slot_probs(piece_len)
    piece_vals = portion.reshape(piece_len, slot_count, head_count, head_dim)
    d_prob = jnp.einsum("ishe,nshe->shin", d_attn, piece_vals, preferred_element_type=jnp.float32)
    weighted = prob_f * d_prob
    grad_acc = jnp.sum(weighted, axis=0)
    grad_acc, delta_all = (grad_acc, jnp.sum(weighted, axis=-1))
    delta_long = jnp.sum(jnp.where(is_long[:, None, None], delta_all, 0.0), axis=0)
    delta_short = jnp.sum(jnp.where(is_long[:, None, None], 0.0, delta_all), axis=0)
    slots_here = d_attn.shape[1]
    col_block = lax.all_to_all(rows_r, "pos", split_axis=2, concat_axis=1, tiled=True)
    lse_all_long = lax.all_gather(lse_long, "pos", axis=1, tiled=True)
    lse_all_short = lax.all_gather(lse_short, "pos", axis=1, tiled=True)
    portion = lax.all_gather(d_attn, "pos", axis=0, tiled=True)
    piece_len = portion.shape[0]
    block = col_block.astype(jnp.float32)
    lse_l = lse_all_long
    lse_s = lse_all_short
    prob_b = prob_block(block, lse_l, lse_s, positions).astype(jnp.bfloat16)
    term = jnp.einsum("shij,ishe->jshe", prob_b, portion, preferred_element_type=jnp.float32)
    dvalue = term.reshape(row_count, slots_here, width)
    full_long = jnp.exp(rows_r.astype(jnp.float32) - lse_long[..., None])
    grad_rows = grad_acc - full_long * delta_long[..., None]
    correction = prob_head * delta_short[..., None]
    grad_rows = grad_rows - jnp.pad(correction, ((0, 0), (0, 0), (0, long_len - SHORT)))
    dvalue_b = dvalue.astype(jnp.bfloat16).reshape(tok_count, width)
    grad_w_value = contract_rows(normed_one, dvalue_b)
    d_normed_one = contract_cols(dvalue_b, value_mat)
    _, norm_back_one = jax.vjp(norm_apply, x_float, gain_first)
    d_x_norm, grad_gain_attn = norm_back_one(d_normed_one)
    grad_tokens = (d_mid + d_x_norm).reshape(row_count, slot_count, width)
    grad_mixer = lax.psum_scatter(
        grad_rows.astype(jnp.bfloat16), "batch", scatter_dimension=2, tiled=True
    ).astype(jnp.float32)
    reduced = (
        lax.psum_scatter(grad_w_value, ("pos", "batch"), scatter_dimension=0, tiled=True),
        lax.psum_scatter(grad_w_output, ("pos", "batch"), scatter_dimension=0, tiled=True),
        lax.psum_scatter(grad_w_in, ("pos", "batch"), scatter_dimension=0, tiled=True),
        lax.psum_scatter(grad_w_out, ("pos", "batch"), scatter_dimension=0, tiled=True),
        lax.psum_scatter(grad_gain_attn, ("pos", "batch"), scatter_dimension=0, tiled=True),
        lax.psum_scatter(grad_gain_ffn, ("pos", "batch"), scatter_dimension=0, tiled=True),
    )
    return (
        output,
        grad_tokens,
        grad_mixer,
        reduced[4],
        reduced[0],
        reduced[1],
        reduced[5],
        reduced[2],
        reduced[3],
        resid_rms,
        branch_rms,
    )


BF = jnp.bfloat16
F32 = jnp.float32
MESH = pl.DeviceIdType.MESH
HEAD = 64
BATCH = 4
LANE = 4 * HEAD


def dot(left, right):
    return jnp.dot(left, right, preferred_element_type=F32)


def dot_tn(left, right):
    return lax.dot_general(left, right, (((0,), (0,)), ((), ())), preferred_element_type=F32)


def dot_nt(left, right):
    return lax.dot_general(left, right, (((1,), (1,)), ((), ())), preferred_element_type=F32)


def up16(rows):
    return -(-rows // 16) * 16


class Sizes:
    def __init__(self, pos, tokens, mixer, w_value, w_in, w_out):
        self.n = pos
        self.r, _, self.d = tokens.shape
        self.heads, _, self.cb = mixer.shape
        self.long = pos * self.r
        self.hb = self.heads // BATCH
        self.fh = self.hb * HEAD
        self.rw = w_value.shape[0]
        self.rf = w_out.shape[0]
        self.ff = w_in.shape[1]
        self.fc = self.ff // BATCH
        self.rp = up16(self.rw + 8)
        self.gr = self.d // 256
        self.wr = BATCH * self.rw
        self.fold = self.wr // 2
        self.wt = self.wr + self.fold + 16
        self.sems = 120 + 9 * pos


def fits(pos, batch, tokens, mixer, w_value, w_in, w_out):
    r, _, d = tokens.shape
    heads = mixer.shape[0]
    rw, rf = w_value.shape[0], w_out.shape[0]
    return (
        batch == BATCH
        and pos >= 4
        and pos % 2 == 0
        and r % 128 == 0
        and SHORT == 2 * r
        and heads % BATCH == 0
        and heads * HEAD == d
        and heads // BATCH * HEAD == 192
        and d % 256 == 0
        and 2 * (d // 256) <= 8
        and rw % 8 == 0
        and rw == 24
        and rf % 32 == 0
        and (BATCH * rw) % 32 == 0
        and w_in.shape[1] // BATCH == d
        and SHORT == mixer.shape[2]
    )


class Net:
    def __init__(self, n, sems):
        self.n = n
        self.sems = sems
        self.used = 0
        self.sent = []
        p, b = lax.axis_index("pos"), lax.axis_index("batch")
        self.p, self.b = p, b
        self.rho = self.ring(p)
        self.right = (self.place(lax.rem(self.rho + 1, n)), b)
        self.left = (self.place(lax.rem(self.rho + n - 1, n)), b)
        self.core_b = b + 1 - 2 * lax.rem(b, 2)
        self.y_b = lax.rem(b + 2, BATCH)
        self.far_b = BATCH - 1 - b
        self.core = (p, self.core_b)
        self.y = (p, self.y_b)
        self.far = (p, self.far_b)
        self.short = p < 2
        rho = self.rho
        self.first, self.second, self.late, self.last = rho == 0, rho == 1, rho == n - 2, rho == n - 1
        self.inner, self.sends_right, self.sends_left = (rho > 0) & (rho < n - 1), rho < n - 2, rho > 1
        self.edge, self.near, self.middle = self.first | self.last, self.second | self.late, (rho > 1) & (rho < n - 2)

    def ring(self, p):
        return jnp.where(lax.rem(p, 2) == 0, p // 2, self.n - 1 - p // 2)

    def place(self, rho):
        half = self.n // 2
        return jnp.where(rho < half, 2 * rho, 2 * (self.n - 1 - rho) + 1)

    def at(self, step):
        return self.place(lax.rem(self.rho + step + 2 * self.n, self.n))

    def sem(self):
        self.used += 1
        return self.sems.at[self.used - 1]


def run_if(cond, body):
    if cond is None:
        body()
    else:
        pl.when(cond)(body)


class Local:
    def __init__(self, net, src, dst, cond=None):
        self.copy = pltpu.make_async_copy(src, dst, net.sem())
        self.cond = cond

    def start(self):
        run_if(self.cond, self.copy.start)
        return self

    def done(self):
        run_if(self.cond, self.copy.wait)


class Copies:
    def __init__(self, net, cond=None):
        self.net, self.cond = net, cond
        self.send, self.recv = net.sem(), net.sem()

    def of(self, src, dst, device):
        return pltpu.make_async_remote_copy(
            src_ref=src, dst_ref=dst, send_sem=self.send, recv_sem=self.recv,
            device_id=device, device_id_type=MESH,
        )

    def start(self, src, dst, device, cond=None):
        run_if(self.cond if cond is None else cond, lambda: self.of(src, dst, device).start())

    def arrive(self, ref, cond=None):
        run_if(self.cond if cond is None else cond, lambda: self.of(ref, ref, self.net.core).wait_recv())

    def finish(self, ref, cond=None):
        run_if(self.cond if cond is None else cond, lambda: self.of(ref, ref, self.net.core).wait_send())


class Arrivals(Copies):
    def __init__(self, net, others):
        self.net, self.cond, self.send, self.recv = net, others.cond, others.send, net.sem()


class Exchange:
    def __init__(self, net, pick, land, cond=None):
        self.net, self.pick, self.land = net, pick, land
        self.copies = Copies(net, cond)

    def start(self):
        net = self.net
        for device, j in ((net.y, net.y_b), (net.far, net.far_b), (net.core, net.core_b)):
            self.copies.start(self.pick(j), self.land.at[net.b], device)
        net.sent.append(lambda: self.copies.finish(self.land.at[0 : BATCH - 1]))

    def done(self):
        self.copies.arrive(self.land.at[0 : BATCH - 1])


class Spread:
    def __init__(self, net, blocks, cond=None):
        self.net, self.blocks = net, blocks
        self.by_y = Copies(net, cond)
        self.by_core = Arrivals(net, self.by_y)

    def start(self):
        net, own = self.net, self.blocks.at[self.net.b]
        self.by_y.start(own, own, net.y)
        self.by_core.start(own, own, net.core)

    def mid(self):
        net, came = self.net, self.blocks.at[self.net.y_b]
        self.by_y.arrive(came)
        self.by_core.start(came, came, net.core)
        net.sent.append(lambda: self.by_y.finish(self.blocks.at[0:3]))

    def done(self):
        self.by_core.arrive(self.blocks.at[0:2])


class Collect:
    def __init__(self, net, part, bufs, cond=None):
        self.net, self.part, self.bufs, self.cond = net, part, bufs, cond
        self.to_other = Copies(net, cond)
        self.to_mine = Arrivals(net, self.to_other)

    def start(self):
        net, (mine, other, _, _) = self.net, self.bufs
        self.to_other.start(self.part.at[net.far_b], other, net.core)
        self.to_mine.start(self.part.at[net.core_b], mine, net.core)

    def mid(self):
        net, (mine, other, stage, across) = self.net, self.bufs
        self.to_other.arrive(other)

        def add():
            stage[...] = (self.part[net.y_b].astype(F32) + other[...].astype(F32)).astype(BF)

        run_if(self.cond, add)
        self.to_mine.start(stage, across, net.y)
        net.sent.append(self.sent)

    def done(self):
        self.to_mine.arrive(self.part.at[0:2])

    def sent(self):
        self.to_other.finish(self.part.at[0:3])

    def sent_now(self):
        self.net.sent.remove(self.sent)
        self.sent()

    def value(self):
        return self.part[self.net.b].astype(F32) + self.bufs[0][...].astype(F32) + self.bufs[3][...].astype(F32)


class Gather:
    def __init__(self, net, slot, first, second, size, skew=False):
        self.net, self.slot, self.size, self.skew = net, slot, size, skew
        self.steps, self.next = net.n // 2, 0
        whole = Copies(net)
        self.hops = [whole] + [Arrivals(net, whole) for _ in range(self.steps - 2)]
        if skew:
            self.end = Copies(net)
            self.ends = (
                ((first, net.sends_right), (slot, net.late)),
                ((second, net.sends_left), (slot, net.second)),
            )
        else:
            self.end = Arrivals(net, whole)
            self.ends = (((first, None),), ((second, None),))

    def hop(self, own=None):
        net, t = self.net, self.next
        if t == self.steps:
            return
        self.next += 1
        if t:
            self.hops[t - 1].arrive(self.size(2))
        for way, sign, device in ((0, -1, net.right), (1, 1, net.left)):
            q = net.at(sign * t)
            if t < self.steps - 1:
                self.hops[t].start(self.slot(q) if own is None else own, self.slot(q), device)
            else:
                for place, cond in self.ends[way]:
                    self.end.start(place(q), place(q), device, cond)
        if t == self.steps - 1:
            net.sent.append(self.sent)

    def sent(self):
        net, count = self.net, 2 * (self.steps - 1)
        if self.skew:
            self.hops[0].finish(self.size(count))
            for blocks, cond in ((0.5, net.edge), (1.5, net.near), (1, net.middle)):
                self.end.finish(self.size(blocks), cond)
        else:
            self.hops[0].finish(self.size(count + 1))

    def done(self):
        while self.next < self.steps:
            self.hop()
        self.end.arrive(self.size(1))


class Scatter:
    def __init__(self, net, own, held, came, cut, skew=False):
        self.net, self.own, self.held, self.came, self.cut, self.skew = net, own, held, came, cut, skew
        self.steps, self.next = net.n // 2, 0
        rows = held.shape[-2]
        spans, every = (slice(0, cut), slice(cut, rows)), slice(0, rows)
        self.head = Copies(net)
        whole = Copies(net)
        self.hops = [whole] + [Arrivals(net, whole) for _ in range(self.steps - 2)]
        if skew:
            self.heads = (
                ((spans[0], net.inner, net.sends_left), (every, net.first, net.second)),
                ((spans[1], net.inner, net.sends_right), (every, net.last, net.late)),
            )
        else:
            self.heads = (((spans[0], None, None),), ((spans[1], None, None),))

    def hop(self):
        net, t = self.net, self.next
        if t == self.steps:
            return
        self.next += 1
        ways = ((0, 1, net.right), (1, -1, net.left))
        if t == 0:
            value = self.own(net.at(self.steps)).astype(BF)
            for way, _, device in ways:
                self.held[way, 0] = value
                for span, cond, _ in self.heads[way]:
                    self.head.start(self.held.at[way, 0, span], self.came.at[way, 0, span], device, cond)
            return
        values = [self.own(net.at(sign * (self.steps - t))) for _, sign, _ in ways]
        if t == 1:
            if self.skew:
                half = slice(0, self.cut)
                self.head.arrive(self.came.at[0, 0, half], net.edge)
                self.head.arrive(self.came.at[0, 0:3, half], net.near)
                self.head.arrive(self.came.at[0, 0], net.middle)
            else:
                self.head.arrive(self.came.at[0, 0])
        else:
            self.hops[t - 2].arrive(self.came.at[:, t - 1])
        for way, _, device in ways:
            if t == 1:
                self.held[way, 1] = values[way].astype(BF)
                for span, _, here in self.heads[way]:
                    self.add(way, span, values[way], here)
            else:
                self.held[way, t] = (values[way] + self.came[way, t - 1].astype(F32)).astype(BF)
            self.hops[t - 1].start(self.held.at[way, t], self.came.at[way, t], device)
        if t == self.steps - 1:
            net.sent.append(self.sent)

    def add(self, way, span, value, here):
        def body():
            self.held[way, 1, span] = (value[span] + self.came[way, 0, span].astype(F32)).astype(BF)

        run_if(here, body)

    def sent(self):
        self.head.finish(self.held.at[0, 0])
        self.hops[0].finish(self.held.at[:, 0 : self.steps - 1])

    def done(self):
        while self.next < self.steps:
            self.hop()
        last = self.steps - 1
        self.hops[-1].arrive(self.came.at[:, last])
        return self.own(self.net.p) + self.came[0, last].astype(F32) + self.came[1, last].astype(F32)


def unit(values):
    inv = lax.rsqrt(jnp.mean(values * values, axis=-1, keepdims=True) + EPSILON)
    return values * inv, inv


def heads_of(rows, z):
    return [
        jnp.concatenate([rows[s * z.r : (s + 1) * z.r, h * HEAD : (h + 1) * HEAD] for s in range(BATCH)], axis=-1)
        for h in range(z.hb)
    ]


def slots_of(by_head, z):
    return [
        jnp.concatenate([by_head[h][:, s * HEAD : (s + 1) * HEAD] for h in range(z.hb)], axis=-1)
        for s in range(BATCH)
    ]


def halved(block):
    cols = block.shape[1] // 2
    return jnp.concatenate([block[:, 0:cols], block[:, cols:]], axis=0)


def whole(block):
    rows = block.shape[0] // 2
    return jnp.concatenate([block[0:rows], block[rows:]], axis=1)


def folded(block):
    rest, half = block[:, 128:], block.shape[0] // 2
    return jnp.concatenate([block[:, 0:128], jnp.concatenate([rest[0:half], rest[half:]], axis=1)], axis=0)


def unfolded(block):
    half = block.shape[0] // 3
    rest = block[2 * half :]
    rest = jnp.concatenate([rest[:, 0:64], rest[:, 64:]], axis=0)
    return jnp.concatenate([block[0 : 2 * half], rest], axis=1)


def folds(lo, hi):
    spans = []
    while lo < hi:
        j, t = lo // 192, lo % 192
        end = min(hi, j * 192 + (128 if t < 128 else 192))
        spans.append((lo, end, j * 128 + t if t < 128 else BATCH * 128 + j * 64 + t - 128))
        lo = end
    return spans


def folded_heads(ref):
    slots = []
    for s in range(BATCH):
        rest = [ref[j, 4 + s // 2][:, s % 2 * 64 : s % 2 * 64 + 64] for j in range(BATCH)]
        slots.append(jnp.concatenate([ref[j, s] for j in range(BATCH)] + rest, axis=1))
    return jnp.concatenate(slots, axis=0)


def fold_slots(blocks):
    low = [block[:, 0:128] for block in blocks]
    return low + [jnp.concatenate([blocks[s][:, 128:192], blocks[s + 1][:, 128:192]], axis=1) for s in (0, 2)]


def scratch(z):
    n, r, d, half = z.n, z.r, z.d, z.n // 2
    vm = pltpu.VMEM
    slots, own = (2, BATCH, r, d), (2, r, d)

    def ring(*shape):
        return vm((2, half) + shape, BF)

    return dict(
        lens=pltpu.SMEM((2,), jnp.int32), gain_1=vm((1, z.rw), BF), gain_2=vm((1, z.rw), BF),
        wv_in=vm((z.rw, d), BF), wo_in=vm((z.rw, d), BF), wi_in=vm((z.rw, z.ff), BF),
        raw=vm((2, r, 2, d), BF), x=vm(slots, BF), c=vm(slots, BF), mx=vm((BATCH, z.hb, r, z.cb), BF),
        wvp=vm((BATCH, z.rp, 256), BF), wip=vm((BATCH, 2 * z.rw, z.fc // 2), BF),
        wvs=vm((BATCH, z.rp, 256), BF), wog=vm((BATCH, n, 2 * z.rw, d // 2), BF), wis=vm((BATCH, 2 * z.rw, z.fc // 2), BF),
        wvg=vm((n, z.wt, 128), BF), wv=vm((d, z.fh), BF), wo=vm((d, d), BF), wi=vm((d, z.fc), BF), wu=vm((z.fc, d), BF),
        gain=vm((2, 1, d), F32),
        h1=vm(slots, BF), vl=vm((z.hb, z.long, LANE), BF), vs=vm((z.hb, SHORT, LANE), BF),
        pf=vm((z.hb, r, z.long), F32), pb=vm((z.hb, r, z.long), BF),
        qf=vm((z.hb, r, SHORT), F32), qb=vm((z.hb, r, SHORT), BF),
        mixed=vm((2, z.hb, r, LANE), F32), attn=vm((BATCH, 2, 6, r, 128), BF),
        mid=vm(own, F32), h2=vm(slots, BF),
        hid=vm((2, BATCH * r, z.fc), BF), dup=vm((2, BATCH * r, z.fc), BF),
        dp=vm(slots, BF), db=vm(own, BF), dmid=vm(own, F32),
        dpb=vm((4,) + own, BF), opb=vm((4,) + own, BF), d1b=vm((4,) + own, BF),
        da=vm((2, z.hb, r, LANE), BF), dv=vm((2, BATCH * r, z.fh), BF), dvs=vm((2, z.hb, r, LANE), BF),
        das=vm((2, 2, BATCH, r * 3 // 4, 128), BF), dal=vm((1, 2, BATCH, r * 3 // 4, 128), BF),
        dals=vm((BATCH, 2, r * 3 // 4, 128), BF), dcs=vm((2, BATCH, r * 3 // 2, 128), BF), dcl=vm((2, BATCH, r * 3 // 2, 128), BF),
        gm0=vm((z.hb, r, z.cb), F32), slope=vm((BATCH * r, z.fc), F32),
        gu=vm((z.fc, d), F32), gi=vm((d, z.fc), F32), go=vm((d, z.fh), F32), gv=vm((d, z.fh), F32),
        gis=vm((BATCH, 2 * z.rw, z.fc // 2), BF), gvs=vm((BATCH, z.rw, 256), F32), gos=vm((BATCH, z.rw, 256), F32), gus=vm((z.rf, d), F32),
        outs=vm(own, BF), gts=vm(own, F32), rms=vm((2, 2, r, 128), F32),
        guh=ring(z.rf, 256), gur=ring(z.rf, 256), gih=ring(BATCH * z.rw, 256), gir=ring(BATCH * z.rw, 256),
        guh2=ring(z.rf, d - 256), gur2=ring(z.rf, d - 256), gih2=ring(BATCH * z.rw, d - 256), gir2=ring(BATCH * z.rw, d - 256),
        goh=ring(z.wr + z.fold, 128), gor=ring(z.wr + z.fold, 128), gvh=ring(z.wr + z.fold, 128), gvr=ring(z.wr + z.fold, 128),
        dvh=vm((z.hb, 2, half, r, LANE), BF), dvr=vm((z.hb, 2, half, r, LANE), BF),
        sems=pltpu.SemaphoreType.DMA((z.sems,)),
    )


def layer_kernel(z, names, *refs):
    lens_in, tok, cot, mix_in, gain_1_in, gain_2_in, wv_hbm, wo_hbm, wi_hbm, wu_in = refs[:10]
    o_out, o_gt, o_gm, o_gv, o_go, o_gi, o_gu, o_rms = refs[10:18]
    k = types.SimpleNamespace(**dict(zip(names, refs[18:])))
    n, r, d = z.n, z.r, z.d
    rows4 = BATCH * r
    rows_o = BATCH * z.rw
    net = Net(n, k.sems)
    p, b, short = net.p, net.b, net.short

    barrier = pltpu.get_barrier_semaphore()
    for device in (net.right, net.left, net.core, net.y, net.far):
        pl.semaphore_signal(barrier, inc=1, device_id=device, device_id_type=MESH)

    x, c, mx, wu, wvp, wip = k.x, k.c, k.mx, k.wu, k.wvp, k.wip

    def span(ref, size, lo=0, hi=None):
        hi = size if hi is None else hi
        return lambda q: ref.at[pl.ds(pl.multiple_of(q * size + lo, 16), hi - lo)]

    wu_span = span(wu, z.rf)
    lens, gain_1, gain_2, wv_in, wo_in, wi_in = k.lens, k.gain_1, k.gain_2, k.wv_in, k.wo_in, k.wi_in
    raw_x = Local(net, tok, k.raw.at[0]).start()
    raw_w = [
        Local(net, src, dst).start()
        for src, dst in (
            (lens_in, lens), (gain_1_in, gain_1), (gain_2_in, gain_2), (wv_hbm, wv_in), (wo_hbm, wo_in), (wi_hbm, wi_in)
        )
    ]
    own_wu = Local(net, wu_in, wu_span(p)).start()
    own_mx = Local(net, mix_in.at[b], mx.at[b]).start()
    raw_c = Local(net, cot, k.raw.at[1]).start()

    def sort_slots(which, into):
        pair = k.raw[which].reshape(2 * r, d)
        behind = jnp.where(lens[0] > SHORT, 0, 1)
        place = lax.broadcasted_iota(jnp.int32, (r, 2 * r), 1) - 2 * lax.broadcasted_iota(jnp.int32, (r, 2 * r), 0)
        for g, slot in enumerate((behind, 1 - behind)):
            into[g, b] = dot((place == slot).astype(BF), pair).astype(BF)

    wvs, wis = k.wvs, k.wis
    for one in raw_w:
        one.done()
    place = lax.broadcasted_iota(jnp.int32, (z.rw, d), 1) - lax.broadcasted_iota(jnp.int32, (z.rw, d), 0)
    place = (place == (BATCH * p + b) * z.rw).astype(BF)
    table = [dot(ref[...], place) for ref in (gain_1, gain_2)]
    tail = [table[g][:, i * 256 : (i + 1) * 256] for g in range(2) for i in range(z.gr)]
    tail = jnp.concatenate(tail + [jnp.zeros((z.rp - z.rw - 2 * z.gr, 256), F32)], axis=0)
    held = wv_in[...].astype(F32)
    for j in range(BATCH):
        piece = jnp.concatenate([held[:, j * z.fh : (j + 1) * z.fh], jnp.zeros((z.rw, 256 - z.fh), F32)], axis=1)
        wvs[j] = jnp.concatenate([piece, tail], axis=0).astype(BF)
    wvp[b] = wvs[b]

    held = wi_in[...].astype(F32)
    for j in range(BATCH):
        cols = [held[:, (BATCH * q + j) * z.rf : (BATCH * q + j + 1) * z.rf] for q in range(n)]
        wis[j] = halved(jnp.concatenate(cols, axis=1)).astype(BF)
    wip[b] = wis[b]
    raw_x.done()
    sort_slots(0, x)
    pl.semaphore_wait(barrier, 5)

    def first_wu(half):
        ag_wu[half].hop(wu_in.at[(slice(0, cut_f), slice(cut_f, z.rf))[half]])

    def start_x():
        sp_x.start()

    def start_c():
        raw_c.done()
        sort_slots(1, c)
        sp_c.start()

    ex_wv = Exchange(net, lambda j: wvs.at[j], wvp)
    ex_wi = Exchange(net, lambda j: wis.at[j], wip)
    ex_mx = Exchange(net, lambda j: mix_in.at[j], mx)
    sp_x, sp_xs = Spread(net, x.at[0]), Spread(net, x.at[1], short)
    sp_c, sp_cs = Spread(net, c.at[0]), Spread(net, c.at[1], short)
    cut_f = up16(z.rf // 2)
    third_f = up16(cut_f // 2)
    third_i = up16(rows_o // 4)

    def two_rings(ref, size, cut, third):
        return (
            Gather(
                net, span(ref, size, 0, cut), span(ref, size, 0, third), span(ref, size, third, cut),
                lambda k: ref.at[0 : k * cut],
            ),
            Gather(
                net, span(ref, size, cut), span(ref, size, cut, size - third), span(ref, size, size - third),
                lambda k: ref.at[0 : k * (size - cut)],
            ),
        )

    ag_wu = two_rings(wu, z.rf, cut_f, third_f)

    wvg = k.wvg
    cut_v = up16(z.wt // 2)
    ag_wv = Gather(
        net, lambda q: wvg.at[q], lambda q: wvg.at[q, 0:cut_v], lambda q: wvg.at[q, cut_v : z.wt], lambda k: wvg.at[0:k]
    )

    def ready_wv():
        ex_wv.done()
        weights = jnp.concatenate([wvp[j].astype(F32)[0 : z.rw] for j in range(BATCH)], axis=0)
        gains = sum(wvp[j].astype(F32)[z.rw : z.rw + 8] for j in range(BATCH))
        wvg[p] = jnp.concatenate([folded(weights[:, 0 : z.fh]), gains[:, 0:128], gains[:, 128:256]], axis=0).astype(BF)

    wo, wog = k.wo, k.wog
    ag_wo = Gather(
        net, lambda q: wog.at[b, q], lambda q: wog.at[b, q, 0:32], lambda q: wog.at[b, q, 32 : 2 * z.rw],
        lambda k: wog.at[0, 0:k],
    )
    sp_wo = Spread(net, wog)

    def ready_wo():
        wog[b, p] = halved(wo_in[...].astype(F32)).astype(BF)

    def spread_wo():
        ag_wo.done()
        sp_wo.start()

    def wo_done():
        sp_wo.done()
        for q in range(n):
            block = jnp.concatenate([whole(wog[j, q].astype(F32)) for j in range(BATCH)], axis=0).astype(BF)
            for lo, hi, at in folds(q * rows_o, (q + 1) * rows_o):
                wo[at : at + hi - lo] = block[lo - q * rows_o : hi - q * rows_o]

    def pack(ref):
        return jnp.concatenate([whole(ref[j].astype(F32)) for j in range(BATCH)], axis=0).astype(BF)

    wi = k.wi
    cut_i = up16(rows_o // 2)
    ag_wi = two_rings(wi, rows_o, cut_i, third_i)

    def ready_wi():
        ex_wi.done()
        wi[pl.ds(pl.multiple_of(p * rows_o, 16), rows_o)] = pack(wip)

    h1, vl, vs, gain = k.h1, k.vl, k.vs, k.gain
    here = pl.ds(pl.multiple_of(p * r, 16), r)
    twin = (1 - p, b)
    other = pl.ds(pl.multiple_of((1 - p) * r, 16), r)
    cp_vs, cp_dvs = Copies(net, short), Copies(net, short)

    def ready_gains():
        ag_wv.done()
        top = z.wr + z.fold
        table = jnp.sum(wvg[:, top : top + 16].astype(F32), axis=0)
        table = jnp.concatenate([table[0:8], table[8:16]], axis=1)
        for g in range(2):
            gain[g] = jnp.concatenate([table[g * z.gr + i : g * z.gr + i + 1] for i in range(z.gr)], axis=1)
        for q in range(n):
            k.wv[q * z.wr : (q + 1) * z.wr] = unfolded(wvg[q, 0 : z.wr + z.fold])

    def values(g, into):
        for s in range(BATCH):
            h1[g, s] = (unit(x[g, s].astype(F32))[0] * gain[0]).astype(BF)
        value = dot(h1[g].reshape(rows4, d), k.wv[...]).astype(BF)
        for h, block in enumerate(heads_of(value, z)):
            into[h, here, :] = block

    def vl_span(h, lo, hi):
        return lambda q: vl.at[h, pl.ds(pl.multiple_of(q * r + lo, 16), hi - lo), :]

    def vl_size(h):
        return lambda blocks: vl.at[h, 0 : int(blocks * r)]

    ag_v = [
        Gather(net, vl_span(h, 0, r), vl_span(h, 0, r // 2), vl_span(h, r // 2, r), vl_size(h), True) for h in range(z.hb)
    ]

    def ready_values():
        sp_x.done()
        values(0, vl)

    def short_values():
        sp_xs.done()

        @pl.when(short)
        def _():
            values(1, vs)

        cp_vs.start(vs.at[:, here, :], vs.at[:, here, :], twin)
        net.sent.append(lambda: cp_vs.finish(vs.at[:, here, :]))

    pf, pb, qf, qb = k.pf, k.pb, k.qf, k.qb

    def probabilities():
        own_mx.done()
        ex_mx.done()
        for h in range(z.hb):
            total, first = 0.0, None
            for j in range(BATCH):
                e = jnp.exp(mx[j, h].astype(F32))
                pf[h, :, j * z.cb : (j + 1) * z.cb] = e
                total = total + jnp.sum(e, axis=-1, keepdims=True)
                first = total if j == 0 else first

            @pl.when(short)
            def _():
                q = pf[h, :, 0:SHORT] * (1.0 / first)
                qf[h] = q
                qb[h] = q.astype(BF)

            scaled = pf[h] * (1.0 / total)
            pf[h] = scaled
            pb[h] = scaled.astype(BF)

    mixed, attn = k.mixed, k.attn
    sp_a, sp_as = Spread(net, attn.at[:, 0]), Spread(net, attn.at[:, 1], short)

    def mix_slots(g):
        for i, block in enumerate(fold_slots(slots_of([mixed[g, h].astype(BF) for h in range(z.hb)], z))):
            attn[b, g, i] = block

    def mix_head(h):
        ag_v[h].done()
        mixed[0, h] = dot(pb[h], vl[h])

    def mix():
        mix_slots(0)
        sp_a.start()

    def short_mix():
        cp_vs.arrive(vs.at[:, other, :])

        @pl.when(short)
        def _():
            for h in range(z.hb):
                mixed[1, h] = dot(qb[h], vs[h])
            mix_slots(1)

        sp_as.start()

    big, mid, h2, rms = k.gu, k.mid, k.h2, k.rms

    def branch_slots(g):
        big[0:rows4] = dot(folded_heads(attn.at[:, g]), wo[...])
        for s in range(BATCH):
            branch = big[s * r : (s + 1) * r]
            total = x[g, s].astype(F32) + branch
            square = jnp.mean(total * total, axis=-1, keepdims=True) + EPSILON
            h2[g, s] = (total * lax.rsqrt(square) * gain[1]).astype(BF)

            @pl.when(b == s)
            def _():
                mid[g] = total
                rms[0, g] = jnp.broadcast_to(jnp.sqrt(square), (r, 128))
                size = jnp.sqrt(jnp.mean(branch * branch, axis=-1, keepdims=True) + EPSILON)
                rms[1, g] = jnp.broadcast_to(size, (r, 128))

    def branches():
        sp_a.done()
        branch_slots(0)

    def short_branches():
        sp_as.done()

        @pl.when(short)
        def _():
            branch_slots(1)

    hid, dup, dp, op = k.hid, k.dup, k.dp, h2
    halves = (slice(0, r // 2), slice(r // 2, r))
    co_d = [Collect(net, dp.at[0, :, rows], [k.dpb.at[i, 0, rows] for i in range(4)]) for rows in halves]
    co_ds = Collect(net, dp.at[1], [k.dpb.at[i, 1] for i in range(4)], short)
    co_o, co_os = (Collect(net, op.at[g], [k.opb.at[i, g] for i in range(4)], w) for g, w in ((0, None), (1, short)))

    slopes = (k.gi, k.slope)

    def feed(g):
        left = h2[g].reshape(rows4, d)
        for q in range(z.fc // 256):
            cols = slice(q * 256, (q + 1) * 256)
            up = dot(left, wi[:, cols])
            cdf = 0.5 + 0.5 * lax.erf(up * 0.7071067811865476)
            hid[g, :, cols] = (up * cdf).astype(BF)
            slopes[g][0:rows4, cols] = cdf + up * (jnp.exp(-0.5 * up * up) * 0.3989422804014327)

    def feed_back(g):
        down = c[g].reshape(rows4, d)
        for q in range(z.fc // 256):
            cols = slice(q * 256, (q + 1) * 256)
            dup[g, :, cols] = (dot_nt(down, wu[cols, :]) * slopes[g][0:rows4, cols]).astype(BF)
        for q in range(d // 256):
            rows = slice(q * 256, (q + 1) * 256)
            dp[g, :, :, rows] = dot_nt(dup[g], wi[rows, :]).reshape(BATCH, r, 256).astype(BF)

    def feeds():
        for ring in ag_wi:
            ring.done()
        feed(0)

    def short_feeds():
        @pl.when(short)
        def _():
            feed(1)

    def feed_backs():
        for ring in ag_wu:
            ring.done()
        own_wu.done()
        feed_back(0)
        for part in co_d:
            part.start()

    def ready_c():
        sp_c.done()

    def ready_cs():
        sp_cs.done()

    def short_feed_backs():
        @pl.when(short)
        def _():
            feed_back(1)

        co_ds.start()

    gu, gi, gv, go = k.gu, k.gi, k.gv, k.go
    parts = (slice(0, 256), slice(256, d))

    def rows_at(ref, size):
        return lambda q: ref[pl.ds(pl.multiple_of(q * size, 8), size)]

    def two_scatters(ref, size, held, came):
        def block(cols):
            return lambda q: ref[pl.ds(pl.multiple_of(q * size, 8), size), cols]

        return [Scatter(net, block(part), held[i], came[i], up16(size // 2)) for i, part in enumerate(parts)]

    rs_gu = two_scatters(gu, z.rf, (k.guh, k.guh2), (k.gur, k.gur2))
    rs_gi = two_scatters(gi, rows_o, (k.gih, k.gih2), (k.gir, k.gir2))
    rs_gv = Scatter(net, lambda q: folded(rows_at(gv, rows_o)(q)), k.gvh, k.gvr, up16((z.wr + z.fold) // 2))

    def weight_grad(into, left, right, g, half):
        cols = parts[half]
        term = dot_tn(left, right(cols))
        into[:, cols] = into[:, cols] + term if g else term

    def grad_out_of(g, half):
        weight_grad(gu, hid[g], lambda cols: c[g, :, :, cols].reshape(rows4, cols.stop - cols.start), g, half)

    def grad_out(half):
        grad_out_of(0, half)

    def short_grad_out(half):
        @pl.when(short)
        def _():
            grad_out_of(1, half)

    def grad_in_of(g, half):
        weight_grad(gi, h2[g].reshape(rows4, d), lambda cols: dup[g, :, cols], g, half)

    def grad_in(half):
        grad_in_of(0, half)

    def short_grad_in(half):
        @pl.when(short)
        def _():
            grad_in_of(1, half)

    def outs(g):
        for q in range(d // 256):
            cols = slice(q * 256, (q + 1) * 256)
            op[g, :, :, cols] = dot(hid[g], wu[:, cols]).reshape(BATCH, r, 256).astype(BF)

    def finals():
        outs(0)
        co_o.start()

    def short_finals():
        @pl.when(short)
        def _():
            outs(1)

        co_os.start()

    db, dmid = k.db, k.dmid
    das, dal, dcs, dcl = k.das, k.dal, k.dcs, k.dcl
    ex_da = [
        Exchange(net, functools.partial(lambda i, j: das.at[0, i, j], i), dal.at[0, i]) for i in range(2)
    ]
    ex_das = Exchange(net, lambda j: das.at[1, :, j], k.dals, short)
    ex_dc = Exchange(net, lambda j: dcs.at[0, j], dcl.at[0])
    ex_dcs = Exchange(net, lambda j: dcs.at[1, j], dcl.at[1], short)

    def norm_back(upper, values, gain):
        normed, inv = unit(values)
        scaled = upper * gain
        return inv * (scaled - normed * jnp.mean(scaled * normed, axis=-1, keepdims=True))

    def middle(g, collect, rows):
        grad = c[g, b, rows].astype(F32) + norm_back(collect.value(), mid[g, rows], gain[1])
        dmid[g, rows] = grad
        db[g, rows] = grad.astype(BF)

    def attn_back(g, i):
        grad = dot_nt(db[g, halves[i]], wo[...])
        for j in range(BATCH):
            rest = grad[:, BATCH * 128 + j * 64 : BATCH * 128 + (j + 1) * 64]
            das[g, i, j] = folded(jnp.concatenate([grad[:, j * 128 : (j + 1) * 128], rest], axis=1)).astype(BF)

    def columns(g):
        held = db[g].astype(F32)
        for j in range(BATCH):
            dcs[g, j] = folded(held[:, j * z.fh : (j + 1) * z.fh]).astype(BF)
        dcl[g, b] = dcs[g, b]

    def middles(i):
        co_d[i].done()
        middle(0, co_d[i], halves[i])
        attn_back(0, i)
        dal[0, i, b] = das[0, i, b]
        ex_da[i].start()

    def spread_db():
        columns(0)
        ex_dc.start()

    def short_middles():
        co_ds.done()

        @pl.when(short)
        def _():
            middle(1, co_ds, slice(0, r))
            for i in range(2):
                attn_back(1, i)
                k.dals[b, i] = das[1, i, b]

        ex_das.start()

    def short_spread_db():
        @pl.when(short)
        def _():
            columns(1)

        ex_dcs.start()

    da, dvs = k.da, k.dvs

    def mix_back(g, land):
        grad = jnp.concatenate([unfolded(land(j, i).astype(F32)) for j in range(BATCH) for i in range(2)], axis=0)
        for h, block in enumerate(heads_of(grad.astype(BF), z)):
            da[g, h] = block

    def dv_own(h):
        return lambda q: dot_tn(pb[h, :, pl.ds(pl.multiple_of(q * r, 128), r)], da[0, h])

    rs_dv = [Scatter(net, dv_own(h), k.dvh.at[h], k.dvr.at[h], r // 2, True) for h in range(z.hb)]

    def hop_dv(h):
        rs_dv[h].hop()

    def mix_backs():
        for part in ex_da:
            part.done()
        mix_back(0, lambda j, i: dal[0, i, j])

    def dvs_own(h, q):
        return dot_tn(qb[h, :, pl.ds(pl.multiple_of(q * r, 128), r)], da[1, h])

    def short_mix_backs():
        ex_das.done()

        @pl.when(short)
        def _():
            mix_back(1, lambda j, i: k.dals[j, i])
            for h in range(z.hb):
                dvs[0, h] = dvs_own(h, 1 - p).astype(BF)

        cp_dvs.start(dvs.at[0], dvs.at[1], twin)
        net.sent.append(lambda: cp_dvs.finish(dvs.at[0]))

    rs_go = Scatter(net, lambda q: folded(rows_at(go, rows_o)(q)), k.goh, k.gor, up16((z.wr + z.fold) // 2))

    def grad_output_of(g):
        cols = jnp.concatenate([unfolded(dcl[g, j].astype(F32)) for j in range(BATCH)], axis=0).astype(BF)
        total = dot_tn(folded_heads(attn.at[:, g]), cols)
        for lo, hi, at in folds(0, d):
            term = total[at : at + hi - lo]
            go[lo:hi] = go[lo:hi] + term if g else term

    def grad_output():
        ex_dc.done()
        grad_output_of(0)

    def short_grad_output():
        ex_dcs.done()

        @pl.when(short)
        def _():
            grad_output_of(1)

    gms, gm0 = mx, k.gm0
    ex_gm = Exchange(net, lambda j: gms.at[j], o_gm)
    own_gm = Local(net, gms.at[b], o_gm.at[b])

    def grad_mixer():
        for h in range(z.hb):
            delta = jnp.sum(da[0, h].astype(F32) * mixed[0, h], axis=-1, keepdims=True)
            for j in range(BATCH):
                cols = slice(j * z.cb, (j + 1) * z.cb)
                part = pf[h, :, cols] * (dot_nt(da[0, h], vl[h, cols, :]) - delta)
                gms[j, h] = part.astype(BF)
                if j == 0:
                    gm0[h] = part

    def short_grad_mixer():
        @pl.when(short)
        def _():
            for h in range(z.hb):
                delta = jnp.sum(da[1, h].astype(F32) * mixed[1, h], axis=-1, keepdims=True)
                gms[0, h] = (gm0[h] + qf[h] * (dot_nt(da[1, h], vs[h]) - delta)).astype(BF)

        ex_gm.start()
        own_gm.start()

    gis, gvs, gos, gus = k.gis, k.gvs, k.gos, k.gus
    ex_gi, ex_gv, ex_go = (
        Exchange(net, functools.partial(lambda ref, j: ref.at[j], ref), land)
        for ref, land in ((gis, o_gi), (gvs, o_gv), (gos, o_go))
    )
    own_gi, own_gv, own_go = (Local(net, ref.at[b], land.at[b]) for ref, land in ((gis, o_gi), (gvs, o_gv), (gos, o_go)))
    out_gu = Local(net, gus, o_gu)

    def deal(ref, total):
        total = unfolded(total)
        for j in range(BATCH):
            part = total[j * z.rw : (j + 1) * z.rw]
            ref[j] = jnp.concatenate([part, jnp.zeros((z.rw, 256 - z.fh), F32)], axis=1)

    def end_gu():
        gus[...] = jnp.concatenate([ring.done() for ring in rs_gu], axis=1)
        out_gu.start()

    def end_gi():
        total = jnp.concatenate([ring.done() for ring in rs_gi], axis=1)
        for j in range(BATCH):
            gis[j] = halved(total[j * z.rw : (j + 1) * z.rw]).astype(BF)
        ex_gi.start()
        own_gi.start()

    def end_gv():
        deal(gvs, rs_gv.done())
        ex_gv.start()
        own_gv.start()

    def end_go():
        deal(gos, rs_go.done())
        ex_go.start()
        own_go.start()

    dv, d1 = k.dv, dp
    co_1, co_1s = (Collect(net, d1.at[g], [k.d1b.at[i, g] for i in range(4)], w) for g, w in ((0, None), (1, short)))

    def values_back(g, total):
        for s, block in enumerate(slots_of([part.astype(BF) for part in total], z)):
            dv[g, s * r : (s + 1) * r] = block
        d1[g] = dot_nt(dv[g], k.wv[...]).reshape(BATCH, r, d).astype(BF)

    def values_backs():
        total = [ring.done() for ring in rs_dv]
        for part in co_d:
            part.sent_now()
        values_back(0, total)
        co_1.start()

    def short_values_backs():
        cp_dvs.arrive(dvs.at[1])
        co_ds.sent_now()

        @pl.when(short)
        def _():
            values_back(1, [dvs_own(h, p) + dvs[1, h].astype(F32) for h in range(z.hb)])

        co_1s.start()

    def grad_value():
        gv[...] = dot_tn(h1[0].reshape(rows4, d), dv[0])

    def short_grad_value():
        @pl.when(short)
        def _():
            gv[...] += dot_tn(h1[1].reshape(rows4, d), dv[1])

    outs_vm, gts = k.outs, k.gts
    out_rms = Local(net, rms, o_rms)
    out_out = [Local(net, outs_vm.at[g], o_out.at[g], w) for g, w in ((0, None), (1, short))]
    out_gt = [Local(net, gts.at[g], o_gt.at[g], w) for g, w in ((0, None), (1, short))]

    def end_out():
        co_o.done()
        outs_vm[0] = (mid[0] + co_o.value()).astype(BF)
        out_out[0].start()

    def short_end_out():
        co_os.done()

        @pl.when(short)
        def _():
            outs_vm[1] = (mid[1] + co_os.value()).astype(BF)

        out_out[1].start()

    def finish_tokens(g, collect):
        gts[g] = dmid[g] + norm_back(collect.value(), x[g, b].astype(F32), gain[0])

    def end_tokens():
        co_1.done()
        finish_tokens(0, co_1)
        out_gt[0].start()

    def short_end_tokens():
        co_1s.done()

        @pl.when(short)
        def _():
            finish_tokens(1, co_1s)

        out_gt[1].start()

    first_wu(1)
    ex_wv.start()
    first_wu(0)
    ex_wi.start()
    start_x()
    ready_wo()
    ready_wv()
    ag_wv.hop()
    sp_xs.start()
    ag_wo.hop()
    start_c()
    ready_wi()
    ag_wi[1].hop()
    ag_wv.hop()
    ag_wi[0].hop()
    ag_wo.hop()
    sp_cs.start()
    ag_wv.hop()
    sp_x.mid()
    ex_mx.start()
    ag_wi[1].hop()
    ag_wo.hop()
    ag_wv.hop()
    sp_xs.mid()
    ag_wu[0].hop()
    ag_wu[1].hop()
    ready_gains()
    ready_values()
    ag_wo.hop()
    ag_v[1].hop()
    ag_v[2].hop()
    spread_wo()
    ag_v[0].hop()
    ag_v[1].hop()
    ag_v[2].hop()
    ag_v[0].hop()
    ag_v[1].hop()
    short_values()
    ag_v[2].hop()
    probabilities()
    ag_v[0].hop()
    ag_wi[0].hop()
    short_mix()
    sp_c.mid()
    ag_v[1].hop()
    sp_cs.mid()
    ag_v[2].hop()
    ag_v[0].hop()
    ag_wu[0].hop()
    ag_wi[1].hop()
    ready_c()
    mix_head(2)
    sp_wo.mid()
    ag_wi[0].hop()
    ag_wu[1].hop()
    mix_head(1)
    mix_head(0)
    mix()
    sp_as.mid()
    ag_wi[1].hop()
    ag_wu[0].hop()
    wo_done()
    ready_cs()
    short_branches()
    ag_wi[0].hop()
    ag_wu[1].hop()
    sp_a.mid()
    branches()
    feeds()
    feed_backs()
    grad_out(1)
    short_feeds()
    short_grad_out(1)
    rs_gu[1].hop()
    co_d[0].mid()
    short_feed_backs()
    co_d[1].mid()
    grad_in(1)
    short_grad_in(1)
    rs_gi[1].hop()
    grad_out(0)
    grad_in(0)
    rs_gu[1].hop()
    short_grad_in(0)
    middles(0)
    rs_gi[1].hop()
    middles(1)
    short_finals()
    rs_gu[1].hop()
    co_ds.mid()
    short_grad_out(0)
    rs_gu[0].hop()
    rs_gi[0].hop()
    mix_backs()
    hop_dv(0)
    hop_dv(2)
    hop_dv(1)
    rs_gi[1].hop()
    finals()
    co_os.mid()
    hop_dv(0)
    hop_dv(2)
    short_middles()
    hop_dv(1)
    rs_gi[0].hop()
    out_rms.start()
    hop_dv(0)
    short_spread_db()
    hop_dv(2)
    co_o.mid()
    hop_dv(1)
    spread_db()
    grad_mixer()
    short_mix_backs()
    hop_dv(0)
    hop_dv(2)
    short_grad_mixer()
    hop_dv(1)
    short_values_backs()
    grad_output()
    short_grad_output()
    rs_gu[0].hop()
    co_1s.mid()
    rs_go.hop()
    rs_gi[1].hop()
    values_backs()
    grad_value()
    short_grad_value()
    rs_gv.hop()
    rs_go.hop()
    rs_gi[0].hop()
    co_1.mid()
    rs_gv.hop()
    rs_go.hop()
    rs_gi[0].hop()
    rs_gv.hop()
    rs_go.hop()
    rs_gu[0].hop()
    rs_gv.hop()
    short_end_out()
    end_gi()
    end_out()
    rs_gu[1].hop()
    end_go()
    short_end_tokens()
    rs_gu[0].hop()
    end_tokens()
    end_gv()
    end_gu()

    ex_gm.done()
    ex_gi.done()
    ex_gv.done()
    ex_go.done()
    for copy in (own_gm, own_gi, own_gv, own_go, out_gu, out_rms, *out_out, *out_gt):
        copy.done()
    for finish_sends in net.sent:
        finish_sends()
    assert net.used == z.sems, net.used


def finish_kernel(
    z, lens_in, outs, gts, gm, gv, go, gi, gu, rms, gain_1, gain_2, wv, wi,
    o_out, o_gt, o_gm, o_g1, o_gv, o_go, o_g2, o_gi, o_gu, o_rms_1, o_rms_2,
    v_out, v_gt, v_gm, v_gv, v_gi, v_rms, v_gu, v_go, v_wv, v_wi, v_g1, v_g2,
    s_out, s_gt, s_gm, s_gv, s_gi, s_go, s_g1, s_g2, s_rms, lens, sems,
):
    n, r = z.n, z.r
    used = []

    def copy(src, dst):
        used.append(pltpu.make_async_copy(src, dst, sems.at[len(used)]))
        used[-1].start()
        return used[-1]

    in_lens = copy(lens_in, lens)
    in_gm = [copy(gm.at[j], v_gm.at[j]) for j in range(BATCH)]
    in_gt, in_out = copy(gts, v_gt), copy(outs, v_out)
    in_gi, in_gv, in_rms = copy(gi, v_gi), copy(gv, v_gv), copy(rms, v_rms)
    in_gu, in_go = copy(gu, v_gu), copy(go, v_go)
    last = []
    has_short = lax.axis_index("pos") < SHORT // r

    def slots(ref):
        first_long = lens[0] > SHORT
        lower = jnp.where(has_short, ref[1].astype(F32), 0.0)
        upper = ref[0].astype(F32)
        return jnp.where(first_long, upper, lower), jnp.where(first_long, lower, upper)

    in_small = [copy(wv, v_wv), copy(wi, v_wi), copy(gain_1, v_g1), copy(gain_2, v_g2)]
    for j in range(BATCH):
        in_gm[j].wait()
        for h in range(z.hb):
            s_gm[j * z.hb + h] = v_gm[j, h].astype(F32)
        part = slice(j * z.hb, (j + 1) * z.hb)
        last.append(copy(s_gm.at[part], o_gm.at[part]))
    in_lens.wait()
    in_gt.wait()
    for s, block in enumerate(slots(v_gt)):
        s_gt[:, s, :] = block
    last.append(copy(s_gt, o_gt))
    in_gu.wait()
    last.append(copy(v_gu, o_gu))
    in_out.wait()
    for s, block in enumerate(slots(v_out)):
        s_out[:, s, :] = block.astype(BF)
    last.append(copy(s_out, o_out))

    def gain_grad(weights, grad, gain):
        ones = jnp.ones((8, grad.shape[1]), F32)
        total = lax.dot_general(
            ones, weights[...].astype(F32) * grad, (((1,), (1,)), ((), ())),
            precision=lax.Precision.HIGHEST, preferred_element_type=F32,
        )
        return total[0:1] / gain[...].astype(F32)

    for one in in_small:
        one.wait()
    in_gi.wait()
    parts = [whole(v_gi[j].astype(F32)) for j in range(BATCH)]
    s_gi[...] = jnp.concatenate([part[:, q * z.rf : (q + 1) * z.rf] for q in range(n) for part in parts], axis=1)
    last.append(copy(s_gi, o_gi))
    s_g2[...] = gain_grad(v_wi, s_gi[...], v_g2)
    last.append(copy(s_g2, o_g2))
    in_gv.wait()
    s_gv[...] = jnp.concatenate([v_gv[j, :, 0 : z.fh] for j in range(BATCH)], axis=1)
    last.append(copy(s_gv, o_gv))
    s_g1[...] = gain_grad(v_wv, s_gv[...], v_g1)
    last.append(copy(s_g1, o_g1))
    in_go.wait()
    s_go[...] = jnp.concatenate([v_go[j, :, 0 : z.fh] for j in range(BATCH)], axis=1)
    last.append(copy(s_go, o_go))
    in_rms.wait()
    for i, ref in enumerate((o_rms_1, o_rms_2)):
        for s, block in enumerate(slots(v_rms.at[i])):
            s_rms[i, s : s + 1] = jnp.transpose(block)[0:1]
        last.append(copy(s_rms.at[i], ref))
    for one in last:
        one.wait()


def finish(z, lens, results, gain_attn, gain_ffn, w_value, w_in):
    n, r, d = z.n, z.r, z.d
    vm, shape = pltpu.VMEM, jax.ShapeDtypeStruct
    hbm = pl.BlockSpec(memory_space=pl.ANY)
    taken = [(array.shape, array.dtype) for array in results]
    staged = [((r, 2, d), BF), ((r, 2, d), F32), ((z.heads, r, z.cb), F32), ((z.rw, d), F32), ((z.rw, z.ff), F32), ((z.rw, d), F32)]
    staged += [((1, z.rw), F32), ((1, z.rw), F32), ((2, 2, r), F32)]
    return pl.pallas_call(
        functools.partial(finish_kernel, z),
        out_shape=[
            shape((r, 2, d), BF), shape((r, 2, d), F32), shape((z.heads, r, z.cb), F32), shape((1, z.rw), F32),
            shape((z.rw, d), F32), shape((z.rw, d), F32), shape((1, z.rw), F32), shape((z.rw, z.ff), F32),
            shape((z.rf, d), F32), shape((2, r), F32), shape((2, r), F32),
        ],
        in_specs=[hbm] * 13,
        out_specs=[hbm] * 11,
        scratch_shapes=[vm(*taken[i]) for i in (0, 1, 2, 3, 5, 7, 6, 4)]
        + [vm(array.shape, array.dtype) for array in (w_value, w_in, gain_attn, gain_ffn)]
        + [vm(*one) for one in staged]
        + [pltpu.SMEM((2,), jnp.int32), pltpu.SemaphoreType.DMA((40,))],
        compiler_params=pltpu.CompilerParams(vmem_limit_bytes=62 << 20),
        name="finish",
    )(lens, *results, gain_attn, gain_ffn, w_value, w_in)


def one_device(
    pos, batch, tokens, seq_lens, mixer, gain_attn, w_value, w_output, gain_ffn, w_in, w_out, cotangent
):
    args = (tokens, seq_lens, mixer, gain_attn, w_value, w_output, gain_ffn, w_in, w_out, cotangent)
    if not fits(pos, batch, tokens, mixer, w_value, w_in, w_out):
        return per_device(*args)
    z = Sizes(pos, tokens, mixer, w_value, w_in, w_out)
    shapes = scratch(z)
    hbm = pl.BlockSpec(memory_space=pl.ANY)
    out_shape = [
        jax.ShapeDtypeStruct((2, z.r, z.d), BF),
        jax.ShapeDtypeStruct((2, z.r, z.d), F32),
        jax.ShapeDtypeStruct((BATCH, z.hb, z.r, z.cb), BF),
        jax.ShapeDtypeStruct((BATCH, z.rw, 256), F32),
        jax.ShapeDtypeStruct((BATCH, z.rw, 256), F32),
        jax.ShapeDtypeStruct((BATCH, 2 * z.rw, z.fc // 2), BF),
        jax.ShapeDtypeStruct((z.rf, z.d), F32),
        jax.ShapeDtypeStruct((2, 2, z.r, 128), F32),
    ]
    gain_attn, gain_ffn = gain_attn.reshape(1, z.rw), gain_ffn.reshape(1, z.rw)
    results = pl.pallas_call(
        functools.partial(layer_kernel, z, list(shapes)),
        out_shape=out_shape,
        in_specs=[hbm] * 10,
        out_specs=[hbm] * len(out_shape),
        scratch_shapes=list(shapes.values()),
        compiler_params=pltpu.CompilerParams(
            collective_id=1, has_side_effects=True, vmem_limit_bytes=62 << 20
        ),
        name="layer",
    )(
        seq_lens,
        tokens,
        cotangent,
        mixer.reshape(BATCH, z.hb, z.r, z.cb),
        gain_attn,
        gain_ffn,
        w_value,
        w_output,
        w_in,
        w_out,
    )
    out, grad_tokens, grad_mixer, grad_1, grad_value, grad_output, grad_2, grad_in, grad_out, rms_1, rms_2 = finish(
        z, seq_lens, results, gain_attn, gain_ffn, w_value, w_in
    )
    return (
        out, grad_tokens, grad_mixer, grad_1.reshape(z.rw), grad_value, grad_output, grad_2.reshape(z.rw),
        grad_in, grad_out, rms_1.T, rms_2.T,
    )


def solution(mesh):
    placed = (
        P("pos", "batch", None),
        P("batch"),
        P(None, "pos", "batch"),
        P(("pos", "batch")),
        P(("pos", "batch"), None),
        P(("pos", "batch"), None),
        P(("pos", "batch")),
        P(("pos", "batch"), None),
        P(("pos", "batch"), None),
        P("pos", "batch", None),
    )
    return jax.shard_map(
        functools.partial(one_device, mesh.shape["pos"], mesh.shape["batch"]),
        mesh=mesh,
        in_specs=placed,
        out_specs=(
            P("pos", "batch", None),
            P("pos", "batch", None),
            P(None, "pos", "batch"),
            P(("pos", "batch")),
            P(("pos", "batch"), None),
            P(("pos", "batch"), None),
            P(("pos", "batch")),
            P(("pos", "batch"), None),
            P(("pos", "batch"), None),
            P("pos", "batch"),
            P("pos", "batch"),
        ),
        check_vma=False,
    )
```

```python
import functools
import types

import jax
import jax.numpy as jnp
from jax import lax
from jax.experimental import pallas as pl
from jax.experimental.pallas import tpu as pltpu
from jax.sharding import PartitionSpec as P

SHORT = 256


EPSILON = 1e-06


def norm_apply(values, gain_vec):
    inv_rms = lax.rsqrt(jnp.mean(values * values, axis=-1, keepdims=True) + EPSILON)
    return values * inv_rms * gain_vec


def gelu_exact(values):
    return jax.nn.gelu(values, approximate=False)


def row_stats(scores):
    top_score = jnp.max(scores, axis=-1)
    return top_score + jnp.log(jnp.sum(jnp.exp(scores - top_score[..., None]), axis=-1))


def contract_rows(left, right):
    return lax.dot_general(
        left, right, (((0,), (0,)), ((), ())), preferred_element_type=jnp.float32
    )


def contract_cols(left, right):
    return lax.dot_general(
        left, right, (((1,), (1,)), ((), ())), preferred_element_type=jnp.float32
    )


def per_device(
    tokens, seq_lens, mixer, gain_attn, w_value, w_output, gain_ffn, w_in, w_out, cotangent
):
    value_mat, output_mat, in_mat, out_mat, gain_one, gain_two = (
        lax.all_gather(w_value, ("pos", "batch"), axis=0, tiled=True),
        lax.all_gather(w_output, ("pos", "batch"), axis=0, tiled=True),
        lax.all_gather(w_in, ("pos", "batch"), axis=0, tiled=True),
        lax.all_gather(w_out, ("pos", "batch"), axis=0, tiled=True),
        lax.all_gather(gain_attn, ("pos", "batch"), axis=0, tiled=True),
        lax.all_gather(gain_ffn, ("pos", "batch"), axis=0, tiled=True),
    )
    rows_r = lax.all_gather(mixer, "batch", axis=2, tiled=True)
    head_count = rows_r.shape[0]
    long_len = rows_r.shape[2]
    row_count, slot_count, width = tokens.shape
    head_dim = width // head_count
    tok_count = row_count * slot_count
    start_row = lax.axis_index("pos") * row_count
    positions = start_row + jnp.arange(row_count, dtype=jnp.int32)
    live_mask = (positions[:, None] < seq_lens[None, :]).astype(jnp.float32)
    live_col = live_mask.reshape(tok_count, 1)
    is_long = seq_lens > SHORT
    gain_first = gain_one.astype(jnp.float32)
    gain_second = gain_two.astype(jnp.float32)
    x_float = tokens.astype(jnp.float32).reshape(tok_count, width)
    normed_one = norm_apply(x_float, gain_first).astype(jnp.bfloat16)
    value = jnp.dot(normed_one, value_mat, preferred_element_type=jnp.float32).astype(jnp.bfloat16)
    value = value.reshape(row_count, slot_count, width)
    lse_long = row_stats(rows_r.astype(jnp.float32))
    head_cols = rows_r[:, :, :SHORT].astype(jnp.float32)
    lse_short = row_stats(head_cols)
    prob_head = jnp.exp(head_cols - lse_short[..., None])

    def prob_block(block, lse_l, lse_s, col_pos):
        prob_long = jnp.exp(block - lse_l[..., None])
        prob_short = jnp.where(col_pos < SHORT, jnp.exp(block - lse_s[..., None]), 0.0)
        return jnp.where(is_long[:, None, None, None], prob_long[None], prob_short[None])

    def slot_probs(piece_len):
        columns = rows_r.astype(jnp.float32)
        col_pos = jnp.arange(piece_len, dtype=jnp.int32)
        return prob_block(columns, lse_long, lse_short, col_pos)

    portion = lax.all_gather(value, "pos", axis=0, tiled=True)
    piece_len = portion.shape[0]
    prob_b = slot_probs(piece_len).astype(jnp.bfloat16)
    piece_vals = portion.reshape(piece_len, slot_count, head_count, head_dim)
    mixed = jnp.einsum("shin,nshe->ishe", prob_b, piece_vals, preferred_element_type=jnp.float32)
    attn_in = (mixed * live_mask[:, :, None, None]).astype(jnp.bfloat16).reshape(tok_count, width)
    branch = jnp.dot(attn_in, output_mat, preferred_element_type=jnp.float32)
    mid_resid = x_float + branch
    normed_two = norm_apply(mid_resid, gain_second).astype(jnp.bfloat16)
    up_proj = jnp.dot(normed_two, in_mat, preferred_element_type=jnp.float32)
    hidden = gelu_exact(up_proj).astype(jnp.bfloat16)
    summed_out = mid_resid + jnp.dot(hidden, out_mat, preferred_element_type=jnp.float32)
    output = (summed_out * live_col).astype(jnp.bfloat16).reshape(row_count, slot_count, width)
    resid_rms = (
        jnp.sqrt(jnp.mean(mid_resid * mid_resid, axis=-1) + EPSILON).reshape(row_count, slot_count)
        * live_mask
    )
    branch_rms = (
        jnp.sqrt(jnp.mean(branch * branch, axis=-1) + EPSILON).reshape(row_count, slot_count)
        * live_mask
    )
    dfinal = cotangent.reshape(tok_count, width) * live_col.astype(jnp.bfloat16)
    grad_w_out = contract_rows(hidden, dfinal)
    dhidden = contract_cols(dfinal, out_mat)
    _, gelu_back = jax.vjp(gelu_exact, up_proj)
    dupper = gelu_back(dhidden)[0].astype(jnp.bfloat16)
    grad_w_in = contract_rows(normed_two, dupper)
    d_normed_two = contract_cols(dupper, in_mat)
    _, norm_back_two = jax.vjp(norm_apply, mid_resid, gain_second)
    d_mid_norm, grad_gain_ffn = norm_back_two(d_normed_two)
    d_mid = dfinal.astype(jnp.float32) + d_mid_norm
    dbranch = d_mid.astype(jnp.bfloat16)
    grad_w_output = contract_rows(attn_in, dbranch)
    d_attn = contract_cols(dbranch, output_mat).astype(jnp.bfloat16)
    d_attn = d_attn.reshape(row_count, slot_count, head_count, head_dim)
    portion = lax.all_gather(value, "pos", axis=0, tiled=True)
    piece_len = portion.shape[0]
    prob_f = slot_probs(piece_len)
    piece_vals = portion.reshape(piece_len, slot_count, head_count, head_dim)
    d_prob = jnp.einsum("ishe,nshe->shin", d_attn, piece_vals, preferred_element_type=jnp.float32)
    weighted = prob_f * d_prob
    grad_acc = jnp.sum(weighted, axis=0)
    grad_acc, delta_all = (grad_acc, jnp.sum(weighted, axis=-1))
    delta_long = jnp.sum(jnp.where(is_long[:, None, None], delta_all, 0.0), axis=0)
    delta_short = jnp.sum(jnp.where(is_long[:, None, None], 0.0, delta_all), axis=0)
    slots_here = d_attn.shape[1]
    col_block = lax.all_to_all(rows_r, "pos", split_axis=2, concat_axis=1, tiled=True)
    lse_all_long = lax.all_gather(lse_long, "pos", axis=1, tiled=True)
    lse_all_short = lax.all_gather(lse_short, "pos", axis=1, tiled=True)
    portion = lax.all_gather(d_attn, "pos", axis=0, tiled=True)
    piece_len = portion.shape[0]
    block = col_block.astype(jnp.float32)
    lse_l = lse_all_long
    lse_s = lse_all_short
    prob_b = prob_block(block, lse_l, lse_s, positions).astype(jnp.bfloat16)
    term = jnp.einsum("shij,ishe->jshe", prob_b, portion, preferred_element_type=jnp.float32)
    dvalue = term.reshape(row_count, slots_here, width)
    full_long = jnp.exp(rows_r.astype(jnp.float32) - lse_long[..., None])
    grad_rows = grad_acc - full_long * delta_long[..., None]
    correction = prob_head * delta_short[..., None]
    grad_rows = grad_rows - jnp.pad(correction, ((0, 0), (0, 0), (0, long_len - SHORT)))
    dvalue_b = dvalue.astype(jnp.bfloat16).reshape(tok_count, width)
    grad_w_value = contract_rows(normed_one, dvalue_b)
    d_normed_one = contract_cols(dvalue_b, value_mat)
    _, norm_back_one = jax.vjp(norm_apply, x_float, gain_first)
    d_x_norm, grad_gain_attn = norm_back_one(d_normed_one)
    grad_tokens = (d_mid + d_x_norm).reshape(row_count, slot_count, width)
    grad_mixer = lax.psum_scatter(
        grad_rows.astype(jnp.bfloat16), "batch", scatter_dimension=2, tiled=True
    ).astype(jnp.float32)
    reduced = (
        lax.psum_scatter(grad_w_value, ("pos", "batch"), scatter_dimension=0, tiled=True),
        lax.psum_scatter(grad_w_output, ("pos", "batch"), scatter_dimension=0, tiled=True),
        lax.psum_scatter(grad_w_in, ("pos", "batch"), scatter_dimension=0, tiled=True),
        lax.psum_scatter(grad_w_out, ("pos", "batch"), scatter_dimension=0, tiled=True),
        lax.psum_scatter(grad_gain_attn, ("pos", "batch"), scatter_dimension=0, tiled=True),
        lax.psum_scatter(grad_gain_ffn, ("pos", "batch"), scatter_dimension=0, tiled=True),
    )
    return (
        output,
        grad_tokens,
        grad_mixer,
        reduced[4],
        reduced[0],
        reduced[1],
        reduced[5],
        reduced[2],
        reduced[3],
        resid_rms,
        branch_rms,
    )


BF = jnp.bfloat16
F32 = jnp.float32
MESH = pl.DeviceIdType.MESH
HEAD = 64
BATCH = 4
LANE = 4 * HEAD


def dot(left, right):
    return jnp.dot(left, right, preferred_element_type=F32)


def dot_tn(left, right):
    return lax.dot_general(left, right, (((0,), (0,)), ((), ())), preferred_element_type=F32)


def dot_nt(left, right):
    return lax.dot_general(left, right, (((1,), (1,)), ((), ())), preferred_element_type=F32)


def up16(rows):
    return -(-rows // 16) * 16


class Sizes:
    def __init__(self, pos, tokens, mixer, w_value, w_in, w_out):
        self.n = pos
        self.r, _, self.d = tokens.shape
        self.heads, _, self.cb = mixer.shape
        self.long = pos * self.r
        self.hb = self.heads // BATCH
        self.fh = self.hb * HEAD
        self.rw = w_value.shape[0]
        self.rf = w_out.shape[0]
        self.ff = w_in.shape[1]
        self.fc = self.ff // BATCH
        self.rp = up16(self.rw + 8)
        self.gr = self.d // 256
        self.wr = BATCH * self.rw
        self.fold = self.wr // 2
        self.wt = self.wr + self.fold + 16
        self.sems = 116 + 9 * pos


def fits(pos, batch, tokens, mixer, w_value, w_in, w_out):
    r, _, d = tokens.shape
    heads = mixer.shape[0]
    rw, rf = w_value.shape[0], w_out.shape[0]
    return (
        batch == BATCH
        and pos >= 4
        and pos % 2 == 0
        and r % 128 == 0
        and SHORT == 2 * r
        and heads % BATCH == 0
        and heads * HEAD == d
        and heads // BATCH * HEAD == 192
        and d % 256 == 0
        and 2 * (d // 256) <= 8
        and rw % 8 == 0
        and rw == 24
        and rf % 32 == 0
        and (BATCH * rw) % 32 == 0
        and w_in.shape[1] // BATCH == d
        and SHORT == mixer.shape[2]
    )


class Net:
    def __init__(self, n, sems):
        self.n = n
        self.sems = sems
        self.used = 0
        self.sent = []
        p, b = lax.axis_index("pos"), lax.axis_index("batch")
        self.p, self.b = p, b
        self.rho = self.ring(p)
        self.right = (self.place(lax.rem(self.rho + 1, n)), b)
        self.left = (self.place(lax.rem(self.rho + n - 1, n)), b)
        self.core_b = b + 1 - 2 * lax.rem(b, 2)
        self.y_b = lax.rem(b + 2, BATCH)
        self.far_b = BATCH - 1 - b
        self.core = (p, self.core_b)
        self.y = (p, self.y_b)
        self.far = (p, self.far_b)
        self.short = p < 2
        rho = self.rho
        self.first, self.second, self.late, self.last = rho == 0, rho == 1, rho == n - 2, rho == n - 1
        self.inner, self.sends_right, self.sends_left = (rho > 0) & (rho < n - 1), rho < n - 2, rho > 1
        self.edge, self.near, self.middle = self.first | self.last, self.second | self.late, (rho > 1) & (rho < n - 2)

    def ring(self, p):
        return jnp.where(lax.rem(p, 2) == 0, p // 2, self.n - 1 - p // 2)

    def place(self, rho):
        half = self.n // 2
        return jnp.where(rho < half, 2 * rho, 2 * (self.n - 1 - rho) + 1)

    def at(self, step):
        return self.place(lax.rem(self.rho + step + 2 * self.n, self.n))

    def sem(self):
        self.used += 1
        return self.sems.at[self.used - 1]


def run_if(cond, body):
    if cond is None:
        body()
    else:
        pl.when(cond)(body)


class Local:
    def __init__(self, net, src, dst, cond=None):
        self.copy = pltpu.make_async_copy(src, dst, net.sem())
        self.cond = cond

    def start(self):
        run_if(self.cond, self.copy.start)
        return self

    def done(self):
        run_if(self.cond, self.copy.wait)


class Copies:
    def __init__(self, net, cond=None):
        self.net, self.cond = net, cond
        self.send, self.recv = net.sem(), net.sem()

    def of(self, src, dst, device):
        return pltpu.make_async_remote_copy(
            src_ref=src, dst_ref=dst, send_sem=self.send, recv_sem=self.recv,
            device_id=device, device_id_type=MESH,
        )

    def start(self, src, dst, device, cond=None):
        run_if(self.cond if cond is None else cond, lambda: self.of(src, dst, device).start())

    def arrive(self, ref, cond=None):
        run_if(self.cond if cond is None else cond, lambda: self.of(ref, ref, self.net.core).wait_recv())

    def finish(self, ref, cond=None):
        run_if(self.cond if cond is None else cond, lambda: self.of(ref, ref, self.net.core).wait_send())


class Arrivals(Copies):
    def __init__(self, net, others):
        self.net, self.cond, self.send, self.recv = net, others.cond, others.send, net.sem()


class Exchange:
    def __init__(self, net, pick, land, cond=None):
        self.net, self.pick, self.land = net, pick, land
        self.copies = Copies(net, cond)

    def start(self):
        net = self.net
        for device, j in ((net.y, net.y_b), (net.far, net.far_b), (net.core, net.core_b)):
            self.copies.start(self.pick(j), self.land.at[net.b], device)
        net.sent.append(lambda: self.copies.finish(self.land.at[0 : BATCH - 1]))

    def done(self):
        self.copies.arrive(self.land.at[0 : BATCH - 1])


class Spread:
    def __init__(self, net, blocks, cond=None):
        self.net, self.blocks = net, blocks
        self.by_y = Copies(net, cond)
        self.by_core = Arrivals(net, self.by_y)

    def start(self):
        net, own = self.net, self.blocks.at[self.net.b]
        self.by_y.start(own, own, net.y)
        self.by_core.start(own, own, net.core)

    def mid(self):
        net, came = self.net, self.blocks.at[self.net.y_b]
        self.by_y.arrive(came)
        self.by_core.start(came, came, net.core)
        net.sent.append(lambda: self.by_y.finish(self.blocks.at[0:3]))

    def done(self):
        self.by_core.arrive(self.blocks.at[0:2])


class Collect:
    def __init__(self, net, part, bufs, cond=None):
        self.net, self.part, self.bufs, self.cond = net, part, bufs, cond
        self.to_other = Copies(net, cond)
        self.to_mine = Arrivals(net, self.to_other)

    def start(self):
        net, (mine, other, _, _) = self.net, self.bufs
        self.to_other.start(self.part.at[net.far_b], other, net.core)
        self.to_mine.start(self.part.at[net.core_b], mine, net.core)

    def mid(self):
        net, (mine, other, stage, across) = self.net, self.bufs
        self.to_other.arrive(other)

        def add():
            stage[...] = (self.part[net.y_b].astype(F32) + other[...].astype(F32)).astype(BF)

        run_if(self.cond, add)
        self.to_mine.start(stage, across, net.y)
        net.sent.append(self.sent)

    def done(self):
        self.to_mine.arrive(self.part.at[0:2])

    def sent(self):
        self.to_other.finish(self.part.at[0:3])

    def sent_now(self):
        self.net.sent.remove(self.sent)
        self.sent()

    def value(self):
        return self.part[self.net.b].astype(F32) + self.bufs[0][...].astype(F32) + self.bufs[3][...].astype(F32)


class Gather:
    def __init__(self, net, slot, first, second, size, skew=False):
        self.net, self.slot, self.size, self.skew = net, slot, size, skew
        self.steps, self.next = net.n // 2, 0
        whole = Copies(net)
        self.hops = [whole] + [Arrivals(net, whole) for _ in range(self.steps - 2)]
        if skew:
            self.end = Copies(net)
            self.ends = (
                ((first, net.sends_right), (slot, net.late)),
                ((second, net.sends_left), (slot, net.second)),
            )
        else:
            self.end = Arrivals(net, whole)
            self.ends = (((first, None),), ((second, None),))

    def hop(self, own=None):
        net, t = self.net, self.next
        if t == self.steps:
            return
        self.next += 1
        if t:
            self.hops[t - 1].arrive(self.size(2))
        for way, sign, device in ((0, -1, net.right), (1, 1, net.left)):
            q = net.at(sign * t)
            if t < self.steps - 1:
                self.hops[t].start(self.slot(q) if own is None else own, self.slot(q), device)
            else:
                for place, cond in self.ends[way]:
                    self.end.start(place(q), place(q), device, cond)
        if t == self.steps - 1:
            net.sent.append(self.sent)

    def sent(self):
        net, count = self.net, 2 * (self.steps - 1)
        if self.skew:
            self.hops[0].finish(self.size(count))
            for blocks, cond in ((0.5, net.edge), (1.5, net.near), (1, net.middle)):
                self.end.finish(self.size(blocks), cond)
        else:
            self.hops[0].finish(self.size(count + 1))

    def done(self):
        while self.next < self.steps:
            self.hop()
        self.end.arrive(self.size(1))


class Scatter:
    def __init__(self, net, own, held, came, cut, skew=False):
        self.net, self.own, self.held, self.came, self.cut, self.skew = net, own, held, came, cut, skew
        self.steps, self.next = net.n // 2, 0
        rows = held.shape[-2]
        spans, every = (slice(0, cut), slice(cut, rows)), slice(0, rows)
        self.head = Copies(net)
        whole = Copies(net)
        self.hops = [whole] + [Arrivals(net, whole) for _ in range(self.steps - 2)]
        if skew:
            self.heads = (
                ((spans[0], net.inner, net.sends_left), (every, net.first, net.second)),
                ((spans[1], net.inner, net.sends_right), (every, net.last, net.late)),
            )
        else:
            self.heads = (((spans[0], None, None),), ((spans[1], None, None),))

    def hop(self):
        net, t = self.net, self.next
        if t == self.steps:
            return
        self.next += 1
        ways = ((0, 1, net.right), (1, -1, net.left))
        if t == 0:
            value = self.own(net.at(self.steps)).astype(BF)
            for way, _, device in ways:
                self.held[way, 0] = value
                for span, cond, _ in self.heads[way]:
                    self.head.start(self.held.at[way, 0, span], self.came.at[way, 0, span], device, cond)
            return
        values = [self.own(net.at(sign * (self.steps - t))) for _, sign, _ in ways]
        if t == 1:
            if self.skew:
                half = slice(0, self.cut)
                self.head.arrive(self.came.at[0, 0, half], net.edge)
                self.head.arrive(self.came.at[0, 0:3, half], net.near)
                self.head.arrive(self.came.at[0, 0], net.middle)
            else:
                self.head.arrive(self.came.at[0, 0])
        else:
            self.hops[t - 2].arrive(self.came.at[:, t - 1])
        for way, _, device in ways:
            if t == 1:
                self.held[way, 1] = values[way].astype(BF)
                for span, _, here in self.heads[way]:
                    self.add(way, span, values[way], here)
            else:
                self.held[way, t] = (values[way] + self.came[way, t - 1].astype(F32)).astype(BF)
            self.hops[t - 1].start(self.held.at[way, t], self.came.at[way, t], device)
        if t == self.steps - 1:
            net.sent.append(self.sent)

    def add(self, way, span, value, here):
        def body():
            self.held[way, 1, span] = (value[span] + self.came[way, 0, span].astype(F32)).astype(BF)

        run_if(here, body)

    def sent(self):
        self.head.finish(self.held.at[0, 0])
        self.hops[0].finish(self.held.at[:, 0 : self.steps - 1])

    def done(self):
        while self.next < self.steps:
            self.hop()
        last = self.steps - 1
        self.hops[-1].arrive(self.came.at[:, last])
        return self.own(self.net.p) + self.came[0, last].astype(F32) + self.came[1, last].astype(F32)


def unit(values):
    inv = lax.rsqrt(jnp.mean(values * values, axis=-1, keepdims=True) + EPSILON)
    return values * inv, inv


def heads_of(rows, z):
    return [
        jnp.concatenate([rows[s * z.r : (s + 1) * z.r, h * HEAD : (h + 1) * HEAD] for s in range(BATCH)], axis=-1)
        for h in range(z.hb)
    ]


def slots_of(by_head, z):
    return [
        jnp.concatenate([by_head[h][:, s * HEAD : (s + 1) * HEAD] for h in range(z.hb)], axis=-1)
        for s in range(BATCH)
    ]


def halved(block):
    cols = block.shape[1] // 2
    return jnp.concatenate([block[:, 0:cols], block[:, cols:]], axis=0)


def whole(block):
    rows = block.shape[0] // 2
    return jnp.concatenate([block[0:rows], block[rows:]], axis=1)


def folded(block):
    rest, half = block[:, 128:], block.shape[0] // 2
    return jnp.concatenate([block[:, 0:128], jnp.concatenate([rest[0:half], rest[half:]], axis=1)], axis=0)


def unfolded(block):
    half = block.shape[0] // 3
    rest = block[2 * half :]
    rest = jnp.concatenate([rest[:, 0:64], rest[:, 64:]], axis=0)
    return jnp.concatenate([block[0 : 2 * half], rest], axis=1)


def folds(lo, hi):
    spans = []
    while lo < hi:
        j, t = lo // 192, lo % 192
        end = min(hi, j * 192 + (128 if t < 128 else 192))
        spans.append((lo, end, j * 128 + t if t < 128 else BATCH * 128 + j * 64 + t - 128))
        lo = end
    return spans


def folded_heads(ref):
    slots = []
    for s in range(BATCH):
        rest = [ref[j, 4 + s // 2][:, s % 2 * 64 : s % 2 * 64 + 64] for j in range(BATCH)]
        slots.append(jnp.concatenate([ref[j, s] for j in range(BATCH)] + rest, axis=1))
    return jnp.concatenate(slots, axis=0)


def fold_slots(blocks):
    low = [block[:, 0:128] for block in blocks]
    return low + [jnp.concatenate([blocks[s][:, 128:192], blocks[s + 1][:, 128:192]], axis=1) for s in (0, 2)]


def scratch(z):
    n, r, d, half = z.n, z.r, z.d, z.n // 2
    vm = pltpu.VMEM
    slots, own = (2, BATCH, r, d), (2, r, d)

    def ring(*shape):
        return vm((2, half) + shape, BF)

    return dict(
        lens=pltpu.SMEM((2,), jnp.int32), pack=vm((z.rp, d + z.ff), BF),
        raw=vm((2, r, 2, d), BF), x=vm(slots, BF), c=vm(slots, BF), mx=vm((BATCH, z.hb, r, z.cb), BF),
        wvp=vm((BATCH, z.rp, 256), BF), wip=vm((BATCH, 2 * z.rw, z.fc // 2), BF),
        wvs=vm((BATCH, z.rp, 256), BF), wog=vm((BATCH, n, 2 * z.rw, d // 2), BF), wis=vm((BATCH, 2 * z.rw, z.fc // 2), BF),
        wvg=vm((n, z.wt, 128), BF), wv=vm((d, z.fh), BF), wo=vm((d, d), BF), wi=vm((d, z.fc), BF), wu=vm((z.fc, d), BF),
        gain=vm((2, 1, d), F32),
        h1=vm(slots, BF), vl=vm((z.hb, z.long, LANE), BF), vs=vm((z.hb, SHORT, LANE), BF),
        pf=vm((z.hb, r, z.long), F32), pb=vm((z.hb, r, z.long), BF),
        qf=vm((z.hb, r, SHORT), F32), qb=vm((z.hb, r, SHORT), BF),
        mixed=vm((2, z.hb, r, LANE), F32), attn=vm((BATCH, 2, 6, r, 128), BF),
        mid=vm(own, F32), h2=vm(slots, BF),
        hid=vm((2, BATCH * r, z.fc), BF), dup=vm((2, BATCH * r, z.fc), BF),
        dp=vm(slots, BF), db=vm(own, BF), dmid=vm(own, F32),
        dpb=vm((4,) + own, BF), opb=vm((4,) + own, BF), d1b=vm((4,) + own, BF),
        da=vm((2, z.hb, r, LANE), BF), dv=vm((2, BATCH * r, z.fh), BF), dvs=vm((2, z.hb, r, LANE), BF),
        das=vm((2, 2, BATCH, r * 3 // 4, 128), BF), dal=vm((1, 2, BATCH, r * 3 // 4, 128), BF),
        dals=vm((BATCH, 2, r * 3 // 4, 128), BF), dcs=vm((2, BATCH, r * 3 // 2, 128), BF), dcl=vm((2, BATCH, r * 3 // 2, 128), BF),
        gm0=vm((z.hb, r, z.cb), F32), slope=vm((BATCH * r, z.fc), F32),
        gu=vm((z.fc, d), F32), gi=vm((d, z.fc), F32), go=vm((d, z.fh), F32), gv=vm((d, z.fh), F32),
        gis=vm((BATCH, 2 * z.rw, z.fc // 2), BF), gvs=vm((BATCH, z.rw, 256), F32), gos=vm((BATCH, z.rw, 256), F32), gus=vm((z.rf, d), F32),
        outs=vm(own, BF), gts=vm(own, F32), rms=vm((2, 2, r, 128), F32),
        guh=ring(z.rf, 256), gur=ring(z.rf, 256), gih=ring(BATCH * z.rw, 256), gir=ring(BATCH * z.rw, 256),
        guh2=ring(z.rf, d - 256), gur2=ring(z.rf, d - 256), gih2=ring(BATCH * z.rw, d - 256), gir2=ring(BATCH * z.rw, d - 256),
        goh=ring(z.wr + z.fold, 128), gor=ring(z.wr + z.fold, 128), gvh=ring(z.wr + z.fold, 128), gvr=ring(z.wr + z.fold, 128),
        dvh=vm((z.hb, 2, half, r, LANE), BF), dvr=vm((z.hb, 2, half, r, LANE), BF),
        sems=pltpu.SemaphoreType.DMA((z.sems,)),
    )


def layer_kernel(z, names, *refs):
    lens_in, tok, cot, mix_in, gain_1, gain_2, wv_in, wo_in, wi_in, wu_in = refs[:10]
    o_out, o_gt, o_gm, o_gv, o_go, o_gi, o_gu, o_rms, o_pack = refs[10:19]
    k = types.SimpleNamespace(**dict(zip(names, refs[19:])))
    n, r, d = z.n, z.r, z.d
    rows4 = BATCH * r
    rows_o = BATCH * z.rw
    net = Net(n, k.sems)
    p, b, short = net.p, net.b, net.short

    barrier = pltpu.get_barrier_semaphore()
    for device in (net.right, net.left, net.core, net.y, net.far):
        pl.semaphore_signal(barrier, inc=1, device_id=device, device_id_type=MESH)

    x, c, mx, wu, wvp, wip = k.x, k.c, k.mx, k.wu, k.wvp, k.wip

    def span(ref, size, lo=0, hi=None):
        hi = size if hi is None else hi
        return lambda q: ref.at[pl.ds(pl.multiple_of(q * size + lo, 16), hi - lo)]

    wu_span = span(wu, z.rf)
    lens = k.lens
    raw_x = Local(net, tok, k.raw.at[0]).start()
    raw_lens = Local(net, lens_in, lens).start()
    out_pack = Local(net, k.pack, o_pack)
    own_wu = Local(net, wu_in, wu_span(p)).start()
    own_mx = Local(net, mix_in.at[b], mx.at[b]).start()
    raw_c = Local(net, cot, k.raw.at[1]).start()

    def sort_slots(which, into):
        pair = k.raw[which].reshape(2 * r, d)
        behind = jnp.where(lens[0] > SHORT, 0, 1)
        place = lax.broadcasted_iota(jnp.int32, (r, 2 * r), 1) - 2 * lax.broadcasted_iota(jnp.int32, (r, 2 * r), 0)
        for g, slot in enumerate((behind, 1 - behind)):
            into[g, b] = dot((place == slot).astype(BF), pair).astype(BF)

    wvs, wis = k.wvs, k.wis
    raw_lens.done()
    place = lax.broadcasted_iota(jnp.int32, (z.rw, d), 1) - lax.broadcasted_iota(jnp.int32, (z.rw, d), 0)
    place = (place == (BATCH * p + b) * z.rw).astype(BF)
    table = [dot(ref[...], place) for ref in (gain_1, gain_2)]
    tail = [table[g][:, i * 256 : (i + 1) * 256] for g in range(2) for i in range(z.gr)]
    tail = jnp.concatenate(tail + [jnp.zeros((z.rp - z.rw - 2 * z.gr, 256), F32)], axis=0)
    held = wv_in[...].astype(F32)
    for j in range(BATCH):
        piece = jnp.concatenate([held[:, j * z.fh : (j + 1) * z.fh], jnp.zeros((z.rw, 256 - z.fh), F32)], axis=1)
        wvs[j] = jnp.concatenate([piece, tail], axis=0).astype(BF)
    wvp[b] = wvs[b]

    held = wi_in[...].astype(F32)
    for j in range(BATCH):
        cols = [held[:, (BATCH * q + j) * z.rf : (BATCH * q + j + 1) * z.rf] for q in range(n)]
        wis[j] = halved(jnp.concatenate(cols, axis=1)).astype(BF)
    wip[b] = wis[b]
    fill = jnp.zeros((1, 128 - z.rw), F32)
    gains = [jnp.concatenate([ref[...].astype(F32), fill], axis=1) for ref in (gain_1, gain_2)]
    gains = jnp.concatenate(gains + [jnp.zeros((z.rp - z.rw - 2, 128), F32)], axis=0)
    for ref, lo in ((wv_in, 0), (wi_in, d)):
        under = jnp.zeros((z.rp - z.rw, ref.shape[1]), F32)
        if lo == 0:
            under = jnp.concatenate([gains, under[:, 128:]], axis=1)
        k.pack[:, lo : lo + ref.shape[1]] = jnp.concatenate([ref[...].astype(F32), under], axis=0).astype(BF)
    out_pack.start()
    raw_x.done()
    sort_slots(0, x)
    pl.semaphore_wait(barrier, 5)

    def first_wu(half):
        ag_wu[half].hop(wu_in.at[(slice(0, cut_f), slice(cut_f, z.rf))[half]])

    def start_x():
        sp_x.start()

    def start_c():
        raw_c.done()
        sort_slots(1, c)
        sp_c.start()

    ex_wv = Exchange(net, lambda j: wvs.at[j], wvp)
    ex_wi = Exchange(net, lambda j: wis.at[j], wip)
    ex_mx = Exchange(net, lambda j: mix_in.at[j], mx)
    sp_x, sp_xs = Spread(net, x.at[0]), Spread(net, x.at[1], short)
    sp_c, sp_cs = Spread(net, c.at[0]), Spread(net, c.at[1], short)
    cut_f = up16(z.rf // 2)
    third_f = up16(cut_f // 2)
    third_i = up16(rows_o // 4)

    def two_rings(ref, size, cut, third):
        return (
            Gather(
                net, span(ref, size, 0, cut), span(ref, size, 0, third), span(ref, size, third, cut),
                lambda k: ref.at[0 : k * cut],
            ),
            Gather(
                net, span(ref, size, cut), span(ref, size, cut, size - third), span(ref, size, size - third),
                lambda k: ref.at[0 : k * (size - cut)],
            ),
        )

    ag_wu = two_rings(wu, z.rf, cut_f, third_f)

    wvg = k.wvg
    cut_v = up16(z.wt // 2)
    ag_wv = Gather(
        net, lambda q: wvg.at[q], lambda q: wvg.at[q, 0:cut_v], lambda q: wvg.at[q, cut_v : z.wt], lambda k: wvg.at[0:k]
    )

    def ready_wv():
        ex_wv.done()
        weights = jnp.concatenate([wvp[j].astype(F32)[0 : z.rw] for j in range(BATCH)], axis=0)
        gains = sum(wvp[j].astype(F32)[z.rw : z.rw + 8] for j in range(BATCH))
        wvg[p] = jnp.concatenate([folded(weights[:, 0 : z.fh]), gains[:, 0:128], gains[:, 128:256]], axis=0).astype(BF)

    wo, wog = k.wo, k.wog
    ag_wo = Gather(
        net, lambda q: wog.at[b, q], lambda q: wog.at[b, q, 0:32], lambda q: wog.at[b, q, 32 : 2 * z.rw],
        lambda k: wog.at[0, 0:k],
    )
    sp_wo = Spread(net, wog)

    def ready_wo():
        wog[b, p] = halved(wo_in[...].astype(F32)).astype(BF)

    def spread_wo():
        ag_wo.done()
        sp_wo.start()

    def wo_done():
        sp_wo.done()
        for q in range(n):
            block = jnp.concatenate([whole(wog[j, q].astype(F32)) for j in range(BATCH)], axis=0).astype(BF)
            for lo, hi, at in folds(q * rows_o, (q + 1) * rows_o):
                wo[at : at + hi - lo] = block[lo - q * rows_o : hi - q * rows_o]

    def pack(ref):
        return jnp.concatenate([whole(ref[j].astype(F32)) for j in range(BATCH)], axis=0).astype(BF)

    wi = k.wi
    cut_i = up16(rows_o // 2)
    ag_wi = two_rings(wi, rows_o, cut_i, third_i)

    def ready_wi():
        ex_wi.done()
        wi[pl.ds(pl.multiple_of(p * rows_o, 16), rows_o)] = pack(wip)

    h1, vl, vs, gain = k.h1, k.vl, k.vs, k.gain
    here = pl.ds(pl.multiple_of(p * r, 16), r)
    twin = (1 - p, b)
    other = pl.ds(pl.multiple_of((1 - p) * r, 16), r)
    cp_vs, cp_dvs = Copies(net, short), Copies(net, short)

    def ready_gains():
        ag_wv.done()
        top = z.wr + z.fold
        table = jnp.sum(wvg[:, top : top + 16].astype(F32), axis=0)
        table = jnp.concatenate([table[0:8], table[8:16]], axis=1)
        for g in range(2):
            gain[g] = jnp.concatenate([table[g * z.gr + i : g * z.gr + i + 1] for i in range(z.gr)], axis=1)
        for q in range(n):
            k.wv[q * z.wr : (q + 1) * z.wr] = unfolded(wvg[q, 0 : z.wr + z.fold])

    def values(g, into):
        for s in range(BATCH):
            h1[g, s] = (unit(x[g, s].astype(F32))[0] * gain[0]).astype(BF)
        value = dot(h1[g].reshape(rows4, d), k.wv[...]).astype(BF)
        for h, block in enumerate(heads_of(value, z)):
            into[h, here, :] = block

    def vl_span(h, lo, hi):
        return lambda q: vl.at[h, pl.ds(pl.multiple_of(q * r + lo, 16), hi - lo), :]

    def vl_size(h):
        return lambda blocks: vl.at[h, 0 : int(blocks * r)]

    ag_v = [
        Gather(net, vl_span(h, 0, r), vl_span(h, 0, r // 2), vl_span(h, r // 2, r), vl_size(h), True) for h in range(z.hb)
    ]

    def ready_values():
        sp_x.done()
        values(0, vl)

    def short_values():
        sp_xs.done()

        @pl.when(short)
        def _():
            values(1, vs)

        cp_vs.start(vs.at[:, here, :], vs.at[:, here, :], twin)
        net.sent.append(lambda: cp_vs.finish(vs.at[:, here, :]))

    pf, pb, qf, qb = k.pf, k.pb, k.qf, k.qb

    def probabilities():
        own_mx.done()
        ex_mx.done()
        for h in range(z.hb):
            total, first = 0.0, None
            for j in range(BATCH):
                e = jnp.exp(mx[j, h].astype(F32))
                pf[h, :, j * z.cb : (j + 1) * z.cb] = e
                total = total + jnp.sum(e, axis=-1, keepdims=True)
                first = total if j == 0 else first

            @pl.when(short)
            def _():
                q = pf[h, :, 0:SHORT] * (1.0 / first)
                qf[h] = q
                qb[h] = q.astype(BF)

            scaled = pf[h] * (1.0 / total)
            pf[h] = scaled
            pb[h] = scaled.astype(BF)

    mixed, attn = k.mixed, k.attn
    sp_a, sp_as = Spread(net, attn.at[:, 0]), Spread(net, attn.at[:, 1], short)

    def mix_slots(g):
        for i, block in enumerate(fold_slots(slots_of([mixed[g, h].astype(BF) for h in range(z.hb)], z))):
            attn[b, g, i] = block

    def mix_head(h):
        ag_v[h].done()
        mixed[0, h] = dot(pb[h], vl[h])

    def mix():
        mix_slots(0)
        sp_a.start()

    def short_mix():
        cp_vs.arrive(vs.at[:, other, :])

        @pl.when(short)
        def _():
            for h in range(z.hb):
                mixed[1, h] = dot(qb[h], vs[h])
            mix_slots(1)

        sp_as.start()

    big, mid, h2, rms = k.gu, k.mid, k.h2, k.rms

    def branch_slots(g):
        big[0:rows4] = dot(folded_heads(attn.at[:, g]), wo[...])
        for s in range(BATCH):
            branch = big[s * r : (s + 1) * r]
            total = x[g, s].astype(F32) + branch
            square = jnp.mean(total * total, axis=-1, keepdims=True) + EPSILON
            h2[g, s] = (total * lax.rsqrt(square) * gain[1]).astype(BF)

            @pl.when(b == s)
            def _():
                mid[g] = total
                rms[0, g] = jnp.broadcast_to(jnp.sqrt(square), (r, 128))
                size = jnp.sqrt(jnp.mean(branch * branch, axis=-1, keepdims=True) + EPSILON)
                rms[1, g] = jnp.broadcast_to(size, (r, 128))

    def branches():
        sp_a.done()
        branch_slots(0)

    def short_branches():
        sp_as.done()

        @pl.when(short)
        def _():
            branch_slots(1)

    hid, dup, dp, op = k.hid, k.dup, k.dp, h2
    halves = (slice(0, r // 2), slice(r // 2, r))
    co_d = [Collect(net, dp.at[0, :, rows], [k.dpb.at[i, 0, rows] for i in range(4)]) for rows in halves]
    co_ds = Collect(net, dp.at[1], [k.dpb.at[i, 1] for i in range(4)], short)
    co_o, co_os = (Collect(net, op.at[g], [k.opb.at[i, g] for i in range(4)], w) for g, w in ((0, None), (1, short)))

    slopes = (k.gi, k.slope)

    def feed(g):
        left = h2[g].reshape(rows4, d)
        for q in range(z.fc // 256):
            cols = slice(q * 256, (q + 1) * 256)
            up = dot(left, wi[:, cols])
            cdf = 0.5 + 0.5 * lax.erf(up * 0.7071067811865476)
            hid[g, :, cols] = (up * cdf).astype(BF)
            slopes[g][0:rows4, cols] = cdf + up * (jnp.exp(-0.5 * up * up) * 0.3989422804014327)

    def feed_back(g):
        down = c[g].reshape(rows4, d)
        for q in range(z.fc // 256):
            cols = slice(q * 256, (q + 1) * 256)
            dup[g, :, cols] = (dot_nt(down, wu[cols, :]) * slopes[g][0:rows4, cols]).astype(BF)
        for q in range(d // 256):
            rows = slice(q * 256, (q + 1) * 256)
            dp[g, :, :, rows] = dot_nt(dup[g], wi[rows, :]).reshape(BATCH, r, 256).astype(BF)

    def feeds():
        for ring in ag_wi:
            ring.done()
        feed(0)

    def short_feeds():
        @pl.when(short)
        def _():
            feed(1)

    def feed_backs():
        for ring in ag_wu:
            ring.done()
        own_wu.done()
        feed_back(0)
        for part in co_d:
            part.start()

    def ready_c():
        sp_c.done()

    def ready_cs():
        sp_cs.done()

    def short_feed_backs():
        @pl.when(short)
        def _():
            feed_back(1)

        co_ds.start()

    gu, gi, gv, go = k.gu, k.gi, k.gv, k.go
    parts = (slice(0, 256), slice(256, d))

    def rows_at(ref, size):
        return lambda q: ref[pl.ds(pl.multiple_of(q * size, 8), size)]

    def two_scatters(ref, size, held, came):
        def block(cols):
            return lambda q: ref[pl.ds(pl.multiple_of(q * size, 8), size), cols]

        return [Scatter(net, block(part), held[i], came[i], up16(size // 2)) for i, part in enumerate(parts)]

    rs_gu = two_scatters(gu, z.rf, (k.guh, k.guh2), (k.gur, k.gur2))
    rs_gi = two_scatters(gi, rows_o, (k.gih, k.gih2), (k.gir, k.gir2))
    rs_gv = Scatter(net, lambda q: folded(rows_at(gv, rows_o)(q)), k.gvh, k.gvr, up16((z.wr + z.fold) // 2))

    def weight_grad(into, left, right, g, half):
        cols = parts[half]
        term = dot_tn(left, right(cols))
        into[:, cols] = into[:, cols] + term if g else term

    def grad_out_of(g, half):
        weight_grad(gu, hid[g], lambda cols: c[g, :, :, cols].reshape(rows4, cols.stop - cols.start), g, half)

    def grad_out(half):
        grad_out_of(0, half)

    def short_grad_out(half):
        @pl.when(short)
        def _():
            grad_out_of(1, half)

    def grad_in_of(g, half):
        weight_grad(gi, h2[g].reshape(rows4, d), lambda cols: dup[g, :, cols], g, half)

    def grad_in(half):
        grad_in_of(0, half)

    def short_grad_in(half):
        @pl.when(short)
        def _():
            grad_in_of(1, half)

    def outs(g):
        for q in range(d // 256):
            cols = slice(q * 256, (q + 1) * 256)
            op[g, :, :, cols] = dot(hid[g], wu[:, cols]).reshape(BATCH, r, 256).astype(BF)

    def finals():
        outs(0)
        co_o.start()

    def short_finals():
        @pl.when(short)
        def _():
            outs(1)

        co_os.start()

    db, dmid = k.db, k.dmid
    das, dal, dcs, dcl = k.das, k.dal, k.dcs, k.dcl
    ex_da = [
        Exchange(net, functools.partial(lambda i, j: das.at[0, i, j], i), dal.at[0, i]) for i in range(2)
    ]
    ex_das = Exchange(net, lambda j: das.at[1, :, j], k.dals, short)
    ex_dc = Exchange(net, lambda j: dcs.at[0, j], dcl.at[0])
    ex_dcs = Exchange(net, lambda j: dcs.at[1, j], dcl.at[1], short)

    def norm_back(upper, values, gain):
        normed, inv = unit(values)
        scaled = upper * gain
        return inv * (scaled - normed * jnp.mean(scaled * normed, axis=-1, keepdims=True))

    def middle(g, collect, rows):
        grad = c[g, b, rows].astype(F32) + norm_back(collect.value(), mid[g, rows], gain[1])
        dmid[g, rows] = grad
        db[g, rows] = grad.astype(BF)

    def attn_back(g, i):
        grad = dot_nt(db[g, halves[i]], wo[...])
        for j in range(BATCH):
            rest = grad[:, BATCH * 128 + j * 64 : BATCH * 128 + (j + 1) * 64]
            das[g, i, j] = folded(jnp.concatenate([grad[:, j * 128 : (j + 1) * 128], rest], axis=1)).astype(BF)

    def columns(g):
        held = db[g].astype(F32)
        for j in range(BATCH):
            dcs[g, j] = folded(held[:, j * z.fh : (j + 1) * z.fh]).astype(BF)
        dcl[g, b] = dcs[g, b]

    def middles(i):
        co_d[i].done()
        middle(0, co_d[i], halves[i])
        attn_back(0, i)
        dal[0, i, b] = das[0, i, b]
        ex_da[i].start()

    def spread_db():
        columns(0)
        ex_dc.start()

    def short_middles():
        co_ds.done()

        @pl.when(short)
        def _():
            middle(1, co_ds, slice(0, r))
            for i in range(2):
                attn_back(1, i)
                k.dals[b, i] = das[1, i, b]

        ex_das.start()

    def short_spread_db():
        @pl.when(short)
        def _():
            columns(1)

        ex_dcs.start()

    da, dvs = k.da, k.dvs

    def mix_back(g, land):
        grad = jnp.concatenate([unfolded(land(j, i).astype(F32)) for j in range(BATCH) for i in range(2)], axis=0)
        for h, block in enumerate(heads_of(grad.astype(BF), z)):
            da[g, h] = block

    def dv_own(h):
        return lambda q: dot_tn(pb[h, :, pl.ds(pl.multiple_of(q * r, 128), r)], da[0, h])

    rs_dv = [Scatter(net, dv_own(h), k.dvh.at[h], k.dvr.at[h], r // 2, True) for h in range(z.hb)]

    def hop_dv(h):
        rs_dv[h].hop()

    def mix_backs():
        for part in ex_da:
            part.done()
        mix_back(0, lambda j, i: dal[0, i, j])

    def dvs_own(h, q):
        return dot_tn(qb[h, :, pl.ds(pl.multiple_of(q * r, 128), r)], da[1, h])

    def short_mix_backs():
        ex_das.done()

        @pl.when(short)
        def _():
            mix_back(1, lambda j, i: k.dals[j, i])
            for h in range(z.hb):
                dvs[0, h] = dvs_own(h, 1 - p).astype(BF)

        cp_dvs.start(dvs.at[0], dvs.at[1], twin)
        net.sent.append(lambda: cp_dvs.finish(dvs.at[0]))

    rs_go = Scatter(net, lambda q: folded(rows_at(go, rows_o)(q)), k.goh, k.gor, up16((z.wr + z.fold) // 2))

    def grad_output_of(g):
        cols = jnp.concatenate([unfolded(dcl[g, j].astype(F32)) for j in range(BATCH)], axis=0).astype(BF)
        total = dot_tn(folded_heads(attn.at[:, g]), cols)
        for lo, hi, at in folds(0, d):
            term = total[at : at + hi - lo]
            go[lo:hi] = go[lo:hi] + term if g else term

    def grad_output():
        ex_dc.done()
        grad_output_of(0)

    def short_grad_output():
        ex_dcs.done()

        @pl.when(short)
        def _():
            grad_output_of(1)

    gms, gm0 = mx, k.gm0
    ex_gm = Exchange(net, lambda j: gms.at[j], o_gm)
    own_gm = Local(net, gms.at[b], o_gm.at[b])

    def grad_mixer():
        for h in range(z.hb):
            delta = jnp.sum(da[0, h].astype(F32) * mixed[0, h], axis=-1, keepdims=True)
            for j in range(BATCH):
                cols = slice(j * z.cb, (j + 1) * z.cb)
                part = pf[h, :, cols] * (dot_nt(da[0, h], vl[h, cols, :]) - delta)
                gms[j, h] = part.astype(BF)
                if j == 0:
                    gm0[h] = part

    def short_grad_mixer():
        @pl.when(short)
        def _():
            for h in range(z.hb):
                delta = jnp.sum(da[1, h].astype(F32) * mixed[1, h], axis=-1, keepdims=True)
                gms[0, h] = (gm0[h] + qf[h] * (dot_nt(da[1, h], vs[h]) - delta)).astype(BF)

        ex_gm.start()
        own_gm.start()

    gis, gvs, gos, gus = k.gis, k.gvs, k.gos, k.gus
    ex_gi, ex_gv, ex_go = (
        Exchange(net, functools.partial(lambda ref, j: ref.at[j], ref), land)
        for ref, land in ((gis, o_gi), (gvs, o_gv), (gos, o_go))
    )
    own_gi, own_gv, own_go = (Local(net, ref.at[b], land.at[b]) for ref, land in ((gis, o_gi), (gvs, o_gv), (gos, o_go)))
    out_gu = Local(net, gus, o_gu)

    def deal(ref, total):
        total = unfolded(total)
        for j in range(BATCH):
            part = total[j * z.rw : (j + 1) * z.rw]
            ref[j] = jnp.concatenate([part, jnp.zeros((z.rw, 256 - z.fh), F32)], axis=1)

    def end_gu():
        gus[...] = jnp.concatenate([ring.done() for ring in rs_gu], axis=1)
        out_gu.start()

    def end_gi():
        total = jnp.concatenate([ring.done() for ring in rs_gi], axis=1)
        for j in range(BATCH):
            gis[j] = halved(total[j * z.rw : (j + 1) * z.rw]).astype(BF)
        ex_gi.start()
        own_gi.start()

    def end_gv():
        deal(gvs, rs_gv.done())
        ex_gv.start()
        own_gv.start()

    def end_go():
        deal(gos, rs_go.done())
        ex_go.start()
        own_go.start()

    dv, d1 = k.dv, dp
    co_1, co_1s = (Collect(net, d1.at[g], [k.d1b.at[i, g] for i in range(4)], w) for g, w in ((0, None), (1, short)))

    def values_back(g, total):
        for s, block in enumerate(slots_of([part.astype(BF) for part in total], z)):
            dv[g, s * r : (s + 1) * r] = block
        d1[g] = dot_nt(dv[g], k.wv[...]).reshape(BATCH, r, d).astype(BF)

    def values_backs():
        total = [ring.done() for ring in rs_dv]
        for part in co_d:
            part.sent_now()
        values_back(0, total)
        co_1.start()

    def short_values_backs():
        cp_dvs.arrive(dvs.at[1])
        co_ds.sent_now()

        @pl.when(short)
        def _():
            values_back(1, [dvs_own(h, p) + dvs[1, h].astype(F32) for h in range(z.hb)])

        co_1s.start()

    def grad_value():
        gv[...] = dot_tn(h1[0].reshape(rows4, d), dv[0])

    def short_grad_value():
        @pl.when(short)
        def _():
            gv[...] += dot_tn(h1[1].reshape(rows4, d), dv[1])

    outs_vm, gts = k.outs, k.gts
    out_rms = Local(net, rms, o_rms)
    out_out = [Local(net, outs_vm.at[g], o_out.at[g], w) for g, w in ((0, None), (1, short))]
    out_gt = [Local(net, gts.at[g], o_gt.at[g], w) for g, w in ((0, None), (1, short))]

    def end_out():
        co_o.done()
        outs_vm[0] = (mid[0] + co_o.value()).astype(BF)
        out_out[0].start()

    def short_end_out():
        co_os.done()

        @pl.when(short)
        def _():
            outs_vm[1] = (mid[1] + co_os.value()).astype(BF)

        out_out[1].start()

    def finish_tokens(g, collect):
        gts[g] = dmid[g] + norm_back(collect.value(), x[g, b].astype(F32), gain[0])

    def end_tokens():
        co_1.done()
        finish_tokens(0, co_1)
        out_gt[0].start()

    def short_end_tokens():
        co_1s.done()

        @pl.when(short)
        def _():
            finish_tokens(1, co_1s)

        out_gt[1].start()

    first_wu(1)
    ex_wv.start()
    first_wu(0)
    ex_wi.start()
    start_x()
    ready_wo()
    ready_wv()
    ag_wv.hop()
    sp_xs.start()
    ag_wo.hop()
    start_c()
    ready_wi()
    ag_wi[1].hop()
    ag_wv.hop()
    ag_wi[0].hop()
    ag_wo.hop()
    sp_cs.start()
    ag_wv.hop()
    sp_x.mid()
    ex_mx.start()
    ag_wi[1].hop()
    ag_wo.hop()
    ag_wv.hop()
    sp_xs.mid()
    ag_wu[0].hop()
    ag_wu[1].hop()
    ready_gains()
    ready_values()
    ag_wo.hop()
    ag_v[1].hop()
    ag_v[2].hop()
    spread_wo()
    ag_v[0].hop()
    ag_v[1].hop()
    ag_v[2].hop()
    ag_v[0].hop()
    ag_v[1].hop()
    short_values()
    ag_v[2].hop()
    probabilities()
    ag_v[0].hop()
    ag_wi[0].hop()
    short_mix()
    sp_c.mid()
    ag_v[1].hop()
    sp_cs.mid()
    ag_v[2].hop()
    ag_v[0].hop()
    ag_wu[0].hop()
    ag_wi[1].hop()
    ready_c()
    mix_head(2)
    sp_wo.mid()
    ag_wi[0].hop()
    ag_wu[1].hop()
    mix_head(1)
    mix_head(0)
    mix()
    sp_as.mid()
    ag_wi[1].hop()
    ag_wu[0].hop()
    wo_done()
    ready_cs()
    short_branches()
    ag_wi[0].hop()
    ag_wu[1].hop()
    sp_a.mid()
    branches()
    feeds()
    feed_backs()
    grad_out(1)
    short_feeds()
    short_grad_out(1)
    rs_gu[1].hop()
    co_d[0].mid()
    short_feed_backs()
    co_d[1].mid()
    grad_in(1)
    short_grad_in(1)
    rs_gi[1].hop()
    grad_out(0)
    grad_in(0)
    rs_gu[1].hop()
    short_grad_in(0)
    middles(0)
    rs_gi[1].hop()
    middles(1)
    short_finals()
    rs_gu[1].hop()
    co_ds.mid()
    short_grad_out(0)
    rs_gu[0].hop()
    rs_gi[0].hop()
    mix_backs()
    hop_dv(0)
    hop_dv(2)
    hop_dv(1)
    rs_gi[1].hop()
    finals()
    co_os.mid()
    hop_dv(0)
    hop_dv(2)
    short_middles()
    hop_dv(1)
    rs_gi[0].hop()
    out_rms.start()
    hop_dv(0)
    short_spread_db()
    hop_dv(2)
    co_o.mid()
    hop_dv(1)
    spread_db()
    grad_mixer()
    short_mix_backs()
    hop_dv(0)
    hop_dv(2)
    short_grad_mixer()
    hop_dv(1)
    short_values_backs()
    grad_output()
    short_grad_output()
    rs_gu[0].hop()
    co_1s.mid()
    rs_go.hop()
    rs_gi[1].hop()
    values_backs()
    grad_value()
    short_grad_value()
    rs_gv.hop()
    rs_go.hop()
    rs_gi[0].hop()
    co_1.mid()
    rs_gv.hop()
    rs_go.hop()
    rs_gi[0].hop()
    rs_gv.hop()
    rs_go.hop()
    rs_gu[0].hop()
    rs_gv.hop()
    short_end_out()
    end_gi()
    end_out()
    rs_gu[1].hop()
    end_go()
    short_end_tokens()
    rs_gu[0].hop()
    end_tokens()
    end_gv()
    end_gu()

    ex_gm.done()
    ex_gi.done()
    ex_gv.done()
    ex_go.done()
    for copy in (own_gm, own_gi, own_gv, own_go, out_gu, out_rms, out_pack, *out_out, *out_gt):
        copy.done()
    for finish_sends in net.sent:
        finish_sends()
    assert net.used == z.sems, net.used


def finish_kernel(
    z, lens_in, outs, gts, gm, gv, go, gi, gu, rms, pack,
    o_out, o_gt, o_gm, o_g1, o_gv, o_go, o_g2, o_gi, o_gu, o_rms_1, o_rms_2,
    v_out, v_gt, v_gm, v_gv, v_gi, v_rms, v_gu, v_go, v_pack,
    s_out, s_gt, s_gm, s_gv, s_gi, s_go, s_g1, s_g2, s_rms, lens, sems,
):
    n, r = z.n, z.r
    used = []

    def copy(src, dst):
        used.append(pltpu.make_async_copy(src, dst, sems.at[len(used)]))
        used[-1].start()
        return used[-1]

    in_lens = copy(lens_in, lens)
    in_gm = [copy(gm.at[j], v_gm.at[j]) for j in range(BATCH)]
    in_gt, in_out = copy(gts, v_gt), copy(outs, v_out)
    in_gi, in_gv, in_rms = copy(gi, v_gi), copy(gv, v_gv), copy(rms, v_rms)
    in_gu, in_go = copy(gu, v_gu), copy(go, v_go)
    last = []
    has_short = lax.axis_index("pos") < SHORT // r

    def slots(ref):
        first_long = lens[0] > SHORT
        lower = jnp.where(has_short, ref[1].astype(F32), 0.0)
        upper = ref[0].astype(F32)
        return jnp.where(first_long, upper, lower), jnp.where(first_long, lower, upper)

    in_pack = copy(pack, v_pack)
    for j in range(BATCH):
        in_gm[j].wait()
        for h in range(z.hb):
            s_gm[j * z.hb + h] = v_gm[j, h].astype(F32)
        part = slice(j * z.hb, (j + 1) * z.hb)
        last.append(copy(s_gm.at[part], o_gm.at[part]))
    in_lens.wait()
    in_gt.wait()
    for s, block in enumerate(slots(v_gt)):
        s_gt[:, s, :] = block
    last.append(copy(s_gt, o_gt))
    in_gu.wait()
    last.append(copy(v_gu, o_gu))
    in_out.wait()
    for s, block in enumerate(slots(v_out)):
        s_out[:, s, :] = block.astype(BF)
    last.append(copy(s_out, o_out))

    def gain_grad(weights, grad, gain):
        ones = jnp.ones((8, grad.shape[1]), F32)
        total = lax.dot_general(
            ones, weights * grad, (((1,), (1,)), ((), ())),
            precision=lax.Precision.HIGHEST, preferred_element_type=F32,
        )
        return total[0:1] / gain

    in_pack.wait()
    gains = v_pack[:, 0:128].astype(F32)[z.rw : z.rw + 2, 0 : z.rw]
    in_gi.wait()
    parts = [whole(v_gi[j].astype(F32)) for j in range(BATCH)]
    s_gi[...] = jnp.concatenate([part[:, q * z.rf : (q + 1) * z.rf] for q in range(n) for part in parts], axis=1)
    last.append(copy(s_gi, o_gi))
    s_g2[...] = gain_grad(v_pack[:, z.d :].astype(F32)[0 : z.rw], s_gi[...], gains[1:2])
    last.append(copy(s_g2, o_g2))
    in_gv.wait()
    s_gv[...] = jnp.concatenate([v_gv[j, :, 0 : z.fh] for j in range(BATCH)], axis=1)
    last.append(copy(s_gv, o_gv))
    s_g1[...] = gain_grad(v_pack[:, 0 : z.d].astype(F32)[0 : z.rw], s_gv[...], gains[0:1])
    last.append(copy(s_g1, o_g1))
    in_go.wait()
    s_go[...] = jnp.concatenate([v_go[j, :, 0 : z.fh] for j in range(BATCH)], axis=1)
    last.append(copy(s_go, o_go))
    in_rms.wait()
    for i, ref in enumerate((o_rms_1, o_rms_2)):
        for s, block in enumerate(slots(v_rms.at[i])):
            s_rms[i, s : s + 1] = jnp.transpose(block)[0:1]
        last.append(copy(s_rms.at[i], ref))
    for one in last:
        one.wait()


def finish(z, lens, results):
    n, r, d = z.n, z.r, z.d
    vm, shape = pltpu.VMEM, jax.ShapeDtypeStruct
    hbm = pl.BlockSpec(memory_space=pl.ANY)
    taken = [(array.shape, array.dtype) for array in results[:8]]
    staged = [((r, 2, d), BF), ((r, 2, d), F32), ((z.heads, r, z.cb), F32), ((z.rw, d), F32), ((z.rw, z.ff), F32), ((z.rw, d), F32)]
    staged += [((1, z.rw), F32), ((1, z.rw), F32), ((2, 2, r), F32)]
    return pl.pallas_call(
        functools.partial(finish_kernel, z),
        out_shape=[
            shape((r, 2, d), BF), shape((r, 2, d), F32), shape((z.heads, r, z.cb), F32), shape((1, z.rw), F32),
            shape((z.rw, d), F32), shape((z.rw, d), F32), shape((1, z.rw), F32), shape((z.rw, z.ff), F32),
            shape((z.rf, d), F32), shape((2, r), F32), shape((2, r), F32),
        ],
        in_specs=[hbm] * 10,
        out_specs=[hbm] * 11,
        scratch_shapes=[vm(*taken[i]) for i in (0, 1, 2, 3, 5, 7, 6, 4)]
        + [vm(results[8].shape, results[8].dtype)]
        + [vm(*one) for one in staged]
        + [pltpu.SMEM((2,), jnp.int32), pltpu.SemaphoreType.DMA((27,))],
        compiler_params=pltpu.CompilerParams(vmem_limit_bytes=62 << 20),
        name="finish",
    )(lens, *results)


def one_device(
    pos, batch, tokens, seq_lens, mixer, gain_attn, w_value, w_output, gain_ffn, w_in, w_out, cotangent
):
    args = (tokens, seq_lens, mixer, gain_attn, w_value, w_output, gain_ffn, w_in, w_out, cotangent)
    if not fits(pos, batch, tokens, mixer, w_value, w_in, w_out):
        return per_device(*args)
    z = Sizes(pos, tokens, mixer, w_value, w_in, w_out)
    shapes = scratch(z)
    hbm, vmem = pl.BlockSpec(memory_space=pl.ANY), pl.BlockSpec(memory_space=pltpu.VMEM)
    out_shape = [
        jax.ShapeDtypeStruct((2, z.r, z.d), BF),
        jax.ShapeDtypeStruct((2, z.r, z.d), F32),
        jax.ShapeDtypeStruct((BATCH, z.hb, z.r, z.cb), BF),
        jax.ShapeDtypeStruct((BATCH, z.rw, 256), F32),
        jax.ShapeDtypeStruct((BATCH, z.rw, 256), F32),
        jax.ShapeDtypeStruct((BATCH, 2 * z.rw, z.fc // 2), BF),
        jax.ShapeDtypeStruct((z.rf, z.d), F32),
        jax.ShapeDtypeStruct((2, 2, z.r, 128), F32),
        jax.ShapeDtypeStruct((z.rp, z.d + z.ff), BF),
    ]
    gain_attn, gain_ffn = gain_attn.reshape(1, z.rw), gain_ffn.reshape(1, z.rw)
    results = pl.pallas_call(
        functools.partial(layer_kernel, z, list(shapes)),
        out_shape=out_shape,
        in_specs=[hbm] * 4 + [vmem] * 5 + [hbm],
        out_specs=[hbm] * len(out_shape),
        scratch_shapes=list(shapes.values()),
        compiler_params=pltpu.CompilerParams(
            collective_id=1, has_side_effects=True, vmem_limit_bytes=62 << 20
        ),
        name="layer",
    )(
        seq_lens,
        tokens,
        cotangent,
        mixer.reshape(BATCH, z.hb, z.r, z.cb),
        gain_attn,
        gain_ffn,
        w_value,
        w_output,
        w_in,
        w_out,
    )
    out, grad_tokens, grad_mixer, grad_1, grad_value, grad_output, grad_2, grad_in, grad_out, rms_1, rms_2 = finish(
        z, seq_lens, results
    )
    return (
        out, grad_tokens, grad_mixer, grad_1.reshape(z.rw), grad_value, grad_output, grad_2.reshape(z.rw),
        grad_in, grad_out, rms_1.T, rms_2.T,
    )


def solution(mesh):
    placed = (
        P("pos", "batch", None),
        P("batch"),
        P(None, "pos", "batch"),
        P(("pos", "batch")),
        P(("pos", "batch"), None),
        P(("pos", "batch"), None),
        P(("pos", "batch")),
        P(("pos", "batch"), None),
        P(("pos", "batch"), None),
        P("pos", "batch", None),
    )
    return jax.shard_map(
        functools.partial(one_device, mesh.shape["pos"], mesh.shape["batch"]),
        mesh=mesh,
        in_specs=placed,
        out_specs=(
            P("pos", "batch", None),
            P("pos", "batch", None),
            P(None, "pos", "batch"),
            P(("pos", "batch")),
            P(("pos", "batch"), None),
            P(("pos", "batch"), None),
            P(("pos", "batch")),
            P(("pos", "batch"), None),
            P(("pos", "batch"), None),
            P("pos", "batch"),
            P("pos", "batch"),
        ),
        check_vma=False,
    )
```

```python
import functools
import types

import jax
import jax.numpy as jnp
from jax import lax
from jax.experimental import pallas as pl
from jax.experimental.pallas import tpu as pltpu
from jax.sharding import PartitionSpec as P

SHORT = 256


EPSILON = 1e-06


def norm_apply(values, gain_vec):
    inv_rms = lax.rsqrt(jnp.mean(values * values, axis=-1, keepdims=True) + EPSILON)
    return values * inv_rms * gain_vec


def gelu_exact(values):
    return jax.nn.gelu(values, approximate=False)


def row_stats(scores):
    top_score = jnp.max(scores, axis=-1)
    return top_score + jnp.log(jnp.sum(jnp.exp(scores - top_score[..., None]), axis=-1))


def contract_rows(left, right):
    return lax.dot_general(
        left, right, (((0,), (0,)), ((), ())), preferred_element_type=jnp.float32
    )


def contract_cols(left, right):
    return lax.dot_general(
        left, right, (((1,), (1,)), ((), ())), preferred_element_type=jnp.float32
    )


def per_device(
    tokens, seq_lens, mixer, gain_attn, w_value, w_output, gain_ffn, w_in, w_out, cotangent
):
    value_mat, output_mat, in_mat, out_mat, gain_one, gain_two = (
        lax.all_gather(w_value, ("pos", "batch"), axis=0, tiled=True),
        lax.all_gather(w_output, ("pos", "batch"), axis=0, tiled=True),
        lax.all_gather(w_in, ("pos", "batch"), axis=0, tiled=True),
        lax.all_gather(w_out, ("pos", "batch"), axis=0, tiled=True),
        lax.all_gather(gain_attn, ("pos", "batch"), axis=0, tiled=True),
        lax.all_gather(gain_ffn, ("pos", "batch"), axis=0, tiled=True),
    )
    rows_r = lax.all_gather(mixer, "batch", axis=2, tiled=True)
    head_count = rows_r.shape[0]
    long_len = rows_r.shape[2]
    row_count, slot_count, width = tokens.shape
    head_dim = width // head_count
    tok_count = row_count * slot_count
    start_row = lax.axis_index("pos") * row_count
    positions = start_row + jnp.arange(row_count, dtype=jnp.int32)
    live_mask = (positions[:, None] < seq_lens[None, :]).astype(jnp.float32)
    live_col = live_mask.reshape(tok_count, 1)
    is_long = seq_lens > SHORT
    gain_first = gain_one.astype(jnp.float32)
    gain_second = gain_two.astype(jnp.float32)
    x_float = tokens.astype(jnp.float32).reshape(tok_count, width)
    normed_one = norm_apply(x_float, gain_first).astype(jnp.bfloat16)
    value = jnp.dot(normed_one, value_mat, preferred_element_type=jnp.float32).astype(jnp.bfloat16)
    value = value.reshape(row_count, slot_count, width)
    lse_long = row_stats(rows_r.astype(jnp.float32))
    head_cols = rows_r[:, :, :SHORT].astype(jnp.float32)
    lse_short = row_stats(head_cols)
    prob_head = jnp.exp(head_cols - lse_short[..., None])

    def prob_block(block, lse_l, lse_s, col_pos):
        prob_long = jnp.exp(block - lse_l[..., None])
        prob_short = jnp.where(col_pos < SHORT, jnp.exp(block - lse_s[..., None]), 0.0)
        return jnp.where(is_long[:, None, None, None], prob_long[None], prob_short[None])

    def slot_probs(piece_len):
        columns = rows_r.astype(jnp.float32)
        col_pos = jnp.arange(piece_len, dtype=jnp.int32)
        return prob_block(columns, lse_long, lse_short, col_pos)

    portion = lax.all_gather(value, "pos", axis=0, tiled=True)
    piece_len = portion.shape[0]
    prob_b = slot_probs(piece_len).astype(jnp.bfloat16)
    piece_vals = portion.reshape(piece_len, slot_count, head_count, head_dim)
    mixed = jnp.einsum("shin,nshe->ishe", prob_b, piece_vals, preferred_element_type=jnp.float32)
    attn_in = (mixed * live_mask[:, :, None, None]).astype(jnp.bfloat16).reshape(tok_count, width)
    branch = jnp.dot(attn_in, output_mat, preferred_element_type=jnp.float32)
    mid_resid = x_float + branch
    normed_two = norm_apply(mid_resid, gain_second).astype(jnp.bfloat16)
    up_proj = jnp.dot(normed_two, in_mat, preferred_element_type=jnp.float32)
    hidden = gelu_exact(up_proj).astype(jnp.bfloat16)
    summed_out = mid_resid + jnp.dot(hidden, out_mat, preferred_element_type=jnp.float32)
    output = (summed_out * live_col).astype(jnp.bfloat16).reshape(row_count, slot_count, width)
    resid_rms = (
        jnp.sqrt(jnp.mean(mid_resid * mid_resid, axis=-1) + EPSILON).reshape(row_count, slot_count)
        * live_mask
    )
    branch_rms = (
        jnp.sqrt(jnp.mean(branch * branch, axis=-1) + EPSILON).reshape(row_count, slot_count)
        * live_mask
    )
    dfinal = cotangent.reshape(tok_count, width) * live_col.astype(jnp.bfloat16)
    grad_w_out = contract_rows(hidden, dfinal)
    dhidden = contract_cols(dfinal, out_mat)
    _, gelu_back = jax.vjp(gelu_exact, up_proj)
    dupper = gelu_back(dhidden)[0].astype(jnp.bfloat16)
    grad_w_in = contract_rows(normed_two, dupper)
    d_normed_two = contract_cols(dupper, in_mat)
    _, norm_back_two = jax.vjp(norm_apply, mid_resid, gain_second)
    d_mid_norm, grad_gain_ffn = norm_back_two(d_normed_two)
    d_mid = dfinal.astype(jnp.float32) + d_mid_norm
    dbranch = d_mid.astype(jnp.bfloat16)
    grad_w_output = contract_rows(attn_in, dbranch)
    d_attn = contract_cols(dbranch, output_mat).astype(jnp.bfloat16)
    d_attn = d_attn.reshape(row_count, slot_count, head_count, head_dim)
    portion = lax.all_gather(value, "pos", axis=0, tiled=True)
    piece_len = portion.shape[0]
    prob_f = slot_probs(piece_len)
    piece_vals = portion.reshape(piece_len, slot_count, head_count, head_dim)
    d_prob = jnp.einsum("ishe,nshe->shin", d_attn, piece_vals, preferred_element_type=jnp.float32)
    weighted = prob_f * d_prob
    grad_acc = jnp.sum(weighted, axis=0)
    grad_acc, delta_all = (grad_acc, jnp.sum(weighted, axis=-1))
    delta_long = jnp.sum(jnp.where(is_long[:, None, None], delta_all, 0.0), axis=0)
    delta_short = jnp.sum(jnp.where(is_long[:, None, None], 0.0, delta_all), axis=0)
    slots_here = d_attn.shape[1]
    col_block = lax.all_to_all(rows_r, "pos", split_axis=2, concat_axis=1, tiled=True)
    lse_all_long = lax.all_gather(lse_long, "pos", axis=1, tiled=True)
    lse_all_short = lax.all_gather(lse_short, "pos", axis=1, tiled=True)
    portion = lax.all_gather(d_attn, "pos", axis=0, tiled=True)
    piece_len = portion.shape[0]
    block = col_block.astype(jnp.float32)
    lse_l = lse_all_long
    lse_s = lse_all_short
    prob_b = prob_block(block, lse_l, lse_s, positions).astype(jnp.bfloat16)
    term = jnp.einsum("shij,ishe->jshe", prob_b, portion, preferred_element_type=jnp.float32)
    dvalue = term.reshape(row_count, slots_here, width)
    full_long = jnp.exp(rows_r.astype(jnp.float32) - lse_long[..., None])
    grad_rows = grad_acc - full_long * delta_long[..., None]
    correction = prob_head * delta_short[..., None]
    grad_rows = grad_rows - jnp.pad(correction, ((0, 0), (0, 0), (0, long_len - SHORT)))
    dvalue_b = dvalue.astype(jnp.bfloat16).reshape(tok_count, width)
    grad_w_value = contract_rows(normed_one, dvalue_b)
    d_normed_one = contract_cols(dvalue_b, value_mat)
    _, norm_back_one = jax.vjp(norm_apply, x_float, gain_first)
    d_x_norm, grad_gain_attn = norm_back_one(d_normed_one)
    grad_tokens = (d_mid + d_x_norm).reshape(row_count, slot_count, width)
    grad_mixer = lax.psum_scatter(
        grad_rows.astype(jnp.bfloat16), "batch", scatter_dimension=2, tiled=True
    ).astype(jnp.float32)
    reduced = (
        lax.psum_scatter(grad_w_value, ("pos", "batch"), scatter_dimension=0, tiled=True),
        lax.psum_scatter(grad_w_output, ("pos", "batch"), scatter_dimension=0, tiled=True),
        lax.psum_scatter(grad_w_in, ("pos", "batch"), scatter_dimension=0, tiled=True),
        lax.psum_scatter(grad_w_out, ("pos", "batch"), scatter_dimension=0, tiled=True),
        lax.psum_scatter(grad_gain_attn, ("pos", "batch"), scatter_dimension=0, tiled=True),
        lax.psum_scatter(grad_gain_ffn, ("pos", "batch"), scatter_dimension=0, tiled=True),
    )
    return (
        output,
        grad_tokens,
        grad_mixer,
        reduced[4],
        reduced[0],
        reduced[1],
        reduced[5],
        reduced[2],
        reduced[3],
        resid_rms,
        branch_rms,
    )


BF = jnp.bfloat16
F32 = jnp.float32
MESH = pl.DeviceIdType.MESH
HEAD = 64
BATCH = 4
LANE = 4 * HEAD


def dot(left, right):
    return jnp.dot(left, right, preferred_element_type=F32)


def dot_tn(left, right):
    return lax.dot_general(left, right, (((0,), (0,)), ((), ())), preferred_element_type=F32)


def dot_nt(left, right):
    return lax.dot_general(left, right, (((1,), (1,)), ((), ())), preferred_element_type=F32)


def up16(rows):
    return -(-rows // 16) * 16


class Sizes:
    def __init__(self, pos, tokens, mixer, w_value, w_in, w_out):
        self.n = pos
        self.r, _, self.d = tokens.shape
        self.heads, _, self.cb = mixer.shape
        self.long = pos * self.r
        self.hb = self.heads // BATCH
        self.fh = self.hb * HEAD
        self.rw = w_value.shape[0]
        self.rf = w_out.shape[0]
        self.ff = w_in.shape[1]
        self.fc = self.ff // BATCH
        self.rp = up16(self.rw + 8)
        self.gr = self.d // 256
        self.wr = BATCH * self.rw
        self.fold = self.wr // 2
        self.wt = self.wr + self.fold + 16
        self.sems = 114 + 9 * pos


def fits(pos, batch, tokens, mixer, w_value, w_in, w_out):
    r, _, d = tokens.shape
    heads = mixer.shape[0]
    rw, rf = w_value.shape[0], w_out.shape[0]
    return (
        batch == BATCH
        and pos >= 4
        and pos % 2 == 0
        and r % 128 == 0
        and SHORT == 2 * r
        and heads % BATCH == 0
        and heads * HEAD == d
        and heads // BATCH * HEAD == 192
        and d % 256 == 0
        and 2 * (d // 256) <= 8
        and rw % 8 == 0
        and rw == 24
        and rf % 32 == 0
        and (BATCH * rw) % 32 == 0
        and w_in.shape[1] // BATCH == d
        and SHORT == mixer.shape[2]
    )


class Net:
    def __init__(self, n, sems):
        self.n = n
        self.sems = sems
        self.used = 0
        self.sent = []
        p, b = lax.axis_index("pos"), lax.axis_index("batch")
        self.p, self.b = p, b
        self.rho = self.ring(p)
        self.right = (self.place(lax.rem(self.rho + 1, n)), b)
        self.left = (self.place(lax.rem(self.rho + n - 1, n)), b)
        self.core_b = b + 1 - 2 * lax.rem(b, 2)
        self.y_b = lax.rem(b + 2, BATCH)
        self.far_b = BATCH - 1 - b
        self.core = (p, self.core_b)
        self.y = (p, self.y_b)
        self.far = (p, self.far_b)
        self.short = p < 2
        rho = self.rho
        self.first, self.second, self.late, self.last = rho == 0, rho == 1, rho == n - 2, rho == n - 1
        self.inner, self.sends_right, self.sends_left = (rho > 0) & (rho < n - 1), rho < n - 2, rho > 1
        self.edge, self.near, self.middle = self.first | self.last, self.second | self.late, (rho > 1) & (rho < n - 2)

    def ring(self, p):
        return jnp.where(lax.rem(p, 2) == 0, p // 2, self.n - 1 - p // 2)

    def place(self, rho):
        half = self.n // 2
        return jnp.where(rho < half, 2 * rho, 2 * (self.n - 1 - rho) + 1)

    def at(self, step):
        return self.place(lax.rem(self.rho + step + 2 * self.n, self.n))

    def sem(self):
        self.used += 1
        return self.sems.at[self.used - 1]


def run_if(cond, body):
    if cond is None:
        body()
    else:
        pl.when(cond)(body)


class Local:
    def __init__(self, net, src, dst, cond=None):
        self.copy = pltpu.make_async_copy(src, dst, net.sem())
        self.cond = cond

    def start(self):
        run_if(self.cond, self.copy.start)
        return self

    def done(self):
        run_if(self.cond, self.copy.wait)


class Copies:
    def __init__(self, net, cond=None):
        self.net, self.cond = net, cond
        self.send, self.recv = net.sem(), net.sem()

    def of(self, src, dst, device):
        return pltpu.make_async_remote_copy(
            src_ref=src, dst_ref=dst, send_sem=self.send, recv_sem=self.recv,
            device_id=device, device_id_type=MESH,
        )

    def start(self, src, dst, device, cond=None):
        run_if(self.cond if cond is None else cond, lambda: self.of(src, dst, device).start())

    def arrive(self, ref, cond=None):
        run_if(self.cond if cond is None else cond, lambda: self.of(ref, ref, self.net.core).wait_recv())

    def finish(self, ref, cond=None):
        run_if(self.cond if cond is None else cond, lambda: self.of(ref, ref, self.net.core).wait_send())


class Arrivals(Copies):
    def __init__(self, net, others):
        self.net, self.cond, self.send, self.recv = net, others.cond, others.send, net.sem()


class Exchange:
    def __init__(self, net, pick, land, cond=None):
        self.net, self.pick, self.land = net, pick, land
        self.copies = Copies(net, cond)

    def start(self):
        net = self.net
        for device, j in ((net.y, net.y_b), (net.far, net.far_b), (net.core, net.core_b)):
            self.copies.start(self.pick(j), self.land.at[net.b], device)
        net.sent.append(lambda: self.copies.finish(self.land.at[0 : BATCH - 1]))

    def done(self):
        self.copies.arrive(self.land.at[0 : BATCH - 1])


class Spread:
    def __init__(self, net, blocks, cond=None):
        self.net, self.blocks = net, blocks
        self.by_y = Copies(net, cond)
        self.by_core = Arrivals(net, self.by_y)

    def start(self):
        net, own = self.net, self.blocks.at[self.net.b]
        self.by_y.start(own, own, net.y)
        self.by_core.start(own, own, net.core)

    def mid(self):
        net, came = self.net, self.blocks.at[self.net.y_b]
        self.by_y.arrive(came)
        self.by_core.start(came, came, net.core)
        net.sent.append(lambda: self.by_y.finish(self.blocks.at[0:3]))

    def done(self):
        self.by_core.arrive(self.blocks.at[0:2])


class Collect:
    def __init__(self, net, part, bufs, cond=None):
        self.net, self.part, self.bufs, self.cond = net, part, bufs, cond
        self.to_other = Copies(net, cond)
        self.to_mine = Arrivals(net, self.to_other)

    def start(self):
        net, (mine, other, _, _) = self.net, self.bufs
        self.to_other.start(self.part.at[net.far_b], other, net.core)
        self.to_mine.start(self.part.at[net.core_b], mine, net.core)

    def mid(self):
        net, (mine, other, stage, across) = self.net, self.bufs
        self.to_other.arrive(other)

        def add():
            stage[...] = (self.part[net.y_b].astype(F32) + other[...].astype(F32)).astype(BF)

        run_if(self.cond, add)
        self.to_mine.start(stage, across, net.y)
        net.sent.append(self.sent)

    def done(self):
        self.to_mine.arrive(self.part.at[0:2])

    def sent(self):
        self.to_other.finish(self.part.at[0:3])

    def sent_now(self):
        self.net.sent.remove(self.sent)
        self.sent()

    def value(self):
        return self.part[self.net.b].astype(F32) + self.bufs[0][...].astype(F32) + self.bufs[3][...].astype(F32)


class Gather:
    def __init__(self, net, slot, first, second, size, skew=False):
        self.net, self.slot, self.size, self.skew = net, slot, size, skew
        self.steps, self.next = net.n // 2, 0
        whole = Copies(net)
        self.hops = [whole] + [Arrivals(net, whole) for _ in range(self.steps - 2)]
        if skew:
            self.end = Copies(net)
            self.ends = (
                ((first, net.sends_right), (slot, net.late)),
                ((second, net.sends_left), (slot, net.second)),
            )
        else:
            self.end = Arrivals(net, whole)
            self.ends = (((first, None),), ((second, None),))

    def hop(self, own=None):
        net, t = self.net, self.next
        if t == self.steps:
            return
        self.next += 1
        if t:
            self.hops[t - 1].arrive(self.size(2))
        for way, sign, device in ((0, -1, net.right), (1, 1, net.left)):
            q = net.at(sign * t)
            if t < self.steps - 1:
                self.hops[t].start(self.slot(q) if own is None else own, self.slot(q), device)
            else:
                for place, cond in self.ends[way]:
                    self.end.start(place(q), place(q), device, cond)
        if t == self.steps - 1:
            net.sent.append(self.sent)

    def sent(self):
        net, count = self.net, 2 * (self.steps - 1)
        if self.skew:
            self.hops[0].finish(self.size(count))
            for blocks, cond in ((0.5, net.edge), (1.5, net.near), (1, net.middle)):
                self.end.finish(self.size(blocks), cond)
        else:
            self.hops[0].finish(self.size(count + 1))

    def done(self):
        while self.next < self.steps:
            self.hop()
        self.end.arrive(self.size(1))


class Scatter:
    def __init__(self, net, own, held, came, cut, skew=False):
        self.net, self.own, self.held, self.came, self.cut, self.skew = net, own, held, came, cut, skew
        self.steps, self.next = net.n // 2, 0
        rows = held.shape[-2]
        spans, every = (slice(0, cut), slice(cut, rows)), slice(0, rows)
        self.head = Copies(net)
        whole = Copies(net)
        self.hops = [whole] + [Arrivals(net, whole) for _ in range(self.steps - 2)]
        if skew:
            self.heads = (
                ((spans[0], net.inner, net.sends_left), (every, net.first, net.second)),
                ((spans[1], net.inner, net.sends_right), (every, net.last, net.late)),
            )
        else:
            self.heads = (((spans[0], None, None),), ((spans[1], None, None),))

    def hop(self):
        net, t = self.net, self.next
        if t == self.steps:
            return
        self.next += 1
        ways = ((0, 1, net.right), (1, -1, net.left))
        if t == 0:
            value = self.own(net.at(self.steps)).astype(BF)
            for way, _, device in ways:
                self.held[way, 0] = value
                for span, cond, _ in self.heads[way]:
                    self.head.start(self.held.at[way, 0, span], self.came.at[way, 0, span], device, cond)
            return
        values = [self.own(net.at(sign * (self.steps - t))) for _, sign, _ in ways]
        if t == 1:
            if self.skew:
                half = slice(0, self.cut)
                self.head.arrive(self.came.at[0, 0, half], net.edge)
                self.head.arrive(self.came.at[0, 0:3, half], net.near)
                self.head.arrive(self.came.at[0, 0], net.middle)
            else:
                self.head.arrive(self.came.at[0, 0])
        else:
            self.hops[t - 2].arrive(self.came.at[:, t - 1])
        for way, _, device in ways:
            if t == 1:
                self.held[way, 1] = values[way].astype(BF)
                for span, _, here in self.heads[way]:
                    self.add(way, span, values[way], here)
            else:
                self.held[way, t] = (values[way] + self.came[way, t - 1].astype(F32)).astype(BF)
            self.hops[t - 1].start(self.held.at[way, t], self.came.at[way, t], device)
        if t == self.steps - 1:
            net.sent.append(self.sent)

    def add(self, way, span, value, here):
        def body():
            self.held[way, 1, span] = (value[span] + self.came[way, 0, span].astype(F32)).astype(BF)

        run_if(here, body)

    def sent(self):
        self.head.finish(self.held.at[0, 0])
        self.hops[0].finish(self.held.at[:, 0 : self.steps - 1])

    def done(self):
        while self.next < self.steps:
            self.hop()
        last = self.steps - 1
        self.hops[-1].arrive(self.came.at[:, last])
        return self.own(self.net.p) + self.came[0, last].astype(F32) + self.came[1, last].astype(F32)


def unit(values):
    inv = lax.rsqrt(jnp.mean(values * values, axis=-1, keepdims=True) + EPSILON)
    return values * inv, inv


def heads_of(rows, z):
    return [
        jnp.concatenate([rows[s * z.r : (s + 1) * z.r, h * HEAD : (h + 1) * HEAD] for s in range(BATCH)], axis=-1)
        for h in range(z.hb)
    ]


def slots_of(by_head, z):
    return [
        jnp.concatenate([by_head[h][:, s * HEAD : (s + 1) * HEAD] for h in range(z.hb)], axis=-1)
        for s in range(BATCH)
    ]


def halved(block):
    cols = block.shape[1] // 2
    return jnp.concatenate([block[:, 0:cols], block[:, cols:]], axis=0)


def whole(block):
    rows = block.shape[0] // 2
    return jnp.concatenate([block[0:rows], block[rows:]], axis=1)


def folded(block):
    rest, half = block[:, 128:], block.shape[0] // 2
    return jnp.concatenate([block[:, 0:128], jnp.concatenate([rest[0:half], rest[half:]], axis=1)], axis=0)


def unfolded(block):
    half = block.shape[0] // 3
    rest = block[2 * half :]
    rest = jnp.concatenate([rest[:, 0:64], rest[:, 64:]], axis=0)
    return jnp.concatenate([block[0 : 2 * half], rest], axis=1)


def folds(lo, hi):
    spans = []
    while lo < hi:
        j, t = lo // 192, lo % 192
        end = min(hi, j * 192 + (128 if t < 128 else 192))
        spans.append((lo, end, j * 128 + t if t < 128 else BATCH * 128 + j * 64 + t - 128))
        lo = end
    return spans


def folded_heads(ref):
    slots = []
    for s in range(BATCH):
        rest = [ref[j, 4 + s // 2][:, s % 2 * 64 : s % 2 * 64 + 64] for j in range(BATCH)]
        slots.append(jnp.concatenate([ref[j, s] for j in range(BATCH)] + rest, axis=1))
    return jnp.concatenate(slots, axis=0)


def fold_slots(blocks):
    low = [block[:, 0:128] for block in blocks]
    return low + [jnp.concatenate([blocks[s][:, 128:192], blocks[s + 1][:, 128:192]], axis=1) for s in (0, 2)]


def scratch(z):
    n, r, d, half = z.n, z.r, z.d, z.n // 2
    vm = pltpu.VMEM
    slots, own = (2, BATCH, r, d), (2, r, d)

    def ring(*shape):
        return vm((2, half) + shape, BF)

    return dict(
        lens=pltpu.SMEM((2,), jnp.int32), pack=vm((z.rp, d + z.ff), BF),
        x=vm(slots, BF), c=vm(slots, BF), mx=vm((BATCH, z.hb, r, z.cb), BF),
        wvp=vm((BATCH, z.rp, 256), BF), wip=vm((BATCH, 2 * z.rw, z.fc // 2), BF),
        wvs=vm((BATCH, z.rp, 256), BF), wog=vm((BATCH, n, 2 * z.rw, d // 2), BF), wis=vm((BATCH, 2 * z.rw, z.fc // 2), BF),
        wvg=vm((n, z.wt, 128), BF), wv=vm((d, z.fh), BF), wo=vm((d, d), BF), wi=vm((d, z.fc), BF), wu=vm((z.fc, d), BF),
        gain=vm((2, 1, d), F32),
        h1=vm(slots, BF), vl=vm((z.hb, z.long, LANE), BF), vs=vm((z.hb, SHORT, LANE), BF),
        pf=vm((z.hb, r, z.long), F32), pb=vm((z.hb, r, z.long), BF),
        qf=vm((z.hb, r, SHORT), F32), qb=vm((z.hb, r, SHORT), BF),
        mixed=vm((2, z.hb, r, LANE), F32), attn=vm((BATCH, 2, 6, r, 128), BF),
        mid=vm(own, F32), h2=vm(slots, BF),
        hid=vm((2, BATCH * r, z.fc), BF), dup=vm((2, BATCH * r, z.fc), BF),
        dp=vm(slots, BF), db=vm(own, BF), dmid=vm(own, F32),
        dpb=vm((4,) + own, BF), opb=vm((4,) + own, BF), d1b=vm((4,) + own, BF),
        da=vm((2, z.hb, r, LANE), BF), dv=vm((2, BATCH * r, z.fh), BF), dvs=vm((2, z.hb, r, LANE), BF),
        das=vm((2, 2, BATCH, r * 3 // 4, 128), BF), dal=vm((1, 2, BATCH, r * 3 // 4, 128), BF),
        dals=vm((BATCH, 2, r * 3 // 4, 128), BF), dcs=vm((2, BATCH, r * 3 // 2, 128), BF), dcl=vm((2, BATCH, r * 3 // 2, 128), BF),
        gm0=vm((z.hb, r, z.cb), F32), slope=vm((BATCH * r, z.fc), F32),
        gu=vm((z.fc, d), F32), gi=vm((d, z.fc), F32), go=vm((d, z.fh), F32), gv=vm((d, z.fh), F32),
        gis=vm((BATCH, 2 * z.rw, z.fc // 2), BF), gvs=vm((BATCH, z.rw, 256), F32), gos=vm((BATCH, z.rw, 256), F32), gus=vm((z.rf, d), F32),
        outs=vm(own, BF), gts=vm(own, F32), rms=vm((2, 2, r, 128), F32),
        guh=ring(z.rf, 256), gur=ring(z.rf, 256), gih=ring(BATCH * z.rw, 256), gir=ring(BATCH * z.rw, 256),
        guh2=ring(z.rf, d - 256), gur2=ring(z.rf, d - 256), gih2=ring(BATCH * z.rw, d - 256), gir2=ring(BATCH * z.rw, d - 256),
        goh=ring(z.wr + z.fold, 128), gor=ring(z.wr + z.fold, 128), gvh=ring(z.wr + z.fold, 128), gvr=ring(z.wr + z.fold, 128),
        dvh=vm((z.hb, 2, half, r, LANE), BF), dvr=vm((z.hb, 2, half, r, LANE), BF),
        sems=pltpu.SemaphoreType.DMA((z.sems,)),
    )


def layer_kernel(z, names, *refs):
    lens_in, tok, cot, mix_in, gain_1, gain_2, wv_in, wo_in, wi_in, wu_in = refs[:10]
    o_out, o_gt, o_gm, o_gv, o_go, o_gi, o_gu, o_rms, o_pack = refs[10:19]
    k = types.SimpleNamespace(**dict(zip(names, refs[19:])))
    n, r, d = z.n, z.r, z.d
    rows4 = BATCH * r
    rows_o = BATCH * z.rw
    net = Net(n, k.sems)
    p, b, short = net.p, net.b, net.short

    barrier = pltpu.get_barrier_semaphore()
    for device in (net.right, net.left, net.core, net.y, net.far):
        pl.semaphore_signal(barrier, inc=1, device_id=device, device_id_type=MESH)

    x, c, mx, wu, wvp, wip = k.x, k.c, k.mx, k.wu, k.wvp, k.wip

    def span(ref, size, lo=0, hi=None):
        hi = size if hi is None else hi
        return lambda q: ref.at[pl.ds(pl.multiple_of(q * size + lo, 16), hi - lo)]

    wu_span = span(wu, z.rf)
    lens = k.lens
    raw_lens = Local(net, lens_in, lens).start()
    out_pack = Local(net, k.pack, o_pack)
    own_wu = Local(net, wu_in, wu_span(p)).start()
    own_mx = Local(net, mix_in.at[b], mx.at[b]).start()

    def sort_slots(which, into):
        pair = (tok, cot)[which][...].reshape(2 * r, d)
        behind = jnp.where(lens[0] > SHORT, 0, 1)
        place = lax.broadcasted_iota(jnp.int32, (r, 2 * r), 1) - 2 * lax.broadcasted_iota(jnp.int32, (r, 2 * r), 0)
        for g, slot in enumerate((behind, 1 - behind)):
            into[g, b] = dot((place == slot).astype(BF), pair).astype(BF)

    wvs, wis = k.wvs, k.wis
    raw_lens.done()
    place = lax.broadcasted_iota(jnp.int32, (z.rw, d), 1) - lax.broadcasted_iota(jnp.int32, (z.rw, d), 0)
    place = (place == (BATCH * p + b) * z.rw).astype(BF)
    table = [dot(ref[...], place) for ref in (gain_1, gain_2)]
    tail = [table[g][:, i * 256 : (i + 1) * 256] for g in range(2) for i in range(z.gr)]
    tail = jnp.concatenate(tail + [jnp.zeros((z.rp - z.rw - 2 * z.gr, 256), F32)], axis=0)
    held = wv_in[...].astype(F32)
    for j in range(BATCH):
        piece = jnp.concatenate([held[:, j * z.fh : (j + 1) * z.fh], jnp.zeros((z.rw, 256 - z.fh), F32)], axis=1)
        wvs[j] = jnp.concatenate([piece, tail], axis=0).astype(BF)
    wvp[b] = wvs[b]

    held = wi_in[...].astype(F32)
    for j in range(BATCH):
        cols = [held[:, (BATCH * q + j) * z.rf : (BATCH * q + j + 1) * z.rf] for q in range(n)]
        wis[j] = halved(jnp.concatenate(cols, axis=1)).astype(BF)
    wip[b] = wis[b]
    fill = jnp.zeros((1, 128 - z.rw), F32)
    gains = [jnp.concatenate([ref[...].astype(F32), fill], axis=1) for ref in (gain_1, gain_2)]
    gains = jnp.concatenate(gains + [jnp.zeros((z.rp - z.rw - 2, 128), F32)], axis=0)
    for ref, lo in ((wv_in, 0), (wi_in, d)):
        under = jnp.zeros((z.rp - z.rw, ref.shape[1]), F32)
        if lo == 0:
            under = jnp.concatenate([gains, under[:, 128:]], axis=1)
        k.pack[:, lo : lo + ref.shape[1]] = jnp.concatenate([ref[...].astype(F32), under], axis=0).astype(BF)
    out_pack.start()
    sort_slots(0, x)
    pl.semaphore_wait(barrier, 5)

    def first_wu(half):
        ag_wu[half].hop(wu_in.at[(slice(0, cut_f), slice(cut_f, z.rf))[half]])

    def start_x():
        sp_x.start()

    def start_c():
        sort_slots(1, c)
        sp_c.start()

    ex_wv = Exchange(net, lambda j: wvs.at[j], wvp)
    ex_wi = Exchange(net, lambda j: wis.at[j], wip)
    ex_mx = Exchange(net, lambda j: mix_in.at[j], mx)
    sp_x, sp_xs = Spread(net, x.at[0]), Spread(net, x.at[1], short)
    sp_c, sp_cs = Spread(net, c.at[0]), Spread(net, c.at[1], short)
    cut_f = up16(z.rf // 2)
    third_f = up16(cut_f // 2)
    third_i = up16(rows_o // 4)

    def two_rings(ref, size, cut, third):
        return (
            Gather(
                net, span(ref, size, 0, cut), span(ref, size, 0, third), span(ref, size, third, cut),
                lambda k: ref.at[0 : k * cut],
            ),
            Gather(
                net, span(ref, size, cut), span(ref, size, cut, size - third), span(ref, size, size - third),
                lambda k: ref.at[0 : k * (size - cut)],
            ),
        )

    ag_wu = two_rings(wu, z.rf, cut_f, third_f)

    wvg = k.wvg
    cut_v = up16(z.wt // 2)
    ag_wv = Gather(
        net, lambda q: wvg.at[q], lambda q: wvg.at[q, 0:cut_v], lambda q: wvg.at[q, cut_v : z.wt], lambda k: wvg.at[0:k]
    )

    def ready_wv():
        ex_wv.done()
        weights = jnp.concatenate([wvp[j].astype(F32)[0 : z.rw] for j in range(BATCH)], axis=0)
        gains = sum(wvp[j].astype(F32)[z.rw : z.rw + 8] for j in range(BATCH))
        wvg[p] = jnp.concatenate([folded(weights[:, 0 : z.fh]), gains[:, 0:128], gains[:, 128:256]], axis=0).astype(BF)

    wo, wog = k.wo, k.wog
    ag_wo = Gather(
        net, lambda q: wog.at[b, q], lambda q: wog.at[b, q, 0:32], lambda q: wog.at[b, q, 32 : 2 * z.rw],
        lambda k: wog.at[0, 0:k],
    )
    sp_wo = Spread(net, wog)

    def ready_wo():
        wog[b, p] = halved(wo_in[...].astype(F32)).astype(BF)

    def spread_wo():
        ag_wo.done()
        sp_wo.start()

    def wo_done():
        sp_wo.done()
        for q in range(n):
            block = jnp.concatenate([whole(wog[j, q].astype(F32)) for j in range(BATCH)], axis=0).astype(BF)
            for lo, hi, at in folds(q * rows_o, (q + 1) * rows_o):
                wo[at : at + hi - lo] = block[lo - q * rows_o : hi - q * rows_o]

    def pack(ref):
        return jnp.concatenate([whole(ref[j].astype(F32)) for j in range(BATCH)], axis=0).astype(BF)

    wi = k.wi
    cut_i = up16(rows_o // 2)
    ag_wi = two_rings(wi, rows_o, cut_i, third_i)

    def ready_wi():
        ex_wi.done()
        wi[pl.ds(pl.multiple_of(p * rows_o, 16), rows_o)] = pack(wip)

    h1, vl, vs, gain = k.h1, k.vl, k.vs, k.gain
    here = pl.ds(pl.multiple_of(p * r, 16), r)
    twin = (1 - p, b)
    other = pl.ds(pl.multiple_of((1 - p) * r, 16), r)
    cp_vs, cp_dvs = Copies(net, short), Copies(net, short)

    def ready_gains():
        ag_wv.done()
        top = z.wr + z.fold
        table = jnp.sum(wvg[:, top : top + 16].astype(F32), axis=0)
        table = jnp.concatenate([table[0:8], table[8:16]], axis=1)
        for g in range(2):
            gain[g] = jnp.concatenate([table[g * z.gr + i : g * z.gr + i + 1] for i in range(z.gr)], axis=1)
        for q in range(n):
            k.wv[q * z.wr : (q + 1) * z.wr] = unfolded(wvg[q, 0 : z.wr + z.fold])

    def values(g, into):
        for s in range(BATCH):
            h1[g, s] = (unit(x[g, s].astype(F32))[0] * gain[0]).astype(BF)
        value = dot(h1[g].reshape(rows4, d), k.wv[...]).astype(BF)
        for h, block in enumerate(heads_of(value, z)):
            into[h, here, :] = block

    def vl_span(h, lo, hi):
        return lambda q: vl.at[h, pl.ds(pl.multiple_of(q * r + lo, 16), hi - lo), :]

    def vl_size(h):
        return lambda blocks: vl.at[h, 0 : int(blocks * r)]

    ag_v = [
        Gather(net, vl_span(h, 0, r), vl_span(h, 0, r // 2), vl_span(h, r // 2, r), vl_size(h), True) for h in range(z.hb)
    ]

    def ready_values():
        sp_x.done()
        values(0, vl)

    def short_values():
        sp_xs.done()

        @pl.when(short)
        def _():
            values(1, vs)

        cp_vs.start(vs.at[:, here, :], vs.at[:, here, :], twin)
        net.sent.append(lambda: cp_vs.finish(vs.at[:, here, :]))

    pf, pb, qf, qb = k.pf, k.pb, k.qf, k.qb

    def probabilities():
        own_mx.done()
        ex_mx.done()
        for h in range(z.hb):
            total, first = 0.0, None
            for j in range(BATCH):
                e = jnp.exp(mx[j, h].astype(F32))
                pf[h, :, j * z.cb : (j + 1) * z.cb] = e
                total = total + jnp.sum(e, axis=-1, keepdims=True)
                first = total if j == 0 else first

            @pl.when(short)
            def _():
                q = pf[h, :, 0:SHORT] * (1.0 / first)
                qf[h] = q
                qb[h] = q.astype(BF)

            scaled = pf[h] * (1.0 / total)
            pf[h] = scaled
            pb[h] = scaled.astype(BF)

    mixed, attn = k.mixed, k.attn
    sp_a, sp_as = Spread(net, attn.at[:, 0]), Spread(net, attn.at[:, 1], short)

    def mix_slots(g):
        for i, block in enumerate(fold_slots(slots_of([mixed[g, h].astype(BF) for h in range(z.hb)], z))):
            attn[b, g, i] = block

    def mix_head(h):
        ag_v[h].done()
        mixed[0, h] = dot(pb[h], vl[h])

    def mix():
        mix_slots(0)
        sp_a.start()

    def short_mix():
        cp_vs.arrive(vs.at[:, other, :])

        @pl.when(short)
        def _():
            for h in range(z.hb):
                mixed[1, h] = dot(qb[h], vs[h])
            mix_slots(1)

        sp_as.start()

    big, mid, h2, rms = k.gu, k.mid, k.h2, k.rms

    def branch_slots(g):
        big[0:rows4] = dot(folded_heads(attn.at[:, g]), wo[...])
        for s in range(BATCH):
            branch = big[s * r : (s + 1) * r]
            total = x[g, s].astype(F32) + branch
            square = jnp.mean(total * total, axis=-1, keepdims=True) + EPSILON
            h2[g, s] = (total * lax.rsqrt(square) * gain[1]).astype(BF)

            @pl.when(b == s)
            def _():
                mid[g] = total
                rms[0, g] = jnp.broadcast_to(jnp.sqrt(square), (r, 128))
                size = jnp.sqrt(jnp.mean(branch * branch, axis=-1, keepdims=True) + EPSILON)
                rms[1, g] = jnp.broadcast_to(size, (r, 128))

    def branches():
        sp_a.done()
        branch_slots(0)

    def short_branches():
        sp_as.done()

        @pl.when(short)
        def _():
            branch_slots(1)

    hid, dup, dp, op = k.hid, k.dup, k.dp, h2
    halves = (slice(0, r // 2), slice(r // 2, r))
    co_d = [Collect(net, dp.at[0, :, rows], [k.dpb.at[i, 0, rows] for i in range(4)]) for rows in halves]
    co_ds = Collect(net, dp.at[1], [k.dpb.at[i, 1] for i in range(4)], short)
    co_o, co_os = (Collect(net, op.at[g], [k.opb.at[i, g] for i in range(4)], w) for g, w in ((0, None), (1, short)))

    slopes = (k.gi, k.slope)

    def feed(g):
        left = h2[g].reshape(rows4, d)
        for q in range(z.fc // 256):
            cols = slice(q * 256, (q + 1) * 256)
            up = dot(left, wi[:, cols])
            cdf = 0.5 + 0.5 * lax.erf(up * 0.7071067811865476)
            hid[g, :, cols] = (up * cdf).astype(BF)
            slopes[g][0:rows4, cols] = cdf + up * (jnp.exp(-0.5 * up * up) * 0.3989422804014327)

    def feed_back(g):
        down = c[g].reshape(rows4, d)
        for q in range(z.fc // 256):
            cols = slice(q * 256, (q + 1) * 256)
            dup[g, :, cols] = (dot_nt(down, wu[cols, :]) * slopes[g][0:rows4, cols]).astype(BF)
        for q in range(d // 256):
            rows = slice(q * 256, (q + 1) * 256)
            dp[g, :, :, rows] = dot_nt(dup[g], wi[rows, :]).reshape(BATCH, r, 256).astype(BF)

    def feeds():
        for ring in ag_wi:
            ring.done()
        feed(0)

    def short_feeds():
        @pl.when(short)
        def _():
            feed(1)

    def feed_backs():
        for ring in ag_wu:
            ring.done()
        own_wu.done()
        feed_back(0)
        for part in co_d:
            part.start()

    def ready_c():
        sp_c.done()

    def ready_cs():
        sp_cs.done()

    def short_feed_backs():
        @pl.when(short)
        def _():
            feed_back(1)

        co_ds.start()

    gu, gi, gv, go = k.gu, k.gi, k.gv, k.go
    parts = (slice(0, 256), slice(256, d))

    def rows_at(ref, size):
        return lambda q: ref[pl.ds(pl.multiple_of(q * size, 8), size)]

    def two_scatters(ref, size, held, came):
        def block(cols):
            return lambda q: ref[pl.ds(pl.multiple_of(q * size, 8), size), cols]

        return [Scatter(net, block(part), held[i], came[i], up16(size // 2)) for i, part in enumerate(parts)]

    rs_gu = two_scatters(gu, z.rf, (k.guh, k.guh2), (k.gur, k.gur2))
    rs_gi = two_scatters(gi, rows_o, (k.gih, k.gih2), (k.gir, k.gir2))
    rs_gv = Scatter(net, lambda q: folded(rows_at(gv, rows_o)(q)), k.gvh, k.gvr, up16((z.wr + z.fold) // 2))

    def weight_grad(into, left, right, g, half):
        cols = parts[half]
        term = dot_tn(left, right(cols))
        into[:, cols] = into[:, cols] + term if g else term

    def grad_out_of(g, half):
        weight_grad(gu, hid[g], lambda cols: c[g, :, :, cols].reshape(rows4, cols.stop - cols.start), g, half)

    def grad_out(half):
        grad_out_of(0, half)

    def short_grad_out(half):
        @pl.when(short)
        def _():
            grad_out_of(1, half)

    def grad_in_of(g, half):
        weight_grad(gi, h2[g].reshape(rows4, d), lambda cols: dup[g, :, cols], g, half)

    def grad_in(half):
        grad_in_of(0, half)

    def short_grad_in(half):
        @pl.when(short)
        def _():
            grad_in_of(1, half)

    def outs(g):
        for q in range(d // 256):
            cols = slice(q * 256, (q + 1) * 256)
            op[g, :, :, cols] = dot(hid[g], wu[:, cols]).reshape(BATCH, r, 256).astype(BF)

    def finals():
        outs(0)
        co_o.start()

    def short_finals():
        @pl.when(short)
        def _():
            outs(1)

        co_os.start()

    db, dmid = k.db, k.dmid
    das, dal, dcs, dcl = k.das, k.dal, k.dcs, k.dcl
    ex_da = [
        Exchange(net, functools.partial(lambda i, j: das.at[0, i, j], i), dal.at[0, i]) for i in range(2)
    ]
    ex_das = Exchange(net, lambda j: das.at[1, :, j], k.dals, short)
    ex_dc = Exchange(net, lambda j: dcs.at[0, j], dcl.at[0])
    ex_dcs = Exchange(net, lambda j: dcs.at[1, j], dcl.at[1], short)

    def norm_back(upper, values, gain):
        normed, inv = unit(values)
        scaled = upper * gain
        return inv * (scaled - normed * jnp.mean(scaled * normed, axis=-1, keepdims=True))

    def middle(g, collect, rows):
        grad = c[g, b, rows].astype(F32) + norm_back(collect.value(), mid[g, rows], gain[1])
        dmid[g, rows] = grad
        db[g, rows] = grad.astype(BF)

    def attn_back(g, i):
        grad = dot_nt(db[g, halves[i]], wo[...])
        for j in range(BATCH):
            rest = grad[:, BATCH * 128 + j * 64 : BATCH * 128 + (j + 1) * 64]
            das[g, i, j] = folded(jnp.concatenate([grad[:, j * 128 : (j + 1) * 128], rest], axis=1)).astype(BF)

    def columns(g):
        held = db[g].astype(F32)
        for j in range(BATCH):
            dcs[g, j] = folded(held[:, j * z.fh : (j + 1) * z.fh]).astype(BF)
        dcl[g, b] = dcs[g, b]

    def middles(i):
        co_d[i].done()
        middle(0, co_d[i], halves[i])
        attn_back(0, i)
        dal[0, i, b] = das[0, i, b]
        ex_da[i].start()

    def spread_db():
        columns(0)
        ex_dc.start()

    def short_middles():
        co_ds.done()

        @pl.when(short)
        def _():
            middle(1, co_ds, slice(0, r))
            for i in range(2):
                attn_back(1, i)
                k.dals[b, i] = das[1, i, b]

        ex_das.start()

    def short_spread_db():
        @pl.when(short)
        def _():
            columns(1)

        ex_dcs.start()

    da, dvs = k.da, k.dvs

    def mix_back(g, land):
        grad = jnp.concatenate([unfolded(land(j, i).astype(F32)) for j in range(BATCH) for i in range(2)], axis=0)
        for h, block in enumerate(heads_of(grad.astype(BF), z)):
            da[g, h] = block

    def dv_own(h):
        return lambda q: dot_tn(pb[h, :, pl.ds(pl.multiple_of(q * r, 128), r)], da[0, h])

    rs_dv = [Scatter(net, dv_own(h), k.dvh.at[h], k.dvr.at[h], r // 2, True) for h in range(z.hb)]

    def hop_dv(h):
        rs_dv[h].hop()

    def mix_backs():
        for part in ex_da:
            part.done()
        mix_back(0, lambda j, i: dal[0, i, j])

    def dvs_own(h, q):
        return dot_tn(qb[h, :, pl.ds(pl.multiple_of(q * r, 128), r)], da[1, h])

    def short_mix_backs():
        ex_das.done()

        @pl.when(short)
        def _():
            mix_back(1, lambda j, i: k.dals[j, i])
            for h in range(z.hb):
                dvs[0, h] = dvs_own(h, 1 - p).astype(BF)

        cp_dvs.start(dvs.at[0], dvs.at[1], twin)
        net.sent.append(lambda: cp_dvs.finish(dvs.at[0]))

    rs_go = Scatter(net, lambda q: folded(rows_at(go, rows_o)(q)), k.goh, k.gor, up16((z.wr + z.fold) // 2))

    def grad_output_of(g):
        cols = jnp.concatenate([unfolded(dcl[g, j].astype(F32)) for j in range(BATCH)], axis=0).astype(BF)
        total = dot_tn(folded_heads(attn.at[:, g]), cols)
        for lo, hi, at in folds(0, d):
            term = total[at : at + hi - lo]
            go[lo:hi] = go[lo:hi] + term if g else term

    def grad_output():
        ex_dc.done()
        grad_output_of(0)

    def short_grad_output():
        ex_dcs.done()

        @pl.when(short)
        def _():
            grad_output_of(1)

    gms, gm0 = mx, k.gm0
    ex_gm = Exchange(net, lambda j: gms.at[j], o_gm)
    own_gm = Local(net, gms.at[b], o_gm.at[b])

    def grad_mixer():
        for h in range(z.hb):
            delta = jnp.sum(da[0, h].astype(F32) * mixed[0, h], axis=-1, keepdims=True)
            for j in range(BATCH):
                cols = slice(j * z.cb, (j + 1) * z.cb)
                part = pf[h, :, cols] * (dot_nt(da[0, h], vl[h, cols, :]) - delta)
                gms[j, h] = part.astype(BF)
                if j == 0:
                    gm0[h] = part

    def short_grad_mixer():
        @pl.when(short)
        def _():
            for h in range(z.hb):
                delta = jnp.sum(da[1, h].astype(F32) * mixed[1, h], axis=-1, keepdims=True)
                gms[0, h] = (gm0[h] + qf[h] * (dot_nt(da[1, h], vs[h]) - delta)).astype(BF)

        ex_gm.start()
        own_gm.start()

    gis, gvs, gos, gus = k.gis, k.gvs, k.gos, k.gus
    ex_gi, ex_gv, ex_go = (
        Exchange(net, functools.partial(lambda ref, j: ref.at[j], ref), land)
        for ref, land in ((gis, o_gi), (gvs, o_gv), (gos, o_go))
    )
    own_gi, own_gv, own_go = (Local(net, ref.at[b], land.at[b]) for ref, land in ((gis, o_gi), (gvs, o_gv), (gos, o_go)))
    out_gu = Local(net, gus, o_gu)

    def deal(ref, total):
        total = unfolded(total)
        for j in range(BATCH):
            part = total[j * z.rw : (j + 1) * z.rw]
            ref[j] = jnp.concatenate([part, jnp.zeros((z.rw, 256 - z.fh), F32)], axis=1)

    def end_gu():
        gus[...] = jnp.concatenate([ring.done() for ring in rs_gu], axis=1)
        out_gu.start()

    def end_gi():
        total = jnp.concatenate([ring.done() for ring in rs_gi], axis=1)
        for j in range(BATCH):
            gis[j] = halved(total[j * z.rw : (j + 1) * z.rw]).astype(BF)
        ex_gi.start()
        own_gi.start()

    def end_gv():
        deal(gvs, rs_gv.done())
        ex_gv.start()
        own_gv.start()

    def end_go():
        deal(gos, rs_go.done())
        ex_go.start()
        own_go.start()

    dv, d1 = k.dv, dp
    co_1, co_1s = (Collect(net, d1.at[g], [k.d1b.at[i, g] for i in range(4)], w) for g, w in ((0, None), (1, short)))

    def values_back(g, total):
        for s, block in enumerate(slots_of([part.astype(BF) for part in total], z)):
            dv[g, s * r : (s + 1) * r] = block
        d1[g] = dot_nt(dv[g], k.wv[...]).reshape(BATCH, r, d).astype(BF)

    def values_backs():
        total = [ring.done() for ring in rs_dv]
        for part in co_d:
            part.sent_now()
        values_back(0, total)
        co_1.start()

    def short_values_backs():
        cp_dvs.arrive(dvs.at[1])
        co_ds.sent_now()

        @pl.when(short)
        def _():
            values_back(1, [dvs_own(h, p) + dvs[1, h].astype(F32) for h in range(z.hb)])

        co_1s.start()

    def grad_value():
        gv[...] = dot_tn(h1[0].reshape(rows4, d), dv[0])

    def short_grad_value():
        @pl.when(short)
        def _():
            gv[...] += dot_tn(h1[1].reshape(rows4, d), dv[1])

    outs_vm, gts = k.outs, k.gts
    out_rms = Local(net, rms, o_rms)
    out_out = [Local(net, outs_vm.at[g], o_out.at[g], w) for g, w in ((0, None), (1, short))]
    out_gt = [Local(net, gts.at[g], o_gt.at[g], w) for g, w in ((0, None), (1, short))]

    def end_out():
        co_o.done()
        outs_vm[0] = (mid[0] + co_o.value()).astype(BF)
        out_out[0].start()

    def short_end_out():
        co_os.done()

        @pl.when(short)
        def _():
            outs_vm[1] = (mid[1] + co_os.value()).astype(BF)

        out_out[1].start()

    def finish_tokens(g, collect):
        gts[g] = dmid[g] + norm_back(collect.value(), x[g, b].astype(F32), gain[0])

    def end_tokens():
        co_1.done()
        finish_tokens(0, co_1)
        out_gt[0].start()

    def short_end_tokens():
        co_1s.done()

        @pl.when(short)
        def _():
            finish_tokens(1, co_1s)

        out_gt[1].start()

    first_wu(1)
    ex_wv.start()
    first_wu(0)
    ex_wi.start()
    start_x()
    ready_wo()
    ready_wv()
    ag_wv.hop()
    sp_xs.start()
    ag_wo.hop()
    start_c()
    ready_wi()
    ag_wi[1].hop()
    ag_wv.hop()
    ag_wi[0].hop()
    ag_wo.hop()
    sp_cs.start()
    ag_wv.hop()
    sp_x.mid()
    ex_mx.start()
    ag_wi[1].hop()
    ag_wo.hop()
    ag_wv.hop()
    sp_xs.mid()
    ag_wu[0].hop()
    ag_wu[1].hop()
    ready_gains()
    ready_values()
    ag_wo.hop()
    ag_v[1].hop()
    ag_v[2].hop()
    spread_wo()
    ag_v[0].hop()
    ag_v[1].hop()
    ag_v[2].hop()
    ag_v[0].hop()
    ag_v[1].hop()
    short_values()
    ag_v[2].hop()
    probabilities()
    ag_v[0].hop()
    ag_wi[0].hop()
    short_mix()
    sp_c.mid()
    ag_v[1].hop()
    sp_cs.mid()
    ag_v[2].hop()
    ag_v[0].hop()
    ag_wu[0].hop()
    ag_wi[1].hop()
    ready_c()
    mix_head(2)
    sp_wo.mid()
    ag_wi[0].hop()
    ag_wu[1].hop()
    mix_head(1)
    mix_head(0)
    mix()
    sp_as.mid()
    ag_wi[1].hop()
    ag_wu[0].hop()
    wo_done()
    ready_cs()
    short_branches()
    ag_wi[0].hop()
    ag_wu[1].hop()
    sp_a.mid()
    branches()
    feeds()
    feed_backs()
    grad_out(1)
    short_feeds()
    short_grad_out(1)
    rs_gu[1].hop()
    co_d[0].mid()
    short_feed_backs()
    co_d[1].mid()
    grad_in(1)
    short_grad_in(1)
    rs_gi[1].hop()
    grad_out(0)
    grad_in(0)
    rs_gu[1].hop()
    short_grad_in(0)
    middles(0)
    rs_gi[1].hop()
    middles(1)
    short_finals()
    rs_gu[1].hop()
    co_ds.mid()
    short_grad_out(0)
    rs_gu[0].hop()
    rs_gi[0].hop()
    mix_backs()
    hop_dv(0)
    hop_dv(2)
    hop_dv(1)
    rs_gi[1].hop()
    finals()
    co_os.mid()
    hop_dv(0)
    hop_dv(2)
    short_middles()
    hop_dv(1)
    rs_gi[0].hop()
    out_rms.start()
    hop_dv(0)
    short_spread_db()
    hop_dv(2)
    co_o.mid()
    hop_dv(1)
    spread_db()
    grad_mixer()
    short_mix_backs()
    hop_dv(0)
    hop_dv(2)
    short_grad_mixer()
    hop_dv(1)
    short_values_backs()
    grad_output()
    short_grad_output()
    rs_gu[0].hop()
    co_1s.mid()
    rs_go.hop()
    rs_gi[1].hop()
    values_backs()
    grad_value()
    short_grad_value()
    rs_gv.hop()
    rs_go.hop()
    rs_gi[0].hop()
    co_1.mid()
    rs_gv.hop()
    rs_go.hop()
    rs_gi[0].hop()
    rs_gv.hop()
    rs_go.hop()
    rs_gu[0].hop()
    rs_gv.hop()
    short_end_out()
    end_gi()
    end_out()
    rs_gu[1].hop()
    end_go()
    short_end_tokens()
    rs_gu[0].hop()
    end_tokens()
    end_gv()
    end_gu()

    ex_gm.done()
    ex_gi.done()
    ex_gv.done()
    ex_go.done()
    for copy in (own_gm, own_gi, own_gv, own_go, out_gu, out_rms, out_pack, *out_out, *out_gt):
        copy.done()
    for finish_sends in net.sent:
        finish_sends()
    assert net.used == z.sems, net.used


def finish_kernel(
    z, lens_in, outs, gts, gm, gv, go, gi, gu, rms, pack,
    o_out, o_gt, o_gm, o_g1, o_gv, o_go, o_g2, o_gi, o_gu, o_rms_1, o_rms_2,
    v_out, v_gt, v_gm, v_gv, v_gi, v_rms, v_gu, v_go, v_pack,
    s_gt, s_gm, s_gv, s_gi, s_go, s_g1, s_g2, s_rms, lens, sems,
):
    n, r = z.n, z.r
    used = []

    def copy(src, dst):
        used.append(pltpu.make_async_copy(src, dst, sems.at[len(used)]))
        used[-1].start()
        return used[-1]

    in_lens = copy(lens_in, lens)
    in_gm = [copy(gm.at[j], v_gm.at[j]) for j in range(BATCH)]
    in_gt, in_out = copy(gts, v_gt), copy(outs, v_out)
    in_gi, in_gv, in_rms = copy(gi, v_gi), copy(gv, v_gv), copy(rms, v_rms)
    in_gu, in_go = copy(gu, v_gu), copy(go, v_go)
    last = []
    has_short = lax.axis_index("pos") < SHORT // r

    def slots(ref):
        first_long = lens[0] > SHORT
        lower = jnp.where(has_short, ref[1].astype(F32), 0.0)
        upper = ref[0].astype(F32)
        return jnp.where(first_long, upper, lower), jnp.where(first_long, lower, upper)

    in_pack = copy(pack, v_pack)
    for j in range(BATCH):
        in_gm[j].wait()
        for h in range(z.hb):
            s_gm[j * z.hb + h] = v_gm[j, h].astype(F32)
        part = slice(j * z.hb, (j + 1) * z.hb)
        last.append(copy(s_gm.at[part], o_gm.at[part]))
    in_lens.wait()
    in_gt.wait()
    for s, block in enumerate(slots(v_gt)):
        s_gt[:, s, :] = block
    last.append(copy(s_gt, o_gt))
    in_gu.wait()
    last.append(copy(v_gu, o_gu))
    in_out.wait()
    for s, block in enumerate(slots(v_out)):
        o_out[:, s, :] = block.astype(BF)

    def gain_grad(weights, grad, gain):
        ones = jnp.ones((8, grad.shape[1]), F32)
        total = lax.dot_general(
            ones, weights * grad, (((1,), (1,)), ((), ())),
            precision=lax.Precision.HIGHEST, preferred_element_type=F32,
        )
        return total[0:1] / gain

    in_pack.wait()
    gains = v_pack[:, 0:128].astype(F32)[z.rw : z.rw + 2, 0 : z.rw]
    in_gi.wait()
    parts = [whole(v_gi[j].astype(F32)) for j in range(BATCH)]
    s_gi[...] = jnp.concatenate([part[:, q * z.rf : (q + 1) * z.rf] for q in range(n) for part in parts], axis=1)
    last.append(copy(s_gi, o_gi))
    s_g2[...] = gain_grad(v_pack[:, z.d :].astype(F32)[0 : z.rw], s_gi[...], gains[1:2])
    last.append(copy(s_g2, o_g2))
    in_gv.wait()
    s_gv[...] = jnp.concatenate([v_gv[j, :, 0 : z.fh] for j in range(BATCH)], axis=1)
    last.append(copy(s_gv, o_gv))
    s_g1[...] = gain_grad(v_pack[:, 0 : z.d].astype(F32)[0 : z.rw], s_gv[...], gains[0:1])
    last.append(copy(s_g1, o_g1))
    in_go.wait()
    s_go[...] = jnp.concatenate([v_go[j, :, 0 : z.fh] for j in range(BATCH)], axis=1)
    last.append(copy(s_go, o_go))
    in_rms.wait()
    for i, ref in enumerate((o_rms_1, o_rms_2)):
        for s, block in enumerate(slots(v_rms.at[i])):
            s_rms[i, s : s + 1] = jnp.transpose(block)[0:1]
        last.append(copy(s_rms.at[i], ref))
    for one in last:
        one.wait()


def finish(z, lens, results):
    n, r, d = z.n, z.r, z.d
    vm, shape = pltpu.VMEM, jax.ShapeDtypeStruct
    hbm = pl.BlockSpec(memory_space=pl.ANY)
    taken = [(array.shape, array.dtype) for array in results[:8]]
    staged = [((r, 2, d), F32), ((z.heads, r, z.cb), F32), ((z.rw, d), F32), ((z.rw, z.ff), F32), ((z.rw, d), F32)]
    staged += [((1, z.rw), F32), ((1, z.rw), F32), ((2, 2, r), F32)]
    return pl.pallas_call(
        functools.partial(finish_kernel, z),
        out_shape=[
            shape((r, 2, d), BF), shape((r, 2, d), F32), shape((z.heads, r, z.cb), F32), shape((1, z.rw), F32),
            shape((z.rw, d), F32), shape((z.rw, d), F32), shape((1, z.rw), F32), shape((z.rw, z.ff), F32),
            shape((z.rf, d), F32), shape((2, r), F32), shape((2, r), F32),
        ],
        in_specs=[hbm] * 10,
        out_specs=[pl.BlockSpec(memory_space=pltpu.VMEM)] + [hbm] * 10,
        scratch_shapes=[vm(*taken[i]) for i in (0, 1, 2, 3, 5, 7, 6, 4)]
        + [vm(results[8].shape, results[8].dtype)]
        + [vm(*one) for one in staged]
        + [pltpu.SMEM((2,), jnp.int32), pltpu.SemaphoreType.DMA((27,))],
        compiler_params=pltpu.CompilerParams(vmem_limit_bytes=62 << 20),
        name="finish",
    )(lens, *results)


def one_device(
    pos, batch, tokens, seq_lens, mixer, gain_attn, w_value, w_output, gain_ffn, w_in, w_out, cotangent
):
    args = (tokens, seq_lens, mixer, gain_attn, w_value, w_output, gain_ffn, w_in, w_out, cotangent)
    if not fits(pos, batch, tokens, mixer, w_value, w_in, w_out):
        return per_device(*args)
    z = Sizes(pos, tokens, mixer, w_value, w_in, w_out)
    shapes = scratch(z)
    hbm, vmem = pl.BlockSpec(memory_space=pl.ANY), pl.BlockSpec(memory_space=pltpu.VMEM)
    out_shape = [
        jax.ShapeDtypeStruct((2, z.r, z.d), BF),
        jax.ShapeDtypeStruct((2, z.r, z.d), F32),
        jax.ShapeDtypeStruct((BATCH, z.hb, z.r, z.cb), BF),
        jax.ShapeDtypeStruct((BATCH, z.rw, 256), F32),
        jax.ShapeDtypeStruct((BATCH, z.rw, 256), F32),
        jax.ShapeDtypeStruct((BATCH, 2 * z.rw, z.fc // 2), BF),
        jax.ShapeDtypeStruct((z.rf, z.d), F32),
        jax.ShapeDtypeStruct((2, 2, z.r, 128), F32),
        jax.ShapeDtypeStruct((z.rp, z.d + z.ff), BF),
    ]
    gain_attn, gain_ffn = gain_attn.reshape(1, z.rw), gain_ffn.reshape(1, z.rw)
    results = pl.pallas_call(
        functools.partial(layer_kernel, z, list(shapes)),
        out_shape=out_shape,
        in_specs=[hbm, vmem, vmem, hbm] + [vmem] * 5 + [hbm],
        out_specs=[hbm] * len(out_shape),
        scratch_shapes=list(shapes.values()),
        compiler_params=pltpu.CompilerParams(
            collective_id=1, has_side_effects=True, vmem_limit_bytes=62 << 20
        ),
        name="layer",
    )(
        seq_lens,
        tokens,
        cotangent,
        mixer.reshape(BATCH, z.hb, z.r, z.cb),
        gain_attn,
        gain_ffn,
        w_value,
        w_output,
        w_in,
        w_out,
    )
    out, grad_tokens, grad_mixer, grad_1, grad_value, grad_output, grad_2, grad_in, grad_out, rms_1, rms_2 = finish(
        z, seq_lens, results
    )
    return (
        out, grad_tokens, grad_mixer, grad_1.reshape(z.rw), grad_value, grad_output, grad_2.reshape(z.rw),
        grad_in, grad_out, rms_1.T, rms_2.T,
    )


def solution(mesh):
    placed = (
        P("pos", "batch", None),
        P("batch"),
        P(None, "pos", "batch"),
        P(("pos", "batch")),
        P(("pos", "batch"), None),
        P(("pos", "batch"), None),
        P(("pos", "batch")),
        P(("pos", "batch"), None),
        P(("pos", "batch"), None),
        P("pos", "batch", None),
    )
    return jax.shard_map(
        functools.partial(one_device, mesh.shape["pos"], mesh.shape["batch"]),
        mesh=mesh,
        in_specs=placed,
        out_specs=(
            P("pos", "batch", None),
            P("pos", "batch", None),
            P(None, "pos", "batch"),
            P(("pos", "batch")),
            P(("pos", "batch"), None),
            P(("pos", "batch"), None),
            P(("pos", "batch")),
            P(("pos", "batch"), None),
            P(("pos", "batch"), None),
            P("pos", "batch"),
            P("pos", "batch"),
        ),
        check_vma=False,
    )
```
